32 devices in a mesh: section: 2 (over core), dp: 4 (over z), seq: 4 (over y, x).
Axes of the slice: x: 2, y: 2, z: 4, core: 2. Of those that a mesh axis runs over, the one named last changes fastest.
Arguments:
- tokens: bfloat16 [2, 4, 1024, 1024], P(None, 'dp', 'seq'), may hold values from -6 to 6
- cotangent: bfloat16 [2, 4, 1024, 1024], P(None, 'dp', 'seq'), may hold values from -6 to 6
- lengths: int32 [2, 4], P(None, 'dp'), may hold values from 128 to 1024, as said below
- norm_gain: float32 [2, 2, 1024], P('section'), may hold values from 0.5 to 1.5
- norm_bias: float32 [2, 2, 1024], P('section'), may hold values from -1.75 to 1.75
- mixer_in: bfloat16 [2, 1024, 3072], P('section', ('dp', 'seq')), may hold values from -0.1875 to 0.1875
- short_kernel: float32 [2, 3, 3072], P('section'), may hold values from -3.5 to 3.5
- filter_first: float32 [2, 33, 64], P('section'), may hold values from -16 to 16
- filter_second: float32 [2, 64, 64], P('section'), may hold values from -6 to 6
- filter_last: float32 [2, 64, 1024], P('section'), may hold values from -0.0625 to 0.0625
- filter_bias: float32 [2, 1024], P('section'), may hold values from -1.75 to 1.75
- decay_rates: float32 [2, 1024], P('section'), may hold values from 0.00024414062 to 0.0234375
- mixer_out: bfloat16 [2, 1024, 1024], P('section', ('dp', 'seq')), may hold values from -0.1875 to 0.1875
- up_weight: bfloat16 [2, 1024, 4096], P('section', ('dp', 'seq')), may hold values from -0.1875 to 0.1875
- down_weight: bfloat16 [2, 4096, 1024], P('section', ('dp', 'seq')), may hold values from -0.09375 to 0.09375
Outputs:
- block_outputs: float32 [2, 2, 4, 1024, 1024], P('section', None, 'dp', 'seq')
- input_grads: float32 [2, 2, 4, 1024, 1024], P('section', None, 'dp', 'seq')
- grad_norm_gain: float32 [2, 2, 1024], P('section')
- grad_norm_bias: float32 [2, 2, 1024], P('section')
- grad_mixer_in: float32 [2, 1024, 3072], P('section', ('dp', 'seq'))
- grad_short_kernel: float32 [2, 3, 3072], P('section')
- grad_filter_first: float32 [2, 33, 64], P('section')
- grad_filter_second: float32 [2, 64, 64], P('section')
- grad_filter_last: float32 [2, 64, 1024], P('section')
- grad_filter_bias: float32 [2, 1024], P('section')
- grad_mixer_out: float32 [2, 1024, 1024], P('section', ('dp', 'seq'))
- grad_up_weight: float32 [2, 1024, 4096], P('section', ('dp', 'seq'))
- grad_down_weight: float32 [2, 4096, 1024], P('section', ('dp', 'seq'))
The draws below stay inside these ranges and needn't reach their ends.
Inputs may be any that keep to these rules, and one draw needn't show every extreme that they name: `lengths`: each row's length is at least 128; for every dp index, one of the 2 micro-batches holds a row of full length 1024.
All inputs are finite; a program needn't handle non-finite values.
Results may differ from the reference program's by a relative error of at most 0.028.
Values may be sent and summed in bfloat16 or wider, within the bound.
A program may use at most 384 MiB of HBM per device.

```python
import math
import jax
import jax.numpy as jnp
from jax import lax

D = 1024
FF = 4096
EMB = 33
FILT = 64
MB = 2
LROW = 1024
N_DP = 4


def draw_lengths(key, part):
    key = jax.random.fold_in(key, 7)
    key_levels, key_extra, key_full = jax.random.split(key, 3)
    levels = jax.random.randint(key_levels, (MB, N_DP), 0, 4)
    base_len = LROW // jnp.left_shift(jnp.ones((MB, N_DP), jnp.int32), levels)
    extra_len = jax.random.randint(key_extra, (MB, N_DP), 0, max(LROW // 8, 1))
    lengths_drawn = jnp.minimum(base_len + extra_len, LROW)
    chosen = jax.random.randint(key_full, (N_DP,), 0, MB)
    full_row = jnp.arange(MB)[:, None] == chosen[None, :]
    return jnp.where(full_row, LROW, lengths_drawn).astype(jnp.int32)


def shard_levels(rng, shape, cuts, low, largest):
    factor_of, own = 1.0, jax.random.fold_in(rng, 6)
    for axis_at, parts in cuts:
        steps = jnp.exp(jax.random.uniform(jax.random.fold_in(own, axis_at), (parts,), jnp.float32, low / len(cuts), largest / len(cuts)))
        factor_of = factor_of * jnp.repeat(steps, shape[axis_at] // parts).reshape([-1 if axis == axis_at else 1 for axis in range(len(shape))])
    return factor_of


def noise(own_key, extent, spread, most, shards=(), kind=jnp.bfloat16):
    entries = spread * jax.random.normal(own_key, extent, jnp.float32)
    if shards:
        entries = entries * shard_levels(own_key, extent, shards, -0.22, 0.18)
    return jnp.clip(entries, -most, most).astype(kind)


def setup_inputs(seed: int = 0) -> dict:
    splits = jax.random.split(jax.random.key(seed), 16)
    return {
        "tokens": noise(splits[0], (MB, N_DP, LROW, D), 1.0, 6.0, ((1, 4), (2, 4))),
        "cotangent": noise(splits[1], (MB, N_DP, LROW, D), 1.0, 6.0, ((1, 4), (2, 4))),
        "lengths": draw_lengths(jax.random.fold_in(splits[15], 71), 0),
        "norm_gain": jnp.clip(1.0 + 0.1 * jax.random.normal(splits[3], (2, 2, D), jnp.float32), 0.5, 1.5),
        "norm_bias": noise(splits[4], (2, 2, D), 0.3, 1.75, ((0, 2),), jnp.float32),
        "mixer_in": noise(splits[5], (2, D, 3 * D), D ** -0.5, 0.1875, ((0, 2), (1, 16))),
        "short_kernel": noise(splits[6], (2, 3, 3 * D), 0.6, 3.5, ((0, 2),), jnp.float32),
        "filter_first": noise(splits[7], (2, EMB, FILT), 3.0, 16.0, ((0, 2),), jnp.float32),
        "filter_second": noise(splits[8], (2, FILT, FILT), 0.5, 6.0, ((0, 2),), jnp.float32),
        "filter_last": noise(splits[9], (2, FILT, D), (8 * LROW) ** -0.5, 0.0625, ((0, 2),), jnp.float32),
        "filter_bias": noise(splits[10], (2, D), 0.3, 1.75, ((0, 2),), jnp.float32),
        "decay_rates": jnp.clip(jnp.exp(math.log(0.0234375) - 4.564348 * jax.random.uniform(splits[11], (2, D), jnp.float32) ** shard_levels(splits[11], (2, D), ((0, 2),), -0.2, 0.2)), 0.00024414062, 0.0234375),
        "mixer_out": noise(splits[12], (2, D, D), D ** -0.5, 0.1875, ((0, 2), (1, 16))),
        "up_weight": noise(splits[13], (2, D, FF), D ** -0.5, 0.1875, ((0, 2), (1, 16))),
        "down_weight": noise(splits[14], (2, FF, D), FF ** -0.5, 0.09375, ((0, 2), (1, 16))),
    }


precise = lax.Precision.HIGHEST

@jax.custom_vjp
def low(v):
    return lax.optimization_barrier(v.astype(jnp.bfloat16)).astype(jnp.float32)

@jax.custom_vjp
def low_back(v):
    return v

def low_keep(v):
    return (low(v), None)

def low_pass(kept, grad):
    return (grad,)

def back_keep(v):
    return (v, None)

def back_low(kept, grad):
    return (low(grad),)
low.defvjp(low_keep, low_pass)
low_back.defvjp(back_keep, back_low)

def matmul(left, right):
    return jnp.dot(left, right, preferred_element_type=jnp.float32, precision=precise)

def layer_norm(values, gain, shift):
    average = lax.optimization_barrier(jnp.mean(values, axis=-1, keepdims=True))
    centred = values - average
    variance = lax.optimization_barrier(jnp.mean(centred * centred, axis=-1, keepdims=True))
    return centred * lax.rsqrt(variance + 1e-05) * gain + shift

def position_table(length):
    offsets = jnp.arange(length, dtype=jnp.float32)
    frequencies = jnp.linspace(0.0001, 15.0, 16, dtype=jnp.float32)
    angles = 2.0 * math.pi * offsets[:, None] * frequencies[None, :] / length
    return jnp.concatenate([offsets[:, None] / (length - 1), jnp.cos(angles), -jnp.sin(angles)], axis=1)

def filter_taps(first_w, second_w, last_w, rates, length):
    embedding = position_table(length)
    hidden = jnp.sin(matmul(embedding, first_w))
    hidden = jnp.sin(matmul(hidden, second_w))
    offsets = jnp.arange(length, dtype=jnp.float32)
    return matmul(hidden, last_w) * jnp.exp(-offsets[:, None] * rates[None, :])

def long_conv(signal, filter_rows):
    padded_len = 2 * signal.shape[0]
    spectrum = jnp.fft.rfft(signal, n=padded_len, axis=0) * jnp.fft.rfft(filter_rows, n=padded_len, axis=0)
    return jnp.fft.irfft(spectrum, n=padded_len, axis=0)[:signal.shape[0]]

def causal_short(values, kernel):
    padded = jnp.pad(values, ((2, 0), (0, 0)))
    return kernel[0] * values + kernel[1] * padded[1:-1] + kernel[2] * padded[:-2]

def row_forward(row_values, row_length, filter_rows, row_params):
    norm_gains, biases, weight_in, kernel, bias_direct, weight_out, weight_up, weight_down = row_params
    row_mask = (jnp.arange(row_values.shape[0]) < row_length).astype(jnp.float32)[:, None]
    normed = layer_norm(row_values, norm_gains[0], biases[0])
    projected = low_back(matmul(low(normed), weight_in))
    mixed_low = low(low_back(causal_short(projected, kernel)))
    first_part = mixed_low[:, :D]
    second_part = mixed_low[:, D:2 * D]
    value_part = mixed_low[:, 2 * D:]
    product = low(low_back(first_part * value_part))
    filtered = low_back(long_conv(product, filter_rows) + product * bias_direct)
    gated_low = low(low_back(second_part * filtered))
    branch = low_back(matmul(gated_low, weight_out))
    middle = row_values + row_mask * branch
    second_low = low(layer_norm(middle, norm_gains[1], biases[1]))
    hidden_pre = low_back(matmul(second_low, weight_up))
    hidden_low = low(jax.nn.gelu(hidden_pre, approximate=True))
    output = low_back(matmul(hidden_low, weight_down))
    return middle + row_mask * output

def layer(inputs, lengths, params, rates):
    norm_gains, biases, weight_in, kernel, first_w, second_w, last_w, bias_direct, weight_out, weight_up, weight_down = params
    row_len = inputs.shape[2]
    filter_rows = filter_taps(first_w, second_w, last_w, rates, row_len)
    row_params = (norm_gains, biases, weight_in, kernel, bias_direct, weight_out, weight_up, weight_down)
    all_rows = inputs.reshape(-1, row_len, inputs.shape[3])
    all_lengths = lengths.reshape(-1).astype(jnp.int32)

    def run_row(row_pair):
        return row_forward(row_pair[0], row_pair[1], filter_rows, row_params)
    outputs = lax.map(jax.checkpoint(run_row), (all_rows, all_lengths))
    return outputs.reshape(inputs.shape)

def reference(tokens, cotangent, lengths, norm_gain, norm_bias, mixer_in, short_kernel, filter_first, filter_second, filter_last, filter_bias, decay_rates, mixer_out, up_weight, down_weight):
    weights = [item.astype(jnp.float32) for item in (norm_gain, norm_bias, mixer_in, short_kernel, filter_first, filter_second, filter_last, filter_bias, mixer_out, up_weight, down_weight)]
    rates = decay_rates.astype(jnp.float32)

    def section_run(section_index):

        def run(inputs, *params):
            return layer(inputs, lengths, params, rates[section_index])
        return run
    first_params = [item[0] for item in weights]
    second_params = [item[1] for item in weights]
    first_out, first_back = jax.vjp(section_run(0), tokens.astype(jnp.float32), *first_params)
    second_out, second_back = jax.vjp(section_run(1), first_out, *second_params)
    second_grads = second_back(cotangent.astype(jnp.float32))
    first_grads = first_back(second_grads[0])
    stacked = [jnp.stack([first_grads[index], second_grads[index]]) for index in range(len(first_grads))]
    return (jnp.stack([first_out, second_out]), stacked[0], stacked[1], stacked[2], stacked[3], stacked[4], stacked[5], stacked[6], stacked[7], stacked[8], stacked[9], stacked[10], stacked[11])
```

```python
from functools import partial
import math

import jax
import jax.numpy as jnp
import numpy as np
from jax import lax
from jax.experimental import pallas as pl
from jax.experimental.pallas import tpu as pltpu
from jax.sharding import PartitionSpec as P

precise = lax.Precision.HIGHEST
low = jnp.bfloat16
f32 = jnp.float32
MESH = pl.DeviceIdType.MESH


def dot(a, b, dims):
    return lax.dot_general(a, b, (dims, ((), ())), preferred_element_type=f32)


def mm(a, b):
    return dot(a, b, ((1,), (0,)))


def mm_t(a, b):
    return dot(a, b, ((1,), (1,)))


def t_mm(a, b):
    return dot(a, b, ((0,), (0,)))


def norm_stats(x):
    mean = jnp.mean(x, axis=-1, keepdims=True)
    centred = x - mean
    inverse = lax.rsqrt(jnp.mean(centred * centred, axis=-1, keepdims=True) + 1e-05)
    return centred * inverse, inverse


def norm_back(grad, x, gain):
    hat, inverse = norm_stats(x)
    scaled = grad * gain
    back = inverse * (
        scaled
        - jnp.mean(scaled, axis=-1, keepdims=True)
        - hat * jnp.mean(scaled * hat, axis=-1, keepdims=True)
    )
    return back, jnp.sum(grad * hat, 0), jnp.sum(grad, 0)


def gelu_both(x):
    scale = math.sqrt(2.0 / math.pi)
    inner = scale * (x + 0.044715 * x * x * x)
    bend = jnp.tanh(inner)
    value = 0.5 * x * (1.0 + bend)
    slope = 0.5 * (1.0 + bend) + 0.5 * x * (1.0 - bend * bend) * scale * (
        1.0 + 3.0 * 0.044715 * x * x
    )
    return value, slope


def position_table(length):
    offsets = jnp.arange(length, dtype=jnp.float32)
    frequencies = jnp.linspace(0.0001, 15.0, 16, dtype=jnp.float32)
    angles = 2.0 * math.pi * offsets[:, None] * frequencies[None, :] / length
    return jnp.concatenate(
        [offsets[:, None] / (length - 1), jnp.cos(angles), -jnp.sin(angles)], axis=1
    )


def position_rows(length):
    offsets = np.arange(length, dtype=np.float32)
    frequencies = np.linspace(0.0001, 15.0, 16, dtype=np.float32)
    angles = np.float32(2.0 * math.pi) * offsets[:, None] * frequencies[None, :] / np.float32(length)
    return np.concatenate(
        [offsets[:, None] / np.float32(length - 1), np.cos(angles), -np.sin(angles)], axis=1
    )


def filter_taps(first_w, second_w, last_w, rates, length):
    embedding = position_table(length)
    hidden = jnp.sin(jnp.dot(embedding, first_w, precision=precise))
    hidden = jnp.sin(jnp.dot(hidden, second_w, precision=precise))
    offsets = jnp.arange(length, dtype=jnp.float32)
    return jnp.dot(hidden, last_w, precision=precise) * jnp.exp(-offsets[:, None] * rates[None, :])


def wave_tables(length):
    turns = (2 * np.arange(length)[:, None] + 1) * np.arange(length)[None, :] % (4 * length)
    angles = turns * (math.pi / (2 * length))
    both = np.concatenate([np.cos(angles), np.sin(angles)], 0)
    return both.astype(jnp.bfloat16)


def shifted(x, by):
    if by > 0:
        return jnp.pad(x[:-by], ((by, 0), (0, 0)))
    return jnp.pad(x[-by:], ((0, -by), (0, 0)))


def neighbours(me):
    return (me + 1 - 2 * (me % 2), (me + 2) % 4, 3 - me)


def greet(devices):
    barrier = pltpu.get_barrier_semaphore()
    for device in devices:
        pl.semaphore_signal(barrier, inc=1, device_id=device, device_id_type=MESH)
    return len(devices)


def all_here(greeted):
    pl.semaphore_wait(pltpu.get_barrier_semaphore(), greeted)


def in_plane(peers):
    return [{"seq": peer} for peer in peers]


def along_planes():
    here = lax.axis_index("dp")
    return here, here + 1 - 2 * (here % 2), (here + 2) % 4


def other_core():
    return {"section": 1 - lax.axis_index("section")}


def plane_devices():
    _, near, far = along_planes()
    return [{"dp": near}, {"dp": far}]


def add_low(target, source):
    def add(at):
        target[at, :] = (target[at, :].astype(f32) + source[at, :].astype(f32)).astype(low)

    by_rows(target.shape[0], 32, add)


def swap_begin(pairs, core_sems):
    section = lax.axis_index("section")
    copies = [
        remote_to(made.at[1 - section], other, core_sems, at, other_core())
        for at, (made, other) in enumerate(pairs)
    ]
    for copy in copies:
        copy.start()
    return copies


def swap_end(copies, pairs):
    section = lax.axis_index("section")
    for copy, (made, other) in zip(copies, pairs):
        copy.wait_recv()
        for block in range(other.shape[0]):
            add_low(made.at[section, block], other.at[block])


class PlaneSum:
    def __init__(self, pack, mine, arrived, sems, load_sems):
        self.here, self.near, self.far = along_planes()
        self.pack, self.mine, self.arrived = pack, mine, arrived
        self.sems, self.load_sems = sems, load_sems

    def begin(self):
        self.sends = [
            remote_to(self.pack.at[block], self.arrived.at[slot], self.sems, slot, {"dp": self.near})
            for slot, block in enumerate(((self.near + 2) % 4, self.near))
        ]
        for copy in self.sends:
            copy.start()
        self.loads = fetch(
            [(self.pack.at[self.far], self.mine.at[0]), (self.pack.at[self.here], self.mine.at[1])],
            self.load_sems,
        )

    def forward(self):
        self.loads[0].wait()
        self.sends[0].wait_recv()
        add_low(self.mine.at[0], self.arrived.at[0])
        copy = remote_to(self.mine.at[0], self.arrived.at[2], self.sems, 2, {"dp": self.far})
        copy.start()
        self.sends.append(copy)

    def end(self, result):
        self.loads[1].wait()
        self.sends[1].wait_recv()
        self.sends[2].wait_recv()

        def add(at):
            total = self.mine[1, at, :].astype(f32)
            for slot in (1, 2):
                total = total + self.arrived[slot, at, :].astype(f32)
            result[at, :] = total.astype(low)

        by_rows(result.shape[0], 32, add)


def plane_sum_scratch(half_pack):
    _, rows, cols = half_pack.shape
    return [
        pltpu.VMEM((2, rows, cols), low),
        pltpu.VMEM((3, rows, cols), low),
        pltpu.SemaphoreType.DMA((2, 3)),
        pltpu.SemaphoreType.DMA((2,)),
    ]


def remote_to(source, target, sems, slot, device):
    return pltpu.make_async_remote_copy(
        src_ref=source,
        dst_ref=target,
        send_sem=sems.at[0, slot],
        recv_sem=sems.at[1, slot],
        device_id=device,
        device_id_type=MESH,
    )


def remote(source, target, sems, slot, peer):
    return remote_to(source, target, sems, slot, {"seq": peer})


def rows_of(index, count):
    return pl.ds(pl.multiple_of(index * count, count), count)


def half_of(ref, index, part, count):
    half = count // 2
    return ref.at[pl.ds(pl.multiple_of(index * count + part * half, half), half)]


def gather_begin(gather, sems, me, peers, count):
    x, y, _ = peers
    first, second = half_of(gather, me, 0, count), half_of(gather, me, 1, count)
    copies = [
        remote(first, first, sems, 0, x),
        remote(second, second, sems, 2, y),
        remote(second, second, sems, 1, x),
        remote(first, first, sems, 3, y),
    ]
    for copy in copies:
        copy.start()
    return copies


def gather_forward(gather, sems, peers, count):
    x, y, _ = peers
    from_x, from_y = half_of(gather, x, 0, count), half_of(gather, y, 1, count)
    remote(from_x, from_x, sems, 0, x).wait_recv()
    onward = remote(from_x, from_x, sems, 4, y)
    onward.start()
    remote(from_y, from_y, sems, 2, y).wait_recv()
    across = remote(from_y, from_y, sems, 5, x)
    across.start()
    return [onward, across]


def gather_wait(gather, sems, slot, peers, count):
    for part, at in (((1, 1),), ((0, 3),), ((0, 4), (1, 5)))[slot]:
        block = half_of(gather, peers[slot], part, count)
        remote(block, block, sems, at, peers[slot]).wait_recv()


HALF_ORDER = ((0, 0), (1, 1), (0, 1), (1, 0), (2, 0), (2, 1))


def half_rows(index, part, count):
    half = count // 2
    return pl.ds(pl.multiple_of(index * count + part * half, half), half)


def gather_wait_half(gather, sems, slot, part, peers, count):
    at = {(0, 1): 1, (1, 0): 3, (2, 0): 4, (2, 1): 5}.get((slot, part))
    if at is not None:
        block = half_of(gather, peers[slot], part, count)
        remote(block, block, sems, at, peers[slot]).wait_recv()


def reduce_send_half(slot, part, send, recv, sems, peers):
    half = send.shape[1] // 2
    quarter = half // 2
    plan = {
        (0, 0): [(0, half, 0, 0)],
        (1, 1): [(half, half, 1, 1)],
        (2, 0): [(0, quarter, 2, 0), (quarter, quarter, 3, 0)],
        (2, 1): [(half, quarter, 4, 1), (half + quarter, quarter, 5, 1)],
    }.get((slot, part), [])
    copies = [
        remote(
            send.at[slot, pl.ds(start, size)], recv.at[slot, pl.ds(start, size)], sems, at,
            peers[to],
        )
        for start, size, at, to in plan
    ]
    for copy in copies:
        copy.start()
    return copies


def reduce_send(slot, send, recv, sems, peers):
    x, y, _ = peers
    half = send.shape[1] // 2
    quarter = half // 2
    if slot == 2:
        plan = [(0, quarter, 2, x), (half, quarter, 4, y), (quarter, quarter, 3, x)]
        plan.append((half + quarter, quarter, 5, y))
    else:
        plan = [(slot * half, half, slot, (x, y)[slot])]
    copies = [
        remote(
            send.at[slot, pl.ds(start, size)], recv.at[slot, pl.ds(start, size)], sems, at, peer
        )
        for start, size, at, peer in plan
    ]
    for copy in copies:
        copy.start()
    return copies


def reduce_pass(send, recv, sems, peers):
    x, y, _ = peers
    half = send.shape[1] // 2
    quarter = half // 2
    copies = []
    for start, at, source, slot, peer in (
        (half, 4, y, 0, x),
        (0, 2, x, 1, y),
        (half + quarter, 5, y, 0, x),
        (quarter, 3, x, 1, y),
    ):
        rows = pl.ds(start, quarter)
        remote(send.at[2, rows], recv.at[2, rows], sems, at, source).wait_recv()
        add_low(send.at[slot, rows], recv.at[2, rows])
        copy = remote(send.at[slot, rows], recv.at[slot, rows], sems, at + 4, peer)
        copy.start()
        copies.append(copy)
    return copies


def reduce_wait(send, recv, sems, peers):
    x, y, _ = peers
    half = send.shape[1] // 2
    quarter = half // 2
    for slot, start, size, at, peer in (
        (0, 0, half, 0, x),
        (1, half, half, 1, y),
        (0, half, quarter, 8, x),
        (1, 0, quarter, 6, y),
        (0, half + quarter, quarter, 9, x),
        (1, quarter, quarter, 7, y),
    ):
        rows = pl.ds(start, size)
        remote(send.at[slot, rows], recv.at[slot, rows], sems, at, peer).wait_recv()


def by_rows(total, step, body):
    def run(i, carry):
        body(pl.ds(pl.multiple_of(i * step, step), step))
        return carry

    lax.fori_loop(0, total // step, run, 0)


def valid_rows(lengths, start, count):
    at = lax.broadcasted_iota(jnp.int32, (count, 1), 0) + start
    return (at < lengths[0, lax.axis_index("section")]).astype(f32)


def normed_rows(x, gain, shift):
    mean = jnp.mean(x, axis=-1, keepdims=True)
    centred = x - mean
    inverse = lax.rsqrt(jnp.mean(centred * centred, axis=-1, keepdims=True) + 1e-05)
    return centred * inverse * gain + shift


def norm_back_rows(grad, x, gain):
    mean = jnp.mean(x, axis=-1, keepdims=True)
    centred = x - mean
    inverse = lax.rsqrt(jnp.mean(centred * centred, axis=-1, keepdims=True) + 1e-05)
    hat = centred * inverse
    scaled = grad * gain
    back = inverse * (
        scaled
        - jnp.mean(scaled, axis=-1, keepdims=True)
        - hat * jnp.mean(scaled * hat, axis=-1, keepdims=True)
    )
    return back, jnp.sum(grad * hat, axis=0, keepdims=True), jnp.sum(grad, axis=0, keepdims=True)


def norm_into(gather, start, x, gain, shift):
    step = 32

    def body(i, carry):
        rows = pl.ds(pl.multiple_of(i * step, step), step)
        at = pl.ds(pl.multiple_of(start + i * step, step), step)
        gather[at, :] = normed_rows(x[rows, :].astype(f32), gain, shift).astype(low)
        return carry

    lax.fori_loop(0, x.shape[0] // step, body, 0)


def masked_into(gather, start, grad, lengths):
    step = 32

    def body(i, carry):
        rows = pl.ds(pl.multiple_of(i * step, step), step)
        at = pl.ds(pl.multiple_of(start + i * step, step), step)
        value = grad[rows, :].astype(f32) * valid_rows(lengths, start + i * step, step)
        gather[at, :] = value.astype(low)
        return carry

    lax.fori_loop(0, grad.shape[0] // step, body, 0)


def add_parts(own, recv, x, start, lengths):
    def body(rows):
        total = own[rows, :] + recv[0, rows, :].astype(f32) + recv[1, rows, :].astype(f32)
        mask = valid_rows(lengths, start + rows.start, 32)
        own[rows, :] = x[rows, :].astype(f32) + mask * total

    by_rows(own.shape[0], 32, body)


def norm_back_parts(own, recv, grad, x, gain, sums):
    sums[...] = jnp.zeros(sums.shape, f32)

    def body(rows):
        total = own[rows, :] + recv[0, rows, :].astype(f32) + recv[1, rows, :].astype(f32)
        back, gain_sum, shift_sum = norm_back_rows(total, x[rows, :].astype(f32), gain)
        own[rows, :] = grad[rows, :].astype(f32) + back
        sums[0:1, :] += gain_sum
        sums[1:2, :] += shift_sum

    by_rows(own.shape[0], 32, body)


def fetch(pairs, sems, first=0):
    copies = [
        pltpu.make_async_copy(source, target, sems.at[first + at])
        for at, (source, target) in enumerate(pairs)
    ]
    for copy in copies:
        copy.start()
    return copies


def weight_pairs_mixer(pack, win, wout):
    rows, cols = wout.shape[2], wout.shape[3] // 4
    split = win.shape[3]
    pairs = [(pack.at[:, :, :, pl.ds(0, split)], win)]
    for q in range(4):
        pairs.append(
            (
                pack.at[:, :, pl.ds(q * rows, rows), pl.ds(split, cols)],
                wout.at[:, :, :, pl.ds(q * cols, cols)],
            )
        )
    return pairs


def half_pairs_mixer(half_pack, win, wout):
    rows, cols = wout.shape[2], wout.shape[3] // 4
    split = win.shape[3]
    section = lax.axis_index("section")
    pairs = [(win.at[section], half_pack.at[:, :, pl.ds(0, split)])]
    for q in range(4):
        pairs.append(
            (
                wout.at[section, :, :, pl.ds(q * cols, cols)],
                half_pack.at[:, pl.ds(q * rows, rows), pl.ds(split, cols)],
            )
        )
    return pairs


class ChipGather:
    def __init__(self, own, pack, plane_sems, core_sems):
        self.section = lax.axis_index("section")
        here, near, far = along_planes()
        self.pack, self.plane_sems, self.core_sems = pack, plane_sems, core_sems
        self.near, self.far = near, far
        self.order = (here, near, far, (near + 2) % 4)
        self.own = own
        self.sends = []

    def move(self, at, sems, slot, device):
        block = self.pack.at[self.section, self.order[at]]
        copy = remote_to(self.own if at == 0 else block, block, sems, slot, device)
        copy.start()
        self.sends.append(copy)

    def to_core(self, slot):
        self.move(slot, self.core_sems, slot, other_core())

    def begin(self, load_sem):
        self.move(0, self.plane_sems, 1, {"dp": self.far})
        self.move(0, self.plane_sems, 0, {"dp": self.near})
        self.to_core(0)
        self.keep = pltpu.make_async_copy(
            self.own, self.pack.at[self.section, self.order[0]], load_sem
        )
        self.keep.start()

    def arrived(self, slot):
        block = self.pack.at[self.section, self.order[slot + 1]]
        remote_to(block, block, self.plane_sems, slot, {"dp": self.near}).wait_recv()

    def forward(self):
        self.arrived(1)
        self.move(2, self.plane_sems, 2, {"dp": self.near})
        self.to_core(2)
        self.arrived(0)
        self.to_core(1)

    def end(self):
        self.arrived(2)
        self.to_core(3)
        self.keep.wait()
        for slot in range(4):
            block = self.pack.at[1 - self.section, self.order[slot]]
            remote_to(block, block, self.core_sems, slot, other_core()).wait_recv()


def sine_pair(x):
    turns = jnp.floor(x * (2.0 / math.pi) + 0.5)
    rest = x - turns * 1.5703125
    rest = rest - turns * 4.837512969970703125e-4
    rest = rest - turns * 7.54978995489188e-8
    square = rest * rest
    sine = -1.9515295891e-4 * square + 8.3321608736e-3
    sine = (sine * square - 1.6666654611e-1) * square * rest + rest
    cosine = 2.443315711809948e-5 * square - 1.388731625493765e-3
    cosine = (cosine * square + 4.166664568298827e-2) * square * square - 0.5 * square + 1.0
    halves = jnp.floor(turns * 0.5)
    odd = turns - 2.0 * halves
    back = halves - 2.0 * jnp.floor(halves * 0.5)
    swapped = odd > 0.5
    side = 1.0 - 2.0 * back
    wave = jnp.where(swapped, cosine, sine) * side
    slope = jnp.where(swapped, -sine, cosine) * side
    return wave, slope


def network_rows(small, embedding, network, taps_low, i):
    step = 256
    waves1, waves2, steep1, steep2 = network
    knots = waves1.shape[1]
    pair = (pl.ds(i * step, step), pl.ds(embedding.shape[0] // 2 + i * step, step))

    def layer(sources, weights, waves, steep):
        inner = jnp.concatenate([dot_exact(item, weights) for item in sources], 1)
        wave, slope = sine_pair(inner)
        for at, rows in enumerate(pair):
            cols = slice(at * knots, (at + 1) * knots)
            waves[rows, :] = wave[:, cols]
            steep[rows, :] = slope[:, cols]

    layer([embedding[rows, 0:64] for rows in pair], small[64:128, 128:192], waves1, steep1)
    layer([waves1[rows, :] for rows in pair], small[64:128, 0:64], waves2, steep2)
    for rows in pair:
        times = lax.broadcasted_iota(jnp.int32, (step, 1), 0) + rows.start
        fade = jnp.exp(-times.astype(f32) * small[154:155, :])
        taps_low[rows, :] = (dot_exact(waves2[rows, :], small[0:64, :]) * fade).astype(low)


def ff_blocks(
    gather, wup, wdown, value, slope, result_out, send, recv, gather_sems, reduce_sems, me, peers,
    pause,
):
    count, width = result_out.shape
    half = wup.shape[3]
    sends = []
    for slot, part in ((None, None), *HALF_ORDER):
        if slot is None:
            rows, sent = rows_of(me, count), None
        else:
            rows = half_rows(peers[slot], part, count)
            sent = slice(part * count // 2, (part + 1) * count // 2)
            gather_wait_half(gather, gather_sems, slot, part, peers, count)

        def hidden(i, carry):
            cols = pl.ds(pl.multiple_of(i * 256, 256), 256)
            for h in range(2):
                pre = mm(gather[rows, :], wup[h, :, :, cols].reshape(width, 256))
                after, steep = gelu_both(pre)
                at = pl.ds(pl.multiple_of(h * half + i * 256, 256), 256)
                value[rows, at] = after.astype(low)
                slope[rows, at] = steep.astype(low)
            return carry

        lax.fori_loop(0, half // 256, hidden, 0)
        for h in range(2):
            cols = slice(h * width // 2, (h + 1) * width // 2)
            out = mm(value[rows, :], wdown[h].reshape(2 * half, width // 2))
            if slot is None:
                result_out[:, cols] = out
            else:
                send[slot, sent, cols] = out.astype(low)
        if slot is not None:
            sends += reduce_send_half(slot, part, send, recv, reduce_sems, peers)
            pause(slot, part)
    return sends


def mixer_forward_kernel(
    s, gathers, x, *refs
):
    if gathers:
        (
            cotangent, embedding, lengths, w_in, w_out, w_up, w_down, gain, shift, tap_rows, first_w,
            second_w, last_w, direct, rates, waves_hbm, back_hbm,
            pack_out, ff_out, late_out, par_out, small_out, next_pack_out, ff_part_out,
            *refs,
        ) = refs
        network_outs, next_outs, refs = refs[:5], refs[5:10], refs[10:]
        second_out, value_out, slope_out, result_out, *refs = refs
        (
            *refs, waves1, waves2, steep1, steep2, taps_low, pack, ff_all, late, next_pack, core_sems,
            plane_sems, ff_core_sems, ff_plane_sems, next_core_sems, next_plane_sems, late_sems,
            pack_sems, mixer_parts, ff_parts, par_all, small_all, stage_in, stage_out, stage_up,
            in_sems, out_sems, up_sems, down_sems, par_sems, small_sems,
            second, ff_send, ff_recv, second_sems, ff_sems, network_sems,
        ) = refs
        x = x.at[lax.axis_index("section"), 0]
        cotangent = cotangent.at[lax.axis_index("section"), 0]
        network = (waves1, waves2, steep1, steep2)
    else:
        par_all, small_all, lengths, weights_hbm, filt_hbm, waves_hbm, back_hbm, *refs = refs
    (
        normed_out, proj_out, stream_out, prod_out, spec_out, filtered_out, gated_out, middle_out,
        gather, win, wout, filt, waves, back, proj, proj_low, streams, prod, spec, mixed, filtered,
        gated, send, recv, gather_sems, reduce_sems, load_sems, store_sems,
    ) = refs
    par, small = par_all.at[s], small_all.at[s]
    me = lax.axis_index("seq")
    peers = neighbours(me)
    count, width = x.shape
    length = gather.shape[0]
    chans = prod.shape[1]
    half = win.shape[3]
    if gathers:
        section = lax.axis_index("section")
        targets = shuffle_targets(section, me, peers)
        greeted = greet([device for _, _, device in targets] + plane_devices())
    else:
        greeted = greet(in_plane(peers[:2]))
    tables = fetch([(waves_hbm, waves), (back_hbm, back)], load_sems)
    sends = []
    if gathers:
        shuffle_stage(w_in, w_out, w_up, stage_in, stage_out, stage_up)
        parameters_stage(
            me, par_all.at[section], small_all.at[section], gain, shift, tap_rows, first_w, second_w,
            last_w, direct, rates,
        )
        all_here(greeted)
        sends += shuffle_send(
            section, me, targets, (stage_in, stage_out, stage_up, w_down), (mixer_parts, ff_parts),
            (par_all, small_all), (in_sems, out_sems, up_sems, down_sems, par_sems, small_sems),
        )
        mixer_pack = ChipGather(mixer_parts.at[0], pack, plane_sems, core_sems)
        ff_pack = ChipGather(ff_parts.at[0], ff_all, ff_plane_sems, ff_core_sems)
        for sems, item in ((par_sems, par_all), (small_sems, small_all)):
            block = item.at[1 - section]
            remote_to(block, block, sems, 0, other_core()).wait_recv()
        norm_into(gather, me * count, x, par[0:1, :], par[1:2, :])
        shuffle_wait_mixer(section, me, targets, mixer_parts, stage_in, in_sems, out_sems)
        mixer_pack.begin(pack_sems.at[0])
        sends += gather_begin(gather, gather_sems, me, peers, count)
        masked_into(late, me * count, cotangent, lengths)
    else:
        weights = fetch(weight_pairs_mixer(weights_hbm, win, wout), load_sems, 2)
        filt_load = fetch([(filt_hbm, filt)], load_sems, 7)
        norm_into(gather, me * count, x, par[0:1, :], par[1:2, :])
        all_here(greeted)
        sends += gather_begin(gather, gather_sems, me, peers, count)
    proj[0:8, :] = jnp.zeros((8, proj.shape[1]), f32)
    tile_rows = 256

    def filter_spectrum(i, carry):
        rows = pl.ds(pl.multiple_of(i * tile_rows, tile_rows), tile_rows)
        filt[rows, :] = mm(waves[rows, :], taps_low[...])
        return carry

    stores = []
    if gathers:
        network_rows(small, embedding, network, taps_low, 0)
    sends += gather_forward(gather, gather_sems, peers, count)
    if gathers:
        sends += gather_begin(late, late_sems, me, peers, count)
        mixer_pack.forward()
        shuffle_wait_ff(section, me, targets, ff_parts, stage_up, up_sems, down_sems)
        ff_pack.begin(pack_sems.at[1])
        network_rows(small, embedding, network, taps_low, 1)
        tables[0].wait()
        lax.fori_loop(0, 2 * length // tile_rows, filter_spectrum, 0)
        network_stores = fetch(list(zip((filt, *network), network_outs)), network_sems)
        mixer_pack.end()
        weights = fetch(weight_pairs_mixer(pack, win, wout), load_sems, 2)
        stores += fetch(
            [
                (pack, pack_out),
                (par_all, par_out),
                (small_all, small_out),
                (ff_parts.at[1], ff_part_out),
            ],
            pack_sems,
            4,
        )
    else:
        tables[0].wait()
    weights[0].wait()
    for slot in (None, 0, 1, 2):
        source = me if slot is None else peers[slot]
        if slot is not None:
            gather_wait(gather, gather_sems, slot, peers, count)
        block = gather[rows_of(source, count), :]
        for h in range(2):
            proj[pl.ds(pl.multiple_of(source * count + 8, 8), count), h * half : (h + 1) * half] = mm(
                block, win[h].reshape(width, half)
            )
    if gathers:
        sends += gather_forward(late, late_sems, peers, count)
    step = 128

    def short_conv(i, carry):
        start = pl.multiple_of(i * step, step)
        for g in range(3):
            cols = slice(g * chans, (g + 1) * chans)
            tile = proj[pl.ds(start, step + 8), cols]
            proj_low[pl.ds(start, step), cols] = tile[8:].astype(low)
            value = (
                small[144 + 3 * g : 145 + 3 * g, :] * tile[8:]
                + small[145 + 3 * g : 146 + 3 * g, :] * pltpu.roll(tile, 1, 0)[8:]
                + small[146 + 3 * g : 147 + 3 * g, :] * pltpu.roll(tile, 2, 0)[8:]
            )
            streams[pl.ds(start, step), cols] = value.astype(low)
        first = streams[pl.ds(start, step), 0:chans].astype(f32)
        third = streams[pl.ds(start, step), 2 * chans : 3 * chans].astype(f32)
        prod[pl.ds(start, step), :] = (first * third * valid_rows(lengths, start, step)).astype(low)
        return carry

    lax.fori_loop(0, length // step, short_conv, 0)
    stores += fetch(
        [(gather, normed_out), (proj_low, proj_out), (streams, stream_out), (prod, prod_out)],
        store_sems,
    )
    if not gathers:
        filt_load[0].wait()

    def spectrum(i, carry):
        up = pl.ds(pl.multiple_of(i * tile_rows, tile_rows), tile_rows)
        down = pl.ds(pl.multiple_of(i * tile_rows + length, tile_rows), tile_rows)
        prod_cos = mm(waves[up, :], prod[...])
        prod_sin = mm(waves[down, :], prod[...])
        filt_cos, filt_sin = filt[up, :], filt[down, :]
        spec[up, :] = prod_cos.astype(low)
        spec[down, :] = prod_sin.astype(low)
        mixed[up, :] = (prod_cos * filt_cos - prod_sin * filt_sin).astype(low)
        mixed[down, :] = (prod_cos * filt_sin + prod_sin * filt_cos).astype(low)
        return carry

    lax.fori_loop(0, length // tile_rows, spectrum, 0)
    tables[1].wait()
    for load in weights[1:]:
        load.wait()
    for slot in (2, 0, 1, None):
        target = me if slot is None else peers[slot]
        rows = rows_of(target, count)
        value = mm(back[rows, :], mixed[...]) * (1.0 / length)
        value = value + small[153:154, :] * prod[rows, :].astype(f32)
        filtered[rows, :] = value
        gate = (streams[rows, chans : 2 * chans].astype(f32) * value).astype(low)
        gated[rows, :] = gate
        outs = [mm(gate, wout[h].reshape(chans, width // 2)) for h in range(2)]
        for h in range(2):
            cols = slice(h * width // 2, (h + 1) * width // 2)
            if slot is None:
                middle_out[:, cols] = outs[h]
            else:
                send[slot, :, cols] = outs[h].astype(low)
        if slot is not None:
            sends += reduce_send(slot, send, recv, reduce_sems, peers)
    if gathers:
        ff_pack.forward()
        for slot in range(3):
            gather_wait(late, late_sems, slot, peers, count)
        stores += fetch([(late, late_out)], pack_sems, 2)
    sends += reduce_pass(send, recv, reduce_sems, peers)
    stores += fetch(
        [(spec, spec_out), (filtered, filtered_out), (gated, gated_out)],
        store_sems,
        4,
    )
    if gathers:
        for store in network_stores:
            store.wait()
        for i in range(2):
            network_rows(small_all.at[1], embedding, network, taps_low, i)
        lax.fori_loop(0, 2 * length // tile_rows, filter_spectrum, 0)
        network_stores = fetch(list(zip((filt, *network), next_outs)), network_sems)
    reduce_wait(send, recv, reduce_sems, peers)
    add_parts(middle_out, recv, x, me * count, lengths)
    if gathers:
        next_mixer = ChipGather(mixer_parts.at[1], next_pack, next_plane_sems, next_core_sems)
        norm_into(second, me * count, middle_out, par[2:3, :], par[3:4, :])
        sends += gather_begin(second, second_sems, me, peers, count)
        sends += gather_forward(second, second_sems, peers, count)
        ff_pack.end()
        next_mixer.begin(pack_sems.at[8])
        stores += fetch([(ff_all, ff_out)], pack_sems, 3)
        rows_up = ff_all.shape[2] // 2
        value, slope = waves.at[pl.ds(0, length)], waves.at[pl.ds(length, length)]

        def pause(slot, part):
            if (slot, part) == (1, 1):
                next_mixer.forward()

        sends += ff_blocks(
            second, ff_all.at[:, :, pl.ds(0, rows_up)], ff_all.at[:, :, pl.ds(rows_up, rows_up)],
            value, slope, result_out, ff_send, ff_recv, second_sems, ff_sems, me, peers, pause,
        )
        sends += reduce_pass(ff_send, ff_recv, ff_sems, peers)
        stores += fetch([(second, second_out), (value, value_out), (slope, slope_out)], pack_sems, 9)
        next_mixer.end()
        stores += fetch([(next_pack, next_pack_out)], pack_sems, 12)
        reduce_wait(ff_send, ff_recv, ff_sems, peers)
        add_parts(result_out, ff_recv, middle_out, me * count, lengths)
        sends += mixer_pack.sends + ff_pack.sends + next_mixer.sends
        stores += network_stores
    for copy in sends:
        copy.wait_send()
    for store in stores:
        store.wait()


def ff_turn_kernel(
    s, cotangent, x, par_all, lengths, pack, late_hbm,
    half_out, result_out, middle_grad_out, sums_out,
    gather, late, wup, wdown, value, pre, wgrad, other, send, recv, send_back, recv_back,
    gather_sems, reduce_sems, load_sems, store_sems, back_sems, core_sems,
):
    par = par_all.at[s]
    grad = cotangent.at[lax.axis_index("section"), 0]
    me = lax.axis_index("seq")
    peers = neighbours(me)
    count, width = x.shape
    half = wup.shape[3]
    rows_up = wup.shape[2]
    greeted = greet(in_plane(peers[:2]) + [other_core()])
    loads = fetch(
        [
            (pack.at[:, :, pl.ds(0, rows_up), :], wup),
            (pack.at[:, :, pl.ds(rows_up, wdown.shape[2]), :], wdown),
            (late_hbm, late),
        ],
        load_sems,
    )
    norm_into(gather, me * count, x, par[2:3, :], par[3:4, :])
    all_here(greeted)
    sends = gather_begin(gather, gather_sems, me, peers, count)
    for load in loads:
        load.wait()
    for slot, part in ((None, None), *HALF_ORDER):
        if slot is None:
            rows, sent = rows_of(me, count), None
        else:
            rows = half_rows(peers[slot], part, count)
            sent = slice(part * count // 2, (part + 1) * count // 2)
            gather_wait_half(gather, gather_sems, slot, part, peers, count)

        def hidden(i, carry):
            cols = pl.ds(pl.multiple_of(i * rows_up, rows_up), rows_up)
            for h in range(2):
                block = h * (half // rows_up) + i
                at = pl.ds(pl.multiple_of(block * rows_up, rows_up), rows_up)
                after, steep = gelu_both(
                    mm(gather[rows, :], wup[h, :, :, cols].reshape(width, rows_up))
                )
                value[rows, at] = after.astype(low)
                back = mm_t(late[rows, : width // 2], wdown[0, block]) + mm_t(
                    late[rows, width // 2 :], wdown[1, block]
                )
                pre[rows, at] = (back * steep).astype(low)
            return carry

        lax.fori_loop(0, half // rows_up, hidden, 0)

        def through(i, carry):
            cols = pl.ds(pl.multiple_of(i * rows_up, rows_up), rows_up)
            back = mm_t(pre[rows, :half], wup[0, i]) + mm_t(pre[rows, half:], wup[1, i])
            if slot is None:
                middle_grad_out[:, cols] = back
            else:
                send_back[slot, sent, cols] = back.astype(low)
            return carry

        lax.fori_loop(0, width // rows_up, through, 0)
        if slot is None:
            sends += gather_forward(gather, gather_sems, peers, count)
        else:
            sends += reduce_send_half(slot, part, send_back, recv_back, back_sems, peers)
    for slot in (2, 0, 1, None):
        rows = rows_of(me if slot is None else peers[slot], count)
        for h in range(2):
            cols = slice(h * width // 2, (h + 1) * width // 2)
            out = mm(value[rows, :], wdown[h].reshape(2 * half, width // 2))
            if slot is None:
                result_out[:, cols] = out
            else:
                send[slot, :, cols] = out.astype(low)
    sends += reduce_pass(send_back, recv_back, back_sems, peers)
    for slot in (2, 0, 1):
        sends += reduce_send(slot, send, recv, reduce_sems, peers)

    def weights(i, carry):
        cols = pl.ds(pl.multiple_of(i * rows_up, rows_up), rows_up)
        for h in range(2):
            wgrad[h, i, 0:rows_up, :] = t_mm(
                gather[:, cols], pre[:, h * half : (h + 1) * half]
            ).astype(low)
            wgrad[h, i, rows_up : 2 * rows_up, :] = t_mm(
                value[:, cols], late[:, h * width // 2 : (h + 1) * width // 2]
            ).astype(low)
        return carry

    lax.fori_loop(0, width // rows_up, weights, 0)
    swapped = [(wgrad, other)]
    swaps = swap_begin(swapped, core_sems)
    sends += swaps
    sends += reduce_pass(send, recv, reduce_sems, peers)
    reduce_wait(send_back, recv_back, back_sems, peers)
    norm_back_parts(middle_grad_out, recv_back, grad, x, par[2:3, :], sums_out)
    swap_end(swaps, swapped)
    stores = fetch([(wgrad.at[lax.axis_index("section")], half_out)], store_sems)
    reduce_wait(send, recv, reduce_sems, peers)
    add_parts(result_out, recv, x, me * count, lengths)
    for copy in sends:
        copy.wait_send()
    for store in stores:
        store.wait()


def ff_backward_kernel(
    s, grad, middle, par_all, lengths, pack, second_hbm, value_hbm, slope_hbm, earlier, out0, out1,
    half_out, middle_grad_out, sums_out, summed, block_outputs,
    gather, wup, wdown, second, value, slope, pre, wgrad, other, send, recv, gather_sems,
    reduce_sems, load_sems, store_sems, mine, arrived, plane_sems, sum_sems, core_sems, layer_sems,
    keep_sems,
):
    par = par_all.at[s]
    me = lax.axis_index("seq")
    peers = neighbours(me)
    count, width = grad.shape
    greeted = greet(in_plane(peers[:2]) + plane_devices() + [other_core()])
    half = wup.shape[3]
    units = 2 * half
    up_rows = wup.shape[2]
    loads = fetch(
        [
            (pack.at[:, :, pl.ds(0, up_rows), :], wup),
            (pack.at[:, :, pl.ds(up_rows, wdown.shape[2]), :], wdown),
            (slope_hbm, slope),
            (second_hbm, second),
            (value_hbm, value),
        ],
        load_sems,
    )
    masked_into(gather, me * count, grad, lengths)
    all_here(greeted)
    sends = gather_begin(gather, gather_sems, me, peers, count)
    plane_sum = PlaneSum(earlier, mine, arrived, plane_sems, sum_sems)
    plane_sum.begin()
    by_layer(True, ((out0, out1, block_outputs),), layer_sems, keep_sems)
    for load in loads[:3]:
        load.wait()
    for slot, part in ((None, None), *HALF_ORDER):
        if slot is None:
            rows, sent = rows_of(me, count), None
        else:
            rows = half_rows(peers[slot], part, count)
            sent = slice(part * count // 2, (part + 1) * count // 2)
            gather_wait_half(gather, gather_sems, slot, part, peers, count)

        def hidden(i, carry):
            cols = pl.ds(pl.multiple_of(i * up_rows, up_rows), up_rows)
            back = mm_t(gather[rows, : width // 2], wdown[0, i]) + mm_t(
                gather[rows, width // 2 :], wdown[1, i]
            )
            pre[rows, cols] = (back * slope[rows, cols].astype(f32)).astype(low)
            return carry

        lax.fori_loop(0, units // up_rows, hidden, 0)

        def through(i, carry):
            cols = pl.ds(pl.multiple_of(i * up_rows, up_rows), up_rows)
            back = mm_t(pre[rows, :half], wup[0, i]) + mm_t(pre[rows, half:], wup[1, i])
            if slot is None:
                middle_grad_out[:, cols] = back
            else:
                send[slot, sent, cols] = back.astype(low)
            return carry

        lax.fori_loop(0, width // up_rows, through, 0)
        if slot is None:
            sends += gather_forward(gather, gather_sems, peers, count)
        else:
            sends += reduce_send_half(slot, part, send, recv, reduce_sems, peers)
    plane_sum.forward()
    for load in loads[3:]:
        load.wait()

    def weights(i, carry):
        cols = pl.ds(pl.multiple_of(i * up_rows, up_rows), up_rows)
        for h in range(2):
            wgrad[h, i, 0:up_rows, :] = t_mm(
                second[:, cols], pre[:, h * half : (h + 1) * half]
            ).astype(low)
            wgrad[h, i, up_rows : 2 * up_rows, :] = t_mm(
                value[:, cols], gather[:, h * width // 2 : (h + 1) * width // 2]
            ).astype(low)
        return carry

    lax.fori_loop(0, width // up_rows, weights, 0)
    swapped = [(wgrad, other)]
    swaps = swap_begin(swapped, core_sems)
    sends += swaps
    sends += reduce_pass(send, recv, reduce_sems, peers)
    swap_end(swaps, swapped)
    stores = fetch([(wgrad.at[lax.axis_index("section")], half_out)], store_sems)
    plane_sum.end(summed)
    sends += plane_sum.sends
    reduce_wait(send, recv, reduce_sems, peers)
    norm_back_parts(middle_grad_out, recv, grad, middle, par[2:3, :], sums_out)
    by_layer(False, ((out0, out1, block_outputs),), layer_sems, keep_sems)
    for copy in sends:
        copy.wait_send()
    for store in stores:
        store.wait()


def t_mm_exact(a, b):
    return lax.dot_general(
        a, b, (((0,), (0,)), ((), ())), preferred_element_type=f32, precision=precise
    )


def mm_t_exact(a, b):
    return lax.dot_general(
        a, b, (((1,), (1,)), ((), ())), preferred_element_type=f32, precision=precise
    )


def dot_exact(a, b):
    return jnp.dot(a, b, preferred_element_type=f32, precision=precise)


def by_layer(begin, triples, layer_sems, keep_sems):
    section = lax.axis_index("section")
    for index in range(2):

        @pl.when(section == index)
        def _():
            for at, (first, second, target) in enumerate(triples):
                kept, sent = (first, second) if index == 0 else (second, first)
                slot = target.at[index]
                copies = (
                    pltpu.make_async_copy(kept, slot, keep_sems.at[at]),
                    remote_to(sent, slot, layer_sems, at, other_core()),
                )
                for copy in copies:
                    if begin:
                        copy.start()
                    else:
                        copy.wait()


def mixer_backward_kernel(
    s, grad, x, par_all, small_all, embedding, late, lengths, pack, filt_hbm, waves_hbm, back_hbm, normed_hbm, proj_hbm,
    stream_hbm, prod_hbm, spec_hbm, filtered_hbm, gated_hbm, waves1_hbm, waves2_hbm, steep1_hbm,
    steep2_hbm, earlier,
    half_out, small_out, input_grad_out, summed,
    gather, win, wout, filt, waves, back, normed, proj, streams, prod, spec, filtered, gated,
    gated_grad, filtered_grad, both, grad_spec, grad_sum, filter_grad, mixed, proj_grad, wgrad_in, wgrad_out_part,
    other_in, other_out, waves1, waves2, steep1, steep2, sums, taps_sum, send, recv, gather_sems, reduce_sems, load_sems, store_sems,
    mine, arrived, plane_sems, sum_sems, core_sems,
):
    par, small = par_all.at[s], small_all.at[s]
    me = lax.axis_index("seq")
    peers = neighbours(me)
    if s == 0:
        x = x.at[lax.axis_index("section"), 0]
    count, width = grad.shape
    greeted = greet(in_plane(peers[:2]) + plane_devices() + [other_core()])
    length = gather.shape[0]
    chans = prod.shape[1]
    half = win.shape[3]
    depth = win.shape[2]
    loads = fetch(
        weight_pairs_mixer(pack, win, wout)
        + [
            (stream_hbm, streams),
            (waves_hbm, waves),
            (filt_hbm, filt),
            (spec_hbm, spec),
            (back_hbm, back),
            (prod_hbm, prod),
            (filtered_hbm, filtered),
            (proj_hbm, proj),
            (normed_hbm, normed),
            (gated_hbm, gated),
            (waves1_hbm, waves1),
            (waves2_hbm, waves2),
            (steep1_hbm, steep1),
            (steep2_hbm, steep2),
        ],
        load_sems,
    )
    masked_into(gather, me * count, grad, lengths)
    all_here(greeted)
    sends = gather_begin(gather, gather_sems, me, peers, count)
    plane_sum = PlaneSum(earlier, mine, arrived, plane_sems, sum_sems)
    plane_sum.begin()
    for load in loads[1:6]:
        load.wait()
    tile_rows = 256
    for slot in (None, 0, 1, 2):
        source = me if slot is None else peers[slot]
        rows = rows_of(source, count)
        if slot is not None:
            gather_wait(gather, gather_sems, slot, peers, count)
        value = (
            mm_t(gather[rows, : width // 2], wout[0].reshape(chans, width // 2))
            + mm_t(gather[rows, width // 2 :], wout[1].reshape(chans, width // 2))
        ).astype(low)
        gated_grad[rows, :] = value
        filtered_grad[rows, :] = (
            value.astype(f32) * streams[rows, chans : 2 * chans].astype(f32)
        ).astype(low)
        if slot is None:
            sends += gather_forward(gather, gather_sems, peers, count)
            for load in loads[6:]:
                load.wait()
            loads[0].wait()
        if slot == 2:
            plane_sum.forward()

        def spectrum(i, carry):
            up = pl.ds(pl.multiple_of(i * tile_rows, tile_rows), tile_rows)
            down = pl.ds(pl.multiple_of(i * tile_rows + length, tile_rows), tile_rows)
            fg_cos = mm(waves[up, rows], filtered_grad[rows, :])
            fg_sin = mm(waves[down, rows], filtered_grad[rows, :])
            if slot is not None:
                fg_cos = fg_cos + grad_sum[up, :]
                fg_sin = fg_sin + grad_sum[down, :]
            if slot != 2:
                grad_sum[up, :] = fg_cos
                grad_sum[down, :] = fg_sin
            else:
                filt_cos, filt_sin = filt[up, :], filt[down, :]
                grad_spec[up, :] = fg_cos.astype(low)
                grad_spec[down, :] = fg_sin.astype(low)
                both[up, :] = (filt_cos * fg_cos + filt_sin * fg_sin).astype(low)
                both[down, :] = (filt_cos * fg_sin - filt_sin * fg_cos).astype(low)
            return carry

        lax.fori_loop(0, length // tile_rows, spectrum, 0)
    mixed[pl.ds(length, 8), :] = jnp.zeros((8, mixed.shape[1]), f32)

    def streams_back(i, carry):
        rows = pl.ds(pl.multiple_of(i * tile_rows, tile_rows), tile_rows)
        value = mm(back[rows, :], both[...]) * (1.0 / length)
        fg = filtered_grad[rows, :].astype(f32)
        prod_grad = (value + small[153:154, :] * fg).astype(low).astype(f32)
        mixed[rows, 0:chans] = (
            (prod_grad * streams[rows, 2 * chans : 3 * chans].astype(f32)).astype(low).astype(f32)
        )
        mixed[rows, chans : 2 * chans] = (
            (gated_grad[rows, :].astype(f32) * filtered[rows, :]).astype(low).astype(f32)
        )
        mixed[rows, 2 * chans : 3 * chans] = (
            (prod_grad * streams[rows, 0:chans].astype(f32)).astype(low).astype(f32)
        )
        return carry + jnp.sum(fg * prod[rows, :].astype(f32), axis=0, keepdims=True)

    small_out[...] = jnp.zeros(small_out.shape, f32)
    small_out[153:154, :] = lax.fori_loop(
        0, length // tile_rows, streams_back, jnp.zeros((1, chans), f32)
    )
    step = 128
    for slot in (2, 0, 1, None):
        target = me if slot is None else peers[slot]

        def short_back(i, carry):
            start = pl.multiple_of(target * count + i * step, step)
            for g in range(3):
                cols = slice(g * chans, (g + 1) * chans)
                tile = mixed[pl.ds(start, step + 8), cols]
                now = tile[:step]
                after = pltpu.roll(tile, step + 7, 0)[:step]
                later = pltpu.roll(tile, step + 6, 0)[:step]
                proj_grad[pl.ds(start, step), cols] = (
                    small[144 + 3 * g : 145 + 3 * g, :] * now
                    + small[145 + 3 * g : 146 + 3 * g, :] * after
                    + small[146 + 3 * g : 147 + 3 * g, :] * later
                ).astype(low)
            return carry

        lax.fori_loop(0, count // step, short_back, 0)
        rows = rows_of(target, count)

        def through(i, carry):
            cols = pl.ds(pl.multiple_of(i * depth, depth), depth)
            value = mm_t(proj_grad[rows, :half], win[0, i]) + mm_t(proj_grad[rows, half:], win[1, i])
            if slot is None:
                input_grad_out[:, cols] = value
            else:
                send[slot, :, cols] = value.astype(low)
            return carry

        lax.fori_loop(0, width // depth, through, 0)
        if slot is not None:
            sends += reduce_send(slot, send, recv, reduce_sems, peers)

    def weights(i, carry):
        cols = pl.ds(pl.multiple_of(i * depth, depth), depth)
        for h in range(2):
            wgrad_in[h, i] = t_mm(normed[:, cols], proj_grad[:, h * half : (h + 1) * half]).astype(
                low
            )
        return carry

    lax.fori_loop(0, width // depth, weights, 0)
    for h in range(2):
        value = t_mm(gated[...], gather[:, h * width // 2 : (h + 1) * width // 2]).astype(low)
        wgrad_out_part[h] = value.reshape(wgrad_out_part.shape[1:])
    swapped = [(wgrad_in, other_in), (wgrad_out_part, other_out)]
    swaps = swap_begin(swapped, core_sems)
    sends += swaps
    sends += reduce_pass(send, recv, reduce_sems, peers)
    taps_sum[...] = jnp.zeros(taps_sum.shape, f32)

    def tap_sums(i, carry):
        start = pl.multiple_of(i * step, step)
        for g in range(3):
            cols = slice(g * chans, (g + 1) * chans)
            tile = mixed[pl.ds(start, step + 8), cols]
            seen = proj[pl.ds(start, step), cols].astype(f32)
            for at in range(3):
                shift = pltpu.roll(tile, step + 8 - at, 0)[:step] if at else tile[:step]
                taps_sum[8 * at : 8 * at + 8, cols] += jnp.sum(
                    (seen * shift).reshape(step // 8, 8, chans), axis=0
                )
        return carry

    lax.fori_loop(0, length // step, tap_sums, 0)

    def filter_spectrum(i, carry):
        up = pl.ds(pl.multiple_of(i * tile_rows, tile_rows), tile_rows)
        down = pl.ds(pl.multiple_of(i * tile_rows + length, tile_rows), tile_rows)
        prod_cos, prod_sin = spec[up, :].astype(f32), spec[down, :].astype(f32)
        fg_cos, fg_sin = grad_spec[up, :].astype(f32), grad_spec[down, :].astype(f32)
        both[up, :] = (prod_cos * fg_cos + prod_sin * fg_sin).astype(low)
        both[down, :] = (prod_cos * fg_sin - prod_sin * fg_cos).astype(low)
        return carry

    lax.fori_loop(0, length // tile_rows, filter_spectrum, 0)

    def filter_back(i, carry):
        rows = pl.ds(pl.multiple_of(i * tile_rows, tile_rows), tile_rows)
        times = lax.broadcasted_iota(jnp.int32, (tile_rows, 1), 0) + i * tile_rows
        fade = jnp.exp(-times.astype(f32) * small[154:155, :])
        filter_grad[rows, :] = mm(back[rows, :], both[...]) * (1.0 / length) * fade
        return carry

    lax.fori_loop(0, length // tile_rows, filter_back, 0)
    small_out[0:64, :] = t_mm_exact(waves2[...], filter_grad[...])
    back2 = mm_t_exact(filter_grad[...], small[0:64, :]) * steep2[...]
    small_out[64:128, 0:64] = t_mm_exact(waves1[...], back2)
    back1 = mm_t_exact(back2, small[64:128, 0:64]) * steep1[...]
    small_out[64:128, 128:192] = t_mm_exact(embedding[:, 0:64], back1)
    for g in range(3):
        for at in range(3):
            small_out[144 + 3 * g + at : 145 + 3 * g + at, :] = jnp.sum(
                taps_sum[8 * at : 8 * at + 8, g * chans : (g + 1) * chans], axis=0, keepdims=True
            )
    swap_end(swaps, swapped)
    stores = fetch(half_pairs_mixer(half_out, wgrad_in, wgrad_out_part), store_sems)
    plane_sum.end(summed)
    sends += plane_sum.sends
    reduce_wait(send, recv, reduce_sems, peers)
    norm_back_parts(input_grad_out, recv, grad, x, par[0:1, :], sums)
    for q in range(width // chans):
        cols = slice(q * chans, (q + 1) * chans)
        small_out[128 + 2 * q : 130 + 2 * q, :] = sums[:, cols]
        small_out[136 + 2 * q : 138 + 2 * q, :] = late[:, cols]
    for copy in sends:
        copy.wait_send()
    for store in stores:
        store.wait()


def run_kernel(kernel, name, collective_id, operands, in_vmem, outs, out_vmem, scratch, flops):
    inside = pl.BlockSpec(memory_space=pltpu.VMEM)
    outside = pl.BlockSpec(memory_space=pl.ANY)
    scalars = pl.BlockSpec(memory_space=pltpu.SMEM)
    return pl.pallas_call(
        kernel,
        out_shape=[jax.ShapeDtypeStruct(shape, kind) for shape, kind in outs],
        in_specs=[
            scalars if item.dtype == jnp.int32 else inside if at in in_vmem else outside
            for at, item in enumerate(operands)
        ],
        out_specs=[inside if at in out_vmem else outside for at in range(len(outs))],
        scratch_shapes=scratch,
        compiler_params=pltpu.CompilerParams(
            collective_id=collective_id, has_side_effects=True, vmem_limit_bytes=60 * 2**20
        ),
        cost_estimate=pl.CostEstimate(flops=flops, bytes_accessed=2**25, transcendentals=0),
        name=name,
    )(*operands)


def exchange_scratch(count, width):
    return [pltpu.VMEM((3, count, width), low), pltpu.VMEM((3, count, width), low)]


def exchange_semaphores(count):
    return [pltpu.SemaphoreType.DMA((2, count)), pltpu.SemaphoreType.DMA((count,))]


def semaphores(loads, stores):
    return [
        pltpu.SemaphoreType.DMA((2, 6)),
        pltpu.SemaphoreType.DMA((2, 10)),
        pltpu.SemaphoreType.DMA((loads,)),
        pltpu.SemaphoreType.DMA((stores,)),
    ]


def mixer_weights_scratch(pack, width):
    _, dp_count, depth, cols = pack.shape
    return [
        pltpu.VMEM((2, dp_count, depth, 3 * cols // 4), low),
        pltpu.VMEM((2, dp_count, depth // 4, cols), low),
    ]


def mixer_forward(s, x, lengths, weights, waves, back, gathered):
    gathers = gathered is not None
    count, width = x.shape[-2:]
    length = waves.shape[1]
    chans, half = width // 4, width // 2
    knots, dp_count = chans // 4, lax.axis_size("dp")
    pack_shape = (2, dp_count, width // dp_count, half)
    pack = jax.ShapeDtypeStruct(pack_shape, low)
    vm, dma = pltpu.VMEM, pltpu.SemaphoreType.DMA
    outs = [
        ((length, width), low),
        ((length, 3 * chans), low),
        ((length, 3 * chans), low),
        ((length, chans), low),
        ((2 * length, chans), low),
        ((length, chans), f32),
        ((length, chans), low),
        ((count, width), f32),
    ]
    more = []
    if gathers:
        cotangent, embedding = gathered
        depth = weights[0].shape[0]
        units = 2 * half
        ff_shape = (2, dp_count, 2 * width // dp_count, half)
        half_in = 3 * chans // 2
        filters = [((2 * length, chans), f32), *[((length, knots), f32)] * 4]
        outs = [
            (pack_shape, low),
            (ff_shape, low),
            ((length, width), low),
            ((2, 8, width), f32),
            ((2, 160, chans), f32),
            (pack_shape, low),
            (ff_shape[2:], low),
            *filters,
            *filters,
            ((length, width), low),
            ((length, units), low),
            ((length, units), low),
            ((count, width), f32),
        ] + outs
        more = [
            *[vm((length, knots), f32)] * 4,
            vm((length, chans), low),
            vm(pack_shape, low),
            vm(ff_shape, low),
            vm((length, width), low),
            vm(pack_shape, low),
            *[dma((2, 4)), dma((2, 3))] * 3,
            dma((2, 6)),
            dma((13,)),
            vm((2, *pack_shape[2:]), low),
            vm((2, *ff_shape[2:]), low),
            vm((2, 8, width), f32),
            vm((2, 160, chans), f32),
            vm((2, 4, depth, half_in), low),
            vm((2, 4 * depth, half_in // 3), low),
            vm((2, 4, depth, half), low),
            dma((2, 7)),
            dma((2, 1)),
            dma((2, 7)),
            dma((2, 1)),
            dma((2, 1)),
            dma((2, 1)),
            vm((length, width), low),
            *exchange_scratch(count, width),
            dma((2, 6)),
            dma((2, 10)),
            dma((5,)),
        ]
        operands = (cotangent, embedding, lengths, *weights, waves, back)
        inside = range(len(operands) - 1)
        out_inside = (len(outs) - 9, len(outs) - 1)
    else:
        par, small, weights, filt = weights
        operands = (par, small, lengths, weights, filt, waves, back)
        inside = range(3)
        out_inside = (len(outs) - 1,)
    return run_kernel(
        partial(mixer_forward_kernel, s, gathers),
        "opening" if gathers else "mixer_forward",
        1 + s,
        (x, *operands),
        inside,
        outs,
        out_inside,
        [vm((length, width), low)]
        + mixer_weights_scratch(pack, width)
        + [
            vm((2 * length, chans), f32),
            vm((2 * length, length), low),
            vm((length, 2 * length), low),
            vm((length + 8, 3 * chans), f32),
            vm((length, 3 * chans), low),
            vm((length, 3 * chans), low),
            vm((length, chans), low),
            vm((2 * length, chans), low),
            vm((2 * length, chans), low),
            vm((length, chans), f32),
            vm((length, chans), low),
        ]
        + exchange_scratch(count, width)
        + semaphores(8, 7)
        + more,
        10**10,
    )


def ff_turn(s, cotangent, x, par, lengths, pack, late):
    count, width = x.shape
    _, dp_count, rows, half = pack.shape
    length, units = 4 * count, 2 * half
    vm = pltpu.VMEM
    return run_kernel(
        partial(ff_turn_kernel, s),
        "ff_turn",
        4,
        (cotangent, x, par, lengths, pack, late),
        range(3),
        [(pack.shape[1:], low), ((count, width), f32), ((count, width), f32), ((2, width), f32)],
        (1, 2, 3),
        [vm((length, width), low)] * 2
        + [vm((2, dp_count, rows // 2, half), low)] * 2
        + [vm((length, units), low)] * 2
        + [vm(pack.shape, low), vm(pack.shape[1:], low)]
        + exchange_scratch(count, width) * 2
        + semaphores(3, 1)
        + [pltpu.SemaphoreType.DMA((2, 10)), pltpu.SemaphoreType.DMA((2, 1))],
        3 * 10**10,
    )


def ff_backward(s, grad, middle, par, lengths, pack, second, value, slope, earlier, results):
    count, width = grad.shape
    _, dp_count, rows, half = pack.shape
    length, units = value.shape
    vm = pltpu.VMEM
    weights = [vm((2, dp_count, rows // 2, half), low)] * 2
    return run_kernel(
        partial(ff_backward_kernel, s),
        "ff_backward",
        5,
        (grad, middle, par, lengths, pack, second, value, slope, earlier, *results),
        (0, 1, 2, 9, 10),
        [
            (pack.shape[1:], low),
            ((count, width), f32),
            ((2, width), f32),
            (earlier.shape[1:], low),
            ((2, count, width), f32),
        ],
        (1, 2, 3),
        [vm((length, width), low)]
        + weights
        + [vm((length, width), low)]
        + [vm((length, units), low)] * 3
        + [vm(pack.shape, low), vm(pack.shape[1:], low)]
        + exchange_scratch(count, width)
        + semaphores(5, 1)
        + plane_sum_scratch(earlier)
        + [pltpu.SemaphoreType.DMA((2, 1))]
        + exchange_semaphores(1),
        2 * 10**10,
    )


def mixer_backward(
    s, grad, x, par, small, embedding, late, lengths, pack, waves, back, kept, earlier
):
    normed, proj, streams, prod, spec, filtered, gated, filt, *network = kept
    count, width = grad.shape
    length, chans = prod.shape
    knots = network[0].shape[1]
    vm = pltpu.VMEM
    weights = mixer_weights_scratch(pack, width)
    return run_kernel(
        partial(mixer_backward_kernel, s),
        "mixer_backward",
        7 + s,
        (grad, x, par, small, embedding, late, lengths, pack, filt, waves, back, normed, proj,
         streams, prod, spec, filtered, gated, *network, earlier),
        range(6),
        [
            (pack.shape[1:], low),
            (small.shape[1:], f32),
            ((count, width), f32),
            (earlier.shape[1:], low),
        ],
        (1, 2, 3),
        [vm((length, width), low)]
        + weights
        + [
            vm((2 * length, chans), f32),
            vm((2 * length, length), low),
            vm((length, 2 * length), low),
            vm((length, width), low),
            vm((length, 3 * chans), low),
            vm((length, 3 * chans), low),
            vm((length, chans), low),
            vm((2 * length, chans), low),
            vm((length, chans), f32),
            vm((length, chans), low),
            vm((length, chans), low),
            vm((length, chans), low),
            vm((2 * length, chans), low),
            vm((2 * length, chans), low),
            vm((2 * length, chans), f32),
            vm((length, chans), f32),
            vm((length + 8, 3 * chans), f32),
            vm((length, 3 * chans), low),
        ]
        + weights
        + [vm(item.shape[1:], low) for item in weights]
        + [vm((length, knots), f32)] * 4
        + [vm((2, width), f32), vm((24, 3 * chans), f32)]
        + exchange_scratch(count, width)
        + semaphores(19, 5)
        + plane_sum_scratch(earlier)
        + [pltpu.SemaphoreType.DMA((2, 2))],
        2 * 10**10,
    )


def shuffle_stage(w_in, w_out, w_up, stage_in, stage_out, stage_up):
    depth, chans = w_in.shape[0], w_out.shape[1] // 4
    count = lax.axis_size("dp")
    half_in = stage_in.shape[3]
    piece = chans // count
    for h in range(2):
        for j in range(4):
            for c in range(0, half_in, 2 * piece):
                pair = []
                for col in (c, c + piece):
                    g, d = divmod((h * half_in + col) // piece, count)
                    at = ((g * count + d) * 4 + j) * piece
                    pair.append(w_in[:, at : at + piece].astype(f32))
                stage_in[h, j, :, c : c + 2 * piece] = jnp.concatenate(pair, 1).astype(low)
            for d in range(2):
                at = ((2 * h + d) * 4 + j) * chans
                stage_up[h, j, :, d * chans : (d + 1) * chans] = w_up[:, at : at + chans]
    part = half_in // 3
    for h in range(2):
        for q in range(4):
            at = (h * 4 + q) * part
            stage_out[h, q * depth : (q + 1) * depth, :] = w_out[:, at : at + part]


def parameters_stage(me, par, small, gain, shift, taps, first, second, last, direct, rates):
    chans = small.shape[1]
    count = lax.axis_size("dp")
    piece = chans // count
    width = last.shape[2]
    par[0:1, :] = gain[0, 0:1, :]
    par[1:2, :] = shift[0, 0:1, :]
    par[2:3, :] = gain[0, 1:2, :]
    par[3:4, :] = shift[0, 1:2, :]
    par[4:8, :] = jnp.zeros((4, width), f32)
    small[64:160, :] = jnp.zeros((96, chans), f32)
    small[64:128, 0:64] = second[0]
    for row in range(first.shape[0]):
        small[64 + row : 65 + row, 128:192] = first[row]
    for j in range(4):

        @pl.when(me == j)
        def _():
            for d in range(0, count, 2):
                cols = slice(d * piece, (d + 2) * piece)

                def picked(ref, rows, base=0):
                    at = [base + ((d + k) * 4 + j) * piece for k in range(2)]
                    return jnp.concatenate([ref[rows, a : a + piece] for a in at], 1)

                small[0:64, cols] = picked(last.at[0], slice(0, 64))
                for g in range(3):
                    for tap in range(3):
                        row = 144 + 3 * g + tap
                        small[row : row + 1, cols] = picked(
                            taps.at[tap], slice(0, 1), g * width
                        )
                small[153:154, cols] = picked(direct, slice(0, 1))
                small[154:155, cols] = picked(rates, slice(0, 1))


def shuffle_send(section, me, targets, sources, parts, parameters, sems):
    stage_in, stage_out, stage_up, w_down = sources
    mixer_parts, ff_parts = parts
    in_sems, out_sems, up_sems, down_sems, par_sems, small_sems = sems
    depth, half_in = stage_in.shape[2:]
    half = stage_up.shape[3]
    copies = [
        remote_to(item.at[section], item.at[section], at, 0, other_core())
        for item, at in zip(parameters, (par_sems, small_sems))
    ]
    for e, (t, seq, device) in enumerate(targets):
        target = mixer_parts.at[section, rows_of(me, depth), pl.ds(0, half_in)]
        copies.append(remote_to(stage_in.at[t, seq], target, in_sems, e, device))
    target = mixer_parts.at[section, :, pl.ds(half_in, half_in // 3)]
    copies.append(remote_to(stage_out.at[1 - section], target, out_sems, 0, other_core()))
    for e, (t, seq, device) in enumerate(targets):
        target = ff_parts.at[section, rows_of(me, depth), :]
        copies.append(remote_to(stage_up.at[t, seq], target, up_sems, e, device))
    cols = pl.ds(pl.multiple_of((1 - section) * half, half), half)
    target = ff_parts.at[section, pl.ds(4 * depth, 4 * depth), :]
    copies.append(remote_to(w_down.at[:, cols], target, down_sems, 0, other_core()))
    for copy in copies:
        copy.start()
    mixer_parts[section, rows_of(me, depth), 0:half_in] = stage_in[section, me]
    mixer_parts[section, :, half_in:] = stage_out[section]
    ff_parts[section, rows_of(me, depth), :] = stage_up[section, me]
    cols = pl.ds(pl.multiple_of(section * half, half), half)
    ff_parts[section, 4 * depth : 8 * depth, :] = w_down[:, cols]
    return copies


def shuffle_wait_mixer(section, me, targets, parts, stage_in, in_sems, out_sems):
    depth, half_in = stage_in.shape[2:]
    for e, (t, seq, device) in enumerate(targets):
        block = parts.at[t, rows_of(seq, depth), pl.ds(0, half_in)]
        remote_to(block, block, in_sems, e, device).wait_recv()
    block = parts.at[1 - section, :, pl.ds(half_in, half_in // 3)]
    remote_to(block, block, out_sems, 0, other_core()).wait_recv()


def shuffle_wait_ff(section, me, targets, parts, stage_up, up_sems, down_sems):
    depth = stage_up.shape[2]
    for e, (t, seq, device) in enumerate(targets):
        block = parts.at[t, rows_of(seq, depth), :]
        remote_to(block, block, up_sems, e, device).wait_recv()
    block = parts.at[1 - section, pl.ds(4 * depth, 4 * depth), :]
    remote_to(block, block, down_sems, 0, other_core()).wait_recv()


def shuffle_targets(section, me, peers):
    targets = [(section, peer, {"seq": peer}) for peer in peers]
    targets.append((1 - section, me, other_core()))
    targets += [(1 - section, peer, {**other_core(), "seq": peer}) for peer in peers]
    return targets


def finish_kernel(
    vec0, vec1, mixer0, mixer1, ff0, ff1, grad0, grad1,
    input_grads, got_in, got_out, got_up, got_down, vec_out,
    mine0, arrived0, plane_sems0, sum_sems0, mine1, arrived1, plane_sems1, sum_sems1,
    vec_other, vec_sum, vec_arrived, vec_all, stage_mixer, stage_ff, own_sems, load_sems,
    layer_sems, keep_sems, vec_core_sems, vec_sum_sems, vec_plane_sems, vec_seq_sems, in_sems, out_sems, up_sems, down_sems,
):
    section = lax.axis_index("section")
    me = lax.axis_index("seq")
    here, near, far = along_planes()
    planes = (near, far, (near + 2) % 4)
    peers = neighbours(me)
    depth, half_in = got_in.shape[2:]
    targets = shuffle_targets(section, me, peers)
    greeted = greet([device for _, _, device in targets] + [{"dp": plane} for plane in planes])
    middle = mixer0.shape[2] // 2
    chunks = (pl.ds(0, middle), pl.ds(middle, middle))
    in_cols = (pl.ds(0, middle), pl.ds(middle, half_in - middle))

    def columns(e, at):
        t, seq, device = targets[e]
        return remote_to(
            stage_mixer.at[t, rows_of(seq, depth), in_cols[at]],
            got_in.at[section, me, :, in_cols[at]],
            in_sems,
            2 * e + at,
            device,
        )

    out_columns = remote_to(
        stage_mixer.at[1 - section, :, pl.ds(half_in, half_in // 3)], got_out.at[section], out_sems,
        0, other_core(),
    )

    def send_layer(s, at):
        for index in range(2):

            @pl.when(section == index)
            def _():
                for e in range(3) if index == s else range(3, 7):
                    columns(e, at).start()
                if at == 1 and index != s:
                    out_columns.start()

    all_here(greeted)
    for index, vec in enumerate((vec1, vec0)):

        @pl.when(section == index)
        def _():
            remote_to(vec, vec_other, vec_core_sems, 0, other_core()).start()

    sends = []
    vec_swap = remote_to(vec_other, vec_other, vec_core_sems, 0, other_core())
    vec_swap.wait_recv()
    sends.append(vec_swap)

    @pl.when(section == 0)
    def _():
        vec_sum[...] = vec0[...] + vec_other[...]

    @pl.when(section == 1)
    def _():
        vec_sum[...] = vec1[...] + vec_other[...]

    count = 4
    chunk = vec_sum.shape[0] // count
    moves = [
        remote_to(
            vec_sum.at[rows_of(plane, chunk)], vec_arrived.at[slot], vec_sum_sems, slot,
            {"dp": plane},
        )
        for slot, plane in enumerate(planes)
    ]
    for copy in moves:
        copy.start()
    sends += moves
    plane_sums = [
        PlaneSum(mixer0.at[:, :, chunks[0]], mine0, arrived0, plane_sems0, sum_sems0),
        PlaneSum(mixer0.at[:, :, chunks[1]], mine1, arrived1, plane_sems1, sum_sems1),
    ]
    for plane_sum in plane_sums:
        plane_sum.begin()
    loads = fetch(
        [(ff0, stage_ff.at[0]), (ff1, stage_ff.at[1]), (mixer1, stage_mixer.at[1])], load_sems
    )
    by_layer(True, ((grad0, grad1, input_grads),), layer_sems, keep_sems)
    for load in loads:
        load.wait()
    ups = []
    for e, (t, seq, device) in enumerate(targets):
        ups.append(
            remote_to(
                stage_ff.at[t, rows_of(seq, depth), :], got_up.at[section, me], up_sems, e, device
            )
        )
    downs = [
        remote_to(
            stage_ff.at[1 - section, pl.ds(4 * depth, 4 * depth), :], got_down.at[section],
            down_sems, 0, other_core(),
        )
    ]
    for copy in ups + downs:
        copy.start()
    sends += ups + downs
    send_layer(1, 0)
    send_layer(1, 1)
    keeps = fetch(
        [
            (stage_ff.at[section, rows_of(me, depth), :], got_up.at[section, me]),
            (stage_ff.at[section, pl.ds(4 * depth, 4 * depth), :], got_down.at[section]),
        ],
        own_sems,
    )

    for copy in moves:
        copy.wait_recv()
    own_chunk = rows_of(here, chunk)
    total = vec_sum[own_chunk, :]
    for slot in range(len(planes)):
        total = total + vec_arrived[slot]
    vec_all[me, own_chunk, :] = total
    moves = [
        remote_to(
            vec_all.at[me, own_chunk], vec_all.at[me, own_chunk], vec_plane_sems, slot,
            {"dp": plane},
        )
        for slot, plane in enumerate(planes)
    ]
    for copy in moves:
        copy.start()
    sends += moves
    for plane_sum in plane_sums:
        plane_sum.forward()
    for slot, plane in enumerate(planes):
        block = vec_all.at[me, rows_of(plane, chunk)]
        remote_to(block, block, vec_plane_sems, slot, {"dp": plane}).wait_recv()
    moves = [
        remote(vec_all.at[me], vec_all.at[me], vec_seq_sems, slot, peer)
        for slot, peer in enumerate(peers)
    ]
    for copy in moves:
        copy.start()
    sends += moves

    for at, plane_sum in enumerate(plane_sums):
        plane_sum.end(stage_mixer.at[0, :, chunks[at]])
        sends += plane_sum.sends
        send_layer(0, at)
    sends += [columns(e, at) for e in range(7) for at in range(2)] + [out_columns]
    keeps += fetch(
        [
            (
                stage_mixer.at[section, rows_of(me, depth), pl.ds(0, half_in)],
                got_in.at[section, me],
            ),
            (stage_mixer.at[section, :, pl.ds(half_in, half_in // 3)], got_out.at[section]),
        ],
        own_sems,
        2,
    )
    for slot, peer in enumerate(peers):
        block = vec_all.at[peer]
        remote(block, block, vec_seq_sems, slot, peer).wait_recv()
    keeps += fetch([(vec_all, vec_out)], own_sems, 4)
    for e, (t, seq, device) in enumerate(targets):
        block = got_up.at[t, seq]
        remote_to(block, block, up_sems, e, device).wait_recv()
        for at in range(2):
            block = got_in.at[t, seq, :, in_cols[at]]
            remote_to(block, block, in_sems, 2 * e + at, device).wait_recv()
    downs[0].wait_recv()
    out_columns.wait_recv()
    by_layer(False, ((grad0, grad1, input_grads),), layer_sems, keep_sems)
    for copy in sends:
        copy.wait_send()
    for keep in keeps:
        keep.wait()


def unpack_kernel(
    blocks, grads, got_in, got_out, got_up, got_down, vec_all,
    block_outputs, input_grads, g_in, g_out, g_up, g_down, g_gain, g_bias, g_taps, g_first,
    g_second, g_last, g_direct,
    stage_blocks, stage_grads, load_sems, copy_sems,
):
    loads = fetch([(blocks, stage_blocks), (grads, stage_grads)], load_sems)
    depth = g_in.shape[0]
    half_in, half_up = got_in.shape[3], got_up.shape[3]
    chans = vec_all.shape[2]
    count = 4
    piece = chans // count
    for j in range(4):
        for d in range(count):
            at = (d * 4 + j) * chans
            h, col = divmod(d * chans, half_up)
            g_up[:, at : at + chans] = got_up[h, j, :, col : col + chans].astype(f32)
    for h in range(2):
        g_down[:, h * half_up : (h + 1) * half_up] = got_down[h].astype(f32)
    for load in loads:
        load.wait()
    copies = fetch([(stage_blocks, block_outputs), (stage_grads, input_grads)], copy_sems)
    for g in range(3):
        for d in range(count):
            h, col = divmod(g * chans + d * piece, half_in)
            for j in range(0, 4, 2):
                at = ((g * count + d) * 4 + j) * piece
                g_in[:, at : at + 2 * piece] = jnp.concatenate(
                    [got_in[h, j + k, :, col : col + piece].astype(f32) for k in range(2)], 1
                )
    part = half_in // 3
    for h in range(2):
        for q in range(4):
            at = (h * 4 + q) * part
            g_out[:, at : at + part] = got_out[h, q * depth : (q + 1) * depth, :].astype(f32)
    first = sum_of(vec_all, slice(64, 64 + g_first.shape[0]), slice(128, 192))
    for row in range(g_first.shape[0]):
        g_first[row] = first[row : row + 1]
    g_second[...] = sum_of(vec_all, slice(64, 128), slice(0, 64))
    for q in range(4):
        cols = slice(q * chans, (q + 1) * chans)
        early = sum_of(vec_all, slice(128 + 2 * q, 130 + 2 * q), slice(None))
        late = sum_of(vec_all, slice(136 + 2 * q, 138 + 2 * q), slice(None))
        g_gain[0:1, cols] = early[0:1]
        g_gain[1:2, cols] = late[0:1]
        g_bias[0:1, cols] = early[1:2]
        g_bias[1:2, cols] = late[1:2]
    for d in range(count):
        cols = slice(d * piece, (d + 1) * piece)
        for j in range(0, 4, 2):
            at = (d * 4 + j) * piece
            pair = slice(at, at + 2 * piece)

            def joined(rows):
                return jnp.concatenate([vec_all[j, rows, cols], vec_all[j + 1, rows, cols]], 1)

            g_last[:, pair] = joined(slice(0, 64))
            for g in range(3):
                for tap in range(3):
                    row = 144 + 3 * g + tap
                    start = g * 4 * chans + at
                    g_taps[tap, :, start : start + 2 * piece] = joined(slice(row, row + 1))
            g_direct[:, pair] = joined(slice(153, 154))

    for copy in copies:
        copy.wait()


def sum_of(blocks, rows, cols):
    return (blocks[0, rows, cols] + blocks[1, rows, cols]) + (
        blocks[2, rows, cols] + blocks[3, rows, cols]
    )


def finish(vec0, vec1, mixer0, mixer1, ff0, ff1, grad0, grad1):
    count, width = grad0.shape
    dp_count, rows, half = mixer0.shape
    depth = rows // 4
    chans = vec0.shape[1]
    half_in = 3 * chans // 2
    vm, dma = pltpu.VMEM, pltpu.SemaphoreType.DMA
    vec_rows = vec0.shape[0]
    chunk = jax.ShapeDtypeStruct((dp_count, rows, half // 2), low)
    return run_kernel(
        finish_kernel,
        "finish",
        10,
        (vec0, vec1, mixer0, mixer1, ff0, ff1, grad0, grad1),
        (0, 1, 6, 7),
        [
            ((2, count, width), f32),
            ((2, 4, depth, half_in), low),
            ((2, rows, half_in // 3), low),
            ((2, 4, depth, half), low),
            ((2, rows, half), low),
            ((4, vec_rows, chans), f32),
        ],
        (),
        plane_sum_scratch(chunk)
        + plane_sum_scratch(chunk)
        + [
            vm((vec_rows, chans), f32),
            vm((vec_rows, chans), f32),
            vm((3, vec_rows // 4, chans), f32),
            vm((4, vec_rows, chans), f32),
            vm((2, *mixer1.shape), low),
            vm((2, *ff1.shape), low),
            dma((5,)),
            dma((3,)),
            *exchange_semaphores(1),
            dma((2, 1)),
            dma((2, 3)),
            dma((2, 3)),
            dma((2, 3)),
            dma((2, 14)),
            dma((2, 1)),
            dma((2, 7)),
            dma((2, 1)),
        ],
        10**9,
    )


def unpack(blocks, grads, got, first_shape):
    width = blocks.shape[2]
    depth = got[0].shape[2]
    units = 4 * 2 * got[2].shape[3]
    knots = first_shape[1]
    inside = pl.BlockSpec(memory_space=pltpu.VMEM)
    outside = pl.BlockSpec(memory_space=pl.ANY)
    shapes = (
        blocks.shape, grads.shape, (depth, 3 * width), (depth, width), (depth, units),
        (4 * depth, width), (2, width), (2, width), (3, 1, 3 * width),
        (first_shape[0], 1, knots), (knots, knots),
        (knots, width), (1, width),
    )
    return pl.pallas_call(
        unpack_kernel,
        out_shape=[jax.ShapeDtypeStruct(shape, f32) for shape in shapes],
        in_specs=[outside] * 2 + [inside] * 5,
        out_specs=[outside] * 2 + [inside] * 11,
        scratch_shapes=[
            pltpu.VMEM(blocks.shape, f32),
            pltpu.VMEM(grads.shape, f32),
            pltpu.SemaphoreType.DMA((2,)),
            pltpu.SemaphoreType.DMA((2,)),
        ],
        compiler_params=pltpu.CompilerParams(vmem_limit_bytes=56 * 2**20),
        name="unpack",
    )(blocks, grads, *got)


def any_device(
    tokens,
    cotangent,
    lengths,
    norm_gain,
    norm_bias,
    mixer_in,
    short_kernel,
    filter_first,
    filter_second,
    filter_last,
    filter_bias,
    decay_rates,
    mixer_out,
    up_weight,
    down_weight,
):
    section = lax.axis_index("section")
    seq_index = lax.axis_index("seq")
    seq_count = lax.axis_size("seq")
    dp_count = lax.axis_size("dp")
    own_layer_first = section == 0
    local_len = tokens.shape[2]
    width = tokens.shape[3]
    hidden = up_weight.shape[2]
    row_len = local_len * seq_count
    chans = width // seq_count
    units = hidden // seq_count

    def share_columns(block, groups):
        rows = block.shape[0]
        inner = block.shape[1] // (groups * dp_count * seq_count)
        split = block.reshape(rows, groups, dp_count, seq_count, inner)
        split = jnp.transpose(split, (3, 0, 1, 2, 4))
        moved = lax.all_to_all(split, "seq", split_axis=0, concat_axis=0, tiled=True)
        return moved.reshape(seq_count * rows, groups * dp_count * inner)

    def unshare_columns(block, groups):
        rows = block.shape[0] // seq_count
        inner = block.shape[1] // (groups * dp_count)
        split = block.reshape(seq_count, rows, groups, dp_count, inner)
        moved = lax.all_to_all(split, "seq", split_axis=0, concat_axis=0, tiled=True)
        moved = jnp.transpose(moved, (1, 2, 3, 0, 4))
        return moved.reshape(rows, groups * dp_count * seq_count * inner)

    def gathered(block):
        whole = lax.all_gather(block, ("section", "dp"))
        return whole.reshape(2, dp_count * block.shape[0], block.shape[1])

    weights = (
        gathered(share_columns(mixer_in[0], 3)),
        gathered(mixer_out[0]),
        gathered(share_columns(up_weight[0], 1)),
        gathered(down_weight[0]),
    )

    def both(value):
        return lax.all_gather(value[0], "section")

    gains, shifts = both(norm_gain), both(norm_bias)
    taps, first_w, second_w = both(short_kernel), both(filter_first), both(filter_second)
    last_w, direct, rates = both(filter_last), both(filter_bias), both(decay_rates)

    def mine(value):
        lead = value.shape[:-1]
        split = value.reshape(*lead, dp_count, seq_count, -1)
        picked = lax.dynamic_index_in_dim(split, seq_index, len(lead) + 1, False)
        return picked.reshape(*lead, chans)

    def placed(value):
        lead = value.shape[:-1]
        split = value.reshape(*lead, dp_count, 1, -1)
        inner = split.shape[-1]
        empty = jnp.zeros((*lead, dp_count, seq_count, inner), value.dtype)
        at = [0] * len(lead) + [0, seq_index, 0]
        return lax.dynamic_update_slice(empty, split, at).reshape(*lead, width)

    waves = jnp.asarray(wave_tables(row_len))
    waves_back = waves

    def to_waves(x):
        both_parts = mm(waves, x)
        return both_parts[:row_len], both_parts[row_len:]

    def from_waves(cos_part, sin_part):
        joined = jnp.concatenate([cos_part, sin_part], 0).astype(low)
        return t_mm(waves_back, joined) * (1.0 / row_len)

    def ag(x):
        return lax.all_gather(x, "seq", axis=0, tiled=True)

    def rs(x):
        return lax.psum_scatter(x.astype(low), "seq", scatter_dimension=0, tiled=True).astype(f32)

    length_now = lax.dynamic_index_in_dim(lengths, section, 0, False)[0]
    positions = seq_index * local_len + jnp.arange(local_len)
    mask = (positions < length_now).astype(f32)[:, None]
    row_mask = (jnp.arange(row_len) < length_now).astype(f32)[:, None]
    own_tokens = lax.dynamic_index_in_dim(tokens, section, 0, False)[0].astype(f32)
    own_cotangent = lax.dynamic_index_in_dim(cotangent, section, 0, False)[0].astype(f32)

    def layer_forward(s, inputs):
        w_in, w_out, w_up, w_down = [w[s] for w in weights]
        kernel = mine(taps[s].reshape(3, 3, width))
        last_mine, direct_mine, rates_mine = mine(last_w[s]), mine(direct[s]), mine(rates[s])

        def own_filter(a, b, c):
            return filter_taps(a, b, c, rates_mine, row_len)

        filter_rows, filter_back = jax.vjp(own_filter, first_w[s], second_w[s], last_mine)
        filt_cos, filt_sin = to_waves(filter_rows.astype(low))
        normed = (norm_stats(inputs)[0] * gains[s, 0] + shifts[s, 0]).astype(low)
        normed = ag(normed)
        projected = [mm(normed, w_in[:, g * chans : (g + 1) * chans]) for g in range(3)]
        streams = [
            (
                kernel[0, g] * projected[g]
                + kernel[1, g] * shifted(projected[g], 1)
                + kernel[2, g] * shifted(projected[g], 2)
            ).astype(low)
            for g in range(3)
        ]
        wide = [x.astype(f32) for x in streams]
        product = (wide[0] * wide[2] * row_mask).astype(low)
        prod_cos, prod_sin = to_waves(product)
        filtered = from_waves(
            prod_cos * filt_cos - prod_sin * filt_sin, prod_cos * filt_sin + prod_sin * filt_cos
        ) + direct_mine * product.astype(f32)
        gated = (wide[1] * filtered).astype(low)
        middle = inputs + mask * rs(mm(gated, w_out))
        second = (norm_stats(middle)[0] * gains[s, 1] + shifts[s, 1]).astype(low)
        second = ag(second)
        value, slope = gelu_both(mm(second, w_up))
        value = value.astype(low)
        slope = slope.astype(low)
        result = middle + mask * rs(mm(value, w_down))
        saved = (
            inputs, normed, projected, wide, product, prod_cos, prod_sin, filt_cos, filt_sin,
            filtered, gated, middle, second, value, slope, kernel, direct_mine, filter_back,
        )
        return result, saved

    def layer_backward(s, grad, saved):
        w_in, w_out, w_up, w_down = [w[s] for w in weights]
        (
            inputs, normed, projected, wide, product, prod_cos, prod_sin, filt_cos, filt_sin,
            filtered, gated, middle, second, value, slope, kernel, direct_mine, filter_back,
        ) = saved
        out_low = ag((grad * mask).astype(low))
        pre = (mm_t(out_low, w_down) * slope.astype(f32)).astype(low)
        grad_down = t_mm(value, out_low)
        grad_up = t_mm(second, pre)
        mid_part, gain_late, bias_late = norm_back(rs(mm_t(pre, w_up)), middle, gains[s, 1])
        middle_grad = grad + mid_part
        branch = ag((middle_grad * mask).astype(low))
        gated_grad = mm_t(branch, w_out).astype(low)
        grad_out = t_mm(gated, branch)
        gated_grad = gated_grad.astype(f32)
        filtered_grad = (gated_grad * wide[1]).astype(low)
        fg_cos, fg_sin = to_waves(filtered_grad)
        fg_wide = filtered_grad.astype(f32)
        prod32 = product.astype(f32)
        product_grad = from_waves(
            filt_cos * fg_cos + filt_sin * fg_sin, filt_cos * fg_sin - filt_sin * fg_cos
        ) + direct_mine * fg_wide
        product_grad = product_grad.astype(low).astype(f32)
        filter_grad = from_waves(
            prod_cos * fg_cos + prod_sin * fg_sin, prod_cos * fg_sin - prod_sin * fg_cos
        )
        grad_first, grad_second, grad_last = filter_back(filter_grad)
        grad_direct = jnp.sum(fg_wide * prod32, 0)
        mixed = [
            (product_grad * wide[2]).astype(low).astype(f32),
            (gated_grad * filtered).astype(low).astype(f32),
            (product_grad * wide[0]).astype(low).astype(f32),
        ]
        proj = [
            (
                kernel[0, g] * mixed[g]
                + kernel[1, g] * shifted(mixed[g], -1)
                + kernel[2, g] * shifted(mixed[g], -2)
            ).astype(low)
            for g in range(3)
        ]
        grad_taps = jnp.stack(
            [
                jnp.stack(
                    [jnp.sum(mixed[g] * (shifted(projected[g], k) if k else projected[g]), 0) for g in range(3)]
                )
                for k in range(3)
            ]
        )
        proj = jnp.concatenate(proj, 1)
        grad_in = t_mm(normed, proj)
        in_part, gain_early, bias_early = norm_back(rs(mm_t(proj, w_in)), inputs, gains[s, 0])
        small = (
            jnp.stack([gain_early, gain_late]),
            jnp.stack([bias_early, bias_late]),
            placed(grad_taps).reshape(3, 3 * width),
            grad_first,
            grad_second,
            placed(grad_last),
            placed(grad_direct),
        )
        large = (grad_in, grad_out, grad_up, grad_down)
        return middle_grad + in_part, small, large

    first_out, first_saved = layer_forward(0, own_tokens)
    second_out, second_saved = layer_forward(1, first_out)
    second_grad, second_small, second_large = layer_backward(1, own_cotangent, second_saved)
    first_grad, first_small, first_large = layer_backward(0, second_grad, first_saved)

    swap = [(0, 1), (1, 0)]

    def by_layer(first, second):
        other = lax.ppermute(jnp.where(own_layer_first, second, first), "section", swap)
        return jnp.where(
            own_layer_first, jnp.stack([first, other]), jnp.stack([other, second])
        )[None, :, None]

    def summed(first, second):
        stacked = jnp.stack([first, second]).astype(low)
        rows = first.shape[0] // dp_count
        stacked = stacked.reshape(2 * dp_count, rows, first.shape[1])
        return lax.psum_scatter(stacked, ("section", "dp"), scatter_dimension=0, tiled=True)[0]

    sums = [summed(a, b) for a, b in zip(first_large, second_large)]
    sum_in = unshare_columns(sums[0], 3).astype(f32)
    sum_out = sums[1].astype(f32)
    sum_up = unshare_columns(sums[2], 1).astype(f32)
    sum_down = sums[3].astype(f32)
    stacked = jax.tree.map(lambda a, b: jnp.stack([a, b]), first_small, second_small)
    small = lax.psum(stacked, ("section", "dp", "seq"))
    small = [lax.dynamic_slice_in_dim(x, section, 1, 0) for x in small]
    sum_gain, sum_bias, sum_taps, sum_first, sum_second, sum_last, sum_direct = small
    return (
        by_layer(first_out, second_out),
        by_layer(first_grad, second_grad),
        sum_gain,
        sum_bias,
        sum_in[None],
        sum_taps,
        sum_first,
        sum_second,
        sum_last,
        sum_direct,
        sum_out[None],
        sum_up[None],
        sum_down[None],
    )


def plane_device(
    tokens,
    cotangent,
    lengths,
    norm_gain,
    norm_bias,
    mixer_in,
    short_kernel,
    filter_first,
    filter_second,
    filter_last,
    filter_bias,
    decay_rates,
    mixer_out,
    up_weight,
    down_weight,
):
    section = lax.axis_index("section")
    seq_count = lax.axis_size("seq")
    dp_count = lax.axis_size("dp")
    row_len = tokens.shape[2] * seq_count
    lengths = jnp.transpose(lengths)
    short_kernel = jnp.transpose(short_kernel, (1, 0, 2))
    filter_first = jnp.transpose(filter_first, (1, 0, 2))

    def gathered(part):
        whole = lax.all_gather(part, ("section", "dp"))
        return whole.reshape(2, dp_count, *part.shape)

    tables = wave_tables(row_len)
    waves = jnp.asarray(tables)
    waves_back = jnp.asarray(np.ascontiguousarray(tables.T))
    embedding = jnp.asarray(np.pad(position_rows(row_len), ((0, 0), (0, 95))))

    weights = (
        mixer_in[0], mixer_out[0], up_weight[0], down_weight[0], norm_gain, norm_bias, short_kernel,
        filter_first, filter_second, filter_last, filter_bias, decay_rates,
    )
    (
        first_mixer_pack, first_ff_pack, cotangent_low, par, small, second_mixer_pack, ff_part,
        *outs,
    ) = mixer_forward(
        0, tokens, lengths, weights, waves, waves_back, (cotangent, embedding)
    )
    first_filter, second_filter, first_saved, outs = outs[:5], outs[5:10], outs[10:13], outs[13:]
    first_out, *first_kept, first_middle = outs
    second_ff_pack = gathered(ff_part)
    *second_kept, second_middle = mixer_forward(
        1, first_out, lengths, (par, small, second_mixer_pack, second_filter[0]), waves, waves_back,
        None,
    )
    first_kept, second_kept = [*first_kept, *first_filter], [*second_kept, *second_filter]
    second_ff, second_out, middle_grad, late = ff_turn(
        1, cotangent, second_middle, par, lengths, second_ff_pack, cotangent_low
    )

    def mixer_back(s, grad, x, late, pack, kept, earlier):
        return mixer_backward(
            s, grad, x, par, small, embedding, late, lengths, pack, waves, waves_back, kept, earlier
        )

    second_mixer, second_vec, second_grad, second_ff = mixer_back(
        1, middle_grad, first_out, late, second_mixer_pack, second_kept, second_ff
    )
    first_ff, middle_grad, late, second_mixer, block_outputs = ff_backward(
        0, second_grad, first_middle, par, lengths, first_ff_pack, *first_saved, second_mixer,
        (first_out, second_out),
    )
    first_mixer, first_vec, first_grad, first_ff = mixer_back(
        0, middle_grad, tokens, late, first_mixer_pack, first_kept, first_ff
    )
    input_grads, *got = finish(
        first_vec, second_vec, first_mixer, second_mixer, first_ff, second_ff, first_grad,
        second_grad,
    )
    (
        block_outputs, input_grads, sum_in, sum_out, sum_up, sum_down, sum_gain, sum_bias, sum_taps,
        sum_first, sum_second, sum_last, sum_direct,
    ) = unpack(block_outputs, input_grads, got, filter_first.shape[::2])
    return (
        block_outputs[None, :, None],
        input_grads[None, :, None],
        sum_gain[None],
        sum_bias[None],
        sum_in[None],
        jnp.transpose(sum_taps, (1, 0, 2)),
        jnp.transpose(sum_first, (1, 0, 2)),
        sum_second[None],
        sum_last[None],
        sum_direct,
        sum_out[None],
        sum_up[None],
        sum_down[None],
    )


def solution(mesh):
    in_specs = (
        P(None, "dp", "seq", None),
        P(None, "dp", "seq", None),
        P(None, "dp"),
        P("section", None, None),
        P("section", None, None),
        P("section", ("dp", "seq"), None),
        P("section", None, None),
        P("section", None, None),
        P("section", None, None),
        P("section", None, None),
        P("section", None),
        P("section", None),
        P("section", ("dp", "seq"), None),
        P("section", ("dp", "seq"), None),
        P("section", ("dp", "seq"), None),
    )
    out_specs = (
        P("section", None, "dp", "seq", None),
        P("section", None, "dp", "seq", None),
        P("section", None, None),
        P("section", None, None),
        P("section", ("dp", "seq"), None),
        P("section", None, None),
        P("section", None, None),
        P("section", None, None),
        P("section", None, None),
        P("section", None),
        P("section", ("dp", "seq"), None),
        P("section", ("dp", "seq"), None),
        P("section", ("dp", "seq"), None),
    )
    planes = mesh.shape["seq"] == 4 and mesh.shape["dp"] == 4
    per_device = plane_device if planes else any_device
    return jax.shard_map(
        per_device, mesh=mesh, in_specs=in_specs, out_specs=out_specs, check_vma=False
    )
```

```python
from functools import partial
import math

import jax
import jax.numpy as jnp
import numpy as np
from jax import lax
from jax.experimental import pallas as pl
from jax.experimental.pallas import tpu as pltpu
from jax.sharding import PartitionSpec as P

precise = lax.Precision.HIGHEST
low = jnp.bfloat16
f32 = jnp.float32
MESH = pl.DeviceIdType.MESH


def dot(a, b, dims):
    return lax.dot_general(a, b, (dims, ((), ())), preferred_element_type=f32)


def mm(a, b):
    return dot(a, b, ((1,), (0,)))


def mm_t(a, b):
    return dot(a, b, ((1,), (1,)))


def t_mm(a, b):
    return dot(a, b, ((0,), (0,)))


def norm_stats(x):
    mean = jnp.mean(x, axis=-1, keepdims=True)
    centred = x - mean
    inverse = lax.rsqrt(jnp.mean(centred * centred, axis=-1, keepdims=True) + 1e-05)
    return centred * inverse, inverse


def norm_back(grad, x, gain):
    hat, inverse = norm_stats(x)
    scaled = grad * gain
    back = inverse * (
        scaled
        - jnp.mean(scaled, axis=-1, keepdims=True)
        - hat * jnp.mean(scaled * hat, axis=-1, keepdims=True)
    )
    return back, jnp.sum(grad * hat, 0), jnp.sum(grad, 0)


def gelu_both(x):
    scale = math.sqrt(2.0 / math.pi)
    inner = scale * (x + 0.044715 * x * x * x)
    bend = jnp.tanh(inner)
    value = 0.5 * x * (1.0 + bend)
    slope = 0.5 * (1.0 + bend) + 0.5 * x * (1.0 - bend * bend) * scale * (
        1.0 + 3.0 * 0.044715 * x * x
    )
    return value, slope


def position_table(length):
    offsets = jnp.arange(length, dtype=jnp.float32)
    frequencies = jnp.linspace(0.0001, 15.0, 16, dtype=jnp.float32)
    angles = 2.0 * math.pi * offsets[:, None] * frequencies[None, :] / length
    return jnp.concatenate(
        [offsets[:, None] / (length - 1), jnp.cos(angles), -jnp.sin(angles)], axis=1
    )


def position_rows(length):
    offsets = np.arange(length, dtype=np.float32)
    frequencies = np.linspace(0.0001, 15.0, 16, dtype=np.float32)
    angles = np.float32(2.0 * math.pi) * offsets[:, None] * frequencies[None, :] / np.float32(length)
    return np.concatenate(
        [offsets[:, None] / np.float32(length - 1), np.cos(angles), -np.sin(angles)], axis=1
    )


def filter_taps(first_w, second_w, last_w, rates, length):
    embedding = position_table(length)
    hidden = jnp.sin(jnp.dot(embedding, first_w, precision=precise))
    hidden = jnp.sin(jnp.dot(hidden, second_w, precision=precise))
    offsets = jnp.arange(length, dtype=jnp.float32)
    return jnp.dot(hidden, last_w, precision=precise) * jnp.exp(-offsets[:, None] * rates[None, :])


def wave_tables(length):
    turns = (2 * np.arange(length)[:, None] + 1) * np.arange(length)[None, :] % (4 * length)
    angles = turns * (math.pi / (2 * length))
    both = np.concatenate([np.cos(angles), np.sin(angles)], 0)
    return both.astype(jnp.bfloat16)


def shifted(x, by):
    if by > 0:
        return jnp.pad(x[:-by], ((by, 0), (0, 0)))
    return jnp.pad(x[-by:], ((0, -by), (0, 0)))


def neighbours(me):
    return (me + 1 - 2 * (me % 2), (me + 2) % 4, 3 - me)


def greet(devices):
    barrier = pltpu.get_barrier_semaphore()
    for device in devices:
        pl.semaphore_signal(barrier, inc=1, device_id=device, device_id_type=MESH)
    return len(devices)


def all_here(greeted):
    pl.semaphore_wait(pltpu.get_barrier_semaphore(), greeted)


def in_plane(peers):
    return [{"seq": peer} for peer in peers]


def along_planes():
    here = lax.axis_index("dp")
    return here, here + 1 - 2 * (here % 2), (here + 2) % 4


def other_core():
    return {"section": 1 - lax.axis_index("section")}


def plane_devices():
    _, near, far = along_planes()
    return [{"dp": near}, {"dp": far}]


def add_low(target, source):
    def add(at):
        target[at, :] = (target[at, :].astype(f32) + source[at, :].astype(f32)).astype(low)

    by_rows(target.shape[0], 32, add)


def swap_begin(pairs, core_sems):
    section = lax.axis_index("section")
    copies = [
        remote_to(made.at[1 - section], other, core_sems, at, other_core())
        for at, (made, other) in enumerate(pairs)
    ]
    for copy in copies:
        copy.start()
    return copies


def swap_end(copies, pairs):
    section = lax.axis_index("section")
    for copy, (made, other) in zip(copies, pairs):
        copy.wait_recv()
        for block in range(other.shape[0]):
            add_low(made.at[section, block], other.at[block])


class PlaneSum:
    def __init__(self, pack, mine, arrived, sems, load_sems):
        self.here, self.near, self.far = along_planes()
        self.pack, self.mine, self.arrived = pack, mine, arrived
        self.sems, self.load_sems = sems, load_sems

    def begin(self):
        self.sends = [
            remote_to(self.pack.at[block], self.arrived.at[slot], self.sems, slot, {"dp": self.near})
            for slot, block in enumerate(((self.near + 2) % 4, self.near))
        ]
        for copy in self.sends:
            copy.start()
        self.loads = fetch(
            [(self.pack.at[self.far], self.mine.at[0]), (self.pack.at[self.here], self.mine.at[1])],
            self.load_sems,
        )

    def forward(self):
        self.loads[0].wait()
        self.sends[0].wait_recv()
        add_low(self.mine.at[0], self.arrived.at[0])
        copy = remote_to(self.mine.at[0], self.arrived.at[2], self.sems, 2, {"dp": self.far})
        copy.start()
        self.sends.append(copy)

    def end(self, result):
        self.loads[1].wait()
        self.sends[1].wait_recv()
        self.sends[2].wait_recv()

        def add(at):
            total = self.mine[1, at, :].astype(f32)
            for slot in (1, 2):
                total = total + self.arrived[slot, at, :].astype(f32)
            result[at, :] = total.astype(low)

        by_rows(result.shape[0], 32, add)


def plane_sum_scratch(half_pack):
    _, rows, cols = half_pack.shape
    return [
        pltpu.VMEM((2, rows, cols), low),
        pltpu.VMEM((3, rows, cols), low),
        pltpu.SemaphoreType.DMA((2, 3)),
        pltpu.SemaphoreType.DMA((2,)),
    ]


def remote_to(source, target, sems, slot, device):
    return pltpu.make_async_remote_copy(
        src_ref=source,
        dst_ref=target,
        send_sem=sems.at[0, slot],
        recv_sem=sems.at[1, slot],
        device_id=device,
        device_id_type=MESH,
    )


def remote(source, target, sems, slot, peer):
    return remote_to(source, target, sems, slot, {"seq": peer})


def rows_of(index, count):
    return pl.ds(pl.multiple_of(index * count, count), count)


def half_of(ref, index, part, count):
    half = count // 2
    return ref.at[pl.ds(pl.multiple_of(index * count + part * half, half), half)]


def gather_begin(gather, sems, me, peers, count):
    x, y, _ = peers
    first, second = half_of(gather, me, 0, count), half_of(gather, me, 1, count)
    copies = [
        remote(first, first, sems, 0, x),
        remote(second, second, sems, 2, y),
        remote(second, second, sems, 1, x),
        remote(first, first, sems, 3, y),
    ]
    for copy in copies:
        copy.start()
    return copies


def gather_forward(gather, sems, peers, count):
    x, y, _ = peers
    from_x, from_y = half_of(gather, x, 0, count), half_of(gather, y, 1, count)
    remote(from_x, from_x, sems, 0, x).wait_recv()
    onward = remote(from_x, from_x, sems, 4, y)
    onward.start()
    remote(from_y, from_y, sems, 2, y).wait_recv()
    across = remote(from_y, from_y, sems, 5, x)
    across.start()
    return [onward, across]


def gather_wait(gather, sems, slot, peers, count):
    for part, at in (((1, 1),), ((0, 3),), ((0, 4), (1, 5)))[slot]:
        block = half_of(gather, peers[slot], part, count)
        remote(block, block, sems, at, peers[slot]).wait_recv()


HALF_ORDER = ((0, 0), (1, 1), (0, 1), (1, 0), (2, 0), (2, 1))


def half_rows(index, part, count):
    half = count // 2
    return pl.ds(pl.multiple_of(index * count + part * half, half), half)


def gather_wait_half(gather, sems, slot, part, peers, count):
    at = {(0, 1): 1, (1, 0): 3, (2, 0): 4, (2, 1): 5}.get((slot, part))
    if at is not None:
        block = half_of(gather, peers[slot], part, count)
        remote(block, block, sems, at, peers[slot]).wait_recv()


def reduce_send_half(slot, part, send, recv, sems, peers):
    half = send.shape[1] // 2
    quarter = half // 2
    plan = {
        (0, 0): [(0, half, 0, 0)],
        (1, 1): [(half, half, 1, 1)],
        (2, 0): [(0, quarter, 2, 0), (quarter, quarter, 3, 0)],
        (2, 1): [(half, quarter, 4, 1), (half + quarter, quarter, 5, 1)],
    }.get((slot, part), [])
    copies = [
        remote(
            send.at[slot, pl.ds(start, size)], recv.at[slot, pl.ds(start, size)], sems, at,
            peers[to],
        )
        for start, size, at, to in plan
    ]
    for copy in copies:
        copy.start()
    return copies


def reduce_send(slot, send, recv, sems, peers):
    x, y, _ = peers
    half = send.shape[1] // 2
    quarter = half // 2
    if slot == 2:
        plan = [(0, quarter, 2, x), (half, quarter, 4, y), (quarter, quarter, 3, x)]
        plan.append((half + quarter, quarter, 5, y))
    else:
        plan = [(slot * half, half, slot, (x, y)[slot])]
    copies = [
        remote(
            send.at[slot, pl.ds(start, size)], recv.at[slot, pl.ds(start, size)], sems, at, peer
        )
        for start, size, at, peer in plan
    ]
    for copy in copies:
        copy.start()
    return copies


def reduce_pass(send, recv, sems, peers):
    x, y, _ = peers
    half = send.shape[1] // 2
    quarter = half // 2
    copies = []
    for start, at, source, slot, peer in (
        (half, 4, y, 0, x),
        (0, 2, x, 1, y),
        (half + quarter, 5, y, 0, x),
        (quarter, 3, x, 1, y),
    ):
        rows = pl.ds(start, quarter)
        remote(send.at[2, rows], recv.at[2, rows], sems, at, source).wait_recv()
        add_low(send.at[slot, rows], recv.at[2, rows])
        copy = remote(send.at[slot, rows], recv.at[slot, rows], sems, at + 4, peer)
        copy.start()
        copies.append(copy)
    return copies


def reduce_wait(send, recv, sems, peers):
    x, y, _ = peers
    half = send.shape[1] // 2
    quarter = half // 2
    for slot, start, size, at, peer in (
        (0, 0, half, 0, x),
        (1, half, half, 1, y),
        (0, half, quarter, 8, x),
        (1, 0, quarter, 6, y),
        (0, half + quarter, quarter, 9, x),
        (1, quarter, quarter, 7, y),
    ):
        rows = pl.ds(start, size)
        remote(send.at[slot, rows], recv.at[slot, rows], sems, at, peer).wait_recv()


def by_rows(total, step, body):
    def run(i, carry):
        body(pl.ds(pl.multiple_of(i * step, step), step))
        return carry

    lax.fori_loop(0, total // step, run, 0)


def valid_rows(lengths, start, count):
    at = lax.broadcasted_iota(jnp.int32, (count, 1), 0) + start
    return (at < lengths[0, lax.axis_index("section")]).astype(f32)


def normed_rows(x, gain, shift):
    mean = jnp.mean(x, axis=-1, keepdims=True)
    centred = x - mean
    inverse = lax.rsqrt(jnp.mean(centred * centred, axis=-1, keepdims=True) + 1e-05)
    return centred * inverse * gain + shift


def norm_back_rows(grad, x, gain):
    mean = jnp.mean(x, axis=-1, keepdims=True)
    centred = x - mean
    inverse = lax.rsqrt(jnp.mean(centred * centred, axis=-1, keepdims=True) + 1e-05)
    hat = centred * inverse
    scaled = grad * gain
    back = inverse * (
        scaled
        - jnp.mean(scaled, axis=-1, keepdims=True)
        - hat * jnp.mean(scaled * hat, axis=-1, keepdims=True)
    )
    return back, jnp.sum(grad * hat, axis=0, keepdims=True), jnp.sum(grad, axis=0, keepdims=True)


def norm_into(gather, start, x, gain, shift):
    step = 32

    def body(i, carry):
        rows = pl.ds(pl.multiple_of(i * step, step), step)
        at = pl.ds(pl.multiple_of(start + i * step, step), step)
        gather[at, :] = normed_rows(x[rows, :].astype(f32), gain, shift).astype(low)
        return carry

    lax.fori_loop(0, x.shape[0] // step, body, 0)


def masked_into(gather, start, grad, lengths):
    step = 32

    def body(i, carry):
        rows = pl.ds(pl.multiple_of(i * step, step), step)
        at = pl.ds(pl.multiple_of(start + i * step, step), step)
        value = grad[rows, :].astype(f32) * valid_rows(lengths, start + i * step, step)
        gather[at, :] = value.astype(low)
        return carry

    lax.fori_loop(0, grad.shape[0] // step, body, 0)


def add_parts(own, recv, x, start, lengths):
    def body(rows):
        total = own[rows, :] + recv[0, rows, :].astype(f32) + recv[1, rows, :].astype(f32)
        mask = valid_rows(lengths, start + rows.start, 32)
        own[rows, :] = x[rows, :].astype(f32) + mask * total

    by_rows(own.shape[0], 32, body)


def norm_back_parts(own, recv, grad, x, gain, sums):
    sums[...] = jnp.zeros(sums.shape, f32)

    def body(rows):
        total = own[rows, :] + recv[0, rows, :].astype(f32) + recv[1, rows, :].astype(f32)
        back, gain_sum, shift_sum = norm_back_rows(total, x[rows, :].astype(f32), gain)
        own[rows, :] = grad[rows, :].astype(f32) + back
        sums[0:1, :] += gain_sum
        sums[1:2, :] += shift_sum

    by_rows(own.shape[0], 32, body)


def fetch(pairs, sems, first=0):
    copies = [
        pltpu.make_async_copy(source, target, sems.at[first + at])
        for at, (source, target) in enumerate(pairs)
    ]
    for copy in copies:
        copy.start()
    return copies


def weight_pairs_mixer(pack, win, wout):
    rows, cols = wout.shape[2], wout.shape[3] // 4
    split = win.shape[3]
    pairs = [(pack.at[:, :, :, pl.ds(0, split)], win)]
    for q in range(4):
        pairs.append(
            (
                pack.at[:, :, pl.ds(q * rows, rows), pl.ds(split, cols)],
                wout.at[:, :, :, pl.ds(q * cols, cols)],
            )
        )
    return pairs


def half_pairs_mixer(half_pack, win, wout):
    rows, cols = wout.shape[2], wout.shape[3] // 4
    split = win.shape[3]
    section = lax.axis_index("section")
    pairs = [(win.at[section], half_pack.at[:, :, pl.ds(0, split)])]
    for q in range(4):
        pairs.append(
            (
                wout.at[section, :, :, pl.ds(q * cols, cols)],
                half_pack.at[:, pl.ds(q * rows, rows), pl.ds(split, cols)],
            )
        )
    return pairs


class ChipGather:
    def __init__(self, own, pack, plane_sems, core_sems):
        self.section = lax.axis_index("section")
        here, near, far = along_planes()
        self.pack, self.plane_sems, self.core_sems = pack, plane_sems, core_sems
        self.near, self.far = near, far
        self.order = (here, near, far, (near + 2) % 4)
        self.own = own
        self.sends = []

    def move(self, at, sems, slot, device):
        block = self.pack.at[self.section, self.order[at]]
        copy = remote_to(self.own if at == 0 else block, block, sems, slot, device)
        copy.start()
        self.sends.append(copy)

    def to_core(self, slot):
        self.move(slot, self.core_sems, slot, other_core())

    def begin(self, load_sem):
        self.move(0, self.plane_sems, 1, {"dp": self.far})
        self.move(0, self.plane_sems, 0, {"dp": self.near})
        self.to_core(0)
        self.keep = pltpu.make_async_copy(
            self.own, self.pack.at[self.section, self.order[0]], load_sem
        )
        self.keep.start()

    def arrived(self, slot):
        block = self.pack.at[self.section, self.order[slot + 1]]
        remote_to(block, block, self.plane_sems, slot, {"dp": self.near}).wait_recv()

    def forward(self):
        self.arrived(1)
        self.move(2, self.plane_sems, 2, {"dp": self.near})
        self.to_core(2)
        self.arrived(0)
        self.to_core(1)

    def end(self):
        self.arrived(2)
        self.to_core(3)
        self.keep.wait()
        for slot in range(4):
            block = self.pack.at[1 - self.section, self.order[slot]]
            remote_to(block, block, self.core_sems, slot, other_core()).wait_recv()


def sine_pair(x):
    turns = jnp.floor(x * (2.0 / math.pi) + 0.5)
    rest = x - turns * 1.5703125
    rest = rest - turns * 4.837512969970703125e-4
    rest = rest - turns * 7.54978995489188e-8
    square = rest * rest
    sine = -1.9515295891e-4 * square + 8.3321608736e-3
    sine = (sine * square - 1.6666654611e-1) * square * rest + rest
    cosine = 2.443315711809948e-5 * square - 1.388731625493765e-3
    cosine = (cosine * square + 4.166664568298827e-2) * square * square - 0.5 * square + 1.0
    halves = jnp.floor(turns * 0.5)
    odd = turns - 2.0 * halves
    back = halves - 2.0 * jnp.floor(halves * 0.5)
    swapped = odd > 0.5
    side = 1.0 - 2.0 * back
    wave = jnp.where(swapped, cosine, sine) * side
    slope = jnp.where(swapped, -sine, cosine) * side
    return wave, slope


def network_rows(small, embedding, network, taps_low, i):
    step = 256
    waves1, waves2, steep1, steep2 = network
    knots = waves1.shape[1]
    pair = (pl.ds(i * step, step), pl.ds(embedding.shape[0] // 2 + i * step, step))

    def layer(sources, weights, waves, steep):
        inner = jnp.concatenate([dot_exact(item, weights) for item in sources], 1)
        wave, slope = sine_pair(inner)
        for at, rows in enumerate(pair):
            cols = slice(at * knots, (at + 1) * knots)
            waves[rows, :] = wave[:, cols]
            steep[rows, :] = slope[:, cols]

    layer([embedding[rows, 0:64] for rows in pair], small[64:128, 128:192], waves1, steep1)
    layer([waves1[rows, :] for rows in pair], small[64:128, 0:64], waves2, steep2)
    for rows in pair:
        times = lax.broadcasted_iota(jnp.int32, (step, 1), 0) + rows.start
        fade = jnp.exp(-times.astype(f32) * small[154:155, :])
        taps_low[rows, :] = (dot_exact(waves2[rows, :], small[0:64, :]) * fade).astype(low)


def ff_blocks(
    gather, wup, wdown, value, slope, result_out, send, recv, gather_sems, reduce_sems, me, peers,
    pause,
):
    count, width = result_out.shape
    half = wup.shape[3]
    sends = []
    for slot, part in ((None, None), *HALF_ORDER):
        if slot is None:
            rows, sent = rows_of(me, count), None
        else:
            rows = half_rows(peers[slot], part, count)
            sent = slice(part * count // 2, (part + 1) * count // 2)
            gather_wait_half(gather, gather_sems, slot, part, peers, count)

        def hidden(i, carry):
            cols = pl.ds(pl.multiple_of(i * 256, 256), 256)
            for h in range(2):
                pre = mm(gather[rows, :], wup[h, :, :, cols].reshape(width, 256))
                after, steep = gelu_both(pre)
                at = pl.ds(pl.multiple_of(h * half + i * 256, 256), 256)
                value[rows, at] = after.astype(low)
                slope[rows, at] = steep.astype(low)
            return carry

        lax.fori_loop(0, half // 256, hidden, 0)
        for h in range(2):
            cols = slice(h * width // 2, (h + 1) * width // 2)
            out = mm(value[rows, :], wdown[h].reshape(2 * half, width // 2))
            if slot is None:
                result_out[:, cols] = out
            else:
                send[slot, sent, cols] = out.astype(low)
        if slot is not None:
            sends += reduce_send_half(slot, part, send, recv, reduce_sems, peers)
            pause(slot, part)
    return sends


def mixer_forward_kernel(
    s, gathers, x, *refs
):
    if gathers:
        (
            cotangent, embedding, lengths, w_in, w_out, w_up, w_down, gain, shift, tap_rows, first_w,
            second_w, last_w, direct, rates, waves_hbm, back_hbm,
            pack_out, ff_out, late_out, par_out, small_out, next_pack_out, ff_part_out,
            *refs,
        ) = refs
        network_outs, next_outs, refs = refs[:5], refs[5:10], refs[10:]
        second_out, value_out, slope_out, result_out, *refs = refs
        (
            *refs, waves1, waves2, steep1, steep2, taps_low, raw_out, ff_all, late, next_pack, core_sems,
            plane_sems, out_core_sems, out_plane_sems, ff_core_sems, ff_plane_sems, next_core_sems, next_plane_sems, late_sems,
            pack_sems, mixer_parts, ff_parts, par_all, small_all, stage_in, stage_out, stage_up,
            in_sems, out_sems, up_sems, down_sems, par_sems, small_sems,
            second, ff_send, ff_recv, second_sems, ff_sems, network_sems,
        ) = refs
        x = x.at[lax.axis_index("section"), 0]
        cotangent = cotangent.at[lax.axis_index("section"), 0]
        network = (waves1, waves2, steep1, steep2)
    else:
        par_all, small_all, lengths, weights_hbm, filt_hbm, waves_hbm, back_hbm, *refs = refs
    (
        normed_out, proj_out, stream_out, prod_out, spec_out, filtered_out, gated_out, middle_out,
        gather, win, wout, filt, waves, back, proj, proj_low, streams, prod, spec, mixed, filtered,
        gated, send, recv, gather_sems, reduce_sems, load_sems, store_sems,
    ) = refs
    par, small = par_all.at[s], small_all.at[s]
    me = lax.axis_index("seq")
    peers = neighbours(me)
    count, width = x.shape
    length = gather.shape[0]
    chans = prod.shape[1]
    half = win.shape[3]
    if gathers:
        section = lax.axis_index("section")
        targets = shuffle_targets(section, me, peers)
        greeted = greet([device for _, _, device in targets] + plane_devices())
    else:
        greeted = greet(in_plane(peers[:2]))
    tables = fetch([(waves_hbm, waves), (back_hbm, back)], load_sems)
    sends = []
    if gathers:
        shuffle_stage(w_in, w_out, w_up, stage_in, stage_out, stage_up)
        parameters_stage(
            me, par_all.at[section], small_all.at[section], gain, shift, tap_rows, first_w, second_w,
            last_w, direct, rates,
        )
        all_here(greeted)
        sends += shuffle_send(
            section, me, targets, (stage_in, stage_out, stage_up, w_down), (mixer_parts, ff_parts),
            (par_all, small_all), (in_sems, out_sems, up_sems, down_sems, par_sems, small_sems),
        )
        in_cols, out_cols = pl.ds(0, half), pl.ds(half, raw_out.shape[3])
        in_pack = ChipGather(mixer_parts.at[0, :, in_cols], win, plane_sems, core_sems)
        out_pack = ChipGather(mixer_parts.at[0, :, out_cols], raw_out, out_plane_sems, out_core_sems)
        ff_pack = ChipGather(ff_parts.at[0], ff_all, ff_plane_sems, ff_core_sems)
        for sems, item in ((par_sems, par_all), (small_sems, small_all)):
            block = item.at[1 - section]
            remote_to(block, block, sems, 0, other_core()).wait_recv()
        norm_into(gather, me * count, x, par[0:1, :], par[1:2, :])
        shuffle_wait_mixer(section, me, targets, mixer_parts, stage_in, in_sems, out_sems)
        in_pack.begin(pack_sems.at[0])
        sends += gather_begin(gather, gather_sems, me, peers, count)
        masked_into(late, me * count, cotangent, lengths)
    else:
        weights = fetch(weight_pairs_mixer(weights_hbm, win, wout), load_sems, 2)
        filt_load = fetch([(filt_hbm, filt)], load_sems, 7)
        norm_into(gather, me * count, x, par[0:1, :], par[1:2, :])
        all_here(greeted)
        sends += gather_begin(gather, gather_sems, me, peers, count)
    proj[0:8, :] = jnp.zeros((8, proj.shape[1]), f32)
    tile_rows = 256

    def filter_spectrum(i, carry):
        rows = pl.ds(pl.multiple_of(i * tile_rows, tile_rows), tile_rows)
        filt[rows, :] = mm(waves[rows, :], taps_low[...])
        return carry

    stores = []
    if gathers:
        network_rows(small, embedding, network, taps_low, 0)
    sends += gather_forward(gather, gather_sems, peers, count)
    if gathers:
        sends += gather_begin(late, late_sems, me, peers, count)
        in_pack.forward()
        out_pack.begin(pack_sems.at[13])
        network_rows(small, embedding, network, taps_low, 1)
        tables[0].wait()
        lax.fori_loop(0, 2 * length // tile_rows, filter_spectrum, 0)
        network_stores = fetch(list(zip((filt, *network), network_outs)), network_sems)
        out_pack.forward()
        shuffle_wait_ff(section, me, targets, ff_parts, stage_up, up_sems, down_sems)
        ff_pack.begin(pack_sems.at[1])
        in_pack.end()
        stores += fetch(
            [
                (win, pack_out.at[:, :, :, in_cols]),
                (par_all, par_out),
                (small_all, small_out),
                (ff_parts.at[1], ff_part_out),
            ],
            pack_sems,
            4,
        )
    else:
        tables[0].wait()
    if not gathers:
        weights[0].wait()
    for slot in (None, 0, 1, 2):
        source = me if slot is None else peers[slot]
        if slot is not None:
            gather_wait(gather, gather_sems, slot, peers, count)
        block = gather[rows_of(source, count), :]
        for h in range(2):
            proj[pl.ds(pl.multiple_of(source * count + 8, 8), count), h * half : (h + 1) * half] = mm(
                block, win[h].reshape(width, half)
            )
    if gathers:
        sends += gather_forward(late, late_sems, peers, count)
    step = 128

    def short_conv(i, carry):
        start = pl.multiple_of(i * step, step)
        for g in range(3):
            cols = slice(g * chans, (g + 1) * chans)
            tile = proj[pl.ds(start, step + 8), cols]
            proj_low[pl.ds(start, step), cols] = tile[8:].astype(low)
            value = (
                small[144 + 3 * g : 145 + 3 * g, :] * tile[8:]
                + small[145 + 3 * g : 146 + 3 * g, :] * pltpu.roll(tile, 1, 0)[8:]
                + small[146 + 3 * g : 147 + 3 * g, :] * pltpu.roll(tile, 2, 0)[8:]
            )
            streams[pl.ds(start, step), cols] = value.astype(low)
        first = streams[pl.ds(start, step), 0:chans].astype(f32)
        third = streams[pl.ds(start, step), 2 * chans : 3 * chans].astype(f32)
        prod[pl.ds(start, step), :] = (first * third * valid_rows(lengths, start, step)).astype(low)
        return carry

    lax.fori_loop(0, length // step, short_conv, 0)
    stores += fetch(
        [(gather, normed_out), (proj_low, proj_out), (streams, stream_out), (prod, prod_out)],
        store_sems,
    )
    if not gathers:
        filt_load[0].wait()

    def spectrum(i, carry):
        up = pl.ds(pl.multiple_of(i * tile_rows, tile_rows), tile_rows)
        down = pl.ds(pl.multiple_of(i * tile_rows + length, tile_rows), tile_rows)
        prod_cos = mm(waves[up, :], prod[...])
        prod_sin = mm(waves[down, :], prod[...])
        filt_cos, filt_sin = filt[up, :], filt[down, :]
        spec[up, :] = prod_cos.astype(low)
        spec[down, :] = prod_sin.astype(low)
        mixed[up, :] = (prod_cos * filt_cos - prod_sin * filt_sin).astype(low)
        mixed[down, :] = (prod_cos * filt_sin + prod_sin * filt_cos).astype(low)
        return carry

    lax.fori_loop(0, length // tile_rows, spectrum, 0)
    tables[1].wait()
    if gathers:
        out_pack.end()
        cols = raw_out.shape[3]
        weights = fetch(
            [
                (
                    raw_out.at[:, :, pl.ds(q * wout.shape[2], wout.shape[2]), :],
                    wout.at[:, :, :, pl.ds(q * cols, cols)],
                )
                for q in range(4)
            ],
            load_sems,
            3,
        )
        stores += fetch([(raw_out, pack_out.at[:, :, :, out_cols])], pack_sems, 14)
        for load in weights:
            load.wait()
    else:
        for load in weights[1:]:
            load.wait()
    for slot in (2, 0, 1, None):
        target = me if slot is None else peers[slot]
        rows = rows_of(target, count)
        value = mm(back[rows, :], mixed[...]) * (1.0 / length)
        value = value + small[153:154, :] * prod[rows, :].astype(f32)
        filtered[rows, :] = value
        gate = (streams[rows, chans : 2 * chans].astype(f32) * value).astype(low)
        gated[rows, :] = gate
        outs = [mm(gate, wout[h].reshape(chans, width // 2)) for h in range(2)]
        for h in range(2):
            cols = slice(h * width // 2, (h + 1) * width // 2)
            if slot is None:
                middle_out[:, cols] = outs[h]
            else:
                send[slot, :, cols] = outs[h].astype(low)
        if slot is not None:
            sends += reduce_send(slot, send, recv, reduce_sems, peers)
    if gathers:
        ff_pack.forward()
        for slot in range(3):
            gather_wait(late, late_sems, slot, peers, count)
        stores += fetch([(late, late_out)], pack_sems, 2)
    sends += reduce_pass(send, recv, reduce_sems, peers)
    stores += fetch(
        [(spec, spec_out), (filtered, filtered_out), (gated, gated_out)],
        store_sems,
        4,
    )
    if gathers:
        for store in network_stores:
            store.wait()
        for i in range(2):
            network_rows(small_all.at[1], embedding, network, taps_low, i)
        lax.fori_loop(0, 2 * length // tile_rows, filter_spectrum, 0)
        network_stores = fetch(list(zip((filt, *network), next_outs)), network_sems)
    reduce_wait(send, recv, reduce_sems, peers)
    add_parts(middle_out, recv, x, me * count, lengths)
    if gathers:
        next_mixer = ChipGather(mixer_parts.at[1], next_pack, next_plane_sems, next_core_sems)
        norm_into(second, me * count, middle_out, par[2:3, :], par[3:4, :])
        sends += gather_begin(second, second_sems, me, peers, count)
        sends += gather_forward(second, second_sems, peers, count)
        ff_pack.end()
        next_mixer.begin(pack_sems.at[8])
        stores += fetch([(ff_all, ff_out)], pack_sems, 3)
        rows_up = ff_all.shape[2] // 2
        value, slope = waves.at[pl.ds(0, length)], waves.at[pl.ds(length, length)]

        def pause(slot, part):
            if (slot, part) == (1, 1):
                next_mixer.forward()

        sends += ff_blocks(
            second, ff_all.at[:, :, pl.ds(0, rows_up)], ff_all.at[:, :, pl.ds(rows_up, rows_up)],
            value, slope, result_out, ff_send, ff_recv, second_sems, ff_sems, me, peers, pause,
        )
        sends += reduce_pass(ff_send, ff_recv, ff_sems, peers)
        stores += fetch([(second, second_out), (value, value_out), (slope, slope_out)], pack_sems, 9)
        next_mixer.end()
        stores += fetch([(next_pack, next_pack_out)], pack_sems, 12)
        reduce_wait(ff_send, ff_recv, ff_sems, peers)
        add_parts(result_out, ff_recv, middle_out, me * count, lengths)
        sends += in_pack.sends + out_pack.sends + ff_pack.sends + next_mixer.sends
        stores += network_stores
    for copy in sends:
        copy.wait_send()
    for store in stores:
        store.wait()


def ff_turn_kernel(
    s, cotangent, x, par_all, lengths, pack, late_hbm,
    half_out, parts_out, result_out, middle_grad_out, sums_out,
    gather, late, wup, wdown, value, pre, wgrad, other, send, send_back, recv_back,
    gather_sems, back_sems, load_sems, store_sems, core_sems,
):
    par = par_all.at[s]
    grad = cotangent.at[lax.axis_index("section"), 0]
    me = lax.axis_index("seq")
    peers = neighbours(me)
    count, width = x.shape
    half = wup.shape[3]
    rows_up = wup.shape[2]
    greeted = greet(in_plane(peers[:2]) + [other_core()])
    loads = fetch(
        [
            (pack.at[:, :, pl.ds(0, rows_up), :], wup),
            (pack.at[:, :, pl.ds(rows_up, wdown.shape[2]), :], wdown),
            (late_hbm, late),
        ],
        load_sems,
    )
    norm_into(gather, me * count, x, par[2:3, :], par[3:4, :])
    all_here(greeted)
    sends = gather_begin(gather, gather_sems, me, peers, count)
    for load in loads:
        load.wait()
    for slot, part in ((None, None), *HALF_ORDER):
        if slot is None:
            rows, sent = rows_of(me, count), None
        else:
            rows = half_rows(peers[slot], part, count)
            sent = slice(part * count // 2, (part + 1) * count // 2)
            gather_wait_half(gather, gather_sems, slot, part, peers, count)

        def hidden(i, carry):
            cols = pl.ds(pl.multiple_of(i * rows_up, rows_up), rows_up)
            for h in range(2):
                block = h * (half // rows_up) + i
                at = pl.ds(pl.multiple_of(block * rows_up, rows_up), rows_up)
                after, steep = gelu_both(
                    mm(gather[rows, :], wup[h, :, :, cols].reshape(width, rows_up))
                )
                value[rows, at] = after.astype(low)
                back = mm_t(late[rows, : width // 2], wdown[0, block]) + mm_t(
                    late[rows, width // 2 :], wdown[1, block]
                )
                pre[rows, at] = (back * steep).astype(low)
            return carry

        lax.fori_loop(0, half // rows_up, hidden, 0)

        def through(i, carry):
            cols = pl.ds(pl.multiple_of(i * rows_up, rows_up), rows_up)
            back = mm_t(pre[rows, :half], wup[0, i]) + mm_t(pre[rows, half:], wup[1, i])
            if slot is None:
                middle_grad_out[:, cols] = back
            else:
                send_back[slot, sent, cols] = back.astype(low)
            return carry

        lax.fori_loop(0, width // rows_up, through, 0)
        if slot is None:
            sends += gather_forward(gather, gather_sems, peers, count)
        else:
            sends += reduce_send_half(slot, part, send_back, recv_back, back_sems, peers)
    for slot in (2, 0, 1, None):
        rows = rows_of(me if slot is None else peers[slot], count)
        for h in range(2):
            cols = slice(h * width // 2, (h + 1) * width // 2)
            out = mm(value[rows, :], wdown[h].reshape(2 * half, width // 2))
            if slot is None:
                result_out[:, cols] = out
            else:
                send[slot, :, cols] = out.astype(low)
    sends += reduce_pass(send_back, recv_back, back_sems, peers)
    stores = fetch([(send, parts_out)], store_sems, 1)

    def weights(i, carry):
        cols = pl.ds(pl.multiple_of(i * rows_up, rows_up), rows_up)
        for h in range(2):
            wgrad[h, i, 0:rows_up, :] = t_mm(
                gather[:, cols], pre[:, h * half : (h + 1) * half]
            ).astype(low)
            wgrad[h, i, rows_up : 2 * rows_up, :] = t_mm(
                value[:, cols], late[:, h * width // 2 : (h + 1) * width // 2]
            ).astype(low)
        return carry

    lax.fori_loop(0, width // rows_up, weights, 0)
    swapped = [(wgrad, other)]
    swaps = swap_begin(swapped, core_sems)
    sends += swaps
    reduce_wait(send_back, recv_back, back_sems, peers)
    norm_back_parts(middle_grad_out, recv_back, grad, x, par[2:3, :], sums_out)
    swap_end(swaps, swapped)
    stores += fetch([(wgrad.at[lax.axis_index("section")], half_out)], store_sems)
    for copy in sends:
        copy.wait_send()
    for store in stores:
        store.wait()


def ff_backward_kernel(
    s, grad, middle, par_all, lengths, pack, second_hbm, value_hbm, slope_hbm, earlier,
    half_out, middle_grad_out, sums_out, summed,
    gather, wup, wdown, second, value, slope, pre, wgrad, other, send, recv, gather_sems,
    reduce_sems, load_sems, store_sems, mine, arrived, plane_sems, sum_sems, core_sems,
):
    par = par_all.at[s]
    me = lax.axis_index("seq")
    peers = neighbours(me)
    count, width = grad.shape
    greeted = greet(in_plane(peers[:2]) + plane_devices() + [other_core()])
    half = wup.shape[3]
    units = 2 * half
    up_rows = wup.shape[2]
    loads = fetch(
        [
            (pack.at[:, :, pl.ds(0, up_rows), :], wup),
            (pack.at[:, :, pl.ds(up_rows, wdown.shape[2]), :], wdown),
            (slope_hbm, slope),
            (second_hbm, second),
            (value_hbm, value),
        ],
        load_sems,
    )
    masked_into(gather, me * count, grad, lengths)
    all_here(greeted)
    sends = gather_begin(gather, gather_sems, me, peers, count)
    plane_sum = PlaneSum(earlier, mine, arrived, plane_sems, sum_sems)
    plane_sum.begin()
    for load in loads[:3]:
        load.wait()
    for slot, part in ((None, None), *HALF_ORDER):
        if slot is None:
            rows, sent = rows_of(me, count), None
        else:
            rows = half_rows(peers[slot], part, count)
            sent = slice(part * count // 2, (part + 1) * count // 2)
            gather_wait_half(gather, gather_sems, slot, part, peers, count)

        def hidden(i, carry):
            cols = pl.ds(pl.multiple_of(i * up_rows, up_rows), up_rows)
            back = mm_t(gather[rows, : width // 2], wdown[0, i]) + mm_t(
                gather[rows, width // 2 :], wdown[1, i]
            )
            pre[rows, cols] = (back * slope[rows, cols].astype(f32)).astype(low)
            return carry

        lax.fori_loop(0, units // up_rows, hidden, 0)

        def through(i, carry):
            cols = pl.ds(pl.multiple_of(i * up_rows, up_rows), up_rows)
            back = mm_t(pre[rows, :half], wup[0, i]) + mm_t(pre[rows, half:], wup[1, i])
            if slot is None:
                middle_grad_out[:, cols] = back
            else:
                send[slot, sent, cols] = back.astype(low)
            return carry

        lax.fori_loop(0, width // up_rows, through, 0)
        if slot is None:
            sends += gather_forward(gather, gather_sems, peers, count)
        else:
            sends += reduce_send_half(slot, part, send, recv, reduce_sems, peers)
    plane_sum.forward()
    for load in loads[3:]:
        load.wait()

    def weights(i, carry):
        cols = pl.ds(pl.multiple_of(i * up_rows, up_rows), up_rows)
        for h in range(2):
            wgrad[h, i, 0:up_rows, :] = t_mm(
                second[:, cols], pre[:, h * half : (h + 1) * half]
            ).astype(low)
            wgrad[h, i, up_rows : 2 * up_rows, :] = t_mm(
                value[:, cols], gather[:, h * width // 2 : (h + 1) * width // 2]
            ).astype(low)
        return carry

    lax.fori_loop(0, width // up_rows, weights, 0)
    swapped = [(wgrad, other)]
    swaps = swap_begin(swapped, core_sems)
    sends += swaps
    sends += reduce_pass(send, recv, reduce_sems, peers)
    swap_end(swaps, swapped)
    stores = fetch([(wgrad.at[lax.axis_index("section")], half_out)], store_sems)
    plane_sum.end(summed)
    sends += plane_sum.sends
    reduce_wait(send, recv, reduce_sems, peers)
    norm_back_parts(middle_grad_out, recv, grad, middle, par[2:3, :], sums_out)
    for copy in sends:
        copy.wait_send()
    for store in stores:
        store.wait()


def t_mm_exact(a, b):
    return lax.dot_general(
        a, b, (((0,), (0,)), ((), ())), preferred_element_type=f32, precision=precise
    )


def mm_t_exact(a, b):
    return lax.dot_general(
        a, b, (((1,), (1,)), ((), ())), preferred_element_type=f32, precision=precise
    )


def dot_exact(a, b):
    return jnp.dot(a, b, preferred_element_type=f32, precision=precise)


def by_layer(begin, triples, layer_sems, keep_sems, base=0):
    section = lax.axis_index("section")
    for index in range(2):

        @pl.when(section == index)
        def _():
            for at, (first, second, target) in enumerate(triples, base):
                kept, sent = (first, second) if index == 0 else (second, first)
                slot = target.at[index]
                copies = (
                    pltpu.make_async_copy(kept, slot, keep_sems.at[at]),
                    remote_to(sent, slot, layer_sems, at, other_core()),
                )
                for copy in copies:
                    if begin:
                        copy.start()
                    else:
                        copy.wait()


def mixer_backward_kernel(
    s, grad, x, par_all, small_all, embedding, late, lengths, pack, filt_hbm, waves_hbm, back_hbm, normed_hbm, proj_hbm,
    stream_hbm, prod_hbm, spec_hbm, filtered_hbm, gated_hbm, waves1_hbm, waves2_hbm, steep1_hbm,
    steep2_hbm, earlier,
    half_out, small_out, input_grad_out, summed,
    gather, win, wout, filt, waves, back, normed, proj, streams, prod, spec, filtered, gated,
    gated_grad, filtered_grad, both, grad_spec, grad_sum, filter_grad, mixed, proj_grad, wgrad_in, wgrad_out_part,
    other_in, other_out, waves1, waves2, steep1, steep2, sums, taps_sum, send, recv, gather_sems, reduce_sems, load_sems, store_sems,
    mine, arrived, plane_sems, sum_sems, core_sems,
):
    par, small = par_all.at[s], small_all.at[s]
    me = lax.axis_index("seq")
    peers = neighbours(me)
    if s == 0:
        x = x.at[lax.axis_index("section"), 0]
    count, width = grad.shape
    greeted = greet(in_plane(peers[:2]) + plane_devices() + [other_core()])
    length = gather.shape[0]
    chans = prod.shape[1]
    half = win.shape[3]
    depth = win.shape[2]
    loads = fetch(
        weight_pairs_mixer(pack, win, wout)
        + [
            (stream_hbm, streams),
            (waves_hbm, waves),
            (filt_hbm, filt),
            (spec_hbm, spec),
            (back_hbm, back),
            (prod_hbm, prod),
            (filtered_hbm, filtered),
            (proj_hbm, proj),
            (normed_hbm, normed),
            (gated_hbm, gated),
            (waves1_hbm, waves1),
            (waves2_hbm, waves2),
            (steep1_hbm, steep1),
            (steep2_hbm, steep2),
        ],
        load_sems,
    )
    masked_into(gather, me * count, grad, lengths)
    all_here(greeted)
    sends = gather_begin(gather, gather_sems, me, peers, count)
    plane_sum = PlaneSum(earlier, mine, arrived, plane_sems, sum_sems)
    plane_sum.begin()
    for load in loads[1:6]:
        load.wait()
    tile_rows = 256
    for slot in (None, 0, 1, 2):
        source = me if slot is None else peers[slot]
        rows = rows_of(source, count)
        if slot is not None:
            gather_wait(gather, gather_sems, slot, peers, count)
        value = (
            mm_t(gather[rows, : width // 2], wout[0].reshape(chans, width // 2))
            + mm_t(gather[rows, width // 2 :], wout[1].reshape(chans, width // 2))
        ).astype(low)
        gated_grad[rows, :] = value
        filtered_grad[rows, :] = (
            value.astype(f32) * streams[rows, chans : 2 * chans].astype(f32)
        ).astype(low)
        if slot is None:
            sends += gather_forward(gather, gather_sems, peers, count)
            for load in loads[6:]:
                load.wait()
            loads[0].wait()
        if slot == 2:
            plane_sum.forward()

        def spectrum(i, carry):
            up = pl.ds(pl.multiple_of(i * tile_rows, tile_rows), tile_rows)
            down = pl.ds(pl.multiple_of(i * tile_rows + length, tile_rows), tile_rows)
            fg_cos = mm(waves[up, rows], filtered_grad[rows, :])
            fg_sin = mm(waves[down, rows], filtered_grad[rows, :])
            if slot is not None:
                fg_cos = fg_cos + grad_sum[up, :]
                fg_sin = fg_sin + grad_sum[down, :]
            if slot != 2:
                grad_sum[up, :] = fg_cos
                grad_sum[down, :] = fg_sin
            else:
                filt_cos, filt_sin = filt[up, :], filt[down, :]
                grad_spec[up, :] = fg_cos.astype(low)
                grad_spec[down, :] = fg_sin.astype(low)
                both[up, :] = (filt_cos * fg_cos + filt_sin * fg_sin).astype(low)
                both[down, :] = (filt_cos * fg_sin - filt_sin * fg_cos).astype(low)
            return carry

        lax.fori_loop(0, length // tile_rows, spectrum, 0)
    mixed[pl.ds(length, 8), :] = jnp.zeros((8, mixed.shape[1]), f32)

    def streams_back(i, carry):
        rows = pl.ds(pl.multiple_of(i * tile_rows, tile_rows), tile_rows)
        value = mm(back[rows, :], both[...]) * (1.0 / length)
        fg = filtered_grad[rows, :].astype(f32)
        prod_grad = (value + small[153:154, :] * fg).astype(low).astype(f32)
        mixed[rows, 0:chans] = (
            (prod_grad * streams[rows, 2 * chans : 3 * chans].astype(f32)).astype(low).astype(f32)
        )
        mixed[rows, chans : 2 * chans] = (
            (gated_grad[rows, :].astype(f32) * filtered[rows, :]).astype(low).astype(f32)
        )
        mixed[rows, 2 * chans : 3 * chans] = (
            (prod_grad * streams[rows, 0:chans].astype(f32)).astype(low).astype(f32)
        )
        return carry + jnp.sum(fg * prod[rows, :].astype(f32), axis=0, keepdims=True)

    small_out[...] = jnp.zeros(small_out.shape, f32)
    small_out[153:154, :] = lax.fori_loop(
        0, length // tile_rows, streams_back, jnp.zeros((1, chans), f32)
    )
    step = 128
    for slot in (2, 0, 1, None):
        target = me if slot is None else peers[slot]

        def short_back(i, carry):
            start = pl.multiple_of(target * count + i * step, step)
            for g in range(3):
                cols = slice(g * chans, (g + 1) * chans)
                tile = mixed[pl.ds(start, step + 8), cols]
                now = tile[:step]
                after = pltpu.roll(tile, step + 7, 0)[:step]
                later = pltpu.roll(tile, step + 6, 0)[:step]
                proj_grad[pl.ds(start, step), cols] = (
                    small[144 + 3 * g : 145 + 3 * g, :] * now
                    + small[145 + 3 * g : 146 + 3 * g, :] * after
                    + small[146 + 3 * g : 147 + 3 * g, :] * later
                ).astype(low)
            return carry

        lax.fori_loop(0, count // step, short_back, 0)
        rows = rows_of(target, count)

        def through(i, carry):
            cols = pl.ds(pl.multiple_of(i * depth, depth), depth)
            value = mm_t(proj_grad[rows, :half], win[0, i]) + mm_t(proj_grad[rows, half:], win[1, i])
            if slot is None:
                input_grad_out[:, cols] = value
            else:
                send[slot, :, cols] = value.astype(low)
            return carry

        lax.fori_loop(0, width // depth, through, 0)
        if slot is not None:
            sends += reduce_send(slot, send, recv, reduce_sems, peers)

    def weights(i, carry):
        cols = pl.ds(pl.multiple_of(i * depth, depth), depth)
        for h in range(2):
            wgrad_in[h, i] = t_mm(normed[:, cols], proj_grad[:, h * half : (h + 1) * half]).astype(
                low
            )
        return carry

    lax.fori_loop(0, width // depth, weights, 0)
    for h in range(2):
        value = t_mm(gated[...], gather[:, h * width // 2 : (h + 1) * width // 2]).astype(low)
        wgrad_out_part[h] = value.reshape(wgrad_out_part.shape[1:])
    swapped = [(wgrad_in, other_in), (wgrad_out_part, other_out)]
    swaps = swap_begin(swapped, core_sems)
    sends += swaps
    sends += reduce_pass(send, recv, reduce_sems, peers)
    taps_sum[...] = jnp.zeros(taps_sum.shape, f32)

    def tap_sums(i, carry):
        start = pl.multiple_of(i * step, step)
        for g in range(3):
            cols = slice(g * chans, (g + 1) * chans)
            tile = mixed[pl.ds(start, step + 8), cols]
            seen = proj[pl.ds(start, step), cols].astype(f32)
            for at in range(3):
                shift = pltpu.roll(tile, step + 8 - at, 0)[:step] if at else tile[:step]
                taps_sum[8 * at : 8 * at + 8, cols] += jnp.sum(
                    (seen * shift).reshape(step // 8, 8, chans), axis=0
                )
        return carry

    lax.fori_loop(0, length // step, tap_sums, 0)

    def filter_spectrum(i, carry):
        up = pl.ds(pl.multiple_of(i * tile_rows, tile_rows), tile_rows)
        down = pl.ds(pl.multiple_of(i * tile_rows + length, tile_rows), tile_rows)
        prod_cos, prod_sin = spec[up, :].astype(f32), spec[down, :].astype(f32)
        fg_cos, fg_sin = grad_spec[up, :].astype(f32), grad_spec[down, :].astype(f32)
        both[up, :] = (prod_cos * fg_cos + prod_sin * fg_sin).astype(low)
        both[down, :] = (prod_cos * fg_sin - prod_sin * fg_cos).astype(low)
        return carry

    lax.fori_loop(0, length // tile_rows, filter_spectrum, 0)

    def filter_back(i, carry):
        rows = pl.ds(pl.multiple_of(i * tile_rows, tile_rows), tile_rows)
        times = lax.broadcasted_iota(jnp.int32, (tile_rows, 1), 0) + i * tile_rows
        fade = jnp.exp(-times.astype(f32) * small[154:155, :])
        filter_grad[rows, :] = mm(back[rows, :], both[...]) * (1.0 / length) * fade
        return carry

    lax.fori_loop(0, length // tile_rows, filter_back, 0)
    small_out[0:64, :] = t_mm_exact(waves2[...], filter_grad[...])
    back2 = mm_t_exact(filter_grad[...], small[0:64, :]) * steep2[...]
    small_out[64:128, 0:64] = t_mm_exact(waves1[...], back2)
    back1 = mm_t_exact(back2, small[64:128, 0:64]) * steep1[...]
    small_out[64:128, 128:192] = t_mm_exact(embedding[:, 0:64], back1)
    for g in range(3):
        for at in range(3):
            small_out[144 + 3 * g + at : 145 + 3 * g + at, :] = jnp.sum(
                taps_sum[8 * at : 8 * at + 8, g * chans : (g + 1) * chans], axis=0, keepdims=True
            )
    swap_end(swaps, swapped)
    stores = fetch(half_pairs_mixer(half_out, wgrad_in, wgrad_out_part), store_sems)
    plane_sum.end(summed)
    sends += plane_sum.sends
    reduce_wait(send, recv, reduce_sems, peers)
    norm_back_parts(input_grad_out, recv, grad, x, par[0:1, :], sums)
    for q in range(width // chans):
        cols = slice(q * chans, (q + 1) * chans)
        small_out[128 + 2 * q : 130 + 2 * q, :] = sums[:, cols]
        small_out[136 + 2 * q : 138 + 2 * q, :] = late[:, cols]
    for copy in sends:
        copy.wait_send()
    for store in stores:
        store.wait()


def run_kernel(kernel, name, collective_id, operands, in_vmem, outs, out_vmem, scratch, flops):
    inside = pl.BlockSpec(memory_space=pltpu.VMEM)
    outside = pl.BlockSpec(memory_space=pl.ANY)
    scalars = pl.BlockSpec(memory_space=pltpu.SMEM)
    return pl.pallas_call(
        kernel,
        out_shape=[jax.ShapeDtypeStruct(shape, kind) for shape, kind in outs],
        in_specs=[
            scalars if item.dtype == jnp.int32 else inside if at in in_vmem else outside
            for at, item in enumerate(operands)
        ],
        out_specs=[inside if at in out_vmem else outside for at in range(len(outs))],
        scratch_shapes=scratch,
        compiler_params=pltpu.CompilerParams(
            collective_id=collective_id, has_side_effects=True, vmem_limit_bytes=60 * 2**20
        ),
        cost_estimate=pl.CostEstimate(flops=flops, bytes_accessed=2**25, transcendentals=0),
        name=name,
    )(*operands)


def exchange_scratch(count, width):
    return [pltpu.VMEM((3, count, width), low), pltpu.VMEM((3, count, width), low)]


def exchange_semaphores(count):
    return [pltpu.SemaphoreType.DMA((2, count)), pltpu.SemaphoreType.DMA((count,))]


def semaphores(loads, stores):
    return [
        pltpu.SemaphoreType.DMA((2, 6)),
        pltpu.SemaphoreType.DMA((2, 10)),
        pltpu.SemaphoreType.DMA((loads,)),
        pltpu.SemaphoreType.DMA((stores,)),
    ]


def mixer_weights_scratch(pack, width):
    _, dp_count, depth, cols = pack.shape
    return [
        pltpu.VMEM((2, dp_count, depth, 3 * cols // 4), low),
        pltpu.VMEM((2, dp_count, depth // 4, cols), low),
    ]


def mixer_forward(s, x, lengths, weights, waves, back, gathered):
    gathers = gathered is not None
    count, width = x.shape[-2:]
    length = waves.shape[1]
    chans, half = width // 4, width // 2
    knots, dp_count = chans // 4, lax.axis_size("dp")
    pack_shape = (2, dp_count, width // dp_count, half)
    pack = jax.ShapeDtypeStruct(pack_shape, low)
    vm, dma = pltpu.VMEM, pltpu.SemaphoreType.DMA
    outs = [
        ((length, width), low),
        ((length, 3 * chans), low),
        ((length, 3 * chans), low),
        ((length, chans), low),
        ((2 * length, chans), low),
        ((length, chans), f32),
        ((length, chans), low),
        ((count, width), f32),
    ]
    more = []
    if gathers:
        cotangent, embedding = gathered
        depth = weights[0].shape[0]
        units = 2 * half
        ff_shape = (2, dp_count, 2 * width // dp_count, half)
        half_in = 3 * chans // 2
        filters = [((2 * length, chans), f32), *[((length, knots), f32)] * 4]
        outs = [
            (pack_shape, low),
            (ff_shape, low),
            ((length, width), low),
            ((2, 8, width), f32),
            ((2, 160, chans), f32),
            (pack_shape, low),
            (ff_shape[2:], low),
            *filters,
            *filters,
            ((length, width), low),
            ((length, units), low),
            ((length, units), low),
            ((count, width), f32),
        ] + outs
        more = [
            *[vm((length, knots), f32)] * 4,
            vm((length, chans), low),
            vm((*pack_shape[:3], half // 4), low),
            vm(ff_shape, low),
            vm((length, width), low),
            vm(pack_shape, low),
            *[dma((2, 4)), dma((2, 3))] * 4,
            dma((2, 6)),
            dma((15,)),
            vm((2, *pack_shape[2:]), low),
            vm((2, *ff_shape[2:]), low),
            vm((2, 8, width), f32),
            vm((2, 160, chans), f32),
            vm((2, 4, depth, half_in), low),
            vm((2, 4 * depth, half_in // 3), low),
            vm((2, 4, depth, half), low),
            dma((2, 7)),
            dma((2, 1)),
            dma((2, 7)),
            dma((2, 1)),
            dma((2, 1)),
            dma((2, 1)),
            vm((length, width), low),
            *exchange_scratch(count, width),
            dma((2, 6)),
            dma((2, 10)),
            dma((5,)),
        ]
        operands = (cotangent, embedding, lengths, *weights, waves, back)
        inside = range(len(operands) - 1)
        out_inside = (len(outs) - 9, len(outs) - 1)
    else:
        par, small, weights, filt = weights
        operands = (par, small, lengths, weights, filt, waves, back)
        inside = range(3)
        out_inside = (len(outs) - 1,)
    return run_kernel(
        partial(mixer_forward_kernel, s, gathers),
        "opening" if gathers else "mixer_forward",
        1 + s,
        (x, *operands),
        inside,
        outs,
        out_inside,
        [vm((length, width), low)]
        + mixer_weights_scratch(pack, width)
        + [
            vm((2 * length, chans), f32),
            vm((2 * length, length), low),
            vm((length, 2 * length), low),
            vm((length + 8, 3 * chans), f32),
            vm((length, 3 * chans), low),
            vm((length, 3 * chans), low),
            vm((length, chans), low),
            vm((2 * length, chans), low),
            vm((2 * length, chans), low),
            vm((length, chans), f32),
            vm((length, chans), low),
        ]
        + exchange_scratch(count, width)
        + semaphores(8, 7)
        + more,
        10**10,
    )


def ff_turn(s, cotangent, x, par, lengths, pack, late):
    count, width = x.shape
    _, dp_count, rows, half = pack.shape
    length, units = 4 * count, 2 * half
    vm = pltpu.VMEM
    return run_kernel(
        partial(ff_turn_kernel, s),
        "ff_turn",
        4,
        (cotangent, x, par, lengths, pack, late),
        range(3),
        [
            (pack.shape[1:], low),
            ((3, count, width), low),
            ((count, width), f32),
            ((count, width), f32),
            ((2, width), f32),
        ],
        (2, 3, 4),
        [vm((length, width), low)] * 2
        + [vm((2, dp_count, rows // 2, half), low)] * 2
        + [vm((length, units), low)] * 2
        + [vm(pack.shape, low), vm(pack.shape[1:], low)]
        + [vm((3, count, width), low)] * 3
        + semaphores(3, 2)
        + [pltpu.SemaphoreType.DMA((2, 1))],
        3 * 10**10,
    )


def ff_backward(s, grad, middle, par, lengths, pack, second, value, slope, earlier):
    count, width = grad.shape
    _, dp_count, rows, half = pack.shape
    length, units = value.shape
    vm = pltpu.VMEM
    weights = [vm((2, dp_count, rows // 2, half), low)] * 2
    return run_kernel(
        partial(ff_backward_kernel, s),
        "ff_backward",
        5,
        (grad, middle, par, lengths, pack, second, value, slope, earlier),
        range(3),
        [
            (pack.shape[1:], low),
            ((count, width), f32),
            ((2, width), f32),
            (earlier.shape[1:], low),
        ],
        (1, 2, 3),
        [vm((length, width), low)]
        + weights
        + [vm((length, width), low)]
        + [vm((length, units), low)] * 3
        + [vm(pack.shape, low), vm(pack.shape[1:], low)]
        + exchange_scratch(count, width)
        + semaphores(5, 1)
        + plane_sum_scratch(earlier)
        + [pltpu.SemaphoreType.DMA((2, 1))],
        2 * 10**10,
    )


def mixer_backward(
    s, grad, x, par, small, embedding, late, lengths, pack, waves, back, kept, earlier
):
    normed, proj, streams, prod, spec, filtered, gated, filt, *network = kept
    count, width = grad.shape
    length, chans = prod.shape
    knots = network[0].shape[1]
    vm = pltpu.VMEM
    weights = mixer_weights_scratch(pack, width)
    return run_kernel(
        partial(mixer_backward_kernel, s),
        "mixer_backward",
        7 + s,
        (grad, x, par, small, embedding, late, lengths, pack, filt, waves, back, normed, proj,
         streams, prod, spec, filtered, gated, *network, earlier),
        range(6),
        [
            (pack.shape[1:], low),
            (small.shape[1:], f32),
            ((count, width), f32),
            (earlier.shape[1:], low),
        ],
        (1, 2, 3),
        [vm((length, width), low)]
        + weights
        + [
            vm((2 * length, chans), f32),
            vm((2 * length, length), low),
            vm((length, 2 * length), low),
            vm((length, width), low),
            vm((length, 3 * chans), low),
            vm((length, 3 * chans), low),
            vm((length, chans), low),
            vm((2 * length, chans), low),
            vm((length, chans), f32),
            vm((length, chans), low),
            vm((length, chans), low),
            vm((length, chans), low),
            vm((2 * length, chans), low),
            vm((2 * length, chans), low),
            vm((2 * length, chans), f32),
            vm((length, chans), f32),
            vm((length + 8, 3 * chans), f32),
            vm((length, 3 * chans), low),
        ]
        + weights
        + [vm(item.shape[1:], low) for item in weights]
        + [vm((length, knots), f32)] * 4
        + [vm((2, width), f32), vm((24, 3 * chans), f32)]
        + exchange_scratch(count, width)
        + semaphores(19, 5)
        + plane_sum_scratch(earlier)
        + [pltpu.SemaphoreType.DMA((2, 2))],
        2 * 10**10,
    )


def shuffle_stage(w_in, w_out, w_up, stage_in, stage_out, stage_up):
    depth, chans = w_in.shape[0], w_out.shape[1] // 4
    count = lax.axis_size("dp")
    half_in = stage_in.shape[3]
    piece = chans // count
    for h in range(2):
        for j in range(4):
            for c in range(0, half_in, 2 * piece):
                pair = []
                for col in (c, c + piece):
                    g, d = divmod((h * half_in + col) // piece, count)
                    at = ((g * count + d) * 4 + j) * piece
                    pair.append(w_in[:, at : at + piece].astype(f32))
                stage_in[h, j, :, c : c + 2 * piece] = jnp.concatenate(pair, 1).astype(low)
            for d in range(2):
                at = ((2 * h + d) * 4 + j) * chans
                stage_up[h, j, :, d * chans : (d + 1) * chans] = w_up[:, at : at + chans]
    part = half_in // 3
    for h in range(2):
        for q in range(4):
            at = (h * 4 + q) * part
            stage_out[h, q * depth : (q + 1) * depth, :] = w_out[:, at : at + part]


def parameters_stage(me, par, small, gain, shift, taps, first, second, last, direct, rates):
    chans = small.shape[1]
    count = lax.axis_size("dp")
    piece = chans // count
    width = last.shape[2]
    par[0:1, :] = gain[0, 0:1, :]
    par[1:2, :] = shift[0, 0:1, :]
    par[2:3, :] = gain[0, 1:2, :]
    par[3:4, :] = shift[0, 1:2, :]
    par[4:8, :] = jnp.zeros((4, width), f32)
    small[64:160, :] = jnp.zeros((96, chans), f32)
    small[64:128, 0:64] = second[0]
    for row in range(first.shape[0]):
        small[64 + row : 65 + row, 128:192] = first[row]
    for j in range(4):

        @pl.when(me == j)
        def _():
            for d in range(0, count, 2):
                cols = slice(d * piece, (d + 2) * piece)

                def picked(ref, rows, base=0):
                    at = [base + ((d + k) * 4 + j) * piece for k in range(2)]
                    return jnp.concatenate([ref[rows, a : a + piece] for a in at], 1)

                small[0:64, cols] = picked(last.at[0], slice(0, 64))
                for g in range(3):
                    for tap in range(3):
                        row = 144 + 3 * g + tap
                        small[row : row + 1, cols] = picked(
                            taps.at[tap], slice(0, 1), g * width
                        )
                small[153:154, cols] = picked(direct, slice(0, 1))
                small[154:155, cols] = picked(rates, slice(0, 1))


def shuffle_send(section, me, targets, sources, parts, parameters, sems):
    stage_in, stage_out, stage_up, w_down = sources
    mixer_parts, ff_parts = parts
    in_sems, out_sems, up_sems, down_sems, par_sems, small_sems = sems
    depth, half_in = stage_in.shape[2:]
    half = stage_up.shape[3]
    copies = [
        remote_to(item.at[section], item.at[section], at, 0, other_core())
        for item, at in zip(parameters, (par_sems, small_sems))
    ]
    for e, (t, seq, device) in enumerate(targets):
        target = mixer_parts.at[section, rows_of(me, depth), pl.ds(0, half_in)]
        copies.append(remote_to(stage_in.at[t, seq], target, in_sems, e, device))
    target = mixer_parts.at[section, :, pl.ds(half_in, half_in // 3)]
    copies.append(remote_to(stage_out.at[1 - section], target, out_sems, 0, other_core()))
    for e, (t, seq, device) in enumerate(targets):
        target = ff_parts.at[section, rows_of(me, depth), :]
        copies.append(remote_to(stage_up.at[t, seq], target, up_sems, e, device))
    cols = pl.ds(pl.multiple_of((1 - section) * half, half), half)
    target = ff_parts.at[section, pl.ds(4 * depth, 4 * depth), :]
    copies.append(remote_to(w_down.at[:, cols], target, down_sems, 0, other_core()))
    for copy in copies:
        copy.start()
    mixer_parts[section, rows_of(me, depth), 0:half_in] = stage_in[section, me]
    mixer_parts[section, :, half_in:] = stage_out[section]
    ff_parts[section, rows_of(me, depth), :] = stage_up[section, me]
    cols = pl.ds(pl.multiple_of(section * half, half), half)
    ff_parts[section, 4 * depth : 8 * depth, :] = w_down[:, cols]
    return copies


def shuffle_wait_mixer(section, me, targets, parts, stage_in, in_sems, out_sems):
    depth, half_in = stage_in.shape[2:]
    for e, (t, seq, device) in enumerate(targets):
        block = parts.at[t, rows_of(seq, depth), pl.ds(0, half_in)]
        remote_to(block, block, in_sems, e, device).wait_recv()
    block = parts.at[1 - section, :, pl.ds(half_in, half_in // 3)]
    remote_to(block, block, out_sems, 0, other_core()).wait_recv()


def shuffle_wait_ff(section, me, targets, parts, stage_up, up_sems, down_sems):
    depth = stage_up.shape[2]
    for e, (t, seq, device) in enumerate(targets):
        block = parts.at[t, rows_of(seq, depth), :]
        remote_to(block, block, up_sems, e, device).wait_recv()
    block = parts.at[1 - section, pl.ds(4 * depth, 4 * depth), :]
    remote_to(block, block, down_sems, 0, other_core()).wait_recv()


def shuffle_targets(section, me, peers):
    targets = [(section, peer, {"seq": peer}) for peer in peers]
    targets.append((1 - section, me, other_core()))
    targets += [(1 - section, peer, {**other_core(), "seq": peer}) for peer in peers]
    return targets


def finish_kernel(
    vec0, vec1, mixer0, mixer1, ff0, ff1, grad0, grad1, parts, own_part, x, out0, lengths,
    block_outputs, input_grads, got_in, got_out, got_up, got_down, vec_out,
    mine0, arrived0, plane_sems0, sum_sems0, mine1, arrived1, plane_sems1, sum_sems1,
    vec_other, vec_sum, vec_arrived, vec_all, stage_mixer, stage_ff, own_sems, load_sems,
    layer_sems, keep_sems, vec_core_sems, vec_sum_sems, vec_plane_sems, vec_seq_sems, in_sems, out_sems, up_sems, down_sems,
    send, recv, out1, reduce_sems,
):
    section = lax.axis_index("section")
    me = lax.axis_index("seq")
    here, near, far = along_planes()
    planes = (near, far, (near + 2) % 4)
    peers = neighbours(me)
    depth, half_in = got_in.shape[2:]
    targets = shuffle_targets(section, me, peers)
    greeted = greet([device for _, _, device in targets] + [{"dp": plane} for plane in planes])
    middle = mixer0.shape[2] // 2
    chunks = (pl.ds(0, middle), pl.ds(middle, middle))
    in_cols = (pl.ds(0, middle), pl.ds(middle, half_in - middle))

    def columns(e, at):
        t, seq, device = targets[e]
        return remote_to(
            stage_mixer.at[t, rows_of(seq, depth), in_cols[at]],
            got_in.at[section, me, :, in_cols[at]],
            in_sems,
            2 * e + at,
            device,
        )

    out_columns = remote_to(
        stage_mixer.at[1 - section, :, pl.ds(half_in, half_in // 3)], got_out.at[section], out_sems,
        0, other_core(),
    )

    def send_layer(s, at):
        for index in range(2):

            @pl.when(section == index)
            def _():
                for e in range(3) if index == s else range(3, 7):
                    columns(e, at).start()
                if at == 1 and index != s:
                    out_columns.start()

    all_here(greeted)
    for index, vec in enumerate((vec1, vec0)):

        @pl.when(section == index)
        def _():
            remote_to(vec, vec_other, vec_core_sems, 0, other_core()).start()

    sends = []
    vec_swap = remote_to(vec_other, vec_other, vec_core_sems, 0, other_core())
    vec_swap.wait_recv()
    sends.append(vec_swap)

    @pl.when(section == 0)
    def _():
        vec_sum[...] = vec0[...] + vec_other[...]

    @pl.when(section == 1)
    def _():
        vec_sum[...] = vec1[...] + vec_other[...]

    count = 4
    chunk = vec_sum.shape[0] // count
    moves = [
        remote_to(
            vec_sum.at[rows_of(plane, chunk)], vec_arrived.at[slot], vec_sum_sems, slot,
            {"dp": plane},
        )
        for slot, plane in enumerate(planes)
    ]
    for copy in moves:
        copy.start()
    sends += moves
    plane_sums = [
        PlaneSum(mixer0.at[:, :, chunks[0]], mine0, arrived0, plane_sems0, sum_sems0),
        PlaneSum(mixer0.at[:, :, chunks[1]], mine1, arrived1, plane_sems1, sum_sems1),
    ]
    for plane_sum in plane_sums:
        plane_sum.begin()
    loads = fetch(
        [
            (parts, send),
            (ff0, stage_ff.at[0]),
            (ff1, stage_ff.at[1]),
            (mixer1, stage_mixer.at[1]),
        ],
        load_sems,
    )
    by_layer(True, ((grad0, grad1, input_grads),), layer_sems, keep_sems)
    loads[0].wait()
    for slot in (2, 0, 1):
        sends += reduce_send(slot, send, recv, reduce_sems, peers)
    for load in loads[1:]:
        load.wait()
    ups = []
    for e, (t, seq, device) in enumerate(targets):
        ups.append(
            remote_to(
                stage_ff.at[t, rows_of(seq, depth), :], got_up.at[section, me], up_sems, e, device
            )
        )
    downs = [
        remote_to(
            stage_ff.at[1 - section, pl.ds(4 * depth, 4 * depth), :], got_down.at[section],
            down_sems, 0, other_core(),
        )
    ]
    for copy in ups + downs:
        copy.start()
    sends += ups + downs
    send_layer(1, 0)
    send_layer(1, 1)
    keeps = fetch(
        [
            (stage_ff.at[section, rows_of(me, depth), :], got_up.at[section, me]),
            (stage_ff.at[section, pl.ds(4 * depth, 4 * depth), :], got_down.at[section]),
        ],
        own_sems,
    )

    for copy in moves:
        copy.wait_recv()
    own_chunk = rows_of(here, chunk)
    total = vec_sum[own_chunk, :]
    for slot in range(len(planes)):
        total = total + vec_arrived[slot]
    vec_all[me, own_chunk, :] = total
    moves = [
        remote_to(
            vec_all.at[me, own_chunk], vec_all.at[me, own_chunk], vec_plane_sems, slot,
            {"dp": plane},
        )
        for slot, plane in enumerate(planes)
    ]
    for copy in moves:
        copy.start()
    sends += moves
    for plane_sum in plane_sums:
        plane_sum.forward()
    sends += reduce_pass(send, recv, reduce_sems, peers)
    for slot, plane in enumerate(planes):
        block = vec_all.at[me, rows_of(plane, chunk)]
        remote_to(block, block, vec_plane_sems, slot, {"dp": plane}).wait_recv()
    moves = [
        remote(vec_all.at[me], vec_all.at[me], vec_seq_sems, slot, peer)
        for slot, peer in enumerate(peers)
    ]
    for copy in moves:
        copy.start()
    sends += moves

    reduce_wait(send, recv, reduce_sems, peers)
    start = me * own_part.shape[0]

    def add(rows):
        total = own_part[rows, :] + recv[0, rows, :].astype(f32) + recv[1, rows, :].astype(f32)
        out1[rows, :] = x[rows, :] + valid_rows(lengths, start + rows.start, 32) * total

    by_rows(own_part.shape[0], 32, add)
    by_layer(True, ((out0, out1, block_outputs),), layer_sems, keep_sems, 1)
    for at, plane_sum in enumerate(plane_sums):
        plane_sum.end(stage_mixer.at[0, :, chunks[at]])
        sends += plane_sum.sends
        send_layer(0, at)
    sends += [columns(e, at) for e in range(7) for at in range(2)] + [out_columns]
    keeps += fetch(
        [
            (
                stage_mixer.at[section, rows_of(me, depth), pl.ds(0, half_in)],
                got_in.at[section, me],
            ),
            (stage_mixer.at[section, :, pl.ds(half_in, half_in // 3)], got_out.at[section]),
        ],
        own_sems,
        2,
    )
    for slot, peer in enumerate(peers):
        block = vec_all.at[peer]
        remote(block, block, vec_seq_sems, slot, peer).wait_recv()
    keeps += fetch([(vec_all, vec_out)], own_sems, 4)
    for e, (t, seq, device) in enumerate(targets):
        block = got_up.at[t, seq]
        remote_to(block, block, up_sems, e, device).wait_recv()
        for at in range(2):
            block = got_in.at[t, seq, :, in_cols[at]]
            remote_to(block, block, in_sems, 2 * e + at, device).wait_recv()
    downs[0].wait_recv()
    out_columns.wait_recv()
    by_layer(False, ((grad0, grad1, input_grads),), layer_sems, keep_sems)
    by_layer(False, ((out0, out1, block_outputs),), layer_sems, keep_sems, 1)
    for copy in sends:
        copy.wait_send()
    for keep in keeps:
        keep.wait()


def unpack_kernel(
    blocks, grads, got_in, got_out, got_up, got_down, vec_all,
    block_outputs, input_grads, g_in, g_out, g_up, g_down, g_gain, g_bias, g_taps, g_first,
    g_second, g_last, g_direct,
    stage_blocks, stage_grads, load_sems, copy_sems,
):
    loads = fetch([(blocks, stage_blocks), (grads, stage_grads)], load_sems)
    depth = g_in.shape[0]
    half_in, half_up = got_in.shape[3], got_up.shape[3]
    chans = vec_all.shape[2]
    count = 4
    piece = chans // count
    for j in range(4):
        for d in range(count):
            at = (d * 4 + j) * chans
            h, col = divmod(d * chans, half_up)
            g_up[:, at : at + chans] = got_up[h, j, :, col : col + chans].astype(f32)
    for h in range(2):
        g_down[:, h * half_up : (h + 1) * half_up] = got_down[h].astype(f32)
    for load in loads:
        load.wait()
    copies = fetch([(stage_blocks, block_outputs), (stage_grads, input_grads)], copy_sems)
    for g in range(3):
        for d in range(count):
            h, col = divmod(g * chans + d * piece, half_in)
            for j in range(0, 4, 2):
                at = ((g * count + d) * 4 + j) * piece
                g_in[:, at : at + 2 * piece] = jnp.concatenate(
                    [got_in[h, j + k, :, col : col + piece].astype(f32) for k in range(2)], 1
                )
    part = half_in // 3
    for h in range(2):
        for q in range(4):
            at = (h * 4 + q) * part
            g_out[:, at : at + part] = got_out[h, q * depth : (q + 1) * depth, :].astype(f32)
    first = sum_of(vec_all, slice(64, 64 + g_first.shape[0]), slice(128, 192))
    for row in range(g_first.shape[0]):
        g_first[row] = first[row : row + 1]
    g_second[...] = sum_of(vec_all, slice(64, 128), slice(0, 64))
    for q in range(4):
        cols = slice(q * chans, (q + 1) * chans)
        early = sum_of(vec_all, slice(128 + 2 * q, 130 + 2 * q), slice(None))
        late = sum_of(vec_all, slice(136 + 2 * q, 138 + 2 * q), slice(None))
        g_gain[0:1, cols] = early[0:1]
        g_gain[1:2, cols] = late[0:1]
        g_bias[0:1, cols] = early[1:2]
        g_bias[1:2, cols] = late[1:2]
    for d in range(count):
        cols = slice(d * piece, (d + 1) * piece)
        for j in range(0, 4, 2):
            at = (d * 4 + j) * piece
            pair = slice(at, at + 2 * piece)

            def joined(rows):
                return jnp.concatenate([vec_all[j, rows, cols], vec_all[j + 1, rows, cols]], 1)

            g_last[:, pair] = joined(slice(0, 64))
            for g in range(3):
                for tap in range(3):
                    row = 144 + 3 * g + tap
                    start = g * 4 * chans + at
                    g_taps[tap, :, start : start + 2 * piece] = joined(slice(row, row + 1))
            g_direct[:, pair] = joined(slice(153, 154))

    for copy in copies:
        copy.wait()


def sum_of(blocks, rows, cols):
    return (blocks[0, rows, cols] + blocks[1, rows, cols]) + (
        blocks[2, rows, cols] + blocks[3, rows, cols]
    )


def finish(vec0, vec1, mixer0, mixer1, ff0, ff1, grad0, grad1, parts, own_part, x, out0, lengths):
    count, width = grad0.shape
    dp_count, rows, half = mixer0.shape
    depth = rows // 4
    chans = vec0.shape[1]
    half_in = 3 * chans // 2
    vm, dma = pltpu.VMEM, pltpu.SemaphoreType.DMA
    vec_rows = vec0.shape[0]
    chunk = jax.ShapeDtypeStruct((dp_count, rows, half // 2), low)
    return run_kernel(
        finish_kernel,
        "finish",
        10,
        (vec0, vec1, mixer0, mixer1, ff0, ff1, grad0, grad1, parts, own_part, x, out0, lengths),
        (0, 1, 6, 7, 9, 10, 11),
        [
            ((2, count, width), f32),
            ((2, count, width), f32),
            ((2, 4, depth, half_in), low),
            ((2, rows, half_in // 3), low),
            ((2, 4, depth, half), low),
            ((2, rows, half), low),
            ((4, vec_rows, chans), f32),
        ],
        (),
        plane_sum_scratch(chunk)
        + plane_sum_scratch(chunk)
        + [
            vm((vec_rows, chans), f32),
            vm((vec_rows, chans), f32),
            vm((3, vec_rows // 4, chans), f32),
            vm((4, vec_rows, chans), f32),
            vm((2, *mixer1.shape), low),
            vm((2, *ff1.shape), low),
            dma((5,)),
            dma((4,)),
            *exchange_semaphores(2),
            dma((2, 1)),
            dma((2, 3)),
            dma((2, 3)),
            dma((2, 3)),
            dma((2, 14)),
            dma((2, 1)),
            dma((2, 7)),
            dma((2, 1)),
            *exchange_scratch(count, width),
            vm((count, width), f32),
            dma((2, 10)),
        ],
        10**9,
    )


def unpack(blocks, grads, got, first_shape):
    width = blocks.shape[2]
    depth = got[0].shape[2]
    units = 4 * 2 * got[2].shape[3]
    knots = first_shape[1]
    inside = pl.BlockSpec(memory_space=pltpu.VMEM)
    outside = pl.BlockSpec(memory_space=pl.ANY)
    shapes = (
        blocks.shape, grads.shape, (depth, 3 * width), (depth, width), (depth, units),
        (4 * depth, width), (2, width), (2, width), (3, 1, 3 * width),
        (first_shape[0], 1, knots), (knots, knots),
        (knots, width), (1, width),
    )
    return pl.pallas_call(
        unpack_kernel,
        out_shape=[jax.ShapeDtypeStruct(shape, f32) for shape in shapes],
        in_specs=[outside] * 2 + [inside] * 5,
        out_specs=[outside] * 2 + [inside] * 11,
        scratch_shapes=[
            pltpu.VMEM(blocks.shape, f32),
            pltpu.VMEM(grads.shape, f32),
            pltpu.SemaphoreType.DMA((2,)),
            pltpu.SemaphoreType.DMA((2,)),
        ],
        compiler_params=pltpu.CompilerParams(vmem_limit_bytes=56 * 2**20),
        name="unpack",
    )(blocks, grads, *got)


def any_device(
    tokens,
    cotangent,
    lengths,
    norm_gain,
    norm_bias,
    mixer_in,
    short_kernel,
    filter_first,
    filter_second,
    filter_last,
    filter_bias,
    decay_rates,
    mixer_out,
    up_weight,
    down_weight,
):
    section = lax.axis_index("section")
    seq_index = lax.axis_index("seq")
    seq_count = lax.axis_size("seq")
    dp_count = lax.axis_size("dp")
    own_layer_first = section == 0
    local_len = tokens.shape[2]
    width = tokens.shape[3]
    hidden = up_weight.shape[2]
    row_len = local_len * seq_count
    chans = width // seq_count
    units = hidden // seq_count

    def share_columns(block, groups):
        rows = block.shape[0]
        inner = block.shape[1] // (groups * dp_count * seq_count)
        split = block.reshape(rows, groups, dp_count, seq_count, inner)
        split = jnp.transpose(split, (3, 0, 1, 2, 4))
        moved = lax.all_to_all(split, "seq", split_axis=0, concat_axis=0, tiled=True)
        return moved.reshape(seq_count * rows, groups * dp_count * inner)

    def unshare_columns(block, groups):
        rows = block.shape[0] // seq_count
        inner = block.shape[1] // (groups * dp_count)
        split = block.reshape(seq_count, rows, groups, dp_count, inner)
        moved = lax.all_to_all(split, "seq", split_axis=0, concat_axis=0, tiled=True)
        moved = jnp.transpose(moved, (1, 2, 3, 0, 4))
        return moved.reshape(rows, groups * dp_count * seq_count * inner)

    def gathered(block):
        whole = lax.all_gather(block, ("section", "dp"))
        return whole.reshape(2, dp_count * block.shape[0], block.shape[1])

    weights = (
        gathered(share_columns(mixer_in[0], 3)),
        gathered(mixer_out[0]),
        gathered(share_columns(up_weight[0], 1)),
        gathered(down_weight[0]),
    )

    def both(value):
        return lax.all_gather(value[0], "section")

    gains, shifts = both(norm_gain), both(norm_bias)
    taps, first_w, second_w = both(short_kernel), both(filter_first), both(filter_second)
    last_w, direct, rates = both(filter_last), both(filter_bias), both(decay_rates)

    def mine(value):
        lead = value.shape[:-1]
        split = value.reshape(*lead, dp_count, seq_count, -1)
        picked = lax.dynamic_index_in_dim(split, seq_index, len(lead) + 1, False)
        return picked.reshape(*lead, chans)

    def placed(value):
        lead = value.shape[:-1]
        split = value.reshape(*lead, dp_count, 1, -1)
        inner = split.shape[-1]
        empty = jnp.zeros((*lead, dp_count, seq_count, inner), value.dtype)
        at = [0] * len(lead) + [0, seq_index, 0]
        return lax.dynamic_update_slice(empty, split, at).reshape(*lead, width)

    waves = jnp.asarray(wave_tables(row_len))
    waves_back = waves

    def to_waves(x):
        both_parts = mm(waves, x)
        return both_parts[:row_len], both_parts[row_len:]

    def from_waves(cos_part, sin_part):
        joined = jnp.concatenate([cos_part, sin_part], 0).astype(low)
        return t_mm(waves_back, joined) * (1.0 / row_len)

    def ag(x):
        return lax.all_gather(x, "seq", axis=0, tiled=True)

    def rs(x):
        return lax.psum_scatter(x.astype(low), "seq", scatter_dimension=0, tiled=True).astype(f32)

    length_now = lax.dynamic_index_in_dim(lengths, section, 0, False)[0]
    positions = seq_index * local_len + jnp.arange(local_len)
    mask = (positions < length_now).astype(f32)[:, None]
    row_mask = (jnp.arange(row_len) < length_now).astype(f32)[:, None]
    own_tokens = lax.dynamic_index_in_dim(tokens, section, 0, False)[0].astype(f32)
    own_cotangent = lax.dynamic_index_in_dim(cotangent, section, 0, False)[0].astype(f32)

    def layer_forward(s, inputs):
        w_in, w_out, w_up, w_down = [w[s] for w in weights]
        kernel = mine(taps[s].reshape(3, 3, width))
        last_mine, direct_mine, rates_mine = mine(last_w[s]), mine(direct[s]), mine(rates[s])

        def own_filter(a, b, c):
            return filter_taps(a, b, c, rates_mine, row_len)

        filter_rows, filter_back = jax.vjp(own_filter, first_w[s], second_w[s], last_mine)
        filt_cos, filt_sin = to_waves(filter_rows.astype(low))
        normed = (norm_stats(inputs)[0] * gains[s, 0] + shifts[s, 0]).astype(low)
        normed = ag(normed)
        projected = [mm(normed, w_in[:, g * chans : (g + 1) * chans]) for g in range(3)]
        streams = [
            (
                kernel[0, g] * projected[g]
                + kernel[1, g] * shifted(projected[g], 1)
                + kernel[2, g] * shifted(projected[g], 2)
            ).astype(low)
            for g in range(3)
        ]
        wide = [x.astype(f32) for x in streams]
        product = (wide[0] * wide[2] * row_mask).astype(low)
        prod_cos, prod_sin = to_waves(product)
        filtered = from_waves(
            prod_cos * filt_cos - prod_sin * filt_sin, prod_cos * filt_sin + prod_sin * filt_cos
        ) + direct_mine * product.astype(f32)
        gated = (wide[1] * filtered).astype(low)
        middle = inputs + mask * rs(mm(gated, w_out))
        second = (norm_stats(middle)[0] * gains[s, 1] + shifts[s, 1]).astype(low)
        second = ag(second)
        value, slope = gelu_both(mm(second, w_up))
        value = value.astype(low)
        slope = slope.astype(low)
        result = middle + mask * rs(mm(value, w_down))
        saved = (
            inputs, normed, projected, wide, product, prod_cos, prod_sin, filt_cos, filt_sin,
            filtered, gated, middle, second, value, slope, kernel, direct_mine, filter_back,
        )
        return result, saved

    def layer_backward(s, grad, saved):
        w_in, w_out, w_up, w_down = [w[s] for w in weights]
        (
            inputs, normed, projected, wide, product, prod_cos, prod_sin, filt_cos, filt_sin,
            filtered, gated, middle, second, value, slope, kernel, direct_mine, filter_back,
        ) = saved
        out_low = ag((grad * mask).astype(low))
        pre = (mm_t(out_low, w_down) * slope.astype(f32)).astype(low)
        grad_down = t_mm(value, out_low)
        grad_up = t_mm(second, pre)
        mid_part, gain_late, bias_late = norm_back(rs(mm_t(pre, w_up)), middle, gains[s, 1])
        middle_grad = grad + mid_part
        branch = ag((middle_grad * mask).astype(low))
        gated_grad = mm_t(branch, w_out).astype(low)
        grad_out = t_mm(gated, branch)
        gated_grad = gated_grad.astype(f32)
        filtered_grad = (gated_grad * wide[1]).astype(low)
        fg_cos, fg_sin = to_waves(filtered_grad)
        fg_wide = filtered_grad.astype(f32)
        prod32 = product.astype(f32)
        product_grad = from_waves(
            filt_cos * fg_cos + filt_sin * fg_sin, filt_cos * fg_sin - filt_sin * fg_cos
        ) + direct_mine * fg_wide
        product_grad = product_grad.astype(low).astype(f32)
        filter_grad = from_waves(
            prod_cos * fg_cos + prod_sin * fg_sin, prod_cos * fg_sin - prod_sin * fg_cos
        )
        grad_first, grad_second, grad_last = filter_back(filter_grad)
        grad_direct = jnp.sum(fg_wide * prod32, 0)
        mixed = [
            (product_grad * wide[2]).astype(low).astype(f32),
            (gated_grad * filtered).astype(low).astype(f32),
            (product_grad * wide[0]).astype(low).astype(f32),
        ]
        proj = [
            (
                kernel[0, g] * mixed[g]
                + kernel[1, g] * shifted(mixed[g], -1)
                + kernel[2, g] * shifted(mixed[g], -2)
            ).astype(low)
            for g in range(3)
        ]
        grad_taps = jnp.stack(
            [
                jnp.stack(
                    [jnp.sum(mixed[g] * (shifted(projected[g], k) if k else projected[g]), 0) for g in range(3)]
                )
                for k in range(3)
            ]
        )
        proj = jnp.concatenate(proj, 1)
        grad_in = t_mm(normed, proj)
        in_part, gain_early, bias_early = norm_back(rs(mm_t(proj, w_in)), inputs, gains[s, 0])
        small = (
            jnp.stack([gain_early, gain_late]),
            jnp.stack([bias_early, bias_late]),
            placed(grad_taps).reshape(3, 3 * width),
            grad_first,
            grad_second,
            placed(grad_last),
            placed(grad_direct),
        )
        large = (grad_in, grad_out, grad_up, grad_down)
        return middle_grad + in_part, small, large

    first_out, first_saved = layer_forward(0, own_tokens)
    second_out, second_saved = layer_forward(1, first_out)
    second_grad, second_small, second_large = layer_backward(1, own_cotangent, second_saved)
    first_grad, first_small, first_large = layer_backward(0, second_grad, first_saved)

    swap = [(0, 1), (1, 0)]

    def by_layer(first, second):
        other = lax.ppermute(jnp.where(own_layer_first, second, first), "section", swap)
        return jnp.where(
            own_layer_first, jnp.stack([first, other]), jnp.stack([other, second])
        )[None, :, None]

    def summed(first, second):
        stacked = jnp.stack([first, second]).astype(low)
        rows = first.shape[0] // dp_count
        stacked = stacked.reshape(2 * dp_count, rows, first.shape[1])
        return lax.psum_scatter(stacked, ("section", "dp"), scatter_dimension=0, tiled=True)[0]

    sums = [summed(a, b) for a, b in zip(first_large, second_large)]
    sum_in = unshare_columns(sums[0], 3).astype(f32)
    sum_out = sums[1].astype(f32)
    sum_up = unshare_columns(sums[2], 1).astype(f32)
    sum_down = sums[3].astype(f32)
    stacked = jax.tree.map(lambda a, b: jnp.stack([a, b]), first_small, second_small)
    small = lax.psum(stacked, ("section", "dp", "seq"))
    small = [lax.dynamic_slice_in_dim(x, section, 1, 0) for x in small]
    sum_gain, sum_bias, sum_taps, sum_first, sum_second, sum_last, sum_direct = small
    return (
        by_layer(first_out, second_out),
        by_layer(first_grad, second_grad),
        sum_gain,
        sum_bias,
        sum_in[None],
        sum_taps,
        sum_first,
        sum_second,
        sum_last,
        sum_direct,
        sum_out[None],
        sum_up[None],
        sum_down[None],
    )


def plane_device(
    tokens,
    cotangent,
    lengths,
    norm_gain,
    norm_bias,
    mixer_in,
    short_kernel,
    filter_first,
    filter_second,
    filter_last,
    filter_bias,
    decay_rates,
    mixer_out,
    up_weight,
    down_weight,
):
    section = lax.axis_index("section")
    seq_count = lax.axis_size("seq")
    dp_count = lax.axis_size("dp")
    row_len = tokens.shape[2] * seq_count
    lengths = jnp.transpose(lengths)
    short_kernel = jnp.transpose(short_kernel, (1, 0, 2))
    filter_first = jnp.transpose(filter_first, (1, 0, 2))

    def gathered(part):
        whole = lax.all_gather(part, ("section", "dp"))
        return whole.reshape(2, dp_count, *part.shape)

    tables = wave_tables(row_len)
    waves = jnp.asarray(tables)
    waves_back = jnp.asarray(np.ascontiguousarray(tables.T))
    embedding = jnp.asarray(np.pad(position_rows(row_len), ((0, 0), (0, 95))))

    weights = (
        mixer_in[0], mixer_out[0], up_weight[0], down_weight[0], norm_gain, norm_bias, short_kernel,
        filter_first, filter_second, filter_last, filter_bias, decay_rates,
    )
    (
        first_mixer_pack, first_ff_pack, cotangent_low, par, small, second_mixer_pack, ff_part,
        *outs,
    ) = mixer_forward(
        0, tokens, lengths, weights, waves, waves_back, (cotangent, embedding)
    )
    first_filter, second_filter, first_saved, outs = outs[:5], outs[5:10], outs[10:13], outs[13:]
    first_out, *first_kept, first_middle = outs
    second_ff_pack = gathered(ff_part)
    *second_kept, second_middle = mixer_forward(
        1, first_out, lengths, (par, small, second_mixer_pack, second_filter[0]), waves, waves_back,
        None,
    )
    first_kept, second_kept = [*first_kept, *first_filter], [*second_kept, *second_filter]
    second_ff, result_parts, own_part, middle_grad, late = ff_turn(
        1, cotangent, second_middle, par, lengths, second_ff_pack, cotangent_low
    )

    def mixer_back(s, grad, x, late, pack, kept, earlier):
        return mixer_backward(
            s, grad, x, par, small, embedding, late, lengths, pack, waves, waves_back, kept, earlier
        )

    second_mixer, second_vec, second_grad, second_ff = mixer_back(
        1, middle_grad, first_out, late, second_mixer_pack, second_kept, second_ff
    )
    first_ff, middle_grad, late, second_mixer = ff_backward(
        0, second_grad, first_middle, par, lengths, first_ff_pack, *first_saved, second_mixer
    )
    first_mixer, first_vec, first_grad, first_ff = mixer_back(
        0, middle_grad, tokens, late, first_mixer_pack, first_kept, first_ff
    )
    block_outputs, input_grads, *got = finish(
        first_vec, second_vec, first_mixer, second_mixer, first_ff, second_ff, first_grad,
        second_grad, result_parts, own_part, second_middle, first_out, lengths,
    )
    (
        block_outputs, input_grads, sum_in, sum_out, sum_up, sum_down, sum_gain, sum_bias, sum_taps,
        sum_first, sum_second, sum_last, sum_direct,
    ) = unpack(block_outputs, input_grads, got, filter_first.shape[::2])
    return (
        block_outputs[None, :, None],
        input_grads[None, :, None],
        sum_gain[None],
        sum_bias[None],
        sum_in[None],
        jnp.transpose(sum_taps, (1, 0, 2)),
        jnp.transpose(sum_first, (1, 0, 2)),
        sum_second[None],
        sum_last[None],
        sum_direct,
        sum_out[None],
        sum_up[None],
        sum_down[None],
    )


def solution(mesh):
    in_specs = (
        P(None, "dp", "seq", None),
        P(None, "dp", "seq", None),
        P(None, "dp"),
        P("section", None, None),
        P("section", None, None),
        P("section", ("dp", "seq"), None),
        P("section", None, None),
        P("section", None, None),
        P("section", None, None),
        P("section", None, None),
        P("section", None),
        P("section", None),
        P("section", ("dp", "seq"), None),
        P("section", ("dp", "seq"), None),
        P("section", ("dp", "seq"), None),
    )
    out_specs = (
        P("section", None, "dp", "seq", None),
        P("section", None, "dp", "seq", None),
        P("section", None, None),
        P("section", None, None),
        P("section", ("dp", "seq"), None),
        P("section", None, None),
        P("section", None, None),
        P("section", None, None),
        P("section", None, None),
        P("section", None),
        P("section", ("dp", "seq"), None),
        P("section", ("dp", "seq"), None),
        P("section", ("dp", "seq"), None),
    )
    planes = mesh.shape["seq"] == 4 and mesh.shape["dp"] == 4
    per_device = plane_device if planes else any_device
    return jax.shard_map(
        per_device, mesh=mesh, in_specs=in_specs, out_specs=out_specs, check_vma=False
    )
```

```python
from functools import partial
import math

import jax
import jax.numpy as jnp
import numpy as np
from jax import lax
from jax.experimental import pallas as pl
from jax.experimental.pallas import tpu as pltpu
from jax.sharding import PartitionSpec as P

precise = lax.Precision.HIGHEST
low = jnp.bfloat16
f32 = jnp.float32
MESH = pl.DeviceIdType.MESH


def dot(a, b, dims):
    return lax.dot_general(a, b, (dims, ((), ())), preferred_element_type=f32)


def mm(a, b):
    return dot(a, b, ((1,), (0,)))


def mm_t(a, b):
    return dot(a, b, ((1,), (1,)))


def t_mm(a, b):
    return dot(a, b, ((0,), (0,)))


def norm_stats(x):
    mean = jnp.mean(x, axis=-1, keepdims=True)
    centred = x - mean
    inverse = lax.rsqrt(jnp.mean(centred * centred, axis=-1, keepdims=True) + 1e-05)
    return centred * inverse, inverse


def norm_back(grad, x, gain):
    hat, inverse = norm_stats(x)
    scaled = grad * gain
    back = inverse * (
        scaled
        - jnp.mean(scaled, axis=-1, keepdims=True)
        - hat * jnp.mean(scaled * hat, axis=-1, keepdims=True)
    )
    return back, jnp.sum(grad * hat, 0), jnp.sum(grad, 0)


def gelu_both(x):
    scale = math.sqrt(2.0 / math.pi)
    inner = scale * (x + 0.044715 * x * x * x)
    bend = jnp.tanh(inner)
    value = 0.5 * x * (1.0 + bend)
    slope = 0.5 * (1.0 + bend) + 0.5 * x * (1.0 - bend * bend) * scale * (
        1.0 + 3.0 * 0.044715 * x * x
    )
    return value, slope


def position_table(length):
    offsets = jnp.arange(length, dtype=jnp.float32)
    frequencies = jnp.linspace(0.0001, 15.0, 16, dtype=jnp.float32)
    angles = 2.0 * math.pi * offsets[:, None] * frequencies[None, :] / length
    return jnp.concatenate(
        [offsets[:, None] / (length - 1), jnp.cos(angles), -jnp.sin(angles)], axis=1
    )


def position_rows(length):
    offsets = np.arange(length, dtype=np.float32)
    frequencies = np.linspace(0.0001, 15.0, 16, dtype=np.float32)
    angles = np.float32(2.0 * math.pi) * offsets[:, None] * frequencies[None, :] / np.float32(length)
    return np.concatenate(
        [offsets[:, None] / np.float32(length - 1), np.cos(angles), -np.sin(angles)], axis=1
    )


def filter_taps(first_w, second_w, last_w, rates, length):
    embedding = position_table(length)
    hidden = jnp.sin(jnp.dot(embedding, first_w, precision=precise))
    hidden = jnp.sin(jnp.dot(hidden, second_w, precision=precise))
    offsets = jnp.arange(length, dtype=jnp.float32)
    return jnp.dot(hidden, last_w, precision=precise) * jnp.exp(-offsets[:, None] * rates[None, :])


def wave_tables(length):
    turns = (2 * np.arange(length)[:, None] + 1) * np.arange(length)[None, :] % (4 * length)
    angles = turns * (math.pi / (2 * length))
    both = np.concatenate([np.cos(angles), np.sin(angles)], 0)
    return both.astype(jnp.bfloat16)


def shifted(x, by):
    if by > 0:
        return jnp.pad(x[:-by], ((by, 0), (0, 0)))
    return jnp.pad(x[-by:], ((0, -by), (0, 0)))


def neighbours(me):
    return (me + 1 - 2 * (me % 2), (me + 2) % 4, 3 - me)


def greet(devices):
    barrier = pltpu.get_barrier_semaphore()
    for device in devices:
        pl.semaphore_signal(barrier, inc=1, device_id=device, device_id_type=MESH)
    return len(devices)


def all_here(greeted):
    pl.semaphore_wait(pltpu.get_barrier_semaphore(), greeted)


def in_plane(peers):
    return [{"seq": peer} for peer in peers]


def along_planes():
    here = lax.axis_index("dp")
    return here, here + 1 - 2 * (here % 2), (here + 2) % 4


def other_core():
    return {"section": 1 - lax.axis_index("section")}


def plane_devices():
    _, near, far = along_planes()
    return [{"dp": near}, {"dp": far}]


def add_low(target, source):
    def add(at):
        target[at, :] = (target[at, :].astype(f32) + source[at, :].astype(f32)).astype(low)

    by_rows(target.shape[0], 32, add)


def swap_begin(pairs, core_sems):
    section = lax.axis_index("section")
    copies = [
        remote_to(made.at[1 - section], other, core_sems, at, other_core())
        for at, (made, other) in enumerate(pairs)
    ]
    for copy in copies:
        copy.start()
    return copies


def swap_end(copies, pairs):
    section = lax.axis_index("section")
    for copy, (made, other) in zip(copies, pairs):
        copy.wait_recv()
        for block in range(other.shape[0]):
            add_low(made.at[section, block], other.at[block])


class PlaneSum:
    def __init__(self, pack, mine, arrived, sems, load_sems):
        self.here, self.near, self.far = along_planes()
        self.pack, self.mine, self.arrived = pack, mine, arrived
        self.sems, self.load_sems = sems, load_sems

    def begin(self):
        self.sends = [
            remote_to(self.pack.at[block], self.arrived.at[slot], self.sems, slot, {"dp": self.near})
            for slot, block in enumerate(((self.near + 2) % 4, self.near))
        ]
        for copy in self.sends:
            copy.start()
        self.loads = fetch(
            [(self.pack.at[self.far], self.mine.at[0]), (self.pack.at[self.here], self.mine.at[1])],
            self.load_sems,
        )

    def forward(self):
        self.loads[0].wait()
        self.sends[0].wait_recv()
        add_low(self.mine.at[0], self.arrived.at[0])
        copy = remote_to(self.mine.at[0], self.arrived.at[2], self.sems, 2, {"dp": self.far})
        copy.start()
        self.sends.append(copy)

    def end(self, result):
        self.loads[1].wait()
        self.sends[1].wait_recv()
        self.sends[2].wait_recv()

        def add(at):
            total = self.mine[1, at, :].astype(f32)
            for slot in (1, 2):
                total = total + self.arrived[slot, at, :].astype(f32)
            result[at, :] = total.astype(low)

        by_rows(result.shape[0], 32, add)


def plane_sum_scratch(half_pack):
    _, rows, cols = half_pack.shape
    return [
        pltpu.VMEM((2, rows, cols), low),
        pltpu.VMEM((3, rows, cols), low),
        pltpu.SemaphoreType.DMA((2, 3)),
        pltpu.SemaphoreType.DMA((2,)),
    ]


def remote_to(source, target, sems, slot, device):
    return pltpu.make_async_remote_copy(
        src_ref=source,
        dst_ref=target,
        send_sem=sems.at[0, slot],
        recv_sem=sems.at[1, slot],
        device_id=device,
        device_id_type=MESH,
    )


def remote(source, target, sems, slot, peer):
    return remote_to(source, target, sems, slot, {"seq": peer})


def rows_of(index, count):
    return pl.ds(pl.multiple_of(index * count, count), count)


def half_of(ref, index, part, count):
    half = count // 2
    return ref.at[pl.ds(pl.multiple_of(index * count + part * half, half), half)]


def gather_begin(gather, sems, me, peers, count):
    x, y, _ = peers
    first, second = half_of(gather, me, 0, count), half_of(gather, me, 1, count)
    copies = [
        remote(first, first, sems, 0, x),
        remote(second, second, sems, 2, y),
        remote(second, second, sems, 1, x),
        remote(first, first, sems, 3, y),
    ]
    for copy in copies:
        copy.start()
    return copies


def gather_forward(gather, sems, peers, count):
    x, y, _ = peers
    from_x, from_y = half_of(gather, x, 0, count), half_of(gather, y, 1, count)
    remote(from_x, from_x, sems, 0, x).wait_recv()
    onward = remote(from_x, from_x, sems, 4, y)
    onward.start()
    remote(from_y, from_y, sems, 2, y).wait_recv()
    across = remote(from_y, from_y, sems, 5, x)
    across.start()
    return [onward, across]


def gather_wait(gather, sems, slot, peers, count):
    for part, at in (((1, 1),), ((0, 3),), ((0, 4), (1, 5)))[slot]:
        block = half_of(gather, peers[slot], part, count)
        remote(block, block, sems, at, peers[slot]).wait_recv()


HALF_ORDER = ((0, 0), (1, 1), (0, 1), (1, 0), (2, 0), (2, 1))


def half_rows(index, part, count):
    half = count // 2
    return pl.ds(pl.multiple_of(index * count + part * half, half), half)


def gather_wait_half(gather, sems, slot, part, peers, count):
    at = {(0, 1): 1, (1, 0): 3, (2, 0): 4, (2, 1): 5}.get((slot, part))
    if at is not None:
        block = half_of(gather, peers[slot], part, count)
        remote(block, block, sems, at, peers[slot]).wait_recv()


def reduce_send_half(slot, part, send, recv, sems, peers):
    half = send.shape[1] // 2
    quarter = half // 2
    plan = {
        (0, 0): [(0, half, 0, 0)],
        (1, 1): [(half, half, 1, 1)],
        (2, 0): [(0, quarter, 2, 0), (quarter, quarter, 3, 0)],
        (2, 1): [(half, quarter, 4, 1), (half + quarter, quarter, 5, 1)],
    }.get((slot, part), [])
    copies = [
        remote(
            send.at[slot, pl.ds(start, size)], recv.at[slot, pl.ds(start, size)], sems, at,
            peers[to],
        )
        for start, size, at, to in plan
    ]
    for copy in copies:
        copy.start()
    return copies


def reduce_send(slot, send, recv, sems, peers):
    x, y, _ = peers
    half = send.shape[1] // 2
    quarter = half // 2
    if slot == 2:
        plan = [(0, quarter, 2, x), (half, quarter, 4, y), (quarter, quarter, 3, x)]
        plan.append((half + quarter, quarter, 5, y))
    else:
        plan = [(slot * half, half, slot, (x, y)[slot])]
    copies = [
        remote(
            send.at[slot, pl.ds(start, size)], recv.at[slot, pl.ds(start, size)], sems, at, peer
        )
        for start, size, at, peer in plan
    ]
    for copy in copies:
        copy.start()
    return copies


def reduce_pass(send, recv, sems, peers):
    x, y, _ = peers
    half = send.shape[1] // 2
    quarter = half // 2
    copies = []
    for start, at, source, slot, peer in (
        (half, 4, y, 0, x),
        (0, 2, x, 1, y),
        (half + quarter, 5, y, 0, x),
        (quarter, 3, x, 1, y),
    ):
        rows = pl.ds(start, quarter)
        remote(send.at[2, rows], recv.at[2, rows], sems, at, source).wait_recv()
        add_low(send.at[slot, rows], recv.at[2, rows])
        copy = remote(send.at[slot, rows], recv.at[slot, rows], sems, at + 4, peer)
        copy.start()
        copies.append(copy)
    return copies


def reduce_wait(send, recv, sems, peers):
    x, y, _ = peers
    half = send.shape[1] // 2
    quarter = half // 2
    for slot, start, size, at, peer in (
        (0, 0, half, 0, x),
        (1, half, half, 1, y),
        (0, half, quarter, 8, x),
        (1, 0, quarter, 6, y),
        (0, half + quarter, quarter, 9, x),
        (1, quarter, quarter, 7, y),
    ):
        rows = pl.ds(start, size)
        remote(send.at[slot, rows], recv.at[slot, rows], sems, at, peer).wait_recv()


def by_rows(total, step, body):
    def run(i, carry):
        body(pl.ds(pl.multiple_of(i * step, step), step))
        return carry

    lax.fori_loop(0, total // step, run, 0)


def valid_rows(lengths, start, count):
    at = lax.broadcasted_iota(jnp.int32, (count, 1), 0) + start
    return (at < lengths[0, lax.axis_index("section")]).astype(f32)


def normed_rows(x, gain, shift):
    mean = jnp.mean(x, axis=-1, keepdims=True)
    centred = x - mean
    inverse = lax.rsqrt(jnp.mean(centred * centred, axis=-1, keepdims=True) + 1e-05)
    return centred * inverse * gain + shift


def norm_back_rows(grad, x, gain):
    mean = jnp.mean(x, axis=-1, keepdims=True)
    centred = x - mean
    inverse = lax.rsqrt(jnp.mean(centred * centred, axis=-1, keepdims=True) + 1e-05)
    hat = centred * inverse
    scaled = grad * gain
    back = inverse * (
        scaled
        - jnp.mean(scaled, axis=-1, keepdims=True)
        - hat * jnp.mean(scaled * hat, axis=-1, keepdims=True)
    )
    return back, jnp.sum(grad * hat, axis=0, keepdims=True), jnp.sum(grad, axis=0, keepdims=True)


def norm_into(gather, start, x, gain, shift):
    step = 32

    def body(i, carry):
        rows = pl.ds(pl.multiple_of(i * step, step), step)
        at = pl.ds(pl.multiple_of(start + i * step, step), step)
        gather[at, :] = normed_rows(x[rows, :].astype(f32), gain, shift).astype(low)
        return carry

    lax.fori_loop(0, x.shape[0] // step, body, 0)


def masked_into(gather, start, grad, lengths):
    step = 32

    def body(i, carry):
        rows = pl.ds(pl.multiple_of(i * step, step), step)
        at = pl.ds(pl.multiple_of(start + i * step, step), step)
        value = grad[rows, :].astype(f32) * valid_rows(lengths, start + i * step, step)
        gather[at, :] = value.astype(low)
        return carry

    lax.fori_loop(0, grad.shape[0] // step, body, 0)


def add_parts(own, recv, x, start, lengths):
    def body(rows):
        total = own[rows, :] + recv[0, rows, :].astype(f32) + recv[1, rows, :].astype(f32)
        mask = valid_rows(lengths, start + rows.start, 32)
        own[rows, :] = x[rows, :].astype(f32) + mask * total

    by_rows(own.shape[0], 32, body)


def norm_back_parts(own, recv, grad, x, gain, sums):
    sums[...] = jnp.zeros(sums.shape, f32)

    def body(rows):
        total = own[rows, :] + recv[0, rows, :].astype(f32) + recv[1, rows, :].astype(f32)
        back, gain_sum, shift_sum = norm_back_rows(total, x[rows, :].astype(f32), gain)
        own[rows, :] = grad[rows, :].astype(f32) + back
        sums[0:1, :] += gain_sum
        sums[1:2, :] += shift_sum

    by_rows(own.shape[0], 32, body)


def fetch(pairs, sems, first=0):
    copies = [
        pltpu.make_async_copy(source, target, sems.at[first + at])
        for at, (source, target) in enumerate(pairs)
    ]
    for copy in copies:
        copy.start()
    return copies


def weight_pairs_mixer(pack, win, wout):
    rows, cols = wout.shape[2], wout.shape[3] // 4
    split = win.shape[3]
    pairs = [(pack.at[:, :, :, pl.ds(0, split)], win)]
    for q in range(4):
        pairs.append(
            (
                pack.at[:, :, pl.ds(q * rows, rows), pl.ds(split, cols)],
                wout.at[:, :, :, pl.ds(q * cols, cols)],
            )
        )
    return pairs


def half_pairs_mixer(half_pack, win, wout):
    rows, cols = wout.shape[2], wout.shape[3] // 4
    split = win.shape[3]
    section = lax.axis_index("section")
    pairs = [(win.at[section], half_pack.at[:, :, pl.ds(0, split)])]
    for q in range(4):
        pairs.append(
            (
                wout.at[section, :, :, pl.ds(q * cols, cols)],
                half_pack.at[:, pl.ds(q * rows, rows), pl.ds(split, cols)],
            )
        )
    return pairs


class ChipGather:
    def __init__(self, own, pack, plane_sems, core_sems):
        self.section = lax.axis_index("section")
        here, near, far = along_planes()
        self.pack, self.plane_sems, self.core_sems = pack, plane_sems, core_sems
        self.near, self.far = near, far
        self.order = (here, near, far, (near + 2) % 4)
        self.own = own
        self.sends = []

    def move(self, at, sems, slot, device):
        block = self.pack.at[self.section, self.order[at]]
        copy = remote_to(self.own if at == 0 else block, block, sems, slot, device)
        copy.start()
        self.sends.append(copy)

    def to_core(self, slot):
        self.move(slot, self.core_sems, slot, other_core())

    def begin(self, load_sem):
        self.move(0, self.plane_sems, 1, {"dp": self.far})
        self.move(0, self.plane_sems, 0, {"dp": self.near})
        self.to_core(0)
        self.keep = pltpu.make_async_copy(
            self.own, self.pack.at[self.section, self.order[0]], load_sem
        )
        self.keep.start()

    def arrived(self, slot):
        block = self.pack.at[self.section, self.order[slot + 1]]
        remote_to(block, block, self.plane_sems, slot, {"dp": self.near}).wait_recv()

    def forward(self):
        self.arrived(1)
        self.move(2, self.plane_sems, 2, {"dp": self.near})
        self.to_core(2)
        self.arrived(0)
        self.to_core(1)

    def end(self):
        self.arrived(2)
        self.to_core(3)
        self.keep.wait()
        for slot in range(4):
            block = self.pack.at[1 - self.section, self.order[slot]]
            remote_to(block, block, self.core_sems, slot, other_core()).wait_recv()


def sine_pair(x):
    turns = jnp.floor(x * (2.0 / math.pi) + 0.5)
    rest = x - turns * 1.5703125
    rest = rest - turns * 4.837512969970703125e-4
    rest = rest - turns * 7.54978995489188e-8
    square = rest * rest
    sine = -1.9515295891e-4 * square + 8.3321608736e-3
    sine = (sine * square - 1.6666654611e-1) * square * rest + rest
    cosine = 2.443315711809948e-5 * square - 1.388731625493765e-3
    cosine = (cosine * square + 4.166664568298827e-2) * square * square - 0.5 * square + 1.0
    halves = jnp.floor(turns * 0.5)
    odd = turns - 2.0 * halves
    back = halves - 2.0 * jnp.floor(halves * 0.5)
    swapped = odd > 0.5
    side = 1.0 - 2.0 * back
    wave = jnp.where(swapped, cosine, sine) * side
    slope = jnp.where(swapped, -sine, cosine) * side
    return wave, slope


def network_rows(small, embedding, network, taps_low, i):
    step = 256
    waves1, waves2, steep1, steep2 = network
    knots = waves1.shape[1]
    pair = (pl.ds(i * step, step), pl.ds(embedding.shape[0] // 2 + i * step, step))

    def layer(sources, weights, waves, steep):
        inner = jnp.concatenate([dot_exact(item, weights) for item in sources], 1)
        wave, slope = sine_pair(inner)
        for at, rows in enumerate(pair):
            cols = slice(at * knots, (at + 1) * knots)
            waves[rows, :] = wave[:, cols]
            steep[rows, :] = slope[:, cols]

    layer([embedding[rows, 0:64] for rows in pair], small[64:128, 128:192], waves1, steep1)
    layer([waves1[rows, :] for rows in pair], small[64:128, 0:64], waves2, steep2)
    for rows in pair:
        times = lax.broadcasted_iota(jnp.int32, (step, 1), 0) + rows.start
        fade = jnp.exp(-times.astype(f32) * small[154:155, :])
        taps_low[rows, :] = (dot_exact(waves2[rows, :], small[0:64, :]) * fade).astype(low)


def ff_blocks(
    gather, wup, wdown, value, slope, result_out, send, recv, gather_sems, reduce_sems, me, peers,
    pause,
):
    count, width = result_out.shape
    half = wup.shape[3]
    sends = []
    for slot, part in ((None, None), *HALF_ORDER):
        if slot is None:
            rows, sent = rows_of(me, count), None
        else:
            rows = half_rows(peers[slot], part, count)
            sent = slice(part * count // 2, (part + 1) * count // 2)
            gather_wait_half(gather, gather_sems, slot, part, peers, count)

        def hidden(i, carry):
            cols = pl.ds(pl.multiple_of(i * 256, 256), 256)
            for h in range(2):
                pre = mm(gather[rows, :], wup[h, :, :, cols].reshape(width, 256))
                after, steep = gelu_both(pre)
                at = pl.ds(pl.multiple_of(h * half + i * 256, 256), 256)
                value[rows, at] = after.astype(low)
                slope[rows, at] = steep.astype(low)
            return carry

        lax.fori_loop(0, half // 256, hidden, 0)
        for h in range(2):
            cols = slice(h * width // 2, (h + 1) * width // 2)
            out = mm(value[rows, :], wdown[h].reshape(2 * half, width // 2))
            if slot is None:
                result_out[:, cols] = out
            else:
                send[slot, sent, cols] = out.astype(low)
        if slot is not None:
            sends += reduce_send_half(slot, part, send, recv, reduce_sems, peers)
            pause(slot, part)
    return sends


def mixer_forward_kernel(
    s, gathers, x, *refs
):
    if gathers:
        (
            cotangent, embedding, lengths, w_in, w_out, w_up, w_down, gain, shift, tap_rows, first_w,
            second_w, last_w, direct, rates, waves_hbm, back_hbm,
            pack_out, ff_out, late_out, par_out, small_out, next_pack_out, ff_part_out,
            *refs,
        ) = refs
        network_outs, next_outs, refs = refs[:5], refs[5:10], refs[10:]
        second_out, value_out, slope_out, result_out, *refs = refs
        (
            *refs, waves1, waves2, steep1, steep2, taps_low, raw_out, ff_all, late, next_pack, core_sems,
            plane_sems, out_core_sems, out_plane_sems, ff_core_sems, ff_plane_sems, next_core_sems, next_plane_sems, late_sems,
            pack_sems, mixer_parts, ff_parts, par_all, small_all, stage_in, stage_out, stage_up,
            in_sems, out_sems, up_sems, down_sems, par_sems, small_sems,
            second, ff_send, ff_recv, second_sems, ff_sems, network_sems,
        ) = refs
        x = x.at[lax.axis_index("section"), 0]
        cotangent = cotangent.at[lax.axis_index("section"), 0]
        network = (waves1, waves2, steep1, steep2)
    else:
        par_all, small_all, lengths, weights_hbm, filt_hbm, waves_hbm, back_hbm, *refs = refs
    (
        normed_out, proj_out, stream_out, prod_out, spec_out, filtered_out, gated_out, middle_out,
        gather, win, wout, filt, waves, back, proj, proj_low, streams, prod, spec, mixed, filtered,
        gated, send, recv, gather_sems, reduce_sems, load_sems, store_sems,
    ) = refs
    par, small = par_all.at[s], small_all.at[s]
    me = lax.axis_index("seq")
    peers = neighbours(me)
    count, width = x.shape
    length = gather.shape[0]
    chans = prod.shape[1]
    half = win.shape[3]
    if gathers:
        section = lax.axis_index("section")
        targets = shuffle_targets(section, me, peers)
        greeted = greet([device for _, _, device in targets] + plane_devices())
    else:
        greeted = greet(in_plane(peers[:2]))
    tables = fetch([(waves_hbm, waves), (back_hbm, back)], load_sems)
    sends = []
    if gathers:
        shuffle_stage(w_in, w_out, w_up, stage_in, stage_out, stage_up)
        parameters_stage(
            me, par_all.at[section], small_all.at[section], gain, shift, tap_rows, first_w, second_w,
            last_w, direct, rates,
        )
        all_here(greeted)
        sends += shuffle_send(
            section, me, targets, (stage_in, stage_out, stage_up, w_down), (mixer_parts, ff_parts),
            (par_all, small_all), (in_sems, out_sems, up_sems, down_sems, par_sems, small_sems),
        )
        in_cols, out_cols = pl.ds(0, half), pl.ds(half, raw_out.shape[3])
        in_pack = ChipGather(mixer_parts.at[0, :, in_cols], win, plane_sems, core_sems)
        out_pack = ChipGather(mixer_parts.at[0, :, out_cols], raw_out, out_plane_sems, out_core_sems)
        ff_pack = ChipGather(ff_parts.at[0], ff_all, ff_plane_sems, ff_core_sems)
        for sems, item in ((par_sems, par_all), (small_sems, small_all)):
            block = item.at[1 - section]
            remote_to(block, block, sems, 0, other_core()).wait_recv()
        norm_into(gather, me * count, x, par[0:1, :], par[1:2, :])
        shuffle_wait_mixer(section, me, targets, mixer_parts, stage_in, in_sems, out_sems)
        in_pack.begin(pack_sems.at[0])
        sends += gather_begin(gather, gather_sems, me, peers, count)
        masked_into(late, me * count, cotangent, lengths)
    else:
        weights = fetch(weight_pairs_mixer(weights_hbm, win, wout), load_sems, 2)
        filt_load = fetch([(filt_hbm, filt)], load_sems, 7)
        norm_into(gather, me * count, x, par[0:1, :], par[1:2, :])
        all_here(greeted)
        sends += gather_begin(gather, gather_sems, me, peers, count)
    proj[0:8, :] = jnp.zeros((8, proj.shape[1]), f32)
    tile_rows = 256

    def filter_spectrum(i, carry):
        rows = pl.ds(pl.multiple_of(i * tile_rows, tile_rows), tile_rows)
        filt[rows, :] = mm(waves[rows, :], taps_low[...])
        return carry

    stores = []
    if gathers:
        network_rows(small, embedding, network, taps_low, 0)
    sends += gather_forward(gather, gather_sems, peers, count)
    if gathers:
        sends += gather_begin(late, late_sems, me, peers, count)
        in_pack.forward()
        out_pack.begin(pack_sems.at[13])
        network_rows(small, embedding, network, taps_low, 1)
        tables[0].wait()
        lax.fori_loop(0, 2 * length // tile_rows, filter_spectrum, 0)
        network_stores = fetch(list(zip((filt, *network), network_outs)), network_sems)
        out_pack.forward()
        shuffle_wait_ff(section, me, targets, ff_parts, stage_up, up_sems, down_sems)
        ff_pack.begin(pack_sems.at[1])
        in_pack.end()
        stores += fetch(
            [
                (win, pack_out.at[:, :, :, in_cols]),
                (par_all, par_out),
                (small_all, small_out),
                (ff_parts.at[1], ff_part_out),
            ],
            pack_sems,
            4,
        )
    else:
        tables[0].wait()
    if not gathers:
        weights[0].wait()
    step = 64
    steps = count // step

    def short_conv(start):
        for g in range(3):
            cols = slice(g * chans, (g + 1) * chans)
            tile = proj[pl.ds(start, step + 8), cols]
            proj_low[pl.ds(start, step), cols] = tile[8:].astype(low)
            value = (
                small[144 + 3 * g : 145 + 3 * g, :] * tile[8:]
                + small[145 + 3 * g : 146 + 3 * g, :] * pltpu.roll(tile, 1, 0)[8:]
                + small[146 + 3 * g : 147 + 3 * g, :] * pltpu.roll(tile, 2, 0)[8:]
            )
            streams[pl.ds(start, step), cols] = value.astype(low)
        first = streams[pl.ds(start, step), 0:chans].astype(f32)
        third = streams[pl.ds(start, step), 2 * chans : 3 * chans].astype(f32)
        prod[pl.ds(start, step), :] = (first * third * valid_rows(lengths, start, step)).astype(low)

    def within(source):
        def body(i, carry):
            short_conv(pl.multiple_of(source * count + i * step, step))
            return carry

        lax.fori_loop(1, steps, body, 0)

    for slot in (None, 0, 1, 2):
        source = me if slot is None else peers[slot]
        if slot is not None:
            gather_wait(gather, gather_sems, slot, peers, count)
        block = gather[rows_of(source, count), :]
        for h in range(2):
            proj[pl.ds(pl.multiple_of(source * count + 8, 8), count), h * half : (h + 1) * half] = mm(
                block, win[h].reshape(width, half)
            )
        within(source)
    if gathers:
        sends += gather_forward(late, late_sems, peers, count)

    def seams(i, carry):
        short_conv(pl.multiple_of(i * count, step))
        return carry

    lax.fori_loop(0, length // count, seams, 0)
    stores += fetch(
        [(gather, normed_out), (proj_low, proj_out), (streams, stream_out), (prod, prod_out)],
        store_sems,
    )
    if not gathers:
        filt_load[0].wait()

    def spectrum(i, carry):
        up = pl.ds(pl.multiple_of(i * tile_rows, tile_rows), tile_rows)
        down = pl.ds(pl.multiple_of(i * tile_rows + length, tile_rows), tile_rows)
        prod_cos = mm(waves[up, :], prod[...])
        prod_sin = mm(waves[down, :], prod[...])
        filt_cos, filt_sin = filt[up, :], filt[down, :]
        spec[up, :] = prod_cos.astype(low)
        spec[down, :] = prod_sin.astype(low)
        mixed[up, :] = (prod_cos * filt_cos - prod_sin * filt_sin).astype(low)
        mixed[down, :] = (prod_cos * filt_sin + prod_sin * filt_cos).astype(low)
        return carry

    lax.fori_loop(0, length // tile_rows, spectrum, 0)
    tables[1].wait()
    if gathers:
        out_pack.end()
        cols = raw_out.shape[3]
        weights = fetch(
            [
                (
                    raw_out.at[:, :, pl.ds(q * wout.shape[2], wout.shape[2]), :],
                    wout.at[:, :, :, pl.ds(q * cols, cols)],
                )
                for q in range(4)
            ],
            load_sems,
            3,
        )
        stores += fetch([(raw_out, pack_out.at[:, :, :, out_cols])], pack_sems, 14)
        for load in weights:
            load.wait()
    else:
        for load in weights[1:]:
            load.wait()
    for slot in (2, 0, 1, None):
        target = me if slot is None else peers[slot]
        rows = rows_of(target, count)
        value = mm(back[rows, :], mixed[...]) * (1.0 / length)
        value = value + small[153:154, :] * prod[rows, :].astype(f32)
        filtered[rows, :] = value
        gate = (streams[rows, chans : 2 * chans].astype(f32) * value).astype(low)
        gated[rows, :] = gate
        outs = [mm(gate, wout[h].reshape(chans, width // 2)) for h in range(2)]
        for h in range(2):
            cols = slice(h * width // 2, (h + 1) * width // 2)
            if slot is None:
                middle_out[:, cols] = outs[h]
            else:
                send[slot, :, cols] = outs[h].astype(low)
        if slot is not None:
            sends += reduce_send(slot, send, recv, reduce_sems, peers)
    if gathers:
        ff_pack.forward()
        for slot in range(3):
            gather_wait(late, late_sems, slot, peers, count)
        stores += fetch([(late, late_out)], pack_sems, 2)
    sends += reduce_pass(send, recv, reduce_sems, peers)
    stores += fetch(
        [(spec, spec_out), (filtered, filtered_out), (gated, gated_out)],
        store_sems,
        4,
    )
    if gathers:
        for store in network_stores:
            store.wait()
        for i in range(2):
            network_rows(small_all.at[1], embedding, network, taps_low, i)
        lax.fori_loop(0, 2 * length // tile_rows, filter_spectrum, 0)
        network_stores = fetch(list(zip((filt, *network), next_outs)), network_sems)
    reduce_wait(send, recv, reduce_sems, peers)
    add_parts(middle_out, recv, x, me * count, lengths)
    if gathers:
        next_mixer = ChipGather(mixer_parts.at[1], next_pack, next_plane_sems, next_core_sems)
        norm_into(second, me * count, middle_out, par[2:3, :], par[3:4, :])
        sends += gather_begin(second, second_sems, me, peers, count)
        sends += gather_forward(second, second_sems, peers, count)
        ff_pack.end()
        next_mixer.begin(pack_sems.at[8])
        stores += fetch([(ff_all, ff_out)], pack_sems, 3)
        rows_up = ff_all.shape[2] // 2
        value, slope = waves.at[pl.ds(0, length)], waves.at[pl.ds(length, length)]

        def pause(slot, part):
            if (slot, part) == (1, 1):
                next_mixer.forward()

        sends += ff_blocks(
            second, ff_all.at[:, :, pl.ds(0, rows_up)], ff_all.at[:, :, pl.ds(rows_up, rows_up)],
            value, slope, result_out, ff_send, ff_recv, second_sems, ff_sems, me, peers, pause,
        )
        sends += reduce_pass(ff_send, ff_recv, ff_sems, peers)
        stores += fetch([(second, second_out), (value, value_out), (slope, slope_out)], pack_sems, 9)
        next_mixer.end()
        stores += fetch([(next_pack, next_pack_out)], pack_sems, 12)
        reduce_wait(ff_send, ff_recv, ff_sems, peers)
        add_parts(result_out, ff_recv, middle_out, me * count, lengths)
        sends += in_pack.sends + out_pack.sends + ff_pack.sends + next_mixer.sends
        stores += network_stores
    for copy in sends:
        copy.wait_send()
    for store in stores:
        store.wait()


def ff_turn_kernel(
    s, cotangent, x, par_all, lengths, pack, late_hbm,
    half_out, parts_out, result_out, middle_grad_out, sums_out,
    gather, late, wup, wdown, value, pre, wgrad, other, send, send_back, recv_back,
    gather_sems, back_sems, load_sems, store_sems, core_sems,
):
    par = par_all.at[s]
    grad = cotangent.at[lax.axis_index("section"), 0]
    me = lax.axis_index("seq")
    peers = neighbours(me)
    count, width = x.shape
    half = wup.shape[3]
    rows_up = wup.shape[2]
    greeted = greet(in_plane(peers[:2]) + [other_core()])
    loads = fetch(
        [
            (pack.at[:, :, pl.ds(0, rows_up), :], wup),
            (pack.at[:, :, pl.ds(rows_up, wdown.shape[2]), :], wdown),
            (late_hbm, late),
        ],
        load_sems,
    )
    norm_into(gather, me * count, x, par[2:3, :], par[3:4, :])
    all_here(greeted)
    sends = gather_begin(gather, gather_sems, me, peers, count)
    for load in loads:
        load.wait()
    for slot, part in ((None, None), *HALF_ORDER):
        if slot is None:
            rows, sent = rows_of(me, count), None
        else:
            rows = half_rows(peers[slot], part, count)
            sent = slice(part * count // 2, (part + 1) * count // 2)
            gather_wait_half(gather, gather_sems, slot, part, peers, count)

        def hidden(i, carry):
            cols = pl.ds(pl.multiple_of(i * rows_up, rows_up), rows_up)
            for h in range(2):
                block = h * (half // rows_up) + i
                at = pl.ds(pl.multiple_of(block * rows_up, rows_up), rows_up)
                after, steep = gelu_both(
                    mm(gather[rows, :], wup[h, :, :, cols].reshape(width, rows_up))
                )
                value[rows, at] = after.astype(low)
                back = mm_t(late[rows, : width // 2], wdown[0, block]) + mm_t(
                    late[rows, width // 2 :], wdown[1, block]
                )
                pre[rows, at] = (back * steep).astype(low)
            return carry

        lax.fori_loop(0, half // rows_up, hidden, 0)

        def through(i, carry):
            cols = pl.ds(pl.multiple_of(i * rows_up, rows_up), rows_up)
            back = mm_t(pre[rows, :half], wup[0, i]) + mm_t(pre[rows, half:], wup[1, i])
            if slot is None:
                middle_grad_out[:, cols] = back
            else:
                send_back[slot, sent, cols] = back.astype(low)
            return carry

        lax.fori_loop(0, width // rows_up, through, 0)
        if slot is None:
            sends += gather_forward(gather, gather_sems, peers, count)
        else:
            sends += reduce_send_half(slot, part, send_back, recv_back, back_sems, peers)
    for slot in (2, 0, 1, None):
        rows = rows_of(me if slot is None else peers[slot], count)
        for h in range(2):
            cols = slice(h * width // 2, (h + 1) * width // 2)
            out = mm(value[rows, :], wdown[h].reshape(2 * half, width // 2))
            if slot is None:
                result_out[:, cols] = out
            else:
                send[slot, :, cols] = out.astype(low)
    sends += reduce_pass(send_back, recv_back, back_sems, peers)
    stores = fetch([(send, parts_out)], store_sems, 1)

    def weights(i, carry):
        cols = pl.ds(pl.multiple_of(i * rows_up, rows_up), rows_up)
        for h in range(2):
            wgrad[h, i, 0:rows_up, :] = t_mm(
                gather[:, cols], pre[:, h * half : (h + 1) * half]
            ).astype(low)
            wgrad[h, i, rows_up : 2 * rows_up, :] = t_mm(
                value[:, cols], late[:, h * width // 2 : (h + 1) * width // 2]
            ).astype(low)
        return carry

    lax.fori_loop(0, width // rows_up, weights, 0)
    swapped = [(wgrad, other)]
    swaps = swap_begin(swapped, core_sems)
    sends += swaps
    swap_end(swaps, swapped)
    stores += fetch([(wgrad.at[lax.axis_index("section")], half_out)], store_sems)
    reduce_wait(send_back, recv_back, back_sems, peers)
    norm_back_parts(middle_grad_out, recv_back, grad, x, par[2:3, :], sums_out)
    for copy in sends:
        copy.wait_send()
    for store in stores:
        store.wait()


def ff_backward_kernel(
    s, grad, middle, par_all, lengths, pack, second_hbm, value_hbm, slope_hbm, earlier,
    half_out, middle_grad_out, sums_out, summed,
    gather, wup, wdown, second, value, slope, pre, wgrad, other, send, recv, gather_sems,
    reduce_sems, load_sems, store_sems, mine, arrived, plane_sems, sum_sems, core_sems,
):
    par = par_all.at[s]
    me = lax.axis_index("seq")
    peers = neighbours(me)
    count, width = grad.shape
    greeted = greet(in_plane(peers[:2]) + plane_devices() + [other_core()])
    half = wup.shape[3]
    units = 2 * half
    up_rows = wup.shape[2]
    loads = fetch(
        [
            (pack.at[:, :, pl.ds(0, up_rows), :], wup),
            (pack.at[:, :, pl.ds(up_rows, wdown.shape[2]), :], wdown),
            (slope_hbm, slope),
            (second_hbm, second),
            (value_hbm, value),
        ],
        load_sems,
    )
    masked_into(gather, me * count, grad, lengths)
    all_here(greeted)
    sends = gather_begin(gather, gather_sems, me, peers, count)
    plane_sum = PlaneSum(earlier, mine, arrived, plane_sems, sum_sems)
    plane_sum.begin()
    for load in loads[:3]:
        load.wait()
    for slot, part in ((None, None), *HALF_ORDER):
        if slot is None:
            rows, sent = rows_of(me, count), None
        else:
            rows = half_rows(peers[slot], part, count)
            sent = slice(part * count // 2, (part + 1) * count // 2)
            gather_wait_half(gather, gather_sems, slot, part, peers, count)

        def hidden(i, carry):
            cols = pl.ds(pl.multiple_of(i * up_rows, up_rows), up_rows)
            back = mm_t(gather[rows, : width // 2], wdown[0, i]) + mm_t(
                gather[rows, width // 2 :], wdown[1, i]
            )
            pre[rows, cols] = (back * slope[rows, cols].astype(f32)).astype(low)
            return carry

        lax.fori_loop(0, units // up_rows, hidden, 0)

        def through(i, carry):
            cols = pl.ds(pl.multiple_of(i * up_rows, up_rows), up_rows)
            back = mm_t(pre[rows, :half], wup[0, i]) + mm_t(pre[rows, half:], wup[1, i])
            if slot is None:
                middle_grad_out[:, cols] = back
            else:
                send[slot, sent, cols] = back.astype(low)
            return carry

        lax.fori_loop(0, width // up_rows, through, 0)
        if slot is None:
            sends += gather_forward(gather, gather_sems, peers, count)
        else:
            sends += reduce_send_half(slot, part, send, recv, reduce_sems, peers)
    plane_sum.forward()
    for load in loads[3:]:
        load.wait()

    def weights(i, carry):
        cols = pl.ds(pl.multiple_of(i * up_rows, up_rows), up_rows)
        for h in range(2):
            wgrad[h, i, 0:up_rows, :] = t_mm(
                second[:, cols], pre[:, h * half : (h + 1) * half]
            ).astype(low)
            wgrad[h, i, up_rows : 2 * up_rows, :] = t_mm(
                value[:, cols], gather[:, h * width // 2 : (h + 1) * width // 2]
            ).astype(low)
        return carry

    lax.fori_loop(0, width // up_rows, weights, 0)
    swapped = [(wgrad, other)]
    swaps = swap_begin(swapped, core_sems)
    sends += swaps
    sends += reduce_pass(send, recv, reduce_sems, peers)
    swap_end(swaps, swapped)
    stores = fetch([(wgrad.at[lax.axis_index("section")], half_out)], store_sems)
    plane_sum.end(summed)
    sends += plane_sum.sends
    reduce_wait(send, recv, reduce_sems, peers)
    norm_back_parts(middle_grad_out, recv, grad, middle, par[2:3, :], sums_out)
    for copy in sends:
        copy.wait_send()
    for store in stores:
        store.wait()


def t_mm_exact(a, b):
    return lax.dot_general(
        a, b, (((0,), (0,)), ((), ())), preferred_element_type=f32, precision=precise
    )


def mm_t_exact(a, b):
    return lax.dot_general(
        a, b, (((1,), (1,)), ((), ())), preferred_element_type=f32, precision=precise
    )


def dot_exact(a, b):
    return jnp.dot(a, b, preferred_element_type=f32, precision=precise)


def by_layer(begin, triples, layer_sems, keep_sems, base=0):
    section = lax.axis_index("section")
    for index in range(2):

        @pl.when(section == index)
        def _():
            for at, (first, second, target) in enumerate(triples, base):
                kept, sent = (first, second) if index == 0 else (second, first)
                slot = target.at[index]
                copies = (
                    pltpu.make_async_copy(kept, slot, keep_sems.at[at]),
                    remote_to(sent, slot, layer_sems, at, other_core()),
                )
                for copy in copies:
                    if begin:
                        copy.start()
                    else:
                        copy.wait()


def mixer_backward_kernel(
    s, grad, x, par_all, small_all, embedding, late, lengths, pack, filt_hbm, waves_hbm, back_hbm, normed_hbm, proj_hbm,
    stream_hbm, prod_hbm, spec_hbm, filtered_hbm, gated_hbm, waves1_hbm, waves2_hbm, steep1_hbm,
    steep2_hbm, earlier,
    half_out, small_out, input_grad_out, summed,
    gather, win, wout, filt, waves, back, normed, proj, streams, prod, spec, filtered, gated,
    gated_grad, filtered_grad, both, grad_spec, grad_sum, filter_grad, mixed, proj_grad, wgrad_in, wgrad_out_part,
    other_in, other_out, waves1, waves2, steep1, steep2, sums, taps_sum, send, recv, gather_sems, reduce_sems, load_sems, store_sems,
    mine, arrived, plane_sems, sum_sems, core_sems,
):
    par, small = par_all.at[s], small_all.at[s]
    me = lax.axis_index("seq")
    peers = neighbours(me)
    if s == 0:
        x = x.at[lax.axis_index("section"), 0]
    count, width = grad.shape
    greeted = greet(in_plane(peers[:2]) + plane_devices() + [other_core()])
    length = gather.shape[0]
    chans = prod.shape[1]
    half = win.shape[3]
    depth = win.shape[2]
    loads = fetch(
        weight_pairs_mixer(pack, win, wout)
        + [
            (stream_hbm, streams),
            (waves_hbm, waves),
            (filt_hbm, filt),
            (spec_hbm, spec),
            (back_hbm, back),
            (prod_hbm, prod),
            (filtered_hbm, filtered),
            (proj_hbm, proj),
            (normed_hbm, normed),
            (gated_hbm, gated),
            (waves1_hbm, waves1),
            (waves2_hbm, waves2),
            (steep1_hbm, steep1),
            (steep2_hbm, steep2),
        ],
        load_sems,
    )
    masked_into(gather, me * count, grad, lengths)
    all_here(greeted)
    sends = gather_begin(gather, gather_sems, me, peers, count)
    plane_sum = PlaneSum(earlier, mine, arrived, plane_sems, sum_sems)
    plane_sum.begin()
    for load in loads[1:6]:
        load.wait()
    tile_rows = 256
    for slot in (None, 0, 1, 2):
        source = me if slot is None else peers[slot]
        rows = rows_of(source, count)
        if slot is not None:
            gather_wait(gather, gather_sems, slot, peers, count)
        value = (
            mm_t(gather[rows, : width // 2], wout[0].reshape(chans, width // 2))
            + mm_t(gather[rows, width // 2 :], wout[1].reshape(chans, width // 2))
        ).astype(low)
        gated_grad[rows, :] = value
        filtered_grad[rows, :] = (
            value.astype(f32) * streams[rows, chans : 2 * chans].astype(f32)
        ).astype(low)
        if slot is None:
            sends += gather_forward(gather, gather_sems, peers, count)
            for load in loads[6:]:
                load.wait()
            loads[0].wait()
        if slot == 2:
            plane_sum.forward()

        def spectrum(i, carry):
            up = pl.ds(pl.multiple_of(i * tile_rows, tile_rows), tile_rows)
            down = pl.ds(pl.multiple_of(i * tile_rows + length, tile_rows), tile_rows)
            fg_cos = mm(waves[up, rows], filtered_grad[rows, :])
            fg_sin = mm(waves[down, rows], filtered_grad[rows, :])
            if slot is not None:
                fg_cos = fg_cos + grad_sum[up, :]
                fg_sin = fg_sin + grad_sum[down, :]
            if slot != 2:
                grad_sum[up, :] = fg_cos
                grad_sum[down, :] = fg_sin
            else:
                filt_cos, filt_sin = filt[up, :], filt[down, :]
                grad_spec[up, :] = fg_cos.astype(low)
                grad_spec[down, :] = fg_sin.astype(low)
                both[up, :] = (filt_cos * fg_cos + filt_sin * fg_sin).astype(low)
                both[down, :] = (filt_cos * fg_sin - filt_sin * fg_cos).astype(low)
            return carry

        lax.fori_loop(0, length // tile_rows, spectrum, 0)
    mixed[pl.ds(length, 8), :] = jnp.zeros((8, mixed.shape[1]), f32)

    def streams_back(i, carry):
        rows = pl.ds(pl.multiple_of(i * tile_rows, tile_rows), tile_rows)
        value = mm(back[rows, :], both[...]) * (1.0 / length)
        fg = filtered_grad[rows, :].astype(f32)
        prod_grad = (value + small[153:154, :] * fg).astype(low).astype(f32)
        mixed[rows, 0:chans] = (
            (prod_grad * streams[rows, 2 * chans : 3 * chans].astype(f32)).astype(low).astype(f32)
        )
        mixed[rows, chans : 2 * chans] = (
            (gated_grad[rows, :].astype(f32) * filtered[rows, :]).astype(low).astype(f32)
        )
        mixed[rows, 2 * chans : 3 * chans] = (
            (prod_grad * streams[rows, 0:chans].astype(f32)).astype(low).astype(f32)
        )
        return carry + jnp.sum(fg * prod[rows, :].astype(f32), axis=0, keepdims=True)

    small_out[...] = jnp.zeros(small_out.shape, f32)
    small_out[153:154, :] = lax.fori_loop(
        0, length // tile_rows, streams_back, jnp.zeros((1, chans), f32)
    )
    step = 128
    for slot in (2, 0, 1, None):
        target = me if slot is None else peers[slot]

        def short_back(i, carry):
            start = pl.multiple_of(target * count + i * step, step)
            for g in range(3):
                cols = slice(g * chans, (g + 1) * chans)
                tile = mixed[pl.ds(start, step + 8), cols]
                now = tile[:step]
                after = pltpu.roll(tile, step + 7, 0)[:step]
                later = pltpu.roll(tile, step + 6, 0)[:step]
                proj_grad[pl.ds(start, step), cols] = (
                    small[144 + 3 * g : 145 + 3 * g, :] * now
                    + small[145 + 3 * g : 146 + 3 * g, :] * after
                    + small[146 + 3 * g : 147 + 3 * g, :] * later
                ).astype(low)
            return carry

        lax.fori_loop(0, count // step, short_back, 0)
        rows = rows_of(target, count)

        def through(i, carry):
            cols = pl.ds(pl.multiple_of(i * depth, depth), depth)
            value = mm_t(proj_grad[rows, :half], win[0, i]) + mm_t(proj_grad[rows, half:], win[1, i])
            if slot is None:
                input_grad_out[:, cols] = value
            else:
                send[slot, :, cols] = value.astype(low)
            return carry

        lax.fori_loop(0, width // depth, through, 0)
        if slot is not None:
            sends += reduce_send(slot, send, recv, reduce_sems, peers)

    def weights(i, carry):
        cols = pl.ds(pl.multiple_of(i * depth, depth), depth)
        for h in range(2):
            wgrad_in[h, i] = t_mm(normed[:, cols], proj_grad[:, h * half : (h + 1) * half]).astype(
                low
            )
        return carry

    lax.fori_loop(0, width // depth, weights, 0)
    for h in range(2):
        value = t_mm(gated[...], gather[:, h * width // 2 : (h + 1) * width // 2]).astype(low)
        wgrad_out_part[h] = value.reshape(wgrad_out_part.shape[1:])
    swapped = [(wgrad_in, other_in), (wgrad_out_part, other_out)]
    swaps = swap_begin(swapped, core_sems)
    sends += swaps
    sends += reduce_pass(send, recv, reduce_sems, peers)
    taps_sum[...] = jnp.zeros(taps_sum.shape, f32)

    def tap_sums(i, carry):
        start = pl.multiple_of(i * step, step)
        for g in range(3):
            cols = slice(g * chans, (g + 1) * chans)
            tile = mixed[pl.ds(start, step + 8), cols]
            seen = proj[pl.ds(start, step), cols].astype(f32)
            for at in range(3):
                shift = pltpu.roll(tile, step + 8 - at, 0)[:step] if at else tile[:step]
                taps_sum[8 * at : 8 * at + 8, cols] += jnp.sum(
                    (seen * shift).reshape(step // 8, 8, chans), axis=0
                )
        return carry

    lax.fori_loop(0, length // step, tap_sums, 0)

    def filter_spectrum(i, carry):
        up = pl.ds(pl.multiple_of(i * tile_rows, tile_rows), tile_rows)
        down = pl.ds(pl.multiple_of(i * tile_rows + length, tile_rows), tile_rows)
        prod_cos, prod_sin = spec[up, :].astype(f32), spec[down, :].astype(f32)
        fg_cos, fg_sin = grad_spec[up, :].astype(f32), grad_spec[down, :].astype(f32)
        both[up, :] = (prod_cos * fg_cos + prod_sin * fg_sin).astype(low)
        both[down, :] = (prod_cos * fg_sin - prod_sin * fg_cos).astype(low)
        return carry

    lax.fori_loop(0, length // tile_rows, filter_spectrum, 0)

    def filter_back(i, carry):
        rows = pl.ds(pl.multiple_of(i * tile_rows, tile_rows), tile_rows)
        times = lax.broadcasted_iota(jnp.int32, (tile_rows, 1), 0) + i * tile_rows
        fade = jnp.exp(-times.astype(f32) * small[154:155, :])
        filter_grad[rows, :] = mm(back[rows, :], both[...]) * (1.0 / length) * fade
        return carry

    lax.fori_loop(0, length // tile_rows, filter_back, 0)
    small_out[0:64, :] = t_mm_exact(waves2[...], filter_grad[...])
    back2 = mm_t_exact(filter_grad[...], small[0:64, :]) * steep2[...]
    small_out[64:128, 0:64] = t_mm_exact(waves1[...], back2)
    back1 = mm_t_exact(back2, small[64:128, 0:64]) * steep1[...]
    small_out[64:128, 128:192] = t_mm_exact(embedding[:, 0:64], back1)
    for g in range(3):
        for at in range(3):
            small_out[144 + 3 * g + at : 145 + 3 * g + at, :] = jnp.sum(
                taps_sum[8 * at : 8 * at + 8, g * chans : (g + 1) * chans], axis=0, keepdims=True
            )
    swap_end(swaps, swapped)
    stores = fetch(half_pairs_mixer(half_out, wgrad_in, wgrad_out_part), store_sems)
    plane_sum.end(summed)
    sends += plane_sum.sends
    reduce_wait(send, recv, reduce_sems, peers)
    norm_back_parts(input_grad_out, recv, grad, x, par[0:1, :], sums)
    for q in range(width // chans):
        cols = slice(q * chans, (q + 1) * chans)
        small_out[128 + 2 * q : 130 + 2 * q, :] = sums[:, cols]
        small_out[136 + 2 * q : 138 + 2 * q, :] = late[:, cols]
    for copy in sends:
        copy.wait_send()
    for store in stores:
        store.wait()


def run_kernel(kernel, name, collective_id, operands, in_vmem, outs, out_vmem, scratch, flops):
    inside = pl.BlockSpec(memory_space=pltpu.VMEM)
    outside = pl.BlockSpec(memory_space=pl.ANY)
    scalars = pl.BlockSpec(memory_space=pltpu.SMEM)
    return pl.pallas_call(
        kernel,
        out_shape=[jax.ShapeDtypeStruct(shape, kind) for shape, kind in outs],
        in_specs=[
            scalars if item.dtype == jnp.int32 else inside if at in in_vmem else outside
            for at, item in enumerate(operands)
        ],
        out_specs=[inside if at in out_vmem else outside for at in range(len(outs))],
        scratch_shapes=scratch,
        compiler_params=pltpu.CompilerParams(
            collective_id=collective_id, has_side_effects=True, vmem_limit_bytes=60 * 2**20
        ),
        cost_estimate=pl.CostEstimate(flops=flops, bytes_accessed=2**25, transcendentals=0),
        name=name,
    )(*operands)


def exchange_scratch(count, width):
    return [pltpu.VMEM((3, count, width), low), pltpu.VMEM((3, count, width), low)]


def exchange_semaphores(count):
    return [pltpu.SemaphoreType.DMA((2, count)), pltpu.SemaphoreType.DMA((count,))]


def semaphores(loads, stores):
    return [
        pltpu.SemaphoreType.DMA((2, 6)),
        pltpu.SemaphoreType.DMA((2, 10)),
        pltpu.SemaphoreType.DMA((loads,)),
        pltpu.SemaphoreType.DMA((stores,)),
    ]


def mixer_weights_scratch(pack, width):
    _, dp_count, depth, cols = pack.shape
    return [
        pltpu.VMEM((2, dp_count, depth, 3 * cols // 4), low),
        pltpu.VMEM((2, dp_count, depth // 4, cols), low),
    ]


def mixer_forward(s, x, lengths, weights, waves, back, gathered):
    gathers = gathered is not None
    count, width = x.shape[-2:]
    length = waves.shape[1]
    chans, half = width // 4, width // 2
    knots, dp_count = chans // 4, lax.axis_size("dp")
    pack_shape = (2, dp_count, width // dp_count, half)
    pack = jax.ShapeDtypeStruct(pack_shape, low)
    vm, dma = pltpu.VMEM, pltpu.SemaphoreType.DMA
    outs = [
        ((length, width), low),
        ((length, 3 * chans), low),
        ((length, 3 * chans), low),
        ((length, chans), low),
        ((2 * length, chans), low),
        ((length, chans), f32),
        ((length, chans), low),
        ((count, width), f32),
    ]
    more = []
    if gathers:
        cotangent, embedding = gathered
        depth = weights[0].shape[0]
        units = 2 * half
        ff_shape = (2, dp_count, 2 * width // dp_count, half)
        half_in = 3 * chans // 2
        filters = [((2 * length, chans), f32), *[((length, knots), f32)] * 4]
        outs = [
            (pack_shape, low),
            (ff_shape, low),
            ((length, width), low),
            ((2, 8, width), f32),
            ((2, 160, chans), f32),
            (pack_shape, low),
            (ff_shape[2:], low),
            *filters,
            *filters,
            ((length, width), low),
            ((length, units), low),
            ((length, units), low),
            ((count, width), f32),
        ] + outs
        more = [
            *[vm((length, knots), f32)] * 4,
            vm((length, chans), low),
            vm((*pack_shape[:3], half // 4), low),
            vm(ff_shape, low),
            vm((length, width), low),
            vm(pack_shape, low),
            *[dma((2, 4)), dma((2, 3))] * 4,
            dma((2, 6)),
            dma((15,)),
            vm((2, *pack_shape[2:]), low),
            vm((2, *ff_shape[2:]), low),
            vm((2, 8, width), f32),
            vm((2, 160, chans), f32),
            vm((2, 4, depth, half_in), low),
            vm((2, 4 * depth, half_in // 3), low),
            vm((2, 4, depth, half), low),
            dma((2, 7)),
            dma((2, 1)),
            dma((2, 7)),
            dma((2, 1)),
            dma((2, 1)),
            dma((2, 1)),
            vm((length, width), low),
            *exchange_scratch(count, width),
            dma((2, 6)),
            dma((2, 10)),
            dma((5,)),
        ]
        operands = (cotangent, embedding, lengths, *weights, waves, back)
        inside = range(len(operands) - 1)
        out_inside = (len(outs) - 9, len(outs) - 1)
    else:
        par, small, weights, filt = weights
        operands = (par, small, lengths, weights, filt, waves, back)
        inside = range(3)
        out_inside = (len(outs) - 1,)
    return run_kernel(
        partial(mixer_forward_kernel, s, gathers),
        "opening" if gathers else "mixer_forward",
        1 + s,
        (x, *operands),
        inside,
        outs,
        out_inside,
        [vm((length, width), low)]
        + mixer_weights_scratch(pack, width)
        + [
            vm((2 * length, chans), f32),
            vm((2 * length, length), low),
            vm((length, 2 * length), low),
            vm((length + 8, 3 * chans), f32),
            vm((length, 3 * chans), low),
            vm((length, 3 * chans), low),
            vm((length, chans), low),
            vm((2 * length, chans), low),
            vm((2 * length, chans), low),
            vm((length, chans), f32),
            vm((length, chans), low),
        ]
        + exchange_scratch(count, width)
        + semaphores(8, 7)
        + more,
        10**10,
    )


def ff_turn(s, cotangent, x, par, lengths, pack, late):
    count, width = x.shape
    _, dp_count, rows, half = pack.shape
    length, units = 4 * count, 2 * half
    vm = pltpu.VMEM
    return run_kernel(
        partial(ff_turn_kernel, s),
        "ff_turn",
        4,
        (cotangent, x, par, lengths, pack, late),
        range(3),
        [
            (pack.shape[1:], low),
            ((3, count, width), low),
            ((count, width), f32),
            ((count, width), f32),
            ((2, width), f32),
        ],
        (2, 3, 4),
        [vm((length, width), low)] * 2
        + [vm((2, dp_count, rows // 2, half), low)] * 2
        + [vm((length, units), low)] * 2
        + [vm(pack.shape, low), vm(pack.shape[1:], low)]
        + [vm((3, count, width), low)] * 3
        + semaphores(3, 2)
        + [pltpu.SemaphoreType.DMA((2, 1))],
        3 * 10**10,
    )


def ff_backward(s, grad, middle, par, lengths, pack, second, value, slope, earlier):
    count, width = grad.shape
    _, dp_count, rows, half = pack.shape
    length, units = value.shape
    vm = pltpu.VMEM
    weights = [vm((2, dp_count, rows // 2, half), low)] * 2
    return run_kernel(
        partial(ff_backward_kernel, s),
        "ff_backward",
        5,
        (grad, middle, par, lengths, pack, second, value, slope, earlier),
        range(3),
        [
            (pack.shape[1:], low),
            ((count, width), f32),
            ((2, width), f32),
            (earlier.shape[1:], low),
        ],
        (1, 2, 3),
        [vm((length, width), low)]
        + weights
        + [vm((length, width), low)]
        + [vm((length, units), low)] * 3
        + [vm(pack.shape, low), vm(pack.shape[1:], low)]
        + exchange_scratch(count, width)
        + semaphores(5, 1)
        + plane_sum_scratch(earlier)
        + [pltpu.SemaphoreType.DMA((2, 1))],
        2 * 10**10,
    )


def mixer_backward(
    s, grad, x, par, small, embedding, late, lengths, pack, waves, back, kept, earlier
):
    normed, proj, streams, prod, spec, filtered, gated, filt, *network = kept
    count, width = grad.shape
    length, chans = prod.shape
    knots = network[0].shape[1]
    vm = pltpu.VMEM
    weights = mixer_weights_scratch(pack, width)
    return run_kernel(
        partial(mixer_backward_kernel, s),
        "mixer_backward",
        7 + s,
        (grad, x, par, small, embedding, late, lengths, pack, filt, waves, back, normed, proj,
         streams, prod, spec, filtered, gated, *network, earlier),
        range(6),
        [
            (pack.shape[1:], low),
            (small.shape[1:], f32),
            ((count, width), f32),
            (earlier.shape[1:], low),
        ],
        (1, 2, 3),
        [vm((length, width), low)]
        + weights
        + [
            vm((2 * length, chans), f32),
            vm((2 * length, length), low),
            vm((length, 2 * length), low),
            vm((length, width), low),
            vm((length, 3 * chans), low),
            vm((length, 3 * chans), low),
            vm((length, chans), low),
            vm((2 * length, chans), low),
            vm((length, chans), f32),
            vm((length, chans), low),
            vm((length, chans), low),
            vm((length, chans), low),
            vm((2 * length, chans), low),
            vm((2 * length, chans), low),
            vm((2 * length, chans), f32),
            vm((length, chans), f32),
            vm((length + 8, 3 * chans), f32),
            vm((length, 3 * chans), low),
        ]
        + weights
        + [vm(item.shape[1:], low) for item in weights]
        + [vm((length, knots), f32)] * 4
        + [vm((2, width), f32), vm((24, 3 * chans), f32)]
        + exchange_scratch(count, width)
        + semaphores(19, 5)
        + plane_sum_scratch(earlier)
        + [pltpu.SemaphoreType.DMA((2, 2))],
        2 * 10**10,
    )


def shuffle_stage(w_in, w_out, w_up, stage_in, stage_out, stage_up):
    depth, chans = w_in.shape[0], w_out.shape[1] // 4
    count = lax.axis_size("dp")
    half_in = stage_in.shape[3]
    piece = chans // count
    for h in range(2):
        for j in range(4):
            for c in range(0, half_in, 2 * piece):
                pair = []
                for col in (c, c + piece):
                    g, d = divmod((h * half_in + col) // piece, count)
                    at = ((g * count + d) * 4 + j) * piece
                    pair.append(w_in[:, at : at + piece].astype(f32))
                stage_in[h, j, :, c : c + 2 * piece] = jnp.concatenate(pair, 1).astype(low)
            for d in range(2):
                at = ((2 * h + d) * 4 + j) * chans
                stage_up[h, j, :, d * chans : (d + 1) * chans] = w_up[:, at : at + chans]
    part = half_in // 3
    for h in range(2):
        for q in range(4):
            at = (h * 4 + q) * part
            stage_out[h, q * depth : (q + 1) * depth, :] = w_out[:, at : at + part]


def parameters_stage(me, par, small, gain, shift, taps, first, second, last, direct, rates):
    chans = small.shape[1]
    count = lax.axis_size("dp")
    piece = chans // count
    width = last.shape[2]
    par[0:1, :] = gain[0, 0:1, :]
    par[1:2, :] = shift[0, 0:1, :]
    par[2:3, :] = gain[0, 1:2, :]
    par[3:4, :] = shift[0, 1:2, :]
    par[4:8, :] = jnp.zeros((4, width), f32)
    small[64:160, :] = jnp.zeros((96, chans), f32)
    small[64:128, 0:64] = second[0]
    for row in range(first.shape[0]):
        small[64 + row : 65 + row, 128:192] = first[row]
    for j in range(4):

        @pl.when(me == j)
        def _():
            for d in range(0, count, 2):
                cols = slice(d * piece, (d + 2) * piece)

                def picked(ref, rows, base=0):
                    at = [base + ((d + k) * 4 + j) * piece for k in range(2)]
                    return jnp.concatenate([ref[rows, a : a + piece] for a in at], 1)

                small[0:64, cols] = picked(last.at[0], slice(0, 64))
                for g in range(3):
                    for tap in range(3):
                        row = 144 + 3 * g + tap
                        small[row : row + 1, cols] = picked(
                            taps.at[tap], slice(0, 1), g * width
                        )
                small[153:154, cols] = picked(direct, slice(0, 1))
                small[154:155, cols] = picked(rates, slice(0, 1))


def shuffle_send(section, me, targets, sources, parts, parameters, sems):
    stage_in, stage_out, stage_up, w_down = sources
    mixer_parts, ff_parts = parts
    in_sems, out_sems, up_sems, down_sems, par_sems, small_sems = sems
    depth, half_in = stage_in.shape[2:]
    half = stage_up.shape[3]
    copies = [
        remote_to(item.at[section], item.at[section], at, 0, other_core())
        for item, at in zip(parameters, (par_sems, small_sems))
    ]
    for e, (t, seq, device) in enumerate(targets):
        target = mixer_parts.at[section, rows_of(me, depth), pl.ds(0, half_in)]
        copies.append(remote_to(stage_in.at[t, seq], target, in_sems, e, device))
    target = mixer_parts.at[section, :, pl.ds(half_in, half_in // 3)]
    copies.append(remote_to(stage_out.at[1 - section], target, out_sems, 0, other_core()))
    for e, (t, seq, device) in enumerate(targets):
        target = ff_parts.at[section, rows_of(me, depth), :]
        copies.append(remote_to(stage_up.at[t, seq], target, up_sems, e, device))
    cols = pl.ds(pl.multiple_of((1 - section) * half, half), half)
    target = ff_parts.at[section, pl.ds(4 * depth, 4 * depth), :]
    copies.append(remote_to(w_down.at[:, cols], target, down_sems, 0, other_core()))
    for copy in copies:
        copy.start()
    mixer_parts[section, rows_of(me, depth), 0:half_in] = stage_in[section, me]
    mixer_parts[section, :, half_in:] = stage_out[section]
    ff_parts[section, rows_of(me, depth), :] = stage_up[section, me]
    cols = pl.ds(pl.multiple_of(section * half, half), half)
    ff_parts[section, 4 * depth : 8 * depth, :] = w_down[:, cols]
    return copies


def shuffle_wait_mixer(section, me, targets, parts, stage_in, in_sems, out_sems):
    depth, half_in = stage_in.shape[2:]
    for e, (t, seq, device) in enumerate(targets):
        block = parts.at[t, rows_of(seq, depth), pl.ds(0, half_in)]
        remote_to(block, block, in_sems, e, device).wait_recv()
    block = parts.at[1 - section, :, pl.ds(half_in, half_in // 3)]
    remote_to(block, block, out_sems, 0, other_core()).wait_recv()


def shuffle_wait_ff(section, me, targets, parts, stage_up, up_sems, down_sems):
    depth = stage_up.shape[2]
    for e, (t, seq, device) in enumerate(targets):
        block = parts.at[t, rows_of(seq, depth), :]
        remote_to(block, block, up_sems, e, device).wait_recv()
    block = parts.at[1 - section, pl.ds(4 * depth, 4 * depth), :]
    remote_to(block, block, down_sems, 0, other_core()).wait_recv()


def shuffle_targets(section, me, peers):
    targets = [(section, peer, {"seq": peer}) for peer in peers]
    targets.append((1 - section, me, other_core()))
    targets += [(1 - section, peer, {**other_core(), "seq": peer}) for peer in peers]
    return targets


def finish_kernel(
    vec0, vec1, mixer0, mixer1, ff0, ff1, grad0, grad1, parts, own_part, x, out0, lengths,
    block_outputs, input_grads, got_in, got_out, got_up, got_down, vec_out,
    mine0, arrived0, plane_sems0, sum_sems0, mine1, arrived1, plane_sems1, sum_sems1,
    vec_other, vec_sum, vec_arrived, vec_all, stage_mixer, stage_ff, own_sems, load_sems,
    layer_sems, keep_sems, vec_core_sems, vec_sum_sems, vec_plane_sems, vec_seq_sems, in_sems, out_sems, up_sems, down_sems,
    send, recv, out1, reduce_sems,
):
    section = lax.axis_index("section")
    me = lax.axis_index("seq")
    here, near, far = along_planes()
    planes = (near, far, (near + 2) % 4)
    peers = neighbours(me)
    depth, half_in = got_in.shape[2:]
    targets = shuffle_targets(section, me, peers)
    greeted = greet([device for _, _, device in targets] + [{"dp": plane} for plane in planes])
    middle = mixer0.shape[2] // 2
    chunks = (pl.ds(0, middle), pl.ds(middle, middle))
    in_cols = (pl.ds(0, middle), pl.ds(middle, half_in - middle))

    def columns(e, at):
        t, seq, device = targets[e]
        return remote_to(
            stage_mixer.at[t, rows_of(seq, depth), in_cols[at]],
            got_in.at[section, me, :, in_cols[at]],
            in_sems,
            2 * e + at,
            device,
        )

    out_columns = remote_to(
        stage_mixer.at[1 - section, :, pl.ds(half_in, half_in // 3)], got_out.at[section], out_sems,
        0, other_core(),
    )

    def send_layer(s, at):
        for index in range(2):

            @pl.when(section == index)
            def _():
                for e in range(3) if index == s else range(3, 7):
                    columns(e, at).start()
                if at == 1 and index != s:
                    out_columns.start()

    all_here(greeted)
    for index, vec in enumerate((vec1, vec0)):

        @pl.when(section == index)
        def _():
            remote_to(vec, vec_other, vec_core_sems, 0, other_core()).start()

    sends = []
    vec_swap = remote_to(vec_other, vec_other, vec_core_sems, 0, other_core())
    vec_swap.wait_recv()
    sends.append(vec_swap)

    @pl.when(section == 0)
    def _():
        vec_sum[...] = vec0[...] + vec_other[...]

    @pl.when(section == 1)
    def _():
        vec_sum[...] = vec1[...] + vec_other[...]

    count = 4
    chunk = vec_sum.shape[0] // count
    moves = [
        remote_to(
            vec_sum.at[rows_of(plane, chunk)], vec_arrived.at[slot], vec_sum_sems, slot,
            {"dp": plane},
        )
        for slot, plane in enumerate(planes)
    ]
    for copy in moves:
        copy.start()
    sends += moves
    plane_sums = [
        PlaneSum(mixer0.at[:, :, chunks[0]], mine0, arrived0, plane_sems0, sum_sems0),
        PlaneSum(mixer0.at[:, :, chunks[1]], mine1, arrived1, plane_sems1, sum_sems1),
    ]
    for plane_sum in plane_sums:
        plane_sum.begin()
    loads = fetch(
        [
            (parts, send),
            (ff0, stage_ff.at[0]),
            (ff1, stage_ff.at[1]),
            (mixer1, stage_mixer.at[1]),
        ],
        load_sems,
    )
    by_layer(True, ((grad0, grad1, input_grads),), layer_sems, keep_sems)
    for load in loads[1:]:
        load.wait()
    ups = []
    for e, (t, seq, device) in enumerate(targets):
        ups.append(
            remote_to(
                stage_ff.at[t, rows_of(seq, depth), :], got_up.at[section, me], up_sems, e, device
            )
        )
    downs = [
        remote_to(
            stage_ff.at[1 - section, pl.ds(4 * depth, 4 * depth), :], got_down.at[section],
            down_sems, 0, other_core(),
        )
    ]
    for copy in ups + downs:
        copy.start()
    sends += ups + downs
    send_layer(1, 0)
    send_layer(1, 1)
    loads[0].wait()
    for slot in (2, 0, 1):
        sends += reduce_send(slot, send, recv, reduce_sems, peers)
    keeps = fetch(
        [
            (stage_ff.at[section, rows_of(me, depth), :], got_up.at[section, me]),
            (stage_ff.at[section, pl.ds(4 * depth, 4 * depth), :], got_down.at[section]),
        ],
        own_sems,
    )

    for copy in moves:
        copy.wait_recv()
    own_chunk = rows_of(here, chunk)
    total = vec_sum[own_chunk, :]
    for slot in range(len(planes)):
        total = total + vec_arrived[slot]
    vec_all[me, own_chunk, :] = total
    moves = [
        remote_to(
            vec_all.at[me, own_chunk], vec_all.at[me, own_chunk], vec_plane_sems, slot,
            {"dp": plane},
        )
        for slot, plane in enumerate(planes)
    ]
    for copy in moves:
        copy.start()
    sends += moves
    for plane_sum in plane_sums:
        plane_sum.forward()
    sends += reduce_pass(send, recv, reduce_sems, peers)
    for slot, plane in enumerate(planes):
        block = vec_all.at[me, rows_of(plane, chunk)]
        remote_to(block, block, vec_plane_sems, slot, {"dp": plane}).wait_recv()
    moves = [
        remote(vec_all.at[me], vec_all.at[me], vec_seq_sems, slot, peer)
        for slot, peer in enumerate(peers)
    ]
    for copy in moves:
        copy.start()
    sends += moves

    for at, plane_sum in enumerate(plane_sums):
        plane_sum.end(stage_mixer.at[0, :, chunks[at]])
        sends += plane_sum.sends
        send_layer(0, at)
    sends += [columns(e, at) for e in range(7) for at in range(2)] + [out_columns]
    reduce_wait(send, recv, reduce_sems, peers)
    start = me * own_part.shape[0]

    def add(rows):
        total = own_part[rows, :] + recv[0, rows, :].astype(f32) + recv[1, rows, :].astype(f32)
        out1[rows, :] = x[rows, :] + valid_rows(lengths, start + rows.start, 32) * total

    by_rows(own_part.shape[0], 32, add)
    by_layer(True, ((out0, out1, block_outputs),), layer_sems, keep_sems, 1)
    keeps += fetch(
        [
            (
                stage_mixer.at[section, rows_of(me, depth), pl.ds(0, half_in)],
                got_in.at[section, me],
            ),
            (stage_mixer.at[section, :, pl.ds(half_in, half_in // 3)], got_out.at[section]),
        ],
        own_sems,
        2,
    )
    for slot, peer in enumerate(peers):
        block = vec_all.at[peer]
        remote(block, block, vec_seq_sems, slot, peer).wait_recv()
    keeps += fetch([(vec_all, vec_out)], own_sems, 4)
    for e, (t, seq, device) in enumerate(targets):
        block = got_up.at[t, seq]
        remote_to(block, block, up_sems, e, device).wait_recv()
        for at in range(2):
            block = got_in.at[t, seq, :, in_cols[at]]
            remote_to(block, block, in_sems, 2 * e + at, device).wait_recv()
    downs[0].wait_recv()
    out_columns.wait_recv()
    by_layer(False, ((grad0, grad1, input_grads),), layer_sems, keep_sems)
    by_layer(False, ((out0, out1, block_outputs),), layer_sems, keep_sems, 1)
    for copy in sends:
        copy.wait_send()
    for keep in keeps:
        keep.wait()


def unpack_kernel(
    blocks, grads, got_in, got_out, got_up, got_down, vec_all,
    block_outputs, input_grads, g_in, g_out, g_up, g_down, g_gain, g_bias, g_taps, g_first,
    g_second, g_last, g_direct,
    stage_blocks, stage_grads, load_sems, copy_sems,
):
    loads = fetch([(blocks, stage_blocks), (grads, stage_grads)], load_sems)
    depth = g_in.shape[0]
    half_in, half_up = got_in.shape[3], got_up.shape[3]
    chans = vec_all.shape[2]
    count = 4
    piece = chans // count
    for j in range(4):
        for d in range(count):
            at = (d * 4 + j) * chans
            h, col = divmod(d * chans, half_up)
            g_up[:, at : at + chans] = got_up[h, j, :, col : col + chans].astype(f32)
    for h in range(2):
        g_down[:, h * half_up : (h + 1) * half_up] = got_down[h].astype(f32)
    for load in loads:
        load.wait()
    copies = fetch([(stage_blocks, block_outputs), (stage_grads, input_grads)], copy_sems)
    for g in range(3):
        for d in range(count):
            h, col = divmod(g * chans + d * piece, half_in)
            for j in range(0, 4, 2):
                at = ((g * count + d) * 4 + j) * piece
                g_in[:, at : at + 2 * piece] = jnp.concatenate(
                    [got_in[h, j + k, :, col : col + piece].astype(f32) for k in range(2)], 1
                )
    part = half_in // 3
    for h in range(2):
        for q in range(4):
            at = (h * 4 + q) * part
            g_out[:, at : at + part] = got_out[h, q * depth : (q + 1) * depth, :].astype(f32)
    first = sum_of(vec_all, slice(64, 64 + g_first.shape[0]), slice(128, 192))
    for row in range(g_first.shape[0]):
        g_first[row] = first[row : row + 1]
    g_second[...] = sum_of(vec_all, slice(64, 128), slice(0, 64))
    for q in range(4):
        cols = slice(q * chans, (q + 1) * chans)
        early = sum_of(vec_all, slice(128 + 2 * q, 130 + 2 * q), slice(None))
        late = sum_of(vec_all, slice(136 + 2 * q, 138 + 2 * q), slice(None))
        g_gain[0:1, cols] = early[0:1]
        g_gain[1:2, cols] = late[0:1]
        g_bias[0:1, cols] = early[1:2]
        g_bias[1:2, cols] = late[1:2]
    for d in range(count):
        cols = slice(d * piece, (d + 1) * piece)
        for j in range(0, 4, 2):
            at = (d * 4 + j) * piece
            pair = slice(at, at + 2 * piece)

            def joined(rows):
                return jnp.concatenate([vec_all[j, rows, cols], vec_all[j + 1, rows, cols]], 1)

            g_last[:, pair] = joined(slice(0, 64))
            for g in range(3):
                for tap in range(3):
                    row = 144 + 3 * g + tap
                    start = g * 4 * chans + at
                    g_taps[tap, :, start : start + 2 * piece] = joined(slice(row, row + 1))
            g_direct[:, pair] = joined(slice(153, 154))

    for copy in copies:
        copy.wait()


def sum_of(blocks, rows, cols):
    return (blocks[0, rows, cols] + blocks[1, rows, cols]) + (
        blocks[2, rows, cols] + blocks[3, rows, cols]
    )


def finish(vec0, vec1, mixer0, mixer1, ff0, ff1, grad0, grad1, parts, own_part, x, out0, lengths):
    count, width = grad0.shape
    dp_count, rows, half = mixer0.shape
    depth = rows // 4
    chans = vec0.shape[1]
    half_in = 3 * chans // 2
    vm, dma = pltpu.VMEM, pltpu.SemaphoreType.DMA
    vec_rows = vec0.shape[0]
    chunk = jax.ShapeDtypeStruct((dp_count, rows, half // 2), low)
    return run_kernel(
        finish_kernel,
        "finish",
        10,
        (vec0, vec1, mixer0, mixer1, ff0, ff1, grad0, grad1, parts, own_part, x, out0, lengths),
        (0, 1, 6, 7, 9, 10, 11),
        [
            ((2, count, width), f32),
            ((2, count, width), f32),
            ((2, 4, depth, half_in), low),
            ((2, rows, half_in // 3), low),
            ((2, 4, depth, half), low),
            ((2, rows, half), low),
            ((4, vec_rows, chans), f32),
        ],
        (),
        plane_sum_scratch(chunk)
        + plane_sum_scratch(chunk)
        + [
            vm((vec_rows, chans), f32),
            vm((vec_rows, chans), f32),
            vm((3, vec_rows // 4, chans), f32),
            vm((4, vec_rows, chans), f32),
            vm((2, *mixer1.shape), low),
            vm((2, *ff1.shape), low),
            dma((5,)),
            dma((4,)),
            *exchange_semaphores(2),
            dma((2, 1)),
            dma((2, 3)),
            dma((2, 3)),
            dma((2, 3)),
            dma((2, 14)),
            dma((2, 1)),
            dma((2, 7)),
            dma((2, 1)),
            *exchange_scratch(count, width),
            vm((count, width), f32),
            dma((2, 10)),
        ],
        10**9,
    )


def unpack(blocks, grads, got, first_shape):
    width = blocks.shape[2]
    depth = got[0].shape[2]
    units = 4 * 2 * got[2].shape[3]
    knots = first_shape[1]
    inside = pl.BlockSpec(memory_space=pltpu.VMEM)
    outside = pl.BlockSpec(memory_space=pl.ANY)
    shapes = (
        blocks.shape, grads.shape, (depth, 3 * width), (depth, width), (depth, units),
        (4 * depth, width), (2, width), (2, width), (3, 1, 3 * width),
        (first_shape[0], 1, knots), (knots, knots),
        (knots, width), (1, width),
    )
    return pl.pallas_call(
        unpack_kernel,
        out_shape=[jax.ShapeDtypeStruct(shape, f32) for shape in shapes],
        in_specs=[outside] * 2 + [inside] * 5,
        out_specs=[outside] * 2 + [inside] * 11,
        scratch_shapes=[
            pltpu.VMEM(blocks.shape, f32),
            pltpu.VMEM(grads.shape, f32),
            pltpu.SemaphoreType.DMA((2,)),
            pltpu.SemaphoreType.DMA((2,)),
        ],
        compiler_params=pltpu.CompilerParams(vmem_limit_bytes=56 * 2**20),
        name="unpack",
    )(blocks, grads, *got)


def any_device(
    tokens,
    cotangent,
    lengths,
    norm_gain,
    norm_bias,
    mixer_in,
    short_kernel,
    filter_first,
    filter_second,
    filter_last,
    filter_bias,
    decay_rates,
    mixer_out,
    up_weight,
    down_weight,
):
    section = lax.axis_index("section")
    seq_index = lax.axis_index("seq")
    seq_count = lax.axis_size("seq")
    dp_count = lax.axis_size("dp")
    own_layer_first = section == 0
    local_len = tokens.shape[2]
    width = tokens.shape[3]
    hidden = up_weight.shape[2]
    row_len = local_len * seq_count
    chans = width // seq_count
    units = hidden // seq_count

    def share_columns(block, groups):
        rows = block.shape[0]
        inner = block.shape[1] // (groups * dp_count * seq_count)
        split = block.reshape(rows, groups, dp_count, seq_count, inner)
        split = jnp.transpose(split, (3, 0, 1, 2, 4))
        moved = lax.all_to_all(split, "seq", split_axis=0, concat_axis=0, tiled=True)
        return moved.reshape(seq_count * rows, groups * dp_count * inner)

    def unshare_columns(block, groups):
        rows = block.shape[0] // seq_count
        inner = block.shape[1] // (groups * dp_count)
        split = block.reshape(seq_count, rows, groups, dp_count, inner)
        moved = lax.all_to_all(split, "seq", split_axis=0, concat_axis=0, tiled=True)
        moved = jnp.transpose(moved, (1, 2, 3, 0, 4))
        return moved.reshape(rows, groups * dp_count * seq_count * inner)

    def gathered(block):
        whole = lax.all_gather(block, ("section", "dp"))
        return whole.reshape(2, dp_count * block.shape[0], block.shape[1])

    weights = (
        gathered(share_columns(mixer_in[0], 3)),
        gathered(mixer_out[0]),
        gathered(share_columns(up_weight[0], 1)),
        gathered(down_weight[0]),
    )

    def both(value):
        return lax.all_gather(value[0], "section")

    gains, shifts = both(norm_gain), both(norm_bias)
    taps, first_w, second_w = both(short_kernel), both(filter_first), both(filter_second)
    last_w, direct, rates = both(filter_last), both(filter_bias), both(decay_rates)

    def mine(value):
        lead = value.shape[:-1]
        split = value.reshape(*lead, dp_count, seq_count, -1)
        picked = lax.dynamic_index_in_dim(split, seq_index, len(lead) + 1, False)
        return picked.reshape(*lead, chans)

    def placed(value):
        lead = value.shape[:-1]
        split = value.reshape(*lead, dp_count, 1, -1)
        inner = split.shape[-1]
        empty = jnp.zeros((*lead, dp_count, seq_count, inner), value.dtype)
        at = [0] * len(lead) + [0, seq_index, 0]
        return lax.dynamic_update_slice(empty, split, at).reshape(*lead, width)

    waves = jnp.asarray(wave_tables(row_len))
    waves_back = waves

    def to_waves(x):
        both_parts = mm(waves, x)
        return both_parts[:row_len], both_parts[row_len:]

    def from_waves(cos_part, sin_part):
        joined = jnp.concatenate([cos_part, sin_part], 0).astype(low)
        return t_mm(waves_back, joined) * (1.0 / row_len)

    def ag(x):
        return lax.all_gather(x, "seq", axis=0, tiled=True)

    def rs(x):
        return lax.psum_scatter(x.astype(low), "seq", scatter_dimension=0, tiled=True).astype(f32)

    length_now = lax.dynamic_index_in_dim(lengths, section, 0, False)[0]
    positions = seq_index * local_len + jnp.arange(local_len)
    mask = (positions < length_now).astype(f32)[:, None]
    row_mask = (jnp.arange(row_len) < length_now).astype(f32)[:, None]
    own_tokens = lax.dynamic_index_in_dim(tokens, section, 0, False)[0].astype(f32)
    own_cotangent = lax.dynamic_index_in_dim(cotangent, section, 0, False)[0].astype(f32)

    def layer_forward(s, inputs):
        w_in, w_out, w_up, w_down = [w[s] for w in weights]
        kernel = mine(taps[s].reshape(3, 3, width))
        last_mine, direct_mine, rates_mine = mine(last_w[s]), mine(direct[s]), mine(rates[s])

        def own_filter(a, b, c):
            return filter_taps(a, b, c, rates_mine, row_len)

        filter_rows, filter_back = jax.vjp(own_filter, first_w[s], second_w[s], last_mine)
        filt_cos, filt_sin = to_waves(filter_rows.astype(low))
        normed = (norm_stats(inputs)[0] * gains[s, 0] + shifts[s, 0]).astype(low)
        normed = ag(normed)
        projected = [mm(normed, w_in[:, g * chans : (g + 1) * chans]) for g in range(3)]
        streams = [
            (
                kernel[0, g] * projected[g]
                + kernel[1, g] * shifted(projected[g], 1)
                + kernel[2, g] * shifted(projected[g], 2)
            ).astype(low)
            for g in range(3)
        ]
        wide = [x.astype(f32) for x in streams]
        product = (wide[0] * wide[2] * row_mask).astype(low)
        prod_cos, prod_sin = to_waves(product)
        filtered = from_waves(
            prod_cos * filt_cos - prod_sin * filt_sin, prod_cos * filt_sin + prod_sin * filt_cos
        ) + direct_mine * product.astype(f32)
        gated = (wide[1] * filtered).astype(low)
        middle = inputs + mask * rs(mm(gated, w_out))
        second = (norm_stats(middle)[0] * gains[s, 1] + shifts[s, 1]).astype(low)
        second = ag(second)
        value, slope = gelu_both(mm(second, w_up))
        value = value.astype(low)
        slope = slope.astype(low)
        result = middle + mask * rs(mm(value, w_down))
        saved = (
            inputs, normed, projected, wide, product, prod_cos, prod_sin, filt_cos, filt_sin,
            filtered, gated, middle, second, value, slope, kernel, direct_mine, filter_back,
        )
        return result, saved

    def layer_backward(s, grad, saved):
        w_in, w_out, w_up, w_down = [w[s] for w in weights]
        (
            inputs, normed, projected, wide, product, prod_cos, prod_sin, filt_cos, filt_sin,
            filtered, gated, middle, second, value, slope, kernel, direct_mine, filter_back,
        ) = saved
        out_low = ag((grad * mask).astype(low))
        pre = (mm_t(out_low, w_down) * slope.astype(f32)).astype(low)
        grad_down = t_mm(value, out_low)
        grad_up = t_mm(second, pre)
        mid_part, gain_late, bias_late = norm_back(rs(mm_t(pre, w_up)), middle, gains[s, 1])
        middle_grad = grad + mid_part
        branch = ag((middle_grad * mask).astype(low))
        gated_grad = mm_t(branch, w_out).astype(low)
        grad_out = t_mm(gated, branch)
        gated_grad = gated_grad.astype(f32)
        filtered_grad = (gated_grad * wide[1]).astype(low)
        fg_cos, fg_sin = to_waves(filtered_grad)
        fg_wide = filtered_grad.astype(f32)
        prod32 = product.astype(f32)
        product_grad = from_waves(
            filt_cos * fg_cos + filt_sin * fg_sin, filt_cos * fg_sin - filt_sin * fg_cos
        ) + direct_mine * fg_wide
        product_grad = product_grad.astype(low).astype(f32)
        filter_grad = from_waves(
            prod_cos * fg_cos + prod_sin * fg_sin, prod_cos * fg_sin - prod_sin * fg_cos
        )
        grad_first, grad_second, grad_last = filter_back(filter_grad)
        grad_direct = jnp.sum(fg_wide * prod32, 0)
        mixed = [
            (product_grad * wide[2]).astype(low).astype(f32),
            (gated_grad * filtered).astype(low).astype(f32),
            (product_grad * wide[0]).astype(low).astype(f32),
        ]
        proj = [
            (
                kernel[0, g] * mixed[g]
                + kernel[1, g] * shifted(mixed[g], -1)
                + kernel[2, g] * shifted(mixed[g], -2)
            ).astype(low)
            for g in range(3)
        ]
        grad_taps = jnp.stack(
            [
                jnp.stack(
                    [jnp.sum(mixed[g] * (shifted(projected[g], k) if k else projected[g]), 0) for g in range(3)]
                )
                for k in range(3)
            ]
        )
        proj = jnp.concatenate(proj, 1)
        grad_in = t_mm(normed, proj)
        in_part, gain_early, bias_early = norm_back(rs(mm_t(proj, w_in)), inputs, gains[s, 0])
        small = (
            jnp.stack([gain_early, gain_late]),
            jnp.stack([bias_early, bias_late]),
            placed(grad_taps).reshape(3, 3 * width),
            grad_first,
            grad_second,
            placed(grad_last),
            placed(grad_direct),
        )
        large = (grad_in, grad_out, grad_up, grad_down)
        return middle_grad + in_part, small, large

    first_out, first_saved = layer_forward(0, own_tokens)
    second_out, second_saved = layer_forward(1, first_out)
    second_grad, second_small, second_large = layer_backward(1, own_cotangent, second_saved)
    first_grad, first_small, first_large = layer_backward(0, second_grad, first_saved)

    swap = [(0, 1), (1, 0)]

    def by_layer(first, second):
        other = lax.ppermute(jnp.where(own_layer_first, second, first), "section", swap)
        return jnp.where(
            own_layer_first, jnp.stack([first, other]), jnp.stack([other, second])
        )[None, :, None]

    def summed(first, second):
        stacked = jnp.stack([first, second]).astype(low)
        rows = first.shape[0] // dp_count
        stacked = stacked.reshape(2 * dp_count, rows, first.shape[1])
        return lax.psum_scatter(stacked, ("section", "dp"), scatter_dimension=0, tiled=True)[0]

    sums = [summed(a, b) for a, b in zip(first_large, second_large)]
    sum_in = unshare_columns(sums[0], 3).astype(f32)
    sum_out = sums[1].astype(f32)
    sum_up = unshare_columns(sums[2], 1).astype(f32)
    sum_down = sums[3].astype(f32)
    stacked = jax.tree.map(lambda a, b: jnp.stack([a, b]), first_small, second_small)
    small = lax.psum(stacked, ("section", "dp", "seq"))
    small = [lax.dynamic_slice_in_dim(x, section, 1, 0) for x in small]
    sum_gain, sum_bias, sum_taps, sum_first, sum_second, sum_last, sum_direct = small
    return (
        by_layer(first_out, second_out),
        by_layer(first_grad, second_grad),
        sum_gain,
        sum_bias,
        sum_in[None],
        sum_taps,
        sum_first,
        sum_second,
        sum_last,
        sum_direct,
        sum_out[None],
        sum_up[None],
        sum_down[None],
    )


def plane_device(
    tokens,
    cotangent,
    lengths,
    norm_gain,
    norm_bias,
    mixer_in,
    short_kernel,
    filter_first,
    filter_second,
    filter_last,
    filter_bias,
    decay_rates,
    mixer_out,
    up_weight,
    down_weight,
):
    section = lax.axis_index("section")
    seq_count = lax.axis_size("seq")
    dp_count = lax.axis_size("dp")
    row_len = tokens.shape[2] * seq_count
    lengths = jnp.transpose(lengths)
    short_kernel = jnp.transpose(short_kernel, (1, 0, 2))
    filter_first = jnp.transpose(filter_first, (1, 0, 2))

    def gathered(part):
        whole = lax.all_gather(part, ("section", "dp"))
        return whole.reshape(2, dp_count, *part.shape)

    tables = wave_tables(row_len)
    waves = jnp.asarray(tables)
    waves_back = jnp.asarray(np.ascontiguousarray(tables.T))
    embedding = jnp.asarray(np.pad(position_rows(row_len), ((0, 0), (0, 95))))

    weights = (
        mixer_in[0], mixer_out[0], up_weight[0], down_weight[0], norm_gain, norm_bias, short_kernel,
        filter_first, filter_second, filter_last, filter_bias, decay_rates,
    )
    (
        first_mixer_pack, first_ff_pack, cotangent_low, par, small, second_mixer_pack, ff_part,
        *outs,
    ) = mixer_forward(
        0, tokens, lengths, weights, waves, waves_back, (cotangent, embedding)
    )
    first_filter, second_filter, first_saved, outs = outs[:5], outs[5:10], outs[10:13], outs[13:]
    first_out, *first_kept, first_middle = outs
    second_ff_pack = gathered(ff_part)
    *second_kept, second_middle = mixer_forward(
        1, first_out, lengths, (par, small, second_mixer_pack, second_filter[0]), waves, waves_back,
        None,
    )
    first_kept, second_kept = [*first_kept, *first_filter], [*second_kept, *second_filter]
    second_ff, result_parts, own_part, middle_grad, late = ff_turn(
        1, cotangent, second_middle, par, lengths, second_ff_pack, cotangent_low
    )

    def mixer_back(s, grad, x, late, pack, kept, earlier):
        return mixer_backward(
            s, grad, x, par, small, embedding, late, lengths, pack, waves, waves_back, kept, earlier
        )

    second_mixer, second_vec, second_grad, second_ff = mixer_back(
        1, middle_grad, first_out, late, second_mixer_pack, second_kept, second_ff
    )
    first_ff, middle_grad, late, second_mixer = ff_backward(
        0, second_grad, first_middle, par, lengths, first_ff_pack, *first_saved, second_mixer
    )
    first_mixer, first_vec, first_grad, first_ff = mixer_back(
        0, middle_grad, tokens, late, first_mixer_pack, first_kept, first_ff
    )
    block_outputs, input_grads, *got = finish(
        first_vec, second_vec, first_mixer, second_mixer, first_ff, second_ff, first_grad,
        second_grad, result_parts, own_part, second_middle, first_out, lengths,
    )
    (
        block_outputs, input_grads, sum_in, sum_out, sum_up, sum_down, sum_gain, sum_bias, sum_taps,
        sum_first, sum_second, sum_last, sum_direct,
    ) = unpack(block_outputs, input_grads, got, filter_first.shape[::2])
    return (
        block_outputs[None, :, None],
        input_grads[None, :, None],
        sum_gain[None],
        sum_bias[None],
        sum_in[None],
        jnp.transpose(sum_taps, (1, 0, 2)),
        jnp.transpose(sum_first, (1, 0, 2)),
        sum_second[None],
        sum_last[None],
        sum_direct,
        sum_out[None],
        sum_up[None],
        sum_down[None],
    )


def solution(mesh):
    in_specs = (
        P(None, "dp", "seq", None),
        P(None, "dp", "seq", None),
        P(None, "dp"),
        P("section", None, None),
        P("section", None, None),
        P("section", ("dp", "seq"), None),
        P("section", None, None),
        P("section", None, None),
        P("section", None, None),
        P("section", None, None),
        P("section", None),
        P("section", None),
        P("section", ("dp", "seq"), None),
        P("section", ("dp", "seq"), None),
        P("section", ("dp", "seq"), None),
    )
    out_specs = (
        P("section", None, "dp", "seq", None),
        P("section", None, "dp", "seq", None),
        P("section", None, None),
        P("section", None, None),
        P("section", ("dp", "seq"), None),
        P("section", None, None),
        P("section", None, None),
        P("section", None, None),
        P("section", None, None),
        P("section", None),
        P("section", ("dp", "seq"), None),
        P("section", ("dp", "seq"), None),
        P("section", ("dp", "seq"), None),
    )
    planes = mesh.shape["seq"] == 4 and mesh.shape["dp"] == 4
    per_device = plane_device if planes else any_device
    return jax.shard_map(
        per_device, mesh=mesh, in_specs=in_specs, out_specs=out_specs, check_vma=False
    )
```

```python
from functools import partial
import math

import jax
import jax.numpy as jnp
import numpy as np
from jax import lax
from jax.experimental import pallas as pl
from jax.experimental.pallas import tpu as pltpu
from jax.sharding import PartitionSpec as P

precise = lax.Precision.HIGHEST
low = jnp.bfloat16
f32 = jnp.float32
MESH = pl.DeviceIdType.MESH


def dot(a, b, dims):
    return lax.dot_general(a, b, (dims, ((), ())), preferred_element_type=f32)


def mm(a, b):
    return dot(a, b, ((1,), (0,)))


def mm_t(a, b):
    return dot(a, b, ((1,), (1,)))


def t_mm(a, b):
    return dot(a, b, ((0,), (0,)))


def norm_stats(x):
    mean = jnp.mean(x, axis=-1, keepdims=True)
    centred = x - mean
    inverse = lax.rsqrt(jnp.mean(centred * centred, axis=-1, keepdims=True) + 1e-05)
    return centred * inverse, inverse


def norm_back(grad, x, gain):
    hat, inverse = norm_stats(x)
    scaled = grad * gain
    back = inverse * (
        scaled
        - jnp.mean(scaled, axis=-1, keepdims=True)
        - hat * jnp.mean(scaled * hat, axis=-1, keepdims=True)
    )
    return back, jnp.sum(grad * hat, 0), jnp.sum(grad, 0)


def gelu_both(x):
    scale = math.sqrt(2.0 / math.pi)
    inner = scale * (x + 0.044715 * x * x * x)
    bend = jnp.tanh(inner)
    value = 0.5 * x * (1.0 + bend)
    slope = 0.5 * (1.0 + bend) + 0.5 * x * (1.0 - bend * bend) * scale * (
        1.0 + 3.0 * 0.044715 * x * x
    )
    return value, slope


def position_table(length):
    offsets = jnp.arange(length, dtype=jnp.float32)
    frequencies = jnp.linspace(0.0001, 15.0, 16, dtype=jnp.float32)
    angles = 2.0 * math.pi * offsets[:, None] * frequencies[None, :] / length
    return jnp.concatenate(
        [offsets[:, None] / (length - 1), jnp.cos(angles), -jnp.sin(angles)], axis=1
    )


def position_rows(length):
    offsets = np.arange(length, dtype=np.float32)
    frequencies = np.linspace(0.0001, 15.0, 16, dtype=np.float32)
    angles = np.float32(2.0 * math.pi) * offsets[:, None] * frequencies[None, :] / np.float32(length)
    return np.concatenate(
        [offsets[:, None] / np.float32(length - 1), np.cos(angles), -np.sin(angles)], axis=1
    )


def filter_taps(first_w, second_w, last_w, rates, length):
    embedding = position_table(length)
    hidden = jnp.sin(jnp.dot(embedding, first_w, precision=precise))
    hidden = jnp.sin(jnp.dot(hidden, second_w, precision=precise))
    offsets = jnp.arange(length, dtype=jnp.float32)
    return jnp.dot(hidden, last_w, precision=precise) * jnp.exp(-offsets[:, None] * rates[None, :])


def wave_tables(length):
    turns = (2 * np.arange(length)[:, None] + 1) * np.arange(length)[None, :] % (4 * length)
    angles = turns * (math.pi / (2 * length))
    both = np.concatenate([np.cos(angles), np.sin(angles)], 0)
    return both.astype(jnp.bfloat16)


def shifted(x, by):
    if by > 0:
        return jnp.pad(x[:-by], ((by, 0), (0, 0)))
    return jnp.pad(x[-by:], ((0, -by), (0, 0)))


def neighbours(me):
    return (me + 1 - 2 * (me % 2), (me + 2) % 4, 3 - me)


def greet(devices):
    barrier = pltpu.get_barrier_semaphore()
    for device in devices:
        pl.semaphore_signal(barrier, inc=1, device_id=device, device_id_type=MESH)
    return len(devices)


def all_here(greeted):
    pl.semaphore_wait(pltpu.get_barrier_semaphore(), greeted)


def in_plane(peers):
    return [{"seq": peer} for peer in peers]


def along_planes():
    here = lax.axis_index("dp")
    return here, here + 1 - 2 * (here % 2), (here + 2) % 4


def other_core():
    return {"section": 1 - lax.axis_index("section")}


def plane_devices():
    _, near, far = along_planes()
    return [{"dp": near}, {"dp": far}]


def add_low(target, source):
    def add(at):
        target[at, :] = (target[at, :].astype(f32) + source[at, :].astype(f32)).astype(low)

    by_rows(target.shape[0], 32, add)


def swap_begin(pairs, core_sems):
    section = lax.axis_index("section")
    copies = [
        remote_to(made.at[1 - section], other, core_sems, at, other_core())
        for at, (made, other) in enumerate(pairs)
    ]
    for copy in copies:
        copy.start()
    return copies


def swap_end(copies, pairs):
    section = lax.axis_index("section")
    for copy, (made, other) in zip(copies, pairs):
        copy.wait_recv()
        for block in range(other.shape[0]):
            add_low(made.at[section, block], other.at[block])


class PlaneSum:
    def __init__(self, pack, mine, arrived, sems, load_sems):
        self.here, self.near, self.far = along_planes()
        self.pack, self.mine, self.arrived = pack, mine, arrived
        self.sems, self.load_sems = sems, load_sems

    def begin(self):
        self.sends = [
            remote_to(self.pack.at[block], self.arrived.at[slot], self.sems, slot, {"dp": self.near})
            for slot, block in enumerate(((self.near + 2) % 4, self.near))
        ]
        for copy in self.sends:
            copy.start()
        self.loads = fetch(
            [(self.pack.at[self.far], self.mine.at[0]), (self.pack.at[self.here], self.mine.at[1])],
            self.load_sems,
        )

    def forward(self):
        self.loads[0].wait()
        self.sends[0].wait_recv()
        add_low(self.mine.at[0], self.arrived.at[0])
        copy = remote_to(self.mine.at[0], self.arrived.at[2], self.sems, 2, {"dp": self.far})
        copy.start()
        self.sends.append(copy)

    def end(self, result):
        self.loads[1].wait()
        self.sends[1].wait_recv()
        self.sends[2].wait_recv()

        def add(at):
            total = self.mine[1, at, :].astype(f32)
            for slot in (1, 2):
                total = total + self.arrived[slot, at, :].astype(f32)
            result[at, :] = total.astype(low)

        by_rows(result.shape[0], 32, add)


def plane_sum_scratch(half_pack):
    _, rows, cols = half_pack.shape
    return [
        pltpu.VMEM((2, rows, cols), low),
        pltpu.VMEM((3, rows, cols), low),
        pltpu.SemaphoreType.DMA((2, 3)),
        pltpu.SemaphoreType.DMA((2,)),
    ]


def remote_to(source, target, sems, slot, device):
    return pltpu.make_async_remote_copy(
        src_ref=source,
        dst_ref=target,
        send_sem=sems.at[0, slot],
        recv_sem=sems.at[1, slot],
        device_id=device,
        device_id_type=MESH,
    )


def remote(source, target, sems, slot, peer):
    return remote_to(source, target, sems, slot, {"seq": peer})


def rows_of(index, count):
    return pl.ds(pl.multiple_of(index * count, count), count)


def half_of(ref, index, part, count):
    half = count // 2
    return ref.at[pl.ds(pl.multiple_of(index * count + part * half, half), half)]


def gather_begin(gather, sems, me, peers, count):
    x, y, _ = peers
    first, second = half_of(gather, me, 0, count), half_of(gather, me, 1, count)
    copies = [
        remote(first, first, sems, 0, x),
        remote(second, second, sems, 2, y),
        remote(second, second, sems, 1, x),
        remote(first, first, sems, 3, y),
    ]
    for copy in copies:
        copy.start()
    return copies


def gather_forward(gather, sems, peers, count):
    x, y, _ = peers
    from_x, from_y = half_of(gather, x, 0, count), half_of(gather, y, 1, count)
    remote(from_x, from_x, sems, 0, x).wait_recv()
    onward = remote(from_x, from_x, sems, 4, y)
    onward.start()
    remote(from_y, from_y, sems, 2, y).wait_recv()
    across = remote(from_y, from_y, sems, 5, x)
    across.start()
    return [onward, across]


def gather_wait(gather, sems, slot, peers, count):
    for part, at in (((1, 1),), ((0, 3),), ((0, 4), (1, 5)))[slot]:
        block = half_of(gather, peers[slot], part, count)
        remote(block, block, sems, at, peers[slot]).wait_recv()


HALF_ORDER = ((0, 0), (1, 1), (0, 1), (1, 0), (2, 0), (2, 1))


def half_rows(index, part, count):
    half = count // 2
    return pl.ds(pl.multiple_of(index * count + part * half, half), half)


def gather_wait_half(gather, sems, slot, part, peers, count):
    at = {(0, 1): 1, (1, 0): 3, (2, 0): 4, (2, 1): 5}.get((slot, part))
    if at is not None:
        block = half_of(gather, peers[slot], part, count)
        remote(block, block, sems, at, peers[slot]).wait_recv()


def reduce_send_half(slot, part, send, recv, sems, peers):
    half = send.shape[1] // 2
    quarter = half // 2
    plan = {
        (0, 0): [(0, half, 0, 0)],
        (1, 1): [(half, half, 1, 1)],
        (2, 0): [(0, quarter, 2, 0), (quarter, quarter, 3, 0)],
        (2, 1): [(half, quarter, 4, 1), (half + quarter, quarter, 5, 1)],
    }.get((slot, part), [])
    copies = [
        remote(
            send.at[slot, pl.ds(start, size)], recv.at[slot, pl.ds(start, size)], sems, at,
            peers[to],
        )
        for start, size, at, to in plan
    ]
    for copy in copies:
        copy.start()
    return copies


def reduce_send(slot, send, recv, sems, peers):
    x, y, _ = peers
    half = send.shape[1] // 2
    quarter = half // 2
    if slot == 2:
        plan = [(0, quarter, 2, x), (half, quarter, 4, y), (quarter, quarter, 3, x)]
        plan.append((half + quarter, quarter, 5, y))
    else:
        plan = [(slot * half, half, slot, (x, y)[slot])]
    copies = [
        remote(
            send.at[slot, pl.ds(start, size)], recv.at[slot, pl.ds(start, size)], sems, at, peer
        )
        for start, size, at, peer in plan
    ]
    for copy in copies:
        copy.start()
    return copies


def reduce_pass(send, recv, sems, peers):
    x, y, _ = peers
    half = send.shape[1] // 2
    quarter = half // 2
    copies = []
    for start, at, source, slot, peer in (
        (half, 4, y, 0, x),
        (0, 2, x, 1, y),
        (half + quarter, 5, y, 0, x),
        (quarter, 3, x, 1, y),
    ):
        rows = pl.ds(start, quarter)
        remote(send.at[2, rows], recv.at[2, rows], sems, at, source).wait_recv()
        add_low(send.at[slot, rows], recv.at[2, rows])
        copy = remote(send.at[slot, rows], recv.at[slot, rows], sems, at + 4, peer)
        copy.start()
        copies.append(copy)
    return copies


def reduce_wait(send, recv, sems, peers):
    x, y, _ = peers
    half = send.shape[1] // 2
    quarter = half // 2
    for slot, start, size, at, peer in (
        (0, 0, half, 0, x),
        (1, half, half, 1, y),
        (0, half, quarter, 8, x),
        (1, 0, quarter, 6, y),
        (0, half + quarter, quarter, 9, x),
        (1, quarter, quarter, 7, y),
    ):
        rows = pl.ds(start, size)
        remote(send.at[slot, rows], recv.at[slot, rows], sems, at, peer).wait_recv()


def by_rows(total, step, body):
    def run(i, carry):
        body(pl.ds(pl.multiple_of(i * step, step), step))
        return carry

    lax.fori_loop(0, total // step, run, 0)


def valid_rows(lengths, start, count):
    at = lax.broadcasted_iota(jnp.int32, (count, 1), 0) + start
    return (at < lengths[0, lax.axis_index("section")]).astype(f32)


def normed_rows(x, gain, shift):
    mean = jnp.mean(x, axis=-1, keepdims=True)
    centred = x - mean
    inverse = lax.rsqrt(jnp.mean(centred * centred, axis=-1, keepdims=True) + 1e-05)
    return centred * inverse * gain + shift


def norm_back_rows(grad, x, gain):
    mean = jnp.mean(x, axis=-1, keepdims=True)
    centred = x - mean
    inverse = lax.rsqrt(jnp.mean(centred * centred, axis=-1, keepdims=True) + 1e-05)
    hat = centred * inverse
    scaled = grad * gain
    back = inverse * (
        scaled
        - jnp.mean(scaled, axis=-1, keepdims=True)
        - hat * jnp.mean(scaled * hat, axis=-1, keepdims=True)
    )
    return back, jnp.sum(grad * hat, axis=0, keepdims=True), jnp.sum(grad, axis=0, keepdims=True)


def norm_into(gather, start, x, gain, shift):
    step = 32

    def body(i, carry):
        rows = pl.ds(pl.multiple_of(i * step, step), step)
        at = pl.ds(pl.multiple_of(start + i * step, step), step)
        gather[at, :] = normed_rows(x[rows, :].astype(f32), gain, shift).astype(low)
        return carry

    lax.fori_loop(0, x.shape[0] // step, body, 0)


def masked_into(gather, start, grad, lengths):
    step = 32

    def body(i, carry):
        rows = pl.ds(pl.multiple_of(i * step, step), step)
        at = pl.ds(pl.multiple_of(start + i * step, step), step)
        value = grad[rows, :].astype(f32) * valid_rows(lengths, start + i * step, step)
        gather[at, :] = value.astype(low)
        return carry

    lax.fori_loop(0, grad.shape[0] // step, body, 0)


def add_parts(own, recv, x, start, lengths):
    def body(rows):
        total = own[rows, :] + recv[0, rows, :].astype(f32) + recv[1, rows, :].astype(f32)
        mask = valid_rows(lengths, start + rows.start, 32)
        own[rows, :] = x[rows, :].astype(f32) + mask * total

    by_rows(own.shape[0], 32, body)


def norm_back_parts(own, recv, grad, x, gain, sums):
    sums[...] = jnp.zeros(sums.shape, f32)

    def body(rows):
        total = own[rows, :] + recv[0, rows, :].astype(f32) + recv[1, rows, :].astype(f32)
        back, gain_sum, shift_sum = norm_back_rows(total, x[rows, :].astype(f32), gain)
        own[rows, :] = grad[rows, :].astype(f32) + back
        sums[0:1, :] += gain_sum
        sums[1:2, :] += shift_sum

    by_rows(own.shape[0], 32, body)


def fetch(pairs, sems, first=0):
    copies = [
        pltpu.make_async_copy(source, target, sems.at[first + at])
        for at, (source, target) in enumerate(pairs)
    ]
    for copy in copies:
        copy.start()
    return copies


def weight_pairs_mixer(pack, win, wout):
    rows, cols = wout.shape[2], wout.shape[3] // 4
    split = win.shape[3]
    pairs = [(pack.at[:, :, :, pl.ds(0, split)], win)]
    for q in range(4):
        pairs.append(
            (
                pack.at[:, :, pl.ds(q * rows, rows), pl.ds(split, cols)],
                wout.at[:, :, :, pl.ds(q * cols, cols)],
            )
        )
    return pairs


def half_pairs_mixer(half_pack, win, wout):
    rows, cols = wout.shape[2], wout.shape[3] // 4
    split = win.shape[3]
    section = lax.axis_index("section")
    pairs = [(win.at[section], half_pack.at[:, :, pl.ds(0, split)])]
    for q in range(4):
        pairs.append(
            (
                wout.at[section, :, :, pl.ds(q * cols, cols)],
                half_pack.at[:, pl.ds(q * rows, rows), pl.ds(split, cols)],
            )
        )
    return pairs


class ChipGather:
    def __init__(self, own, pack, plane_sems, core_sems):
        self.section = lax.axis_index("section")
        here, near, far = along_planes()
        self.pack, self.plane_sems, self.core_sems = pack, plane_sems, core_sems
        self.near, self.far = near, far
        self.order = (here, near, far, (near + 2) % 4)
        self.own = own
        self.sends = []

    def move(self, at, sems, slot, device):
        block = self.pack.at[self.section, self.order[at]]
        copy = remote_to(self.own if at == 0 else block, block, sems, slot, device)
        copy.start()
        self.sends.append(copy)

    def to_core(self, slot):
        self.move(slot, self.core_sems, slot, other_core())

    def begin(self, load_sem):
        self.move(0, self.plane_sems, 1, {"dp": self.far})
        self.move(0, self.plane_sems, 0, {"dp": self.near})
        self.to_core(0)
        self.keep = pltpu.make_async_copy(
            self.own, self.pack.at[self.section, self.order[0]], load_sem
        )
        self.keep.start()

    def arrived(self, slot):
        block = self.pack.at[self.section, self.order[slot + 1]]
        remote_to(block, block, self.plane_sems, slot, {"dp": self.near}).wait_recv()

    def forward(self):
        self.arrived(1)
        self.move(2, self.plane_sems, 2, {"dp": self.near})
        self.to_core(2)
        self.arrived(0)
        self.to_core(1)

    def end(self):
        self.arrived(2)
        self.to_core(3)
        self.keep.wait()
        for slot in range(4):
            block = self.pack.at[1 - self.section, self.order[slot]]
            remote_to(block, block, self.core_sems, slot, other_core()).wait_recv()


def sine_pair(x):
    turns = jnp.floor(x * (2.0 / math.pi) + 0.5)
    rest = x - turns * 1.5703125
    rest = rest - turns * 4.837512969970703125e-4
    rest = rest - turns * 7.54978995489188e-8
    square = rest * rest
    sine = -1.9515295891e-4 * square + 8.3321608736e-3
    sine = (sine * square - 1.6666654611e-1) * square * rest + rest
    cosine = 2.443315711809948e-5 * square - 1.388731625493765e-3
    cosine = (cosine * square + 4.166664568298827e-2) * square * square - 0.5 * square + 1.0
    halves = jnp.floor(turns * 0.5)
    odd = turns - 2.0 * halves
    back = halves - 2.0 * jnp.floor(halves * 0.5)
    swapped = odd > 0.5
    side = 1.0 - 2.0 * back
    wave = jnp.where(swapped, cosine, sine) * side
    slope = jnp.where(swapped, -sine, cosine) * side
    return wave, slope


def network_rows(small, embedding, network, taps_low, i):
    step = 256
    waves1, waves2, steep1, steep2 = network
    knots = waves1.shape[1]
    pair = (pl.ds(i * step, step), pl.ds(embedding.shape[0] // 2 + i * step, step))

    def layer(sources, weights, waves, steep):
        inner = jnp.concatenate([dot_exact(item, weights) for item in sources], 1)
        wave, slope = sine_pair(inner)
        for at, rows in enumerate(pair):
            cols = slice(at * knots, (at + 1) * knots)
            waves[rows, :] = wave[:, cols]
            steep[rows, :] = slope[:, cols]

    layer([embedding[rows, 0:64] for rows in pair], small[64:128, 128:192], waves1, steep1)
    layer([waves1[rows, :] for rows in pair], small[64:128, 0:64], waves2, steep2)
    for rows in pair:
        times = lax.broadcasted_iota(jnp.int32, (step, 1), 0) + rows.start
        fade = jnp.exp(-times.astype(f32) * small[154:155, :])
        taps_low[rows, :] = (dot_exact(waves2[rows, :], small[0:64, :]) * fade).astype(low)


def ff_blocks(
    gather, wup, wdown, value, slope, result_out, send, recv, gather_sems, reduce_sems, me, peers,
    pause,
):
    count, width = result_out.shape
    half = wup.shape[3]
    sends = []
    for slot, part in ((None, None), *HALF_ORDER):
        if slot is None:
            rows, sent = rows_of(me, count), None
        else:
            rows = half_rows(peers[slot], part, count)
            sent = slice(part * count // 2, (part + 1) * count // 2)
            gather_wait_half(gather, gather_sems, slot, part, peers, count)

        def hidden(i, carry):
            cols = pl.ds(pl.multiple_of(i * 256, 256), 256)
            for h in range(2):
                pre = mm(gather[rows, :], wup[h, :, :, cols].reshape(width, 256))
                after, steep = gelu_both(pre)
                at = pl.ds(pl.multiple_of(h * half + i * 256, 256), 256)
                value[rows, at] = after.astype(low)
                slope[rows, at] = steep.astype(low)
            return carry

        lax.fori_loop(0, half // 256, hidden, 0)
        for h in range(2):
            cols = slice(h * width // 2, (h + 1) * width // 2)
            out = mm(value[rows, :], wdown[h].reshape(2 * half, width // 2))
            if slot is None:
                result_out[:, cols] = out
            else:
                send[slot, sent, cols] = out.astype(low)
        if slot is not None:
            sends += reduce_send_half(slot, part, send, recv, reduce_sems, peers)
            pause(slot, part)
    return sends


def mixer_forward_kernel(
    s, gathers, x, *refs
):
    if gathers:
        (
            cotangent, embedding, lengths, w_in, w_out, w_up, w_down, gain, shift, tap_rows, first_w,
            second_w, last_w, direct, rates, waves_hbm, back_hbm,
            pack_out, ff_out, late_out, par_out, small_out, next_pack_out, ff_part_out,
            *refs,
        ) = refs
        network_outs, next_outs, refs = refs[:5], refs[5:10], refs[10:]
        second_out, value_out, slope_out, result_out, *refs = refs
        (
            *refs, waves1, waves2, steep1, steep2, taps_low, raw_out, ff_all, late, next_pack, core_sems,
            plane_sems, out_core_sems, out_plane_sems, ff_core_sems, ff_plane_sems, next_core_sems, next_plane_sems, late_sems,
            pack_sems, mixer_parts, ff_parts, par_all, small_all, stage_in, stage_out, stage_up,
            in_sems, out_sems, up_sems, down_sems, par_sems, small_sems,
            second, ff_send, ff_recv, second_sems, ff_sems, network_sems,
        ) = refs
        x = x.at[lax.axis_index("section"), 0]
        cotangent = cotangent.at[lax.axis_index("section"), 0]
        network = (waves1, waves2, steep1, steep2)
    else:
        par_all, small_all, lengths, weights_hbm, filt_hbm, waves_hbm, back_hbm, *refs = refs
    (
        normed_out, proj_out, stream_out, prod_out, spec_out, filtered_out, gated_out, middle_out,
        gather, win, wout, filt, waves, back, proj, proj_low, streams, prod, spec, mixed, filtered,
        gated, send, recv, gather_sems, reduce_sems, load_sems, store_sems,
    ) = refs
    par, small = par_all.at[s], small_all.at[s]
    me = lax.axis_index("seq")
    peers = neighbours(me)
    count, width = x.shape
    length = gather.shape[0]
    chans = prod.shape[1]
    half = win.shape[3]
    if gathers:
        section = lax.axis_index("section")
        targets = shuffle_targets(section, me, peers)
        greeted = greet([device for _, _, device in targets] + plane_devices())
    else:
        greeted = greet(in_plane(peers[:2]))
    tables = fetch([(waves_hbm, waves), (back_hbm, back)], load_sems)
    sends = []
    if gathers:
        shuffle_stage(w_in, w_out, w_up, stage_in, stage_out, stage_up)
        parameters_stage(
            me, par_all.at[section], small_all.at[section], gain, shift, tap_rows, first_w, second_w,
            last_w, direct, rates,
        )
        all_here(greeted)
        sends += shuffle_send(
            section, me, targets, (stage_in, stage_out, stage_up, w_down), (mixer_parts, ff_parts),
            (par_all, small_all), (in_sems, out_sems, up_sems, down_sems, par_sems, small_sems),
        )
        in_cols, out_cols = pl.ds(0, half), pl.ds(half, raw_out.shape[3])
        in_pack = ChipGather(mixer_parts.at[0, :, in_cols], win, plane_sems, core_sems)
        out_pack = ChipGather(mixer_parts.at[0, :, out_cols], raw_out, out_plane_sems, out_core_sems)
        ff_pack = ChipGather(ff_parts.at[0], ff_all, ff_plane_sems, ff_core_sems)
        for sems, item in ((par_sems, par_all), (small_sems, small_all)):
            block = item.at[1 - section]
            remote_to(block, block, sems, 0, other_core()).wait_recv()
        norm_into(gather, me * count, x, par[0:1, :], par[1:2, :])
        shuffle_wait_mixer(section, me, targets, mixer_parts, stage_in, in_sems, out_sems)
        in_pack.begin(pack_sems.at[0])
        sends += gather_begin(gather, gather_sems, me, peers, count)
        masked_into(late, me * count, cotangent, lengths)
    else:
        weights = fetch(weight_pairs_mixer(weights_hbm, win, wout), load_sems, 2)
        filt_load = fetch([(filt_hbm, filt)], load_sems, 7)
        norm_into(gather, me * count, x, par[0:1, :], par[1:2, :])
        all_here(greeted)
        sends += gather_begin(gather, gather_sems, me, peers, count)
    proj[0:8, :] = jnp.zeros((8, proj.shape[1]), f32)
    tile_rows = 256

    def filter_spectrum(i, carry):
        rows = pl.ds(pl.multiple_of(i * tile_rows, tile_rows), tile_rows)
        filt[rows, :] = mm(waves[rows, :], taps_low[...])
        return carry

    stores = []
    if gathers:
        network_rows(small, embedding, network, taps_low, 0)
    sends += gather_forward(gather, gather_sems, peers, count)
    if gathers:
        sends += gather_begin(late, late_sems, me, peers, count)
        in_pack.forward()
        out_pack.begin(pack_sems.at[13])
        network_rows(small, embedding, network, taps_low, 1)
        tables[0].wait()
        lax.fori_loop(0, 2 * length // tile_rows, filter_spectrum, 0)
        network_stores = fetch(list(zip((filt, *network), network_outs)), network_sems)
        out_pack.forward()
        shuffle_wait_ff(section, me, targets, ff_parts, stage_up, up_sems, down_sems)
        ff_pack.begin(pack_sems.at[1])
        in_pack.end()
        stores += fetch(
            [
                (win, pack_out.at[:, :, :, in_cols]),
                (par_all, par_out),
                (small_all, small_out),
                (ff_parts.at[1], ff_part_out),
            ],
            pack_sems,
            4,
        )
    else:
        tables[0].wait()
    if not gathers:
        weights[0].wait()
    step = 64
    steps = count // step

    def short_conv(start):
        for g in range(3):
            cols = slice(g * chans, (g + 1) * chans)
            tile = proj[pl.ds(start, step + 8), cols]
            proj_low[pl.ds(start, step), cols] = tile[8:].astype(low)
            value = (
                small[144 + 3 * g : 145 + 3 * g, :] * tile[8:]
                + small[145 + 3 * g : 146 + 3 * g, :] * pltpu.roll(tile, 1, 0)[8:]
                + small[146 + 3 * g : 147 + 3 * g, :] * pltpu.roll(tile, 2, 0)[8:]
            )
            streams[pl.ds(start, step), cols] = value.astype(low)
        first = streams[pl.ds(start, step), 0:chans].astype(f32)
        third = streams[pl.ds(start, step), 2 * chans : 3 * chans].astype(f32)
        prod[pl.ds(start, step), :] = (first * third * valid_rows(lengths, start, step)).astype(low)

    def within(source):
        def body(i, carry):
            short_conv(pl.multiple_of(source * count + i * step, step))
            return carry

        lax.fori_loop(1, steps, body, 0)

    for slot in (None, 0, 1, 2):
        source = me if slot is None else peers[slot]
        if slot is not None:
            gather_wait(gather, gather_sems, slot, peers, count)
        block = gather[rows_of(source, count), :]
        for h in range(2):
            proj[pl.ds(pl.multiple_of(source * count + 8, 8), count), h * half : (h + 1) * half] = mm(
                block, win[h].reshape(width, half)
            )
        within(source)
    if gathers:
        sends += gather_forward(late, late_sems, peers, count)

    def seams(i, carry):
        short_conv(pl.multiple_of(i * count, step))
        return carry

    lax.fori_loop(0, length // count, seams, 0)
    stores += fetch(
        [(gather, normed_out), (proj_low, proj_out), (streams, stream_out), (prod, prod_out)],
        store_sems,
    )
    if not gathers:
        filt_load[0].wait()

    def spectrum(i, carry):
        up = pl.ds(pl.multiple_of(i * tile_rows, tile_rows), tile_rows)
        down = pl.ds(pl.multiple_of(i * tile_rows + length, tile_rows), tile_rows)
        prod_cos = mm(waves[up, :], prod[...])
        prod_sin = mm(waves[down, :], prod[...])
        filt_cos, filt_sin = filt[up, :], filt[down, :]
        spec[up, :] = prod_cos.astype(low)
        spec[down, :] = prod_sin.astype(low)
        mixed[up, :] = (prod_cos * filt_cos - prod_sin * filt_sin).astype(low)
        mixed[down, :] = (prod_cos * filt_sin + prod_sin * filt_cos).astype(low)
        return carry

    lax.fori_loop(0, length // tile_rows, spectrum, 0)
    tables[1].wait()
    if gathers:
        out_pack.end()
        cols = raw_out.shape[3]
        weights = fetch(
            [
                (
                    raw_out.at[:, :, pl.ds(q * wout.shape[2], wout.shape[2]), :],
                    wout.at[:, :, :, pl.ds(q * cols, cols)],
                )
                for q in range(4)
            ],
            load_sems,
            3,
        )
        stores += fetch([(raw_out, pack_out.at[:, :, :, out_cols])], pack_sems, 14)
        for load in weights:
            load.wait()
    else:
        for load in weights[1:]:
            load.wait()
    for slot in (2, 0, 1, None):
        target = me if slot is None else peers[slot]
        rows = rows_of(target, count)
        value = mm(back[rows, :], mixed[...]) * (1.0 / length)
        value = value + small[153:154, :] * prod[rows, :].astype(f32)
        filtered[rows, :] = value
        gate = (streams[rows, chans : 2 * chans].astype(f32) * value).astype(low)
        gated[rows, :] = gate
        outs = [mm(gate, wout[h].reshape(chans, width // 2)) for h in range(2)]
        for h in range(2):
            cols = slice(h * width // 2, (h + 1) * width // 2)
            if slot is None:
                middle_out[:, cols] = outs[h]
            else:
                send[slot, :, cols] = outs[h].astype(low)
        if slot is not None:
            sends += reduce_send(slot, send, recv, reduce_sems, peers)
    if gathers:
        ff_pack.forward()
        for slot in range(3):
            gather_wait(late, late_sems, slot, peers, count)
        stores += fetch([(late, late_out)], pack_sems, 2)
    sends += reduce_pass(send, recv, reduce_sems, peers)
    stores += fetch(
        [(spec, spec_out), (filtered, filtered_out), (gated, gated_out)],
        store_sems,
        4,
    )
    if gathers:
        for store in network_stores:
            store.wait()
        for i in range(2):
            network_rows(small_all.at[1], embedding, network, taps_low, i)
        lax.fori_loop(0, 2 * length // tile_rows, filter_spectrum, 0)
        network_stores = fetch(list(zip((filt, *network), next_outs)), network_sems)
    reduce_wait(send, recv, reduce_sems, peers)
    add_parts(middle_out, recv, x, me * count, lengths)
    if gathers:
        next_mixer = ChipGather(mixer_parts.at[1], next_pack, next_plane_sems, next_core_sems)
        norm_into(second, me * count, middle_out, par[2:3, :], par[3:4, :])
        sends += gather_begin(second, second_sems, me, peers, count)
        sends += gather_forward(second, second_sems, peers, count)
        ff_pack.end()
        next_mixer.begin(pack_sems.at[8])
        stores += fetch([(ff_all, ff_out)], pack_sems, 3)
        rows_up = ff_all.shape[2] // 2
        value, slope = waves.at[pl.ds(0, length)], waves.at[pl.ds(length, length)]

        def pause(slot, part):
            if (slot, part) == (1, 1):
                next_mixer.forward()

        sends += ff_blocks(
            second, ff_all.at[:, :, pl.ds(0, rows_up)], ff_all.at[:, :, pl.ds(rows_up, rows_up)],
            value, slope, result_out, ff_send, ff_recv, second_sems, ff_sems, me, peers, pause,
        )
        sends += reduce_pass(ff_send, ff_recv, ff_sems, peers)
        stores += fetch([(second, second_out), (value, value_out), (slope, slope_out)], pack_sems, 9)
        next_mixer.end()
        stores += fetch([(next_pack, next_pack_out)], pack_sems, 12)
        reduce_wait(ff_send, ff_recv, ff_sems, peers)
        add_parts(result_out, ff_recv, middle_out, me * count, lengths)
        sends += in_pack.sends + out_pack.sends + ff_pack.sends + next_mixer.sends
        stores += network_stores
    for copy in sends:
        copy.wait_send()
    for store in stores:
        store.wait()


def ff_turn_kernel(
    s, cotangent, x, par_all, lengths, pack, late_hbm,
    half_out, value_out, middle_grad_out, sums_out,
    gather, late, wup, wdown, value, pre, wgrad, other, send_back, recv_back,
    gather_sems, back_sems, load_sems, store_sems, core_sems,
):
    par = par_all.at[s]
    grad = cotangent.at[lax.axis_index("section"), 0]
    me = lax.axis_index("seq")
    peers = neighbours(me)
    count, width = x.shape
    half = wup.shape[3]
    rows_up = wup.shape[2]
    greeted = greet(in_plane(peers[:2]) + [other_core()])
    loads = fetch(
        [
            (pack.at[:, :, pl.ds(0, rows_up), :], wup),
            (pack.at[:, :, pl.ds(rows_up, wdown.shape[2]), :], wdown),
            (late_hbm, late),
        ],
        load_sems,
    )
    norm_into(gather, me * count, x, par[2:3, :], par[3:4, :])
    all_here(greeted)
    sends = gather_begin(gather, gather_sems, me, peers, count)
    for load in loads:
        load.wait()
    for slot, part in ((None, None), *HALF_ORDER):
        if slot is None:
            rows, sent = rows_of(me, count), None
        else:
            rows = half_rows(peers[slot], part, count)
            sent = slice(part * count // 2, (part + 1) * count // 2)
            gather_wait_half(gather, gather_sems, slot, part, peers, count)

        def hidden(i, carry):
            cols = pl.ds(pl.multiple_of(i * rows_up, rows_up), rows_up)
            for h in range(2):
                block = h * (half // rows_up) + i
                at = pl.ds(pl.multiple_of(block * rows_up, rows_up), rows_up)
                after, steep = gelu_both(
                    mm(gather[rows, :], wup[h, :, :, cols].reshape(width, rows_up))
                )
                value[rows, at] = after.astype(low)
                back = mm_t(late[rows, : width // 2], wdown[0, block]) + mm_t(
                    late[rows, width // 2 :], wdown[1, block]
                )
                pre[rows, at] = (back * steep).astype(low)
            return carry

        lax.fori_loop(0, half // rows_up, hidden, 0)

        def through(i, carry):
            cols = pl.ds(pl.multiple_of(i * rows_up, rows_up), rows_up)
            back = mm_t(pre[rows, :half], wup[0, i]) + mm_t(pre[rows, half:], wup[1, i])
            if slot is None:
                middle_grad_out[:, cols] = back
            else:
                send_back[slot, sent, cols] = back.astype(low)
            return carry

        lax.fori_loop(0, width // rows_up, through, 0)
        if slot is None:
            sends += gather_forward(gather, gather_sems, peers, count)
        else:
            sends += reduce_send_half(slot, part, send_back, recv_back, back_sems, peers)
    sends += reduce_pass(send_back, recv_back, back_sems, peers)
    stores = fetch([(value, value_out)], store_sems, 1)

    def weights(i, carry):
        cols = pl.ds(pl.multiple_of(i * rows_up, rows_up), rows_up)
        for h in range(2):
            wgrad[h, i, 0:rows_up, :] = t_mm(
                gather[:, cols], pre[:, h * half : (h + 1) * half]
            ).astype(low)
            wgrad[h, i, rows_up : 2 * rows_up, :] = t_mm(
                value[:, cols], late[:, h * width // 2 : (h + 1) * width // 2]
            ).astype(low)
        return carry

    lax.fori_loop(0, width // rows_up, weights, 0)
    swapped = [(wgrad, other)]
    swaps = swap_begin(swapped, core_sems)
    sends += swaps
    reduce_wait(send_back, recv_back, back_sems, peers)
    norm_back_parts(middle_grad_out, recv_back, grad, x, par[2:3, :], sums_out)
    swap_end(swaps, swapped)
    stores += fetch([(wgrad.at[lax.axis_index("section")], half_out)], store_sems)
    for copy in sends:
        copy.wait_send()
    for store in stores:
        store.wait()


def ff_backward_kernel(
    s, grad, middle, par_all, lengths, pack, second_hbm, value_hbm, slope_hbm, earlier,
    half_out, middle_grad_out, sums_out, summed,
    gather, wup, wdown, second, value, slope, pre, wgrad, other, send, recv, gather_sems,
    reduce_sems, load_sems, store_sems, mine, arrived, plane_sems, sum_sems, core_sems,
):
    par = par_all.at[s]
    me = lax.axis_index("seq")
    peers = neighbours(me)
    count, width = grad.shape
    greeted = greet(in_plane(peers[:2]) + plane_devices() + [other_core()])
    half = wup.shape[3]
    units = 2 * half
    up_rows = wup.shape[2]
    loads = fetch(
        [
            (pack.at[:, :, pl.ds(0, up_rows), :], wup),
            (pack.at[:, :, pl.ds(up_rows, wdown.shape[2]), :], wdown),
            (slope_hbm, slope),
            (second_hbm, second),
            (value_hbm, value),
        ],
        load_sems,
    )
    masked_into(gather, me * count, grad, lengths)
    all_here(greeted)
    sends = gather_begin(gather, gather_sems, me, peers, count)
    plane_sum = PlaneSum(earlier, mine, arrived, plane_sems, sum_sems)
    plane_sum.begin()
    for load in loads[:3]:
        load.wait()
    for slot, part in ((None, None), *HALF_ORDER):
        if slot is None:
            rows, sent = rows_of(me, count), None
        else:
            rows = half_rows(peers[slot], part, count)
            sent = slice(part * count // 2, (part + 1) * count // 2)
            gather_wait_half(gather, gather_sems, slot, part, peers, count)

        def hidden(i, carry):
            cols = pl.ds(pl.multiple_of(i * up_rows, up_rows), up_rows)
            back = mm_t(gather[rows, : width // 2], wdown[0, i]) + mm_t(
                gather[rows, width // 2 :], wdown[1, i]
            )
            pre[rows, cols] = (back * slope[rows, cols].astype(f32)).astype(low)
            return carry

        lax.fori_loop(0, units // up_rows, hidden, 0)

        def through(i, carry):
            cols = pl.ds(pl.multiple_of(i * up_rows, up_rows), up_rows)
            back = mm_t(pre[rows, :half], wup[0, i]) + mm_t(pre[rows, half:], wup[1, i])
            if slot is None:
                middle_grad_out[:, cols] = back
            else:
                send[slot, sent, cols] = back.astype(low)
            return carry

        lax.fori_loop(0, width // up_rows, through, 0)
        if slot is None:
            sends += gather_forward(gather, gather_sems, peers, count)
        else:
            sends += reduce_send_half(slot, part, send, recv, reduce_sems, peers)
    plane_sum.forward()
    for load in loads[3:]:
        load.wait()

    def weights(i, carry):
        cols = pl.ds(pl.multiple_of(i * up_rows, up_rows), up_rows)
        for h in range(2):
            wgrad[h, i, 0:up_rows, :] = t_mm(
                second[:, cols], pre[:, h * half : (h + 1) * half]
            ).astype(low)
            wgrad[h, i, up_rows : 2 * up_rows, :] = t_mm(
                value[:, cols], gather[:, h * width // 2 : (h + 1) * width // 2]
            ).astype(low)
        return carry

    lax.fori_loop(0, width // up_rows, weights, 0)
    swapped = [(wgrad, other)]
    swaps = swap_begin(swapped, core_sems)
    sends += swaps
    sends += reduce_pass(send, recv, reduce_sems, peers)
    swap_end(swaps, swapped)
    stores = fetch([(wgrad.at[lax.axis_index("section")], half_out)], store_sems)
    plane_sum.end(summed)
    sends += plane_sum.sends
    reduce_wait(send, recv, reduce_sems, peers)
    norm_back_parts(middle_grad_out, recv, grad, middle, par[2:3, :], sums_out)
    for copy in sends:
        copy.wait_send()
    for store in stores:
        store.wait()


def t_mm_exact(a, b):
    return lax.dot_general(
        a, b, (((0,), (0,)), ((), ())), preferred_element_type=f32, precision=precise
    )


def mm_t_exact(a, b):
    return lax.dot_general(
        a, b, (((1,), (1,)), ((), ())), preferred_element_type=f32, precision=precise
    )


def dot_exact(a, b):
    return jnp.dot(a, b, preferred_element_type=f32, precision=precise)


def by_layer(begin, triples, layer_sems, keep_sems, base=0):
    section = lax.axis_index("section")
    for index in range(2):

        @pl.when(section == index)
        def _():
            for at, (first, second, target) in enumerate(triples, base):
                kept, sent = (first, second) if index == 0 else (second, first)
                slot = target.at[index]
                copies = (
                    pltpu.make_async_copy(kept, slot, keep_sems.at[at]),
                    remote_to(sent, slot, layer_sems, at, other_core()),
                )
                for copy in copies:
                    if begin:
                        copy.start()
                    else:
                        copy.wait()


def mixer_backward_kernel(
    s, grad, x, par_all, small_all, embedding, late, lengths, pack, filt_hbm, waves_hbm, back_hbm, normed_hbm, proj_hbm,
    stream_hbm, prod_hbm, spec_hbm, filtered_hbm, gated_hbm, waves1_hbm, waves2_hbm, steep1_hbm,
    steep2_hbm, earlier,
    half_out, small_out, input_grad_out, summed,
    gather, win, wout, filt, waves, back, normed, proj, streams, prod, spec, filtered, gated,
    gated_grad, filtered_grad, both, grad_spec, grad_sum, filter_grad, mixed, proj_grad, wgrad_in, wgrad_out_part,
    other_in, other_out, waves1, waves2, steep1, steep2, sums, taps_sum, send, recv, gather_sems, reduce_sems, load_sems, store_sems,
    mine, arrived, plane_sems, sum_sems, core_sems,
):
    par, small = par_all.at[s], small_all.at[s]
    me = lax.axis_index("seq")
    peers = neighbours(me)
    if s == 0:
        x = x.at[lax.axis_index("section"), 0]
    count, width = grad.shape
    greeted = greet(in_plane(peers[:2]) + plane_devices() + [other_core()])
    length = gather.shape[0]
    chans = prod.shape[1]
    half = win.shape[3]
    depth = win.shape[2]
    loads = fetch(
        weight_pairs_mixer(pack, win, wout)
        + [
            (stream_hbm, streams),
            (waves_hbm, waves),
            (filt_hbm, filt),
            (spec_hbm, spec),
            (back_hbm, back),
            (prod_hbm, prod),
            (filtered_hbm, filtered),
            (proj_hbm, proj),
            (normed_hbm, normed),
            (gated_hbm, gated),
            (waves1_hbm, waves1),
            (waves2_hbm, waves2),
            (steep1_hbm, steep1),
            (steep2_hbm, steep2),
        ],
        load_sems,
    )
    masked_into(gather, me * count, grad, lengths)
    all_here(greeted)
    sends = gather_begin(gather, gather_sems, me, peers, count)
    plane_sum = PlaneSum(earlier, mine, arrived, plane_sems, sum_sems)
    plane_sum.begin()
    for load in loads[1:6]:
        load.wait()
    tile_rows = 256
    for slot in (None, 0, 1, 2):
        source = me if slot is None else peers[slot]
        rows = rows_of(source, count)
        if slot is not None:
            gather_wait(gather, gather_sems, slot, peers, count)
        value = (
            mm_t(gather[rows, : width // 2], wout[0].reshape(chans, width // 2))
            + mm_t(gather[rows, width // 2 :], wout[1].reshape(chans, width // 2))
        ).astype(low)
        gated_grad[rows, :] = value
        filtered_grad[rows, :] = (
            value.astype(f32) * streams[rows, chans : 2 * chans].astype(f32)
        ).astype(low)
        if slot is None:
            sends += gather_forward(gather, gather_sems, peers, count)
            for load in loads[6:]:
                load.wait()
            loads[0].wait()
        if slot == 2:
            plane_sum.forward()

        def spectrum(i, carry):
            up = pl.ds(pl.multiple_of(i * tile_rows, tile_rows), tile_rows)
            down = pl.ds(pl.multiple_of(i * tile_rows + length, tile_rows), tile_rows)
            fg_cos = mm(waves[up, rows], filtered_grad[rows, :])
            fg_sin = mm(waves[down, rows], filtered_grad[rows, :])
            if slot is not None:
                fg_cos = fg_cos + grad_sum[up, :]
                fg_sin = fg_sin + grad_sum[down, :]
            if slot != 2:
                grad_sum[up, :] = fg_cos
                grad_sum[down, :] = fg_sin
            else:
                filt_cos, filt_sin = filt[up, :], filt[down, :]
                grad_spec[up, :] = fg_cos.astype(low)
                grad_spec[down, :] = fg_sin.astype(low)
                both[up, :] = (filt_cos * fg_cos + filt_sin * fg_sin).astype(low)
                both[down, :] = (filt_cos * fg_sin - filt_sin * fg_cos).astype(low)
            return carry

        lax.fori_loop(0, length // tile_rows, spectrum, 0)
    mixed[pl.ds(length, 8), :] = jnp.zeros((8, mixed.shape[1]), f32)

    def streams_back(i, carry):
        rows = pl.ds(pl.multiple_of(i * tile_rows, tile_rows), tile_rows)
        value = mm(back[rows, :], both[...]) * (1.0 / length)
        fg = filtered_grad[rows, :].astype(f32)
        prod_grad = (value + small[153:154, :] * fg).astype(low).astype(f32)
        mixed[rows, 0:chans] = (
            (prod_grad * streams[rows, 2 * chans : 3 * chans].astype(f32)).astype(low).astype(f32)
        )
        mixed[rows, chans : 2 * chans] = (
            (gated_grad[rows, :].astype(f32) * filtered[rows, :]).astype(low).astype(f32)
        )
        mixed[rows, 2 * chans : 3 * chans] = (
            (prod_grad * streams[rows, 0:chans].astype(f32)).astype(low).astype(f32)
        )
        return carry + jnp.sum(fg * prod[rows, :].astype(f32), axis=0, keepdims=True)

    small_out[...] = jnp.zeros(small_out.shape, f32)
    small_out[153:154, :] = lax.fori_loop(
        0, length // tile_rows, streams_back, jnp.zeros((1, chans), f32)
    )
    step = 128
    for slot in (2, 0, 1, None):
        target = me if slot is None else peers[slot]

        def short_back(i, carry):
            start = pl.multiple_of(target * count + i * step, step)
            for g in range(3):
                cols = slice(g * chans, (g + 1) * chans)
                tile = mixed[pl.ds(start, step + 8), cols]
                now = tile[:step]
                after = pltpu.roll(tile, step + 7, 0)[:step]
                later = pltpu.roll(tile, step + 6, 0)[:step]
                proj_grad[pl.ds(start, step), cols] = (
                    small[144 + 3 * g : 145 + 3 * g, :] * now
                    + small[145 + 3 * g : 146 + 3 * g, :] * after
                    + small[146 + 3 * g : 147 + 3 * g, :] * later
                ).astype(low)
            return carry

        lax.fori_loop(0, count // step, short_back, 0)
        rows = rows_of(target, count)

        def through(i, carry):
            cols = pl.ds(pl.multiple_of(i * depth, depth), depth)
            value = mm_t(proj_grad[rows, :half], win[0, i]) + mm_t(proj_grad[rows, half:], win[1, i])
            if slot is None:
                input_grad_out[:, cols] = value
            else:
                send[slot, :, cols] = value.astype(low)
            return carry

        lax.fori_loop(0, width // depth, through, 0)
        if slot is not None:
            sends += reduce_send(slot, send, recv, reduce_sems, peers)

    def weights(i, carry):
        cols = pl.ds(pl.multiple_of(i * depth, depth), depth)
        for h in range(2):
            wgrad_in[h, i] = t_mm(normed[:, cols], proj_grad[:, h * half : (h + 1) * half]).astype(
                low
            )
        return carry

    lax.fori_loop(0, width // depth, weights, 0)
    for h in range(2):
        value = t_mm(gated[...], gather[:, h * width // 2 : (h + 1) * width // 2]).astype(low)
        wgrad_out_part[h] = value.reshape(wgrad_out_part.shape[1:])
    swapped = [(wgrad_in, other_in), (wgrad_out_part, other_out)]
    swaps = swap_begin(swapped, core_sems)
    sends += swaps
    sends += reduce_pass(send, recv, reduce_sems, peers)
    taps_sum[...] = jnp.zeros(taps_sum.shape, f32)

    def tap_sums(i, carry):
        start = pl.multiple_of(i * step, step)
        for g in range(3):
            cols = slice(g * chans, (g + 1) * chans)
            tile = mixed[pl.ds(start, step + 8), cols]
            seen = proj[pl.ds(start, step), cols].astype(f32)
            for at in range(3):
                shift = pltpu.roll(tile, step + 8 - at, 0)[:step] if at else tile[:step]
                taps_sum[8 * at : 8 * at + 8, cols] += jnp.sum(
                    (seen * shift).reshape(step // 8, 8, chans), axis=0
                )
        return carry

    lax.fori_loop(0, length // step, tap_sums, 0)

    def filter_spectrum(i, carry):
        up = pl.ds(pl.multiple_of(i * tile_rows, tile_rows), tile_rows)
        down = pl.ds(pl.multiple_of(i * tile_rows + length, tile_rows), tile_rows)
        prod_cos, prod_sin = spec[up, :].astype(f32), spec[down, :].astype(f32)
        fg_cos, fg_sin = grad_spec[up, :].astype(f32), grad_spec[down, :].astype(f32)
        both[up, :] = (prod_cos * fg_cos + prod_sin * fg_sin).astype(low)
        both[down, :] = (prod_cos * fg_sin - prod_sin * fg_cos).astype(low)
        return carry

    lax.fori_loop(0, length // tile_rows, filter_spectrum, 0)

    def filter_back(i, carry):
        rows = pl.ds(pl.multiple_of(i * tile_rows, tile_rows), tile_rows)
        times = lax.broadcasted_iota(jnp.int32, (tile_rows, 1), 0) + i * tile_rows
        fade = jnp.exp(-times.astype(f32) * small[154:155, :])
        filter_grad[rows, :] = mm(back[rows, :], both[...]) * (1.0 / length) * fade
        return carry

    lax.fori_loop(0, length // tile_rows, filter_back, 0)
    small_out[0:64, :] = t_mm_exact(waves2[...], filter_grad[...])
    back2 = mm_t_exact(filter_grad[...], small[0:64, :]) * steep2[...]
    small_out[64:128, 0:64] = t_mm_exact(waves1[...], back2)
    back1 = mm_t_exact(back2, small[64:128, 0:64]) * steep1[...]
    small_out[64:128, 128:192] = t_mm_exact(embedding[:, 0:64], back1)
    for g in range(3):
        for at in range(3):
            small_out[144 + 3 * g + at : 145 + 3 * g + at, :] = jnp.sum(
                taps_sum[8 * at : 8 * at + 8, g * chans : (g + 1) * chans], axis=0, keepdims=True
            )
    swap_end(swaps, swapped)
    stores = fetch(half_pairs_mixer(half_out, wgrad_in, wgrad_out_part), store_sems)
    plane_sum.end(summed)
    sends += plane_sum.sends
    reduce_wait(send, recv, reduce_sems, peers)
    norm_back_parts(input_grad_out, recv, grad, x, par[0:1, :], sums)
    for q in range(width // chans):
        cols = slice(q * chans, (q + 1) * chans)
        small_out[128 + 2 * q : 130 + 2 * q, :] = sums[:, cols]
        small_out[136 + 2 * q : 138 + 2 * q, :] = late[:, cols]
    for copy in sends:
        copy.wait_send()
    for store in stores:
        store.wait()


def run_kernel(kernel, name, collective_id, operands, in_vmem, outs, out_vmem, scratch, flops):
    inside = pl.BlockSpec(memory_space=pltpu.VMEM)
    outside = pl.BlockSpec(memory_space=pl.ANY)
    scalars = pl.BlockSpec(memory_space=pltpu.SMEM)
    return pl.pallas_call(
        kernel,
        out_shape=[jax.ShapeDtypeStruct(shape, kind) for shape, kind in outs],
        in_specs=[
            scalars if item.dtype == jnp.int32 else inside if at in in_vmem else outside
            for at, item in enumerate(operands)
        ],
        out_specs=[inside if at in out_vmem else outside for at in range(len(outs))],
        scratch_shapes=scratch,
        compiler_params=pltpu.CompilerParams(
            collective_id=collective_id, has_side_effects=True, vmem_limit_bytes=60 * 2**20
        ),
        cost_estimate=pl.CostEstimate(flops=flops, bytes_accessed=2**25, transcendentals=0),
        name=name,
    )(*operands)


def exchange_scratch(count, width):
    return [pltpu.VMEM((3, count, width), low), pltpu.VMEM((3, count, width), low)]


def exchange_semaphores(count):
    return [pltpu.SemaphoreType.DMA((2, count)), pltpu.SemaphoreType.DMA((count,))]


def semaphores(loads, stores):
    return [
        pltpu.SemaphoreType.DMA((2, 6)),
        pltpu.SemaphoreType.DMA((2, 10)),
        pltpu.SemaphoreType.DMA((loads,)),
        pltpu.SemaphoreType.DMA((stores,)),
    ]


def mixer_weights_scratch(pack, width):
    _, dp_count, depth, cols = pack.shape
    return [
        pltpu.VMEM((2, dp_count, depth, 3 * cols // 4), low),
        pltpu.VMEM((2, dp_count, depth // 4, cols), low),
    ]


def mixer_forward(s, x, lengths, weights, waves, back, gathered):
    gathers = gathered is not None
    count, width = x.shape[-2:]
    length = waves.shape[1]
    chans, half = width // 4, width // 2
    knots, dp_count = chans // 4, lax.axis_size("dp")
    pack_shape = (2, dp_count, width // dp_count, half)
    pack = jax.ShapeDtypeStruct(pack_shape, low)
    vm, dma = pltpu.VMEM, pltpu.SemaphoreType.DMA
    outs = [
        ((length, width), low),
        ((length, 3 * chans), low),
        ((length, 3 * chans), low),
        ((length, chans), low),
        ((2 * length, chans), low),
        ((length, chans), f32),
        ((length, chans), low),
        ((count, width), f32),
    ]
    more = []
    if gathers:
        cotangent, embedding = gathered
        depth = weights[0].shape[0]
        units = 2 * half
        ff_shape = (2, dp_count, 2 * width // dp_count, half)
        half_in = 3 * chans // 2
        filters = [((2 * length, chans), f32), *[((length, knots), f32)] * 4]
        outs = [
            (pack_shape, low),
            (ff_shape, low),
            ((length, width), low),
            ((2, 8, width), f32),
            ((2, 160, chans), f32),
            (pack_shape, low),
            (ff_shape[2:], low),
            *filters,
            *filters,
            ((length, width), low),
            ((length, units), low),
            ((length, units), low),
            ((count, width), f32),
        ] + outs
        more = [
            *[vm((length, knots), f32)] * 4,
            vm((length, chans), low),
            vm((*pack_shape[:3], half // 4), low),
            vm(ff_shape, low),
            vm((length, width), low),
            vm(pack_shape, low),
            *[dma((2, 4)), dma((2, 3))] * 4,
            dma((2, 6)),
            dma((15,)),
            vm((2, *pack_shape[2:]), low),
            vm((2, *ff_shape[2:]), low),
            vm((2, 8, width), f32),
            vm((2, 160, chans), f32),
            vm((2, 4, depth, half_in), low),
            vm((2, 4 * depth, half_in // 3), low),
            vm((2, 4, depth, half), low),
            dma((2, 7)),
            dma((2, 1)),
            dma((2, 7)),
            dma((2, 1)),
            dma((2, 1)),
            dma((2, 1)),
            vm((length, width), low),
            *exchange_scratch(count, width),
            dma((2, 6)),
            dma((2, 10)),
            dma((5,)),
        ]
        operands = (cotangent, embedding, lengths, *weights, waves, back)
        inside = range(len(operands) - 1)
        out_inside = (len(outs) - 9, len(outs) - 1)
    else:
        par, small, weights, filt = weights
        operands = (par, small, lengths, weights, filt, waves, back)
        inside = range(3)
        out_inside = (len(outs) - 1,)
    return run_kernel(
        partial(mixer_forward_kernel, s, gathers),
        "opening" if gathers else "mixer_forward",
        1 + s,
        (x, *operands),
        inside,
        outs,
        out_inside,
        [vm((length, width), low)]
        + mixer_weights_scratch(pack, width)
        + [
            vm((2 * length, chans), f32),
            vm((2 * length, length), low),
            vm((length, 2 * length), low),
            vm((length + 8, 3 * chans), f32),
            vm((length, 3 * chans), low),
            vm((length, 3 * chans), low),
            vm((length, chans), low),
            vm((2 * length, chans), low),
            vm((2 * length, chans), low),
            vm((length, chans), f32),
            vm((length, chans), low),
        ]
        + exchange_scratch(count, width)
        + semaphores(8, 7)
        + more,
        10**10,
    )


def ff_turn(s, cotangent, x, par, lengths, pack, late):
    count, width = x.shape
    _, dp_count, rows, half = pack.shape
    length, units = 4 * count, 2 * half
    vm = pltpu.VMEM
    return run_kernel(
        partial(ff_turn_kernel, s),
        "ff_turn",
        4,
        (cotangent, x, par, lengths, pack, late),
        range(3),
        [
            (pack.shape[1:], low),
            ((length, units), low),
            ((count, width), f32),
            ((2, width), f32),
        ],
        (2, 3),
        [vm((length, width), low)] * 2
        + [vm((2, dp_count, rows // 2, half), low)] * 2
        + [vm((length, units), low)] * 2
        + [vm(pack.shape, low), vm(pack.shape[1:], low)]
        + exchange_scratch(count, width)
        + semaphores(3, 2)
        + [pltpu.SemaphoreType.DMA((2, 1))],
        3 * 10**10,
    )


def ff_backward(s, grad, middle, par, lengths, pack, second, value, slope, earlier):
    count, width = grad.shape
    _, dp_count, rows, half = pack.shape
    length, units = value.shape
    vm = pltpu.VMEM
    weights = [vm((2, dp_count, rows // 2, half), low)] * 2
    return run_kernel(
        partial(ff_backward_kernel, s),
        "ff_backward",
        5,
        (grad, middle, par, lengths, pack, second, value, slope, earlier),
        range(3),
        [
            (pack.shape[1:], low),
            ((count, width), f32),
            ((2, width), f32),
            (earlier.shape[1:], low),
        ],
        (1, 2, 3),
        [vm((length, width), low)]
        + weights
        + [vm((length, width), low)]
        + [vm((length, units), low)] * 3
        + [vm(pack.shape, low), vm(pack.shape[1:], low)]
        + exchange_scratch(count, width)
        + semaphores(5, 1)
        + plane_sum_scratch(earlier)
        + [pltpu.SemaphoreType.DMA((2, 1))],
        2 * 10**10,
    )


def mixer_backward(
    s, grad, x, par, small, embedding, late, lengths, pack, waves, back, kept, earlier
):
    normed, proj, streams, prod, spec, filtered, gated, filt, *network = kept
    count, width = grad.shape
    length, chans = prod.shape
    knots = network[0].shape[1]
    vm = pltpu.VMEM
    weights = mixer_weights_scratch(pack, width)
    return run_kernel(
        partial(mixer_backward_kernel, s),
        "mixer_backward",
        7 + s,
        (grad, x, par, small, embedding, late, lengths, pack, filt, waves, back, normed, proj,
         streams, prod, spec, filtered, gated, *network, earlier),
        range(6),
        [
            (pack.shape[1:], low),
            (small.shape[1:], f32),
            ((count, width), f32),
            (earlier.shape[1:], low),
        ],
        (1, 2, 3),
        [vm((length, width), low)]
        + weights
        + [
            vm((2 * length, chans), f32),
            vm((2 * length, length), low),
            vm((length, 2 * length), low),
            vm((length, width), low),
            vm((length, 3 * chans), low),
            vm((length, 3 * chans), low),
            vm((length, chans), low),
            vm((2 * length, chans), low),
            vm((length, chans), f32),
            vm((length, chans), low),
            vm((length, chans), low),
            vm((length, chans), low),
            vm((2 * length, chans), low),
            vm((2 * length, chans), low),
            vm((2 * length, chans), f32),
            vm((length, chans), f32),
            vm((length + 8, 3 * chans), f32),
            vm((length, 3 * chans), low),
        ]
        + weights
        + [vm(item.shape[1:], low) for item in weights]
        + [vm((length, knots), f32)] * 4
        + [vm((2, width), f32), vm((24, 3 * chans), f32)]
        + exchange_scratch(count, width)
        + semaphores(19, 5)
        + plane_sum_scratch(earlier)
        + [pltpu.SemaphoreType.DMA((2, 2))],
        2 * 10**10,
    )


def shuffle_stage(w_in, w_out, w_up, stage_in, stage_out, stage_up):
    depth, chans = w_in.shape[0], w_out.shape[1] // 4
    count = lax.axis_size("dp")
    half_in = stage_in.shape[3]
    piece = chans // count
    for h in range(2):
        for j in range(4):
            for c in range(0, half_in, 2 * piece):
                pair = []
                for col in (c, c + piece):
                    g, d = divmod((h * half_in + col) // piece, count)
                    at = ((g * count + d) * 4 + j) * piece
                    pair.append(w_in[:, at : at + piece].astype(f32))
                stage_in[h, j, :, c : c + 2 * piece] = jnp.concatenate(pair, 1).astype(low)
            for d in range(2):
                at = ((2 * h + d) * 4 + j) * chans
                stage_up[h, j, :, d * chans : (d + 1) * chans] = w_up[:, at : at + chans]
    part = half_in // 3
    for h in range(2):
        for q in range(4):
            at = (h * 4 + q) * part
            stage_out[h, q * depth : (q + 1) * depth, :] = w_out[:, at : at + part]


def parameters_stage(me, par, small, gain, shift, taps, first, second, last, direct, rates):
    chans = small.shape[1]
    count = lax.axis_size("dp")
    piece = chans // count
    width = last.shape[2]
    par[0:1, :] = gain[0, 0:1, :]
    par[1:2, :] = shift[0, 0:1, :]
    par[2:3, :] = gain[0, 1:2, :]
    par[3:4, :] = shift[0, 1:2, :]
    par[4:8, :] = jnp.zeros((4, width), f32)
    small[64:160, :] = jnp.zeros((96, chans), f32)
    small[64:128, 0:64] = second[0]
    for row in range(first.shape[0]):
        small[64 + row : 65 + row, 128:192] = first[row]
    for j in range(4):

        @pl.when(me == j)
        def _():
            for d in range(0, count, 2):
                cols = slice(d * piece, (d + 2) * piece)

                def picked(ref, rows, base=0):
                    at = [base + ((d + k) * 4 + j) * piece for k in range(2)]
                    return jnp.concatenate([ref[rows, a : a + piece] for a in at], 1)

                small[0:64, cols] = picked(last.at[0], slice(0, 64))
                for g in range(3):
                    for tap in range(3):
                        row = 144 + 3 * g + tap
                        small[row : row + 1, cols] = picked(
                            taps.at[tap], slice(0, 1), g * width
                        )
                small[153:154, cols] = picked(direct, slice(0, 1))
                small[154:155, cols] = picked(rates, slice(0, 1))


def shuffle_send(section, me, targets, sources, parts, parameters, sems):
    stage_in, stage_out, stage_up, w_down = sources
    mixer_parts, ff_parts = parts
    in_sems, out_sems, up_sems, down_sems, par_sems, small_sems = sems
    depth, half_in = stage_in.shape[2:]
    half = stage_up.shape[3]
    copies = [
        remote_to(item.at[section], item.at[section], at, 0, other_core())
        for item, at in zip(parameters, (par_sems, small_sems))
    ]
    for e, (t, seq, device) in enumerate(targets):
        target = mixer_parts.at[section, rows_of(me, depth), pl.ds(0, half_in)]
        copies.append(remote_to(stage_in.at[t, seq], target, in_sems, e, device))
    target = mixer_parts.at[section, :, pl.ds(half_in, half_in // 3)]
    copies.append(remote_to(stage_out.at[1 - section], target, out_sems, 0, other_core()))
    for e, (t, seq, device) in enumerate(targets):
        target = ff_parts.at[section, rows_of(me, depth), :]
        copies.append(remote_to(stage_up.at[t, seq], target, up_sems, e, device))
    cols = pl.ds(pl.multiple_of((1 - section) * half, half), half)
    target = ff_parts.at[section, pl.ds(4 * depth, 4 * depth), :]
    copies.append(remote_to(w_down.at[:, cols], target, down_sems, 0, other_core()))
    for copy in copies:
        copy.start()
    mixer_parts[section, rows_of(me, depth), 0:half_in] = stage_in[section, me]
    mixer_parts[section, :, half_in:] = stage_out[section]
    ff_parts[section, rows_of(me, depth), :] = stage_up[section, me]
    cols = pl.ds(pl.multiple_of(section * half, half), half)
    ff_parts[section, 4 * depth : 8 * depth, :] = w_down[:, cols]
    return copies


def shuffle_wait_mixer(section, me, targets, parts, stage_in, in_sems, out_sems):
    depth, half_in = stage_in.shape[2:]
    for e, (t, seq, device) in enumerate(targets):
        block = parts.at[t, rows_of(seq, depth), pl.ds(0, half_in)]
        remote_to(block, block, in_sems, e, device).wait_recv()
    block = parts.at[1 - section, :, pl.ds(half_in, half_in // 3)]
    remote_to(block, block, out_sems, 0, other_core()).wait_recv()


def shuffle_wait_ff(section, me, targets, parts, stage_up, up_sems, down_sems):
    depth = stage_up.shape[2]
    for e, (t, seq, device) in enumerate(targets):
        block = parts.at[t, rows_of(seq, depth), :]
        remote_to(block, block, up_sems, e, device).wait_recv()
    block = parts.at[1 - section, pl.ds(4 * depth, 4 * depth), :]
    remote_to(block, block, down_sems, 0, other_core()).wait_recv()


def shuffle_targets(section, me, peers):
    targets = [(section, peer, {"seq": peer}) for peer in peers]
    targets.append((1 - section, me, other_core()))
    targets += [(1 - section, peer, {**other_core(), "seq": peer}) for peer in peers]
    return targets


def finish_kernel(
    vec0, vec1, mixer0, mixer1, ff0, ff1, grad0, grad1, value_hbm, pack_hbm, x, out0, lengths,
    block_outputs, input_grads, got_in, got_out, got_up, got_down, vec_out,
    mine0, arrived0, plane_sems0, sum_sems0, mine1, arrived1, plane_sems1, sum_sems1,
    vec_other, vec_sum, vec_arrived, vec_all, stage_mixer, stage_ff, own_sems, load_sems,
    layer_sems, keep_sems, vec_core_sems, vec_sum_sems, vec_plane_sems, vec_seq_sems, in_sems, out_sems, up_sems, down_sems,
    send, recv, out1, reduce_sems, value, wdown, early_sems,
):
    section = lax.axis_index("section")
    me = lax.axis_index("seq")
    here, near, far = along_planes()
    planes = (near, far, (near + 2) % 4)
    peers = neighbours(me)
    depth, half_in = got_in.shape[2:]
    targets = shuffle_targets(section, me, peers)
    greeted = greet([device for _, _, device in targets] + [{"dp": plane} for plane in planes])
    inner = wdown.shape[2]
    early = fetch(
        [(value_hbm, value), (pack_hbm.at[:, :, pl.ds(inner, inner)], wdown)], early_sems
    )
    middle = mixer0.shape[2] // 2
    chunks = (pl.ds(0, middle), pl.ds(middle, middle))
    in_cols = (pl.ds(0, middle), pl.ds(middle, half_in - middle))

    def columns(e, at):
        t, seq, device = targets[e]
        return remote_to(
            stage_mixer.at[t, rows_of(seq, depth), in_cols[at]],
            got_in.at[section, me, :, in_cols[at]],
            in_sems,
            2 * e + at,
            device,
        )

    out_columns = remote_to(
        stage_mixer.at[1 - section, :, pl.ds(half_in, half_in // 3)], got_out.at[section], out_sems,
        0, other_core(),
    )

    def send_layer(s, at):
        for index in range(2):

            @pl.when(section == index)
            def _():
                for e in range(3) if index == s else range(3, 7):
                    columns(e, at).start()
                if at == 1 and index != s:
                    out_columns.start()

    all_here(greeted)
    for index, vec in enumerate((vec1, vec0)):

        @pl.when(section == index)
        def _():
            remote_to(vec, vec_other, vec_core_sems, 0, other_core()).start()

    sends = []
    count, width = x.shape

    def result_part(slot):
        rows = rows_of(me if slot is None else peers[slot], count)
        for h in range(2):
            cols = slice(h * width // 2, (h + 1) * width // 2)
            out = mm(value[rows, :], wdown[h].reshape(4 * inner, width // 2))
            if slot is None:
                out1[:, cols] = out
            else:
                send[slot, :, cols] = out.astype(low)
        return [] if slot is None else reduce_send(slot, send, recv, reduce_sems, peers)

    for load in early:
        load.wait()
    sends += result_part(2)
    vec_swap = remote_to(vec_other, vec_other, vec_core_sems, 0, other_core())
    vec_swap.wait_recv()
    sends.append(vec_swap)

    @pl.when(section == 0)
    def _():
        vec_sum[...] = vec0[...] + vec_other[...]

    @pl.when(section == 1)
    def _():
        vec_sum[...] = vec1[...] + vec_other[...]

    chunk = vec_sum.shape[0] // 4
    moves = [
        remote_to(
            vec_sum.at[rows_of(plane, chunk)], vec_arrived.at[slot], vec_sum_sems, slot,
            {"dp": plane},
        )
        for slot, plane in enumerate(planes)
    ]
    for copy in moves:
        copy.start()
    sends += moves
    plane_sums = [
        PlaneSum(mixer0.at[:, :, chunks[0]], mine0, arrived0, plane_sems0, sum_sems0),
        PlaneSum(mixer0.at[:, :, chunks[1]], mine1, arrived1, plane_sems1, sum_sems1),
    ]
    for plane_sum in plane_sums:
        plane_sum.begin()
    loads = fetch(
        [
            (ff0, stage_ff.at[0]),
            (ff1, stage_ff.at[1]),
            (mixer1, stage_mixer.at[1]),
        ],
        load_sems,
    )
    by_layer(True, ((grad0, grad1, input_grads),), layer_sems, keep_sems)
    sends += result_part(0)
    sends += result_part(1)
    for load in loads:
        load.wait()
    ups = []
    for e, (t, seq, device) in enumerate(targets):
        ups.append(
            remote_to(
                stage_ff.at[t, rows_of(seq, depth), :], got_up.at[section, me], up_sems, e, device
            )
        )
    downs = [
        remote_to(
            stage_ff.at[1 - section, pl.ds(4 * depth, 4 * depth), :], got_down.at[section],
            down_sems, 0, other_core(),
        )
    ]
    for copy in ups + downs:
        copy.start()
    sends += ups + downs
    send_layer(1, 0)
    send_layer(1, 1)
    keeps = fetch(
        [
            (stage_ff.at[section, rows_of(me, depth), :], got_up.at[section, me]),
            (stage_ff.at[section, pl.ds(4 * depth, 4 * depth), :], got_down.at[section]),
        ],
        own_sems,
    )

    result_part(None)
    for copy in moves:
        copy.wait_recv()
    own_chunk = rows_of(here, chunk)
    total = vec_sum[own_chunk, :]
    for slot in range(len(planes)):
        total = total + vec_arrived[slot]
    vec_all[me, own_chunk, :] = total
    moves = [
        remote_to(
            vec_all.at[me, own_chunk], vec_all.at[me, own_chunk], vec_plane_sems, slot,
            {"dp": plane},
        )
        for slot, plane in enumerate(planes)
    ]
    for copy in moves:
        copy.start()
    sends += moves
    for plane_sum in plane_sums:
        plane_sum.forward()
    sends += reduce_pass(send, recv, reduce_sems, peers)
    for slot, plane in enumerate(planes):
        block = vec_all.at[me, rows_of(plane, chunk)]
        remote_to(block, block, vec_plane_sems, slot, {"dp": plane}).wait_recv()
    moves = [
        remote(vec_all.at[me], vec_all.at[me], vec_seq_sems, slot, peer)
        for slot, peer in enumerate(peers)
    ]
    for copy in moves:
        copy.start()
    sends += moves

    for at, plane_sum in enumerate(plane_sums):
        plane_sum.end(stage_mixer.at[0, :, chunks[at]])
        sends += plane_sum.sends
        send_layer(0, at)
    sends += [columns(e, at) for e in range(7) for at in range(2)] + [out_columns]
    reduce_wait(send, recv, reduce_sems, peers)
    add_parts(out1, recv, x, me * count, lengths)
    by_layer(True, ((out0, out1, block_outputs),), layer_sems, keep_sems, 1)
    keeps += fetch(
        [
            (
                stage_mixer.at[section, rows_of(me, depth), pl.ds(0, half_in)],
                got_in.at[section, me],
            ),
            (stage_mixer.at[section, :, pl.ds(half_in, half_in // 3)], got_out.at[section]),
        ],
        own_sems,
        2,
    )
    for slot, peer in enumerate(peers):
        block = vec_all.at[peer]
        remote(block, block, vec_seq_sems, slot, peer).wait_recv()
    keeps += fetch([(vec_all, vec_out)], own_sems, 4)
    for e, (t, seq, device) in enumerate(targets):
        block = got_up.at[t, seq]
        remote_to(block, block, up_sems, e, device).wait_recv()
        for at in range(2):
            block = got_in.at[t, seq, :, in_cols[at]]
            remote_to(block, block, in_sems, 2 * e + at, device).wait_recv()
    downs[0].wait_recv()
    out_columns.wait_recv()
    by_layer(False, ((grad0, grad1, input_grads),), layer_sems, keep_sems)
    by_layer(False, ((out0, out1, block_outputs),), layer_sems, keep_sems, 1)
    for copy in sends:
        copy.wait_send()
    for keep in keeps:
        keep.wait()


def unpack_kernel(
    blocks, grads, got_in, got_out, got_up, got_down, vec_all,
    block_outputs, input_grads, g_in, g_out, g_up, g_down, g_gain, g_bias, g_taps, g_first,
    g_second, g_last, g_direct,
    stage_blocks, stage_grads, load_sems, copy_sems,
):
    loads = fetch([(blocks, stage_blocks), (grads, stage_grads)], load_sems)
    depth = g_in.shape[0]
    half_in, half_up = got_in.shape[3], got_up.shape[3]
    chans = vec_all.shape[2]
    count = 4
    piece = chans // count
    for j in range(4):
        for d in range(count):
            at = (d * 4 + j) * chans
            h, col = divmod(d * chans, half_up)
            g_up[:, at : at + chans] = got_up[h, j, :, col : col + chans].astype(f32)
    for h in range(2):
        g_down[:, h * half_up : (h + 1) * half_up] = got_down[h].astype(f32)
    for load in loads:
        load.wait()
    copies = fetch([(stage_blocks, block_outputs), (stage_grads, input_grads)], copy_sems)
    for g in range(3):
        for d in range(count):
            h, col = divmod(g * chans + d * piece, half_in)
            for j in range(0, 4, 2):
                at = ((g * count + d) * 4 + j) * piece
                g_in[:, at : at + 2 * piece] = jnp.concatenate(
                    [got_in[h, j + k, :, col : col + piece].astype(f32) for k in range(2)], 1
                )
    part = half_in // 3
    for h in range(2):
        for q in range(4):
            at = (h * 4 + q) * part
            g_out[:, at : at + part] = got_out[h, q * depth : (q + 1) * depth, :].astype(f32)
    first = sum_of(vec_all, slice(64, 64 + g_first.shape[0]), slice(128, 192))
    for row in range(g_first.shape[0]):
        g_first[row] = first[row : row + 1]
    g_second[...] = sum_of(vec_all, slice(64, 128), slice(0, 64))
    for q in range(4):
        cols = slice(q * chans, (q + 1) * chans)
        early = sum_of(vec_all, slice(128 + 2 * q, 130 + 2 * q), slice(None))
        late = sum_of(vec_all, slice(136 + 2 * q, 138 + 2 * q), slice(None))
        g_gain[0:1, cols] = early[0:1]
        g_gain[1:2, cols] = late[0:1]
        g_bias[0:1, cols] = early[1:2]
        g_bias[1:2, cols] = late[1:2]
    for d in range(count):
        cols = slice(d * piece, (d + 1) * piece)
        for j in range(0, 4, 2):
            at = (d * 4 + j) * piece
            pair = slice(at, at + 2 * piece)

            def joined(rows):
                return jnp.concatenate([vec_all[j, rows, cols], vec_all[j + 1, rows, cols]], 1)

            g_last[:, pair] = joined(slice(0, 64))
            for g in range(3):
                for tap in range(3):
                    row = 144 + 3 * g + tap
                    start = g * 4 * chans + at
                    g_taps[tap, :, start : start + 2 * piece] = joined(slice(row, row + 1))
            g_direct[:, pair] = joined(slice(153, 154))

    for copy in copies:
        copy.wait()


def sum_of(blocks, rows, cols):
    return (blocks[0, rows, cols] + blocks[1, rows, cols]) + (
        blocks[2, rows, cols] + blocks[3, rows, cols]
    )


def finish(
    vec0, vec1, mixer0, mixer1, ff0, ff1, grad0, grad1, value, pack, x, out0, lengths
):
    count, width = grad0.shape
    dp_count, rows, half = mixer0.shape
    depth = rows // 4
    chans = vec0.shape[1]
    half_in = 3 * chans // 2
    vm, dma = pltpu.VMEM, pltpu.SemaphoreType.DMA
    vec_rows = vec0.shape[0]
    chunk = jax.ShapeDtypeStruct((dp_count, rows, half // 2), low)
    return run_kernel(
        finish_kernel,
        "finish",
        10,
        (vec0, vec1, mixer0, mixer1, ff0, ff1, grad0, grad1, value, pack, x, out0, lengths),
        (0, 1, 6, 7, 10, 11),
        [
            ((2, count, width), f32),
            ((2, count, width), f32),
            ((2, 4, depth, half_in), low),
            ((2, rows, half_in // 3), low),
            ((2, 4, depth, half), low),
            ((2, rows, half), low),
            ((4, vec_rows, chans), f32),
        ],
        (),
        plane_sum_scratch(chunk)
        + plane_sum_scratch(chunk)
        + [
            vm((vec_rows, chans), f32),
            vm((vec_rows, chans), f32),
            vm((3, vec_rows // 4, chans), f32),
            vm((4, vec_rows, chans), f32),
            vm((2, *mixer1.shape), low),
            vm((2, *ff1.shape), low),
            dma((5,)),
            dma((3,)),
            *exchange_semaphores(2),
            dma((2, 1)),
            dma((2, 3)),
            dma((2, 3)),
            dma((2, 3)),
            dma((2, 14)),
            dma((2, 1)),
            dma((2, 7)),
            dma((2, 1)),
            *exchange_scratch(count, width),
            vm((count, width), f32),
            dma((2, 10)),
            vm(value.shape, low),
            vm((*pack.shape[:2], pack.shape[2] // 2, pack.shape[3]), low),
            dma((2,)),
        ],
        10**9,
    )


def unpack(blocks, grads, got, first_shape):
    width = blocks.shape[2]
    depth = got[0].shape[2]
    units = 4 * 2 * got[2].shape[3]
    knots = first_shape[1]
    inside = pl.BlockSpec(memory_space=pltpu.VMEM)
    outside = pl.BlockSpec(memory_space=pl.ANY)
    shapes = (
        blocks.shape, grads.shape, (depth, 3 * width), (depth, width), (depth, units),
        (4 * depth, width), (2, width), (2, width), (3, 1, 3 * width),
        (first_shape[0], 1, knots), (knots, knots),
        (knots, width), (1, width),
    )
    return pl.pallas_call(
        unpack_kernel,
        out_shape=[jax.ShapeDtypeStruct(shape, f32) for shape in shapes],
        in_specs=[outside] * 2 + [inside] * 5,
        out_specs=[outside] * 2 + [inside] * 11,
        scratch_shapes=[
            pltpu.VMEM(blocks.shape, f32),
            pltpu.VMEM(grads.shape, f32),
            pltpu.SemaphoreType.DMA((2,)),
            pltpu.SemaphoreType.DMA((2,)),
        ],
        compiler_params=pltpu.CompilerParams(vmem_limit_bytes=56 * 2**20),
        name="unpack",
    )(blocks, grads, *got)


def any_device(
    tokens,
    cotangent,
    lengths,
    norm_gain,
    norm_bias,
    mixer_in,
    short_kernel,
    filter_first,
    filter_second,
    filter_last,
    filter_bias,
    decay_rates,
    mixer_out,
    up_weight,
    down_weight,
):
    section = lax.axis_index("section")
    seq_index = lax.axis_index("seq")
    seq_count = lax.axis_size("seq")
    dp_count = lax.axis_size("dp")
    own_layer_first = section == 0
    local_len = tokens.shape[2]
    width = tokens.shape[3]
    hidden = up_weight.shape[2]
    row_len = local_len * seq_count
    chans = width // seq_count
    units = hidden // seq_count

    def share_columns(block, groups):
        rows = block.shape[0]
        inner = block.shape[1] // (groups * dp_count * seq_count)
        split = block.reshape(rows, groups, dp_count, seq_count, inner)
        split = jnp.transpose(split, (3, 0, 1, 2, 4))
        moved = lax.all_to_all(split, "seq", split_axis=0, concat_axis=0, tiled=True)
        return moved.reshape(seq_count * rows, groups * dp_count * inner)

    def unshare_columns(block, groups):
        rows = block.shape[0] // seq_count
        inner = block.shape[1] // (groups * dp_count)
        split = block.reshape(seq_count, rows, groups, dp_count, inner)
        moved = lax.all_to_all(split, "seq", split_axis=0, concat_axis=0, tiled=True)
        moved = jnp.transpose(moved, (1, 2, 3, 0, 4))
        return moved.reshape(rows, groups * dp_count * seq_count * inner)

    def gathered(block):
        whole = lax.all_gather(block, ("section", "dp"))
        return whole.reshape(2, dp_count * block.shape[0], block.shape[1])

    weights = (
        gathered(share_columns(mixer_in[0], 3)),
        gathered(mixer_out[0]),
        gathered(share_columns(up_weight[0], 1)),
        gathered(down_weight[0]),
    )

    def both(value):
        return lax.all_gather(value[0], "section")

    gains, shifts = both(norm_gain), both(norm_bias)
    taps, first_w, second_w = both(short_kernel), both(filter_first), both(filter_second)
    last_w, direct, rates = both(filter_last), both(filter_bias), both(decay_rates)

    def mine(value):
        lead = value.shape[:-1]
        split = value.reshape(*lead, dp_count, seq_count, -1)
        picked = lax.dynamic_index_in_dim(split, seq_index, len(lead) + 1, False)
        return picked.reshape(*lead, chans)

    def placed(value):
        lead = value.shape[:-1]
        split = value.reshape(*lead, dp_count, 1, -1)
        inner = split.shape[-1]
        empty = jnp.zeros((*lead, dp_count, seq_count, inner), value.dtype)
        at = [0] * len(lead) + [0, seq_index, 0]
        return lax.dynamic_update_slice(empty, split, at).reshape(*lead, width)

    waves = jnp.asarray(wave_tables(row_len))
    waves_back = waves

    def to_waves(x):
        both_parts = mm(waves, x)
        return both_parts[:row_len], both_parts[row_len:]

    def from_waves(cos_part, sin_part):
        joined = jnp.concatenate([cos_part, sin_part], 0).astype(low)
        return t_mm(waves_back, joined) * (1.0 / row_len)

    def ag(x):
        return lax.all_gather(x, "seq", axis=0, tiled=True)

    def rs(x):
        return lax.psum_scatter(x.astype(low), "seq", scatter_dimension=0, tiled=True).astype(f32)

    length_now = lax.dynamic_index_in_dim(lengths, section, 0, False)[0]
    positions = seq_index * local_len + jnp.arange(local_len)
    mask = (positions < length_now).astype(f32)[:, None]
    row_mask = (jnp.arange(row_len) < length_now).astype(f32)[:, None]
    own_tokens = lax.dynamic_index_in_dim(tokens, section, 0, False)[0].astype(f32)
    own_cotangent = lax.dynamic_index_in_dim(cotangent, section, 0, False)[0].astype(f32)

    def layer_forward(s, inputs):
        w_in, w_out, w_up, w_down = [w[s] for w in weights]
        kernel = mine(taps[s].reshape(3, 3, width))
        last_mine, direct_mine, rates_mine = mine(last_w[s]), mine(direct[s]), mine(rates[s])

        def own_filter(a, b, c):
            return filter_taps(a, b, c, rates_mine, row_len)

        filter_rows, filter_back = jax.vjp(own_filter, first_w[s], second_w[s], last_mine)
        filt_cos, filt_sin = to_waves(filter_rows.astype(low))
        normed = (norm_stats(inputs)[0] * gains[s, 0] + shifts[s, 0]).astype(low)
        normed = ag(normed)
        projected = [mm(normed, w_in[:, g * chans : (g + 1) * chans]) for g in range(3)]
        streams = [
            (
                kernel[0, g] * projected[g]
                + kernel[1, g] * shifted(projected[g], 1)
                + kernel[2, g] * shifted(projected[g], 2)
            ).astype(low)
            for g in range(3)
        ]
        wide = [x.astype(f32) for x in streams]
        product = (wide[0] * wide[2] * row_mask).astype(low)
        prod_cos, prod_sin = to_waves(product)
        filtered = from_waves(
            prod_cos * filt_cos - prod_sin * filt_sin, prod_cos * filt_sin + prod_sin * filt_cos
        ) + direct_mine * product.astype(f32)
        gated = (wide[1] * filtered).astype(low)
        middle = inputs + mask * rs(mm(gated, w_out))
        second = (norm_stats(middle)[0] * gains[s, 1] + shifts[s, 1]).astype(low)
        second = ag(second)
        value, slope = gelu_both(mm(second, w_up))
        value = value.astype(low)
        slope = slope.astype(low)
        result = middle + mask * rs(mm(value, w_down))
        saved = (
            inputs, normed, projected, wide, product, prod_cos, prod_sin, filt_cos, filt_sin,
            filtered, gated, middle, second, value, slope, kernel, direct_mine, filter_back,
        )
        return result, saved

    def layer_backward(s, grad, saved):
        w_in, w_out, w_up, w_down = [w[s] for w in weights]
        (
            inputs, normed, projected, wide, product, prod_cos, prod_sin, filt_cos, filt_sin,
            filtered, gated, middle, second, value, slope, kernel, direct_mine, filter_back,
        ) = saved
        out_low = ag((grad * mask).astype(low))
        pre = (mm_t(out_low, w_down) * slope.astype(f32)).astype(low)
        grad_down = t_mm(value, out_low)
        grad_up = t_mm(second, pre)
        mid_part, gain_late, bias_late = norm_back(rs(mm_t(pre, w_up)), middle, gains[s, 1])
        middle_grad = grad + mid_part
        branch = ag((middle_grad * mask).astype(low))
        gated_grad = mm_t(branch, w_out).astype(low)
        grad_out = t_mm(gated, branch)
        gated_grad = gated_grad.astype(f32)
        filtered_grad = (gated_grad * wide[1]).astype(low)
        fg_cos, fg_sin = to_waves(filtered_grad)
        fg_wide = filtered_grad.astype(f32)
        prod32 = product.astype(f32)
        product_grad = from_waves(
            filt_cos * fg_cos + filt_sin * fg_sin, filt_cos * fg_sin - filt_sin * fg_cos
        ) + direct_mine * fg_wide
        product_grad = product_grad.astype(low).astype(f32)
        filter_grad = from_waves(
            prod_cos * fg_cos + prod_sin * fg_sin, prod_cos * fg_sin - prod_sin * fg_cos
        )
        grad_first, grad_second, grad_last = filter_back(filter_grad)
        grad_direct = jnp.sum(fg_wide * prod32, 0)
        mixed = [
            (product_grad * wide[2]).astype(low).astype(f32),
            (gated_grad * filtered).astype(low).astype(f32),
            (product_grad * wide[0]).astype(low).astype(f32),
        ]
        proj = [
            (
                kernel[0, g] * mixed[g]
                + kernel[1, g] * shifted(mixed[g], -1)
                + kernel[2, g] * shifted(mixed[g], -2)
            ).astype(low)
            for g in range(3)
        ]
        grad_taps = jnp.stack(
            [
                jnp.stack(
                    [jnp.sum(mixed[g] * (shifted(projected[g], k) if k else projected[g]), 0) for g in range(3)]
                )
                for k in range(3)
            ]
        )
        proj = jnp.concatenate(proj, 1)
        grad_in = t_mm(normed, proj)
        in_part, gain_early, bias_early = norm_back(rs(mm_t(proj, w_in)), inputs, gains[s, 0])
        small = (
            jnp.stack([gain_early, gain_late]),
            jnp.stack([bias_early, bias_late]),
            placed(grad_taps).reshape(3, 3 * width),
            grad_first,
            grad_second,
            placed(grad_last),
            placed(grad_direct),
        )
        large = (grad_in, grad_out, grad_up, grad_down)
        return middle_grad + in_part, small, large

    first_out, first_saved = layer_forward(0, own_tokens)
    second_out, second_saved = layer_forward(1, first_out)
    second_grad, second_small, second_large = layer_backward(1, own_cotangent, second_saved)
    first_grad, first_small, first_large = layer_backward(0, second_grad, first_saved)

    swap = [(0, 1), (1, 0)]

    def by_layer(first, second):
        other = lax.ppermute(jnp.where(own_layer_first, second, first), "section", swap)
        return jnp.where(
            own_layer_first, jnp.stack([first, other]), jnp.stack([other, second])
        )[None, :, None]

    def summed(first, second):
        stacked = jnp.stack([first, second]).astype(low)
        rows = first.shape[0] // dp_count
        stacked = stacked.reshape(2 * dp_count, rows, first.shape[1])
        return lax.psum_scatter(stacked, ("section", "dp"), scatter_dimension=0, tiled=True)[0]

    sums = [summed(a, b) for a, b in zip(first_large, second_large)]
    sum_in = unshare_columns(sums[0], 3).astype(f32)
    sum_out = sums[1].astype(f32)
    sum_up = unshare_columns(sums[2], 1).astype(f32)
    sum_down = sums[3].astype(f32)
    stacked = jax.tree.map(lambda a, b: jnp.stack([a, b]), first_small, second_small)
    small = lax.psum(stacked, ("section", "dp", "seq"))
    small = [lax.dynamic_slice_in_dim(x, section, 1, 0) for x in small]
    sum_gain, sum_bias, sum_taps, sum_first, sum_second, sum_last, sum_direct = small
    return (
        by_layer(first_out, second_out),
        by_layer(first_grad, second_grad),
        sum_gain,
        sum_bias,
        sum_in[None],
        sum_taps,
        sum_first,
        sum_second,
        sum_last,
        sum_direct,
        sum_out[None],
        sum_up[None],
        sum_down[None],
    )


def plane_device(
    tokens,
    cotangent,
    lengths,
    norm_gain,
    norm_bias,
    mixer_in,
    short_kernel,
    filter_first,
    filter_second,
    filter_last,
    filter_bias,
    decay_rates,
    mixer_out,
    up_weight,
    down_weight,
):
    section = lax.axis_index("section")
    seq_count = lax.axis_size("seq")
    dp_count = lax.axis_size("dp")
    row_len = tokens.shape[2] * seq_count
    lengths = jnp.transpose(lengths)
    short_kernel = jnp.transpose(short_kernel, (1, 0, 2))
    filter_first = jnp.transpose(filter_first, (1, 0, 2))

    def gathered(part):
        whole = lax.all_gather(part, ("section", "dp"))
        return whole.reshape(2, dp_count, *part.shape)

    tables = wave_tables(row_len)
    waves = jnp.asarray(tables)
    waves_back = jnp.asarray(np.ascontiguousarray(tables.T))
    embedding = jnp.asarray(np.pad(position_rows(row_len), ((0, 0), (0, 95))))

    weights = (
        mixer_in[0], mixer_out[0], up_weight[0], down_weight[0], norm_gain, norm_bias, short_kernel,
        filter_first, filter_second, filter_last, filter_bias, decay_rates,
    )
    (
        first_mixer_pack, first_ff_pack, cotangent_low, par, small, second_mixer_pack, ff_part,
        *outs,
    ) = mixer_forward(
        0, tokens, lengths, weights, waves, waves_back, (cotangent, embedding)
    )
    first_filter, second_filter, first_saved, outs = outs[:5], outs[5:10], outs[10:13], outs[13:]
    first_out, *first_kept, first_middle = outs
    second_ff_pack = gathered(ff_part)
    *second_kept, second_middle = mixer_forward(
        1, first_out, lengths, (par, small, second_mixer_pack, second_filter[0]), waves, waves_back,
        None,
    )
    first_kept, second_kept = [*first_kept, *first_filter], [*second_kept, *second_filter]
    second_ff, second_value, middle_grad, late = ff_turn(
        1, cotangent, second_middle, par, lengths, second_ff_pack, cotangent_low
    )

    def mixer_back(s, grad, x, late, pack, kept, earlier):
        return mixer_backward(
            s, grad, x, par, small, embedding, late, lengths, pack, waves, waves_back, kept, earlier
        )

    second_mixer, second_vec, second_grad, second_ff = mixer_back(
        1, middle_grad, first_out, late, second_mixer_pack, second_kept, second_ff
    )
    first_ff, middle_grad, late, second_mixer = ff_backward(
        0, second_grad, first_middle, par, lengths, first_ff_pack, *first_saved, second_mixer
    )
    first_mixer, first_vec, first_grad, first_ff = mixer_back(
        0, middle_grad, tokens, late, first_mixer_pack, first_kept, first_ff
    )
    block_outputs, input_grads, *got = finish(
        first_vec, second_vec, first_mixer, second_mixer, first_ff, second_ff, first_grad,
        second_grad, second_value, second_ff_pack, second_middle, first_out, lengths,
    )
    (
        block_outputs, input_grads, sum_in, sum_out, sum_up, sum_down, sum_gain, sum_bias, sum_taps,
        sum_first, sum_second, sum_last, sum_direct,
    ) = unpack(block_outputs, input_grads, got, filter_first.shape[::2])
    return (
        block_outputs[None, :, None],
        input_grads[None, :, None],
        sum_gain[None],
        sum_bias[None],
        sum_in[None],
        jnp.transpose(sum_taps, (1, 0, 2)),
        jnp.transpose(sum_first, (1, 0, 2)),
        sum_second[None],
        sum_last[None],
        sum_direct,
        sum_out[None],
        sum_up[None],
        sum_down[None],
    )


def solution(mesh):
    in_specs = (
        P(None, "dp", "seq", None),
        P(None, "dp", "seq", None),
        P(None, "dp"),
        P("section", None, None),
        P("section", None, None),
        P("section", ("dp", "seq"), None),
        P("section", None, None),
        P("section", None, None),
        P("section", None, None),
        P("section", None, None),
        P("section", None),
        P("section", None),
        P("section", ("dp", "seq"), None),
        P("section", ("dp", "seq"), None),
        P("section", ("dp", "seq"), None),
    )
    out_specs = (
        P("section", None, "dp", "seq", None),
        P("section", None, "dp", "seq", None),
        P("section", None, None),
        P("section", None, None),
        P("section", ("dp", "seq"), None),
        P("section", None, None),
        P("section", None, None),
        P("section", None, None),
        P("section", None, None),
        P("section", None),
        P("section", ("dp", "seq"), None),
        P("section", ("dp", "seq"), None),
        P("section", ("dp", "seq"), None),
    )
    planes = mesh.shape["seq"] == 4 and mesh.shape["dp"] == 4
    per_device = plane_device if planes else any_device
    return jax.shard_map(
        per_device, mesh=mesh, in_specs=in_specs, out_specs=out_specs, check_vma=False
    )
```

```python
from functools import partial
import math

import jax
import jax.numpy as jnp
import numpy as np
from jax import lax
from jax.experimental import pallas as pl
from jax.experimental.pallas import tpu as pltpu
from jax.sharding import PartitionSpec as P

precise = lax.Precision.HIGHEST
low = jnp.bfloat16
f32 = jnp.float32
MESH = pl.DeviceIdType.MESH


def dot(a, b, dims):
    return lax.dot_general(a, b, (dims, ((), ())), preferred_element_type=f32)


def mm(a, b):
    return dot(a, b, ((1,), (0,)))


def mm_t(a, b):
    return dot(a, b, ((1,), (1,)))


def t_mm(a, b):
    return dot(a, b, ((0,), (0,)))


def norm_stats(x):
    mean = jnp.mean(x, axis=-1, keepdims=True)
    centred = x - mean
    inverse = lax.rsqrt(jnp.mean(centred * centred, axis=-1, keepdims=True) + 1e-05)
    return centred * inverse, inverse


def norm_back(grad, x, gain):
    hat, inverse = norm_stats(x)
    scaled = grad * gain
    back = inverse * (
        scaled
        - jnp.mean(scaled, axis=-1, keepdims=True)
        - hat * jnp.mean(scaled * hat, axis=-1, keepdims=True)
    )
    return back, jnp.sum(grad * hat, 0), jnp.sum(grad, 0)


def gelu_both(x):
    scale = math.sqrt(2.0 / math.pi)
    inner = scale * (x + 0.044715 * x * x * x)
    bend = jnp.tanh(inner)
    value = 0.5 * x * (1.0 + bend)
    slope = 0.5 * (1.0 + bend) + 0.5 * x * (1.0 - bend * bend) * scale * (
        1.0 + 3.0 * 0.044715 * x * x
    )
    return value, slope


def position_table(length):
    offsets = jnp.arange(length, dtype=jnp.float32)
    frequencies = jnp.linspace(0.0001, 15.0, 16, dtype=jnp.float32)
    angles = 2.0 * math.pi * offsets[:, None] * frequencies[None, :] / length
    return jnp.concatenate(
        [offsets[:, None] / (length - 1), jnp.cos(angles), -jnp.sin(angles)], axis=1
    )


def position_rows(length):
    offsets = np.arange(length, dtype=np.float32)
    frequencies = np.linspace(0.0001, 15.0, 16, dtype=np.float32)
    angles = np.float32(2.0 * math.pi) * offsets[:, None] * frequencies[None, :] / np.float32(length)
    return np.concatenate(
        [offsets[:, None] / np.float32(length - 1), np.cos(angles), -np.sin(angles)], axis=1
    )


def filter_taps(first_w, second_w, last_w, rates, length):
    embedding = position_table(length)
    hidden = jnp.sin(jnp.dot(embedding, first_w, precision=precise))
    hidden = jnp.sin(jnp.dot(hidden, second_w, precision=precise))
    offsets = jnp.arange(length, dtype=jnp.float32)
    return jnp.dot(hidden, last_w, precision=precise) * jnp.exp(-offsets[:, None] * rates[None, :])


def wave_tables(length):
    turns = (2 * np.arange(length)[:, None] + 1) * np.arange(length)[None, :] % (4 * length)
    angles = turns * (math.pi / (2 * length))
    both = np.concatenate([np.cos(angles), np.sin(angles)], 0)
    return both.astype(jnp.bfloat16)


def shifted(x, by):
    if by > 0:
        return jnp.pad(x[:-by], ((by, 0), (0, 0)))
    return jnp.pad(x[-by:], ((0, -by), (0, 0)))


def neighbours(me):
    return (me + 1 - 2 * (me % 2), (me + 2) % 4, 3 - me)


def greet(devices):
    barrier = pltpu.get_barrier_semaphore()
    for device in devices:
        pl.semaphore_signal(barrier, inc=1, device_id=device, device_id_type=MESH)
    return len(devices)


def all_here(greeted):
    pl.semaphore_wait(pltpu.get_barrier_semaphore(), greeted)


def in_plane(peers):
    return [{"seq": peer} for peer in peers]


def along_planes():
    here = lax.axis_index("dp")
    return here, here + 1 - 2 * (here % 2), (here + 2) % 4


def other_core():
    return {"section": 1 - lax.axis_index("section")}


def plane_devices():
    _, near, far = along_planes()
    return [{"dp": near}, {"dp": far}]


def add_low(target, source):
    def add(at):
        target[at, :] = (target[at, :].astype(f32) + source[at, :].astype(f32)).astype(low)

    by_rows(target.shape[0], 32, add)


def swap_begin(pairs, core_sems):
    section = lax.axis_index("section")
    copies = [
        remote_to(made.at[1 - section], other, core_sems, at, other_core())
        for at, (made, other) in enumerate(pairs)
    ]
    for copy in copies:
        copy.start()
    return copies


def swap_end(copies, pairs):
    section = lax.axis_index("section")
    for copy, (made, other) in zip(copies, pairs):
        copy.wait_recv()
        for block in range(other.shape[0]):
            add_low(made.at[section, block], other.at[block])


class PlaneSum:
    def __init__(self, pack, mine, arrived, sems, load_sems):
        self.here, self.near, self.far = along_planes()
        self.pack, self.mine, self.arrived = pack, mine, arrived
        self.sems, self.load_sems = sems, load_sems

    def begin(self):
        self.sends = [
            remote_to(self.pack.at[block], self.arrived.at[slot], self.sems, slot, {"dp": self.near})
            for slot, block in enumerate(((self.near + 2) % 4, self.near))
        ]
        for copy in self.sends:
            copy.start()
        self.loads = fetch(
            [(self.pack.at[self.far], self.mine.at[0]), (self.pack.at[self.here], self.mine.at[1])],
            self.load_sems,
        )

    def forward(self):
        self.loads[0].wait()
        self.sends[0].wait_recv()
        add_low(self.mine.at[0], self.arrived.at[0])
        copy = remote_to(self.mine.at[0], self.arrived.at[2], self.sems, 2, {"dp": self.far})
        copy.start()
        self.sends.append(copy)

    def end(self, result):
        self.loads[1].wait()
        self.sends[1].wait_recv()
        self.sends[2].wait_recv()

        def add(at):
            total = self.mine[1, at, :].astype(f32)
            for slot in (1, 2):
                total = total + self.arrived[slot, at, :].astype(f32)
            result[at, :] = total.astype(low)

        by_rows(result.shape[0], 32, add)


def plane_sum_scratch(half_pack):
    _, rows, cols = half_pack.shape
    return [
        pltpu.VMEM((2, rows, cols), low),
        pltpu.VMEM((3, rows, cols), low),
        pltpu.SemaphoreType.DMA((2, 3)),
        pltpu.SemaphoreType.DMA((2,)),
    ]


def remote_to(source, target, sems, slot, device):
    return pltpu.make_async_remote_copy(
        src_ref=source,
        dst_ref=target,
        send_sem=sems.at[0, slot],
        recv_sem=sems.at[1, slot],
        device_id=device,
        device_id_type=MESH,
    )


def remote(source, target, sems, slot, peer):
    return remote_to(source, target, sems, slot, {"seq": peer})


def rows_of(index, count):
    return pl.ds(pl.multiple_of(index * count, count), count)


def half_of(ref, index, part, count):
    half = count // 2
    return ref.at[pl.ds(pl.multiple_of(index * count + part * half, half), half)]


def gather_begin(gather, sems, me, peers, count):
    x, y, _ = peers
    first, second = half_of(gather, me, 0, count), half_of(gather, me, 1, count)
    copies = [
        remote(first, first, sems, 0, x),
        remote(second, second, sems, 2, y),
        remote(second, second, sems, 1, x),
        remote(first, first, sems, 3, y),
    ]
    for copy in copies:
        copy.start()
    return copies


def gather_forward(gather, sems, peers, count):
    x, y, _ = peers
    from_x, from_y = half_of(gather, x, 0, count), half_of(gather, y, 1, count)
    remote(from_x, from_x, sems, 0, x).wait_recv()
    onward = remote(from_x, from_x, sems, 4, y)
    onward.start()
    remote(from_y, from_y, sems, 2, y).wait_recv()
    across = remote(from_y, from_y, sems, 5, x)
    across.start()
    return [onward, across]


def gather_wait(gather, sems, slot, peers, count):
    for part, at in (((1, 1),), ((0, 3),), ((0, 4), (1, 5)))[slot]:
        block = half_of(gather, peers[slot], part, count)
        remote(block, block, sems, at, peers[slot]).wait_recv()


HALF_ORDER = ((0, 0), (1, 1), (0, 1), (1, 0), (2, 0), (2, 1))


def half_rows(index, part, count):
    half = count // 2
    return pl.ds(pl.multiple_of(index * count + part * half, half), half)


def gather_wait_half(gather, sems, slot, part, peers, count):
    at = {(0, 1): 1, (1, 0): 3, (2, 0): 4, (2, 1): 5}.get((slot, part))
    if at is not None:
        block = half_of(gather, peers[slot], part, count)
        remote(block, block, sems, at, peers[slot]).wait_recv()


def reduce_send_half(slot, part, send, recv, sems, peers):
    half = send.shape[1] // 2
    quarter = half // 2
    plan = {
        (0, 0): [(0, half, 0, 0)],
        (1, 1): [(half, half, 1, 1)],
        (2, 0): [(0, quarter, 2, 0), (quarter, quarter, 3, 0)],
        (2, 1): [(half, quarter, 4, 1), (half + quarter, quarter, 5, 1)],
    }.get((slot, part), [])
    copies = [
        remote(
            send.at[slot, pl.ds(start, size)], recv.at[slot, pl.ds(start, size)], sems, at,
            peers[to],
        )
        for start, size, at, to in plan
    ]
    for copy in copies:
        copy.start()
    return copies


def reduce_send(slot, send, recv, sems, peers):
    x, y, _ = peers
    half = send.shape[1] // 2
    quarter = half // 2
    if slot == 2:
        plan = [(0, quarter, 2, x), (half, quarter, 4, y), (quarter, quarter, 3, x)]
        plan.append((half + quarter, quarter, 5, y))
    else:
        plan = [(slot * half, half, slot, (x, y)[slot])]
    copies = [
        remote(
            send.at[slot, pl.ds(start, size)], recv.at[slot, pl.ds(start, size)], sems, at, peer
        )
        for start, size, at, peer in plan
    ]
    for copy in copies:
        copy.start()
    return copies


def reduce_pass(send, recv, sems, peers):
    x, y, _ = peers
    half = send.shape[1] // 2
    quarter = half // 2
    copies = []
    for start, at, source, slot, peer in (
        (half, 4, y, 0, x),
        (0, 2, x, 1, y),
        (half + quarter, 5, y, 0, x),
        (quarter, 3, x, 1, y),
    ):
        rows = pl.ds(start, quarter)
        remote(send.at[2, rows], recv.at[2, rows], sems, at, source).wait_recv()
        add_low(send.at[slot, rows], recv.at[2, rows])
        copy = remote(send.at[slot, rows], recv.at[slot, rows], sems, at + 4, peer)
        copy.start()
        copies.append(copy)
    return copies


def reduce_wait(send, recv, sems, peers):
    x, y, _ = peers
    half = send.shape[1] // 2
    quarter = half // 2
    for slot, start, size, at, peer in (
        (0, 0, half, 0, x),
        (1, half, half, 1, y),
        (0, half, quarter, 8, x),
        (1, 0, quarter, 6, y),
        (0, half + quarter, quarter, 9, x),
        (1, quarter, quarter, 7, y),
    ):
        rows = pl.ds(start, size)
        remote(send.at[slot, rows], recv.at[slot, rows], sems, at, peer).wait_recv()


def by_rows(total, step, body):
    def run(i, carry):
        body(pl.ds(pl.multiple_of(i * step, step), step))
        return carry

    lax.fori_loop(0, total // step, run, 0)


def valid_rows(lengths, start, count):
    at = lax.broadcasted_iota(jnp.int32, (count, 1), 0) + start
    return (at < lengths[0, lax.axis_index("section")]).astype(f32)


def normed_rows(x, gain, shift):
    mean = jnp.mean(x, axis=-1, keepdims=True)
    centred = x - mean
    inverse = lax.rsqrt(jnp.mean(centred * centred, axis=-1, keepdims=True) + 1e-05)
    return centred * inverse * gain + shift


def norm_back_rows(grad, x, gain):
    mean = jnp.mean(x, axis=-1, keepdims=True)
    centred = x - mean
    inverse = lax.rsqrt(jnp.mean(centred * centred, axis=-1, keepdims=True) + 1e-05)
    hat = centred * inverse
    scaled = grad * gain
    back = inverse * (
        scaled
        - jnp.mean(scaled, axis=-1, keepdims=True)
        - hat * jnp.mean(scaled * hat, axis=-1, keepdims=True)
    )
    return back, jnp.sum(grad * hat, axis=0, keepdims=True), jnp.sum(grad, axis=0, keepdims=True)


def norm_into(gather, start, x, gain, shift):
    step = 32

    def body(i, carry):
        rows = pl.ds(pl.multiple_of(i * step, step), step)
        at = pl.ds(pl.multiple_of(start + i * step, step), step)
        gather[at, :] = normed_rows(x[rows, :].astype(f32), gain, shift).astype(low)
        return carry

    lax.fori_loop(0, x.shape[0] // step, body, 0)


def masked_into(gather, start, grad, lengths):
    step = 32

    def body(i, carry):
        rows = pl.ds(pl.multiple_of(i * step, step), step)
        at = pl.ds(pl.multiple_of(start + i * step, step), step)
        value = grad[rows, :].astype(f32) * valid_rows(lengths, start + i * step, step)
        gather[at, :] = value.astype(low)
        return carry

    lax.fori_loop(0, grad.shape[0] // step, body, 0)


def add_parts(own, recv, x, start, lengths):
    def body(rows):
        total = own[rows, :] + recv[0, rows, :].astype(f32) + recv[1, rows, :].astype(f32)
        mask = valid_rows(lengths, start + rows.start, 32)
        own[rows, :] = x[rows, :].astype(f32) + mask * total

    by_rows(own.shape[0], 32, body)


def norm_back_parts(own, recv, grad, x, gain, sums):
    sums[...] = jnp.zeros(sums.shape, f32)

    def body(rows):
        total = own[rows, :] + recv[0, rows, :].astype(f32) + recv[1, rows, :].astype(f32)
        back, gain_sum, shift_sum = norm_back_rows(total, x[rows, :].astype(f32), gain)
        own[rows, :] = grad[rows, :].astype(f32) + back
        sums[0:1, :] += gain_sum
        sums[1:2, :] += shift_sum

    by_rows(own.shape[0], 32, body)


def fetch(pairs, sems, first=0):
    copies = [
        pltpu.make_async_copy(source, target, sems.at[first + at])
        for at, (source, target) in enumerate(pairs)
    ]
    for copy in copies:
        copy.start()
    return copies


def weight_pairs_mixer(pack, win, wout):
    rows, cols = wout.shape[2], wout.shape[3] // 4
    split = win.shape[3]
    pairs = [(pack.at[:, :, :, pl.ds(0, split)], win)]
    for q in range(4):
        pairs.append(
            (
                pack.at[:, :, pl.ds(q * rows, rows), pl.ds(split, cols)],
                wout.at[:, :, :, pl.ds(q * cols, cols)],
            )
        )
    return pairs


def half_pairs_mixer(half_pack, win, wout):
    rows, cols = wout.shape[2], wout.shape[3] // 4
    split = win.shape[3]
    section = lax.axis_index("section")
    pairs = [(win.at[section], half_pack.at[:, :, pl.ds(0, split)])]
    for q in range(4):
        pairs.append(
            (
                wout.at[section, :, :, pl.ds(q * cols, cols)],
                half_pack.at[:, pl.ds(q * rows, rows), pl.ds(split, cols)],
            )
        )
    return pairs


class ChipGather:
    def __init__(self, own, pack, plane_sems, core_sems):
        self.section = lax.axis_index("section")
        here, near, far = along_planes()
        self.pack, self.plane_sems, self.core_sems = pack, plane_sems, core_sems
        self.near, self.far = near, far
        self.order = (here, near, far, (near + 2) % 4)
        self.own = own
        self.sends = []

    def move(self, at, sems, slot, device):
        block = self.pack.at[self.section, self.order[at]]
        copy = remote_to(self.own if at == 0 else block, block, sems, slot, device)
        copy.start()
        self.sends.append(copy)

    def to_core(self, slot):
        self.move(slot, self.core_sems, slot, other_core())

    def begin(self, load_sem):
        self.move(0, self.plane_sems, 1, {"dp": self.far})
        self.move(0, self.plane_sems, 0, {"dp": self.near})
        self.to_core(0)
        self.keep = pltpu.make_async_copy(
            self.own, self.pack.at[self.section, self.order[0]], load_sem
        )
        self.keep.start()

    def arrived(self, slot):
        block = self.pack.at[self.section, self.order[slot + 1]]
        remote_to(block, block, self.plane_sems, slot, {"dp": self.near}).wait_recv()

    def forward(self):
        self.arrived(1)
        self.move(2, self.plane_sems, 2, {"dp": self.near})
        self.to_core(2)
        self.arrived(0)
        self.to_core(1)

    def end(self):
        self.arrived(2)
        self.to_core(3)
        self.keep.wait()
        for slot in range(4):
            block = self.pack.at[1 - self.section, self.order[slot]]
            remote_to(block, block, self.core_sems, slot, other_core()).wait_recv()


def sine_pair(x):
    turns = jnp.floor(x * (2.0 / math.pi) + 0.5)
    rest = x - turns * 1.5703125
    rest = rest - turns * 4.837512969970703125e-4
    rest = rest - turns * 7.54978995489188e-8
    square = rest * rest
    sine = -1.9515295891e-4 * square + 8.3321608736e-3
    sine = (sine * square - 1.6666654611e-1) * square * rest + rest
    cosine = 2.443315711809948e-5 * square - 1.388731625493765e-3
    cosine = (cosine * square + 4.166664568298827e-2) * square * square - 0.5 * square + 1.0
    halves = jnp.floor(turns * 0.5)
    odd = turns - 2.0 * halves
    back = halves - 2.0 * jnp.floor(halves * 0.5)
    swapped = odd > 0.5
    side = 1.0 - 2.0 * back
    wave = jnp.where(swapped, cosine, sine) * side
    slope = jnp.where(swapped, -sine, cosine) * side
    return wave, slope


def network_rows(small, embedding, network, taps_low, i):
    step = 256
    waves1, waves2, steep1, steep2 = network
    knots = waves1.shape[1]
    pair = (pl.ds(i * step, step), pl.ds(embedding.shape[0] // 2 + i * step, step))

    def layer(sources, weights, waves, steep):
        inner = jnp.concatenate([dot_exact(item, weights) for item in sources], 1)
        wave, slope = sine_pair(inner)
        for at, rows in enumerate(pair):
            cols = slice(at * knots, (at + 1) * knots)
            waves[rows, :] = wave[:, cols]
            steep[rows, :] = slope[:, cols]

    layer([embedding[rows, 0:64] for rows in pair], small[64:128, 128:192], waves1, steep1)
    layer([waves1[rows, :] for rows in pair], small[64:128, 0:64], waves2, steep2)
    for rows in pair:
        times = lax.broadcasted_iota(jnp.int32, (step, 1), 0) + rows.start
        fade = jnp.exp(-times.astype(f32) * small[154:155, :])
        taps_low[rows, :] = (dot_exact(waves2[rows, :], small[0:64, :]) * fade).astype(low)


def ff_blocks(
    gather, wup, wdown, value, slope, result_out, send, recv, gather_sems, reduce_sems, me, peers,
    pause,
):
    count, width = result_out.shape
    half = wup.shape[3]
    sends = []
    for slot, part in ((None, None), *HALF_ORDER):
        if slot is None:
            rows, sent = rows_of(me, count), None
        else:
            rows = half_rows(peers[slot], part, count)
            sent = slice(part * count // 2, (part + 1) * count // 2)
            gather_wait_half(gather, gather_sems, slot, part, peers, count)

        def hidden(i, carry):
            cols = pl.ds(pl.multiple_of(i * 256, 256), 256)
            for h in range(2):
                pre = mm(gather[rows, :], wup[h, :, :, cols].reshape(width, 256))
                after, steep = gelu_both(pre)
                at = pl.ds(pl.multiple_of(h * half + i * 256, 256), 256)
                value[rows, at] = after.astype(low)
                slope[rows, at] = steep.astype(low)
            return carry

        lax.fori_loop(0, half // 256, hidden, 0)
        for h in range(2):
            cols = slice(h * width // 2, (h + 1) * width // 2)
            out = mm(value[rows, :], wdown[h].reshape(2 * half, width // 2))
            if slot is None:
                result_out[:, cols] = out
            else:
                send[slot, sent, cols] = out.astype(low)
        if slot is not None:
            sends += reduce_send_half(slot, part, send, recv, reduce_sems, peers)
            pause(slot, part)
    return sends


def mixer_forward_kernel(
    s, gathers, x, *refs
):
    if gathers:
        (
            cotangent, embedding, lengths, w_in, w_out, w_up, w_down, gain, shift, tap_rows, first_w,
            second_w, last_w, direct, rates, waves_hbm, back_hbm,
            pack_out, ff_out, late_out, par_out, small_out, next_pack_out, ff_part_out,
            *refs,
        ) = refs
        network_outs, next_outs, refs = refs[:5], refs[5:10], refs[10:]
        second_out, value_out, slope_out, result_out, *refs = refs
        (
            *refs, waves1, waves2, steep1, steep2, taps_low, raw_out, ff_all, late, next_pack, core_sems,
            plane_sems, out_core_sems, out_plane_sems, ff_core_sems, ff_plane_sems, next_core_sems, next_plane_sems, late_sems,
            pack_sems, mixer_parts, ff_parts, par_all, small_all, stage_in, stage_out, stage_up,
            in_sems, out_sems, up_sems, down_sems, par_sems, small_sems,
            second, ff_send, ff_recv, second_sems, ff_sems, network_sems,
        ) = refs
        x = x.at[lax.axis_index("section"), 0]
        cotangent = cotangent.at[lax.axis_index("section"), 0]
        network = (waves1, waves2, steep1, steep2)
    else:
        par_all, small_all, lengths, weights_hbm, filt_hbm, waves_hbm, back_hbm, *refs = refs
    (
        normed_out, proj_out, stream_out, prod_out, spec_out, filtered_out, gated_out, middle_out,
        gather, win, wout, filt, waves, back, proj, proj_low, streams, prod, spec, mixed, filtered,
        gated, send, recv, gather_sems, reduce_sems, load_sems, store_sems,
    ) = refs
    par, small = par_all.at[s], small_all.at[s]
    me = lax.axis_index("seq")
    peers = neighbours(me)
    count, width = x.shape
    length = gather.shape[0]
    chans = prod.shape[1]
    half = win.shape[3]
    if gathers:
        section = lax.axis_index("section")
        targets = shuffle_targets(section, me, peers)
        greeted = greet([device for _, _, device in targets] + plane_devices())
    else:
        greeted = greet(in_plane(peers[:2]))
    tables = fetch([(waves_hbm, waves), (back_hbm, back)], load_sems)
    sends = []
    if gathers:
        shuffle_stage(w_in, w_out, w_up, stage_in, stage_out, stage_up)
        parameters_stage(
            me, par_all.at[section], small_all.at[section], gain, shift, tap_rows, first_w, second_w,
            last_w, direct, rates,
        )
        all_here(greeted)
        sends += shuffle_send(
            section, me, targets, (stage_in, stage_out, stage_up, w_down), (mixer_parts, ff_parts),
            (par_all, small_all), (in_sems, out_sems, up_sems, down_sems, par_sems, small_sems),
        )
        in_cols, out_cols = pl.ds(0, half), pl.ds(half, raw_out.shape[3])
        in_pack = ChipGather(mixer_parts.at[0, :, in_cols], win, plane_sems, core_sems)
        out_pack = ChipGather(mixer_parts.at[0, :, out_cols], raw_out, out_plane_sems, out_core_sems)
        ff_pack = ChipGather(ff_parts.at[0], ff_all, ff_plane_sems, ff_core_sems)
        for sems, item in ((par_sems, par_all), (small_sems, small_all)):
            block = item.at[1 - section]
            remote_to(block, block, sems, 0, other_core()).wait_recv()
        norm_into(gather, me * count, x, par[0:1, :], par[1:2, :])
        shuffle_wait_mixer(section, me, targets, mixer_parts, stage_in, in_sems, out_sems)
        in_pack.begin(pack_sems.at[0])
        sends += gather_begin(gather, gather_sems, me, peers, count)
        masked_into(late, me * count, cotangent, lengths)
    else:
        weights = fetch(weight_pairs_mixer(weights_hbm, win, wout), load_sems, 2)
        filt_load = fetch([(filt_hbm, filt)], load_sems, 7)
        norm_into(gather, me * count, x, par[0:1, :], par[1:2, :])
        all_here(greeted)
        sends += gather_begin(gather, gather_sems, me, peers, count)
    proj[0:8, :] = jnp.zeros((8, proj.shape[1]), f32)
    tile_rows = 256

    def filter_spectrum(i, carry):
        rows = pl.ds(pl.multiple_of(i * tile_rows, tile_rows), tile_rows)
        filt[rows, :] = mm(waves[rows, :], taps_low[...])
        return carry

    stores = []
    if gathers:
        network_rows(small, embedding, network, taps_low, 0)
    sends += gather_forward(gather, gather_sems, peers, count)
    if gathers:
        sends += gather_begin(late, late_sems, me, peers, count)
        in_pack.forward()
        out_pack.begin(pack_sems.at[13])
        network_rows(small, embedding, network, taps_low, 1)
        tables[0].wait()
        lax.fori_loop(0, 2 * length // tile_rows, filter_spectrum, 0)
        network_stores = fetch(list(zip((filt, *network), network_outs)), network_sems)
        out_pack.forward()
        shuffle_wait_ff(section, me, targets, ff_parts, stage_up, up_sems, down_sems)
        ff_pack.begin(pack_sems.at[1])
        in_pack.end()
        stores += fetch(
            [
                (win, pack_out.at[:, :, :, in_cols]),
                (par_all, par_out),
                (small_all, small_out),
                (ff_parts.at[1], ff_part_out),
            ],
            pack_sems,
            4,
        )
    else:
        tables[0].wait()
    if not gathers:
        weights[0].wait()
    step = 64
    steps = count // step

    def short_conv(start):
        for g in range(3):
            cols = slice(g * chans, (g + 1) * chans)
            tile = proj[pl.ds(start, step + 8), cols]
            proj_low[pl.ds(start, step), cols] = tile[8:].astype(low)
            value = (
                small[144 + 3 * g : 145 + 3 * g, :] * tile[8:]
                + small[145 + 3 * g : 146 + 3 * g, :] * pltpu.roll(tile, 1, 0)[8:]
                + small[146 + 3 * g : 147 + 3 * g, :] * pltpu.roll(tile, 2, 0)[8:]
            )
            streams[pl.ds(start, step), cols] = value.astype(low)
        first = streams[pl.ds(start, step), 0:chans].astype(f32)
        third = streams[pl.ds(start, step), 2 * chans : 3 * chans].astype(f32)
        prod[pl.ds(start, step), :] = (first * third * valid_rows(lengths, start, step)).astype(low)

    def within(source):
        def body(i, carry):
            short_conv(pl.multiple_of(source * count + i * step, step))
            return carry

        lax.fori_loop(1, steps, body, 0)

    for slot in (None, 0, 1, 2):
        source = me if slot is None else peers[slot]
        if slot is not None:
            gather_wait(gather, gather_sems, slot, peers, count)
        block = gather[rows_of(source, count), :]
        for h in range(2):
            proj[pl.ds(pl.multiple_of(source * count + 8, 8), count), h * half : (h + 1) * half] = mm(
                block, win[h].reshape(width, half)
            )
        within(source)
    if gathers:
        sends += gather_forward(late, late_sems, peers, count)

    def seams(i, carry):
        short_conv(pl.multiple_of(i * count, step))
        return carry

    lax.fori_loop(0, length // count, seams, 0)
    stores += fetch(
        [(gather, normed_out), (proj_low, proj_out), (streams, stream_out), (prod, prod_out)],
        store_sems,
    )
    if not gathers:
        filt_load[0].wait()

    def spectrum(i, carry):
        up = pl.ds(pl.multiple_of(i * tile_rows, tile_rows), tile_rows)
        down = pl.ds(pl.multiple_of(i * tile_rows + length, tile_rows), tile_rows)
        prod_cos = mm(waves[up, :], prod[...])
        prod_sin = mm(waves[down, :], prod[...])
        filt_cos, filt_sin = filt[up, :], filt[down, :]
        spec[up, :] = prod_cos.astype(low)
        spec[down, :] = prod_sin.astype(low)
        mixed[up, :] = (prod_cos * filt_cos - prod_sin * filt_sin).astype(low)
        mixed[down, :] = (prod_cos * filt_sin + prod_sin * filt_cos).astype(low)
        return carry

    lax.fori_loop(0, length // tile_rows, spectrum, 0)
    tables[1].wait()
    if gathers:
        out_pack.end()
        cols = raw_out.shape[3]
        weights = fetch(
            [
                (
                    raw_out.at[:, :, pl.ds(q * wout.shape[2], wout.shape[2]), :],
                    wout.at[:, :, :, pl.ds(q * cols, cols)],
                )
                for q in range(4)
            ],
            load_sems,
            3,
        )
        stores += fetch([(raw_out, pack_out.at[:, :, :, out_cols])], pack_sems, 14)
        for load in weights:
            load.wait()
    else:
        for load in weights[1:]:
            load.wait()
    for slot in (2, 0, 1, None):
        target = me if slot is None else peers[slot]
        rows = rows_of(target, count)
        value = mm(back[rows, :], mixed[...]) * (1.0 / length)
        value = value + small[153:154, :] * prod[rows, :].astype(f32)
        filtered[rows, :] = value
        gate = (streams[rows, chans : 2 * chans].astype(f32) * value).astype(low)
        gated[rows, :] = gate
        outs = [mm(gate, wout[h].reshape(chans, width // 2)) for h in range(2)]
        for h in range(2):
            cols = slice(h * width // 2, (h + 1) * width // 2)
            if slot is None:
                middle_out[:, cols] = outs[h]
            else:
                send[slot, :, cols] = outs[h].astype(low)
        if slot is not None:
            sends += reduce_send(slot, send, recv, reduce_sems, peers)
    if gathers:
        ff_pack.forward()
        for slot in range(3):
            gather_wait(late, late_sems, slot, peers, count)
        stores += fetch([(late, late_out)], pack_sems, 2)
    sends += reduce_pass(send, recv, reduce_sems, peers)
    stores += fetch(
        [(spec, spec_out), (filtered, filtered_out), (gated, gated_out)],
        store_sems,
        4,
    )
    if gathers:
        for store in network_stores:
            store.wait()
        for i in range(2):
            network_rows(small_all.at[1], embedding, network, taps_low, i)
        lax.fori_loop(0, 2 * length // tile_rows, filter_spectrum, 0)
        network_stores = fetch(list(zip((filt, *network), next_outs)), network_sems)
    reduce_wait(send, recv, reduce_sems, peers)
    add_parts(middle_out, recv, x, me * count, lengths)
    if gathers:
        next_mixer = ChipGather(mixer_parts.at[1], next_pack, next_plane_sems, next_core_sems)
        norm_into(second, me * count, middle_out, par[2:3, :], par[3:4, :])
        sends += gather_begin(second, second_sems, me, peers, count)
        sends += gather_forward(second, second_sems, peers, count)
        ff_pack.end()
        next_mixer.begin(pack_sems.at[8])
        stores += fetch([(ff_all, ff_out)], pack_sems, 3)
        rows_up = ff_all.shape[2] // 2
        value, slope = waves.at[pl.ds(0, length)], waves.at[pl.ds(length, length)]

        def pause(slot, part):
            if (slot, part) == (1, 1):
                next_mixer.forward()

        sends += ff_blocks(
            second, ff_all.at[:, :, pl.ds(0, rows_up)], ff_all.at[:, :, pl.ds(rows_up, rows_up)],
            value, slope, result_out, ff_send, ff_recv, second_sems, ff_sems, me, peers, pause,
        )
        sends += reduce_pass(ff_send, ff_recv, ff_sems, peers)
        stores += fetch([(second, second_out), (value, value_out), (slope, slope_out)], pack_sems, 9)
        next_mixer.end()
        stores += fetch([(next_pack, next_pack_out)], pack_sems, 12)
        reduce_wait(ff_send, ff_recv, ff_sems, peers)
        add_parts(result_out, ff_recv, middle_out, me * count, lengths)
        sends += in_pack.sends + out_pack.sends + ff_pack.sends + next_mixer.sends
        stores += network_stores
    for copy in sends:
        copy.wait_send()
    for store in stores:
        store.wait()


def ff_turn_kernel(
    s, cotangent, x, par_all, lengths, pack, late_hbm,
    half_out, value_out, middle_grad_out, sums_out,
    gather, late, wup, wdown, value, pre, wgrad, other, send_back, recv_back,
    gather_sems, back_sems, load_sems, store_sems, core_sems,
):
    par = par_all.at[s]
    grad = cotangent.at[lax.axis_index("section"), 0]
    me = lax.axis_index("seq")
    peers = neighbours(me)
    count, width = x.shape
    half = wup.shape[3]
    rows_up = wup.shape[2]
    greeted = greet(in_plane(peers[:2]) + [other_core()])
    loads = fetch(
        [
            (pack.at[:, :, pl.ds(0, rows_up), :], wup),
            (pack.at[:, :, pl.ds(rows_up, wdown.shape[2]), :], wdown),
            (late_hbm, late),
        ],
        load_sems,
    )
    norm_into(gather, me * count, x, par[2:3, :], par[3:4, :])
    all_here(greeted)
    sends = gather_begin(gather, gather_sems, me, peers, count)
    for load in loads:
        load.wait()
    for slot, part in ((None, None), *HALF_ORDER):
        if slot is None:
            rows, sent = rows_of(me, count), None
        else:
            rows = half_rows(peers[slot], part, count)
            sent = slice(part * count // 2, (part + 1) * count // 2)
            gather_wait_half(gather, gather_sems, slot, part, peers, count)

        def hidden(i, carry):
            cols = pl.ds(pl.multiple_of(i * rows_up, rows_up), rows_up)
            for h in range(2):
                block = h * (half // rows_up) + i
                at = pl.ds(pl.multiple_of(block * rows_up, rows_up), rows_up)
                after, steep = gelu_both(
                    mm(gather[rows, :], wup[h, :, :, cols].reshape(width, rows_up))
                )
                value[rows, at] = after.astype(low)
                back = mm_t(late[rows, : width // 2], wdown[0, block]) + mm_t(
                    late[rows, width // 2 :], wdown[1, block]
                )
                pre[rows, at] = (back * steep).astype(low)
            return carry

        lax.fori_loop(0, half // rows_up, hidden, 0)

        def through(i, carry):
            cols = pl.ds(pl.multiple_of(i * rows_up, rows_up), rows_up)
            back = mm_t(pre[rows, :half], wup[0, i]) + mm_t(pre[rows, half:], wup[1, i])
            if slot is None:
                middle_grad_out[:, cols] = back
            else:
                send_back[slot, sent, cols] = back.astype(low)
            return carry

        lax.fori_loop(0, width // rows_up, through, 0)
        if slot is None:
            sends += gather_forward(gather, gather_sems, peers, count)
        else:
            sends += reduce_send_half(slot, part, send_back, recv_back, back_sems, peers)
    stores = fetch([(value, value_out)], store_sems, 1)

    def weights(i, carry):
        cols = pl.ds(pl.multiple_of(i * rows_up, rows_up), rows_up)
        for h in range(2):
            wgrad[h, i, 0:rows_up, :] = t_mm(
                gather[:, cols], pre[:, h * half : (h + 1) * half]
            ).astype(low)
            wgrad[h, i, rows_up : 2 * rows_up, :] = t_mm(
                value[:, cols], late[:, h * width // 2 : (h + 1) * width // 2]
            ).astype(low)
        return carry

    middle = width // rows_up // 2
    early, late_part = pl.ds(0, middle), pl.ds(middle, middle)
    lax.fori_loop(0, middle, weights, 0)
    swapped = [(wgrad.at[:, early], other.at[early])]
    swaps = swap_begin(swapped, core_sems.at[0])
    sends += reduce_pass(send_back, recv_back, back_sems, peers)
    lax.fori_loop(middle, 2 * middle, weights, 0)
    swapped_late = [(wgrad.at[:, late_part], other.at[late_part])]
    swaps_late = swap_begin(swapped_late, core_sems.at[1])
    sends += swaps + swaps_late
    swap_end(swaps, swapped)
    reduce_wait(send_back, recv_back, back_sems, peers)
    norm_back_parts(middle_grad_out, recv_back, grad, x, par[2:3, :], sums_out)
    swap_end(swaps_late, swapped_late)
    stores += fetch([(wgrad.at[lax.axis_index("section")], half_out)], store_sems)
    for copy in sends:
        copy.wait_send()
    for store in stores:
        store.wait()


def ff_backward_kernel(
    s, grad, middle, par_all, lengths, pack, second_hbm, value_hbm, slope_hbm, earlier,
    half_out, middle_grad_out, sums_out, summed,
    gather, wup, wdown, second, value, slope, pre, wgrad, other, send, recv, gather_sems,
    reduce_sems, load_sems, store_sems, mine, arrived, plane_sems, sum_sems, core_sems,
):
    par = par_all.at[s]
    me = lax.axis_index("seq")
    peers = neighbours(me)
    count, width = grad.shape
    greeted = greet(in_plane(peers[:2]) + plane_devices() + [other_core()])
    half = wup.shape[3]
    units = 2 * half
    up_rows = wup.shape[2]
    loads = fetch(
        [
            (pack.at[:, :, pl.ds(0, up_rows), :], wup),
            (pack.at[:, :, pl.ds(up_rows, wdown.shape[2]), :], wdown),
            (slope_hbm, slope),
            (second_hbm, second),
            (value_hbm, value),
        ],
        load_sems,
    )
    masked_into(gather, me * count, grad, lengths)
    all_here(greeted)
    sends = gather_begin(gather, gather_sems, me, peers, count)
    plane_sum = PlaneSum(earlier, mine, arrived, plane_sems, sum_sems)
    plane_sum.begin()
    for load in loads[:3]:
        load.wait()
    for slot, part in ((None, None), *HALF_ORDER):
        if slot is None:
            rows, sent = rows_of(me, count), None
        else:
            rows = half_rows(peers[slot], part, count)
            sent = slice(part * count // 2, (part + 1) * count // 2)
            gather_wait_half(gather, gather_sems, slot, part, peers, count)

        def hidden(i, carry):
            cols = pl.ds(pl.multiple_of(i * up_rows, up_rows), up_rows)
            back = mm_t(gather[rows, : width // 2], wdown[0, i]) + mm_t(
                gather[rows, width // 2 :], wdown[1, i]
            )
            pre[rows, cols] = (back * slope[rows, cols].astype(f32)).astype(low)
            return carry

        lax.fori_loop(0, units // up_rows, hidden, 0)

        def through(i, carry):
            cols = pl.ds(pl.multiple_of(i * up_rows, up_rows), up_rows)
            back = mm_t(pre[rows, :half], wup[0, i]) + mm_t(pre[rows, half:], wup[1, i])
            if slot is None:
                middle_grad_out[:, cols] = back
            else:
                send[slot, sent, cols] = back.astype(low)
            return carry

        lax.fori_loop(0, width // up_rows, through, 0)
        if slot is None:
            sends += gather_forward(gather, gather_sems, peers, count)
        else:
            sends += reduce_send_half(slot, part, send, recv, reduce_sems, peers)
    plane_sum.forward()
    for load in loads[3:]:
        load.wait()

    def weights(i, carry):
        cols = pl.ds(pl.multiple_of(i * up_rows, up_rows), up_rows)
        for h in range(2):
            wgrad[h, i, 0:up_rows, :] = t_mm(
                second[:, cols], pre[:, h * half : (h + 1) * half]
            ).astype(low)
            wgrad[h, i, up_rows : 2 * up_rows, :] = t_mm(
                value[:, cols], gather[:, h * width // 2 : (h + 1) * width // 2]
            ).astype(low)
        return carry

    half_blocks = width // up_rows // 2
    early, late_part = pl.ds(0, half_blocks), pl.ds(half_blocks, half_blocks)
    lax.fori_loop(0, half_blocks, weights, 0)
    swapped = [(wgrad.at[:, early], other.at[early])]
    swaps = swap_begin(swapped, core_sems.at[0])
    sends += reduce_pass(send, recv, reduce_sems, peers)
    lax.fori_loop(half_blocks, 2 * half_blocks, weights, 0)
    swapped_late = [(wgrad.at[:, late_part], other.at[late_part])]
    swaps_late = swap_begin(swapped_late, core_sems.at[1])
    sends += swaps + swaps_late
    plane_sum.end(summed)
    sends += plane_sum.sends
    swap_end(swaps, swapped)
    swap_end(swaps_late, swapped_late)
    stores = fetch([(wgrad.at[lax.axis_index("section")], half_out)], store_sems)
    reduce_wait(send, recv, reduce_sems, peers)
    norm_back_parts(middle_grad_out, recv, grad, middle, par[2:3, :], sums_out)
    for copy in sends:
        copy.wait_send()
    for store in stores:
        store.wait()


def t_mm_exact(a, b):
    return lax.dot_general(
        a, b, (((0,), (0,)), ((), ())), preferred_element_type=f32, precision=precise
    )


def mm_t_exact(a, b):
    return lax.dot_general(
        a, b, (((1,), (1,)), ((), ())), preferred_element_type=f32, precision=precise
    )


def dot_exact(a, b):
    return jnp.dot(a, b, preferred_element_type=f32, precision=precise)


def by_layer(begin, triples, layer_sems, keep_sems, base=0):
    section = lax.axis_index("section")
    for index in range(2):

        @pl.when(section == index)
        def _():
            for at, (first, second, target) in enumerate(triples, base):
                kept, sent = (first, second) if index == 0 else (second, first)
                slot = target.at[index]
                copies = (
                    pltpu.make_async_copy(kept, slot, keep_sems.at[at]),
                    remote_to(sent, slot, layer_sems, at, other_core()),
                )
                for copy in copies:
                    if begin:
                        copy.start()
                    else:
                        copy.wait()


def mixer_backward_kernel(
    s, grad, x, par_all, small_all, embedding, late, lengths, pack, filt_hbm, waves_hbm, back_hbm, normed_hbm, proj_hbm,
    stream_hbm, prod_hbm, spec_hbm, filtered_hbm, gated_hbm, waves1_hbm, waves2_hbm, steep1_hbm,
    steep2_hbm, earlier,
    half_out, small_out, input_grad_out, summed,
    gather, win, wout, filt, waves, back, normed, proj, streams, prod, spec, filtered, gated,
    gated_grad, filtered_grad, both, grad_spec, grad_sum, filter_grad, mixed, proj_grad, wgrad_in, wgrad_out_part,
    other_in, other_out, waves1, waves2, steep1, steep2, sums, taps_sum, send, recv, gather_sems, reduce_sems, load_sems, store_sems,
    mine, arrived, plane_sems, sum_sems, core_sems,
):
    par, small = par_all.at[s], small_all.at[s]
    me = lax.axis_index("seq")
    peers = neighbours(me)
    if s == 0:
        x = x.at[lax.axis_index("section"), 0]
    count, width = grad.shape
    greeted = greet(in_plane(peers[:2]) + plane_devices() + [other_core()])
    length = gather.shape[0]
    chans = prod.shape[1]
    half = win.shape[3]
    depth = win.shape[2]
    loads = fetch(
        weight_pairs_mixer(pack, win, wout)
        + [
            (stream_hbm, streams),
            (waves_hbm, waves),
            (filt_hbm, filt),
            (spec_hbm, spec),
            (back_hbm, back),
            (prod_hbm, prod),
            (filtered_hbm, filtered),
            (proj_hbm, proj),
            (normed_hbm, normed),
            (gated_hbm, gated),
            (waves1_hbm, waves1),
            (waves2_hbm, waves2),
            (steep1_hbm, steep1),
            (steep2_hbm, steep2),
        ],
        load_sems,
    )
    masked_into(gather, me * count, grad, lengths)
    all_here(greeted)
    sends = gather_begin(gather, gather_sems, me, peers, count)
    plane_sum = PlaneSum(earlier, mine, arrived, plane_sems, sum_sems)
    plane_sum.begin()
    for load in loads[1:6]:
        load.wait()
    tile_rows = 256
    for slot in (None, 0, 1, 2):
        source = me if slot is None else peers[slot]
        rows = rows_of(source, count)
        if slot is not None:
            gather_wait(gather, gather_sems, slot, peers, count)
        value = (
            mm_t(gather[rows, : width // 2], wout[0].reshape(chans, width // 2))
            + mm_t(gather[rows, width // 2 :], wout[1].reshape(chans, width // 2))
        ).astype(low)
        gated_grad[rows, :] = value
        filtered_grad[rows, :] = (
            value.astype(f32) * streams[rows, chans : 2 * chans].astype(f32)
        ).astype(low)
        if slot is None:
            sends += gather_forward(gather, gather_sems, peers, count)
            for load in loads[6:]:
                load.wait()
            loads[0].wait()
        if slot == 2:
            plane_sum.forward()

        def spectrum(i, carry):
            up = pl.ds(pl.multiple_of(i * tile_rows, tile_rows), tile_rows)
            down = pl.ds(pl.multiple_of(i * tile_rows + length, tile_rows), tile_rows)
            fg_cos = mm(waves[up, rows], filtered_grad[rows, :])
            fg_sin = mm(waves[down, rows], filtered_grad[rows, :])
            if slot is not None:
                fg_cos = fg_cos + grad_sum[up, :]
                fg_sin = fg_sin + grad_sum[down, :]
            if slot != 2:
                grad_sum[up, :] = fg_cos
                grad_sum[down, :] = fg_sin
            else:
                filt_cos, filt_sin = filt[up, :], filt[down, :]
                grad_spec[up, :] = fg_cos.astype(low)
                grad_spec[down, :] = fg_sin.astype(low)
                both[up, :] = (filt_cos * fg_cos + filt_sin * fg_sin).astype(low)
                both[down, :] = (filt_cos * fg_sin - filt_sin * fg_cos).astype(low)
            return carry

        lax.fori_loop(0, length // tile_rows, spectrum, 0)
    mixed[pl.ds(length, 8), :] = jnp.zeros((8, mixed.shape[1]), f32)

    def streams_back(i, carry):
        rows = pl.ds(pl.multiple_of(i * tile_rows, tile_rows), tile_rows)
        value = mm(back[rows, :], both[...]) * (1.0 / length)
        fg = filtered_grad[rows, :].astype(f32)
        prod_grad = (value + small[153:154, :] * fg).astype(low).astype(f32)
        mixed[rows, 0:chans] = (
            (prod_grad * streams[rows, 2 * chans : 3 * chans].astype(f32)).astype(low).astype(f32)
        )
        mixed[rows, chans : 2 * chans] = (
            (gated_grad[rows, :].astype(f32) * filtered[rows, :]).astype(low).astype(f32)
        )
        mixed[rows, 2 * chans : 3 * chans] = (
            (prod_grad * streams[rows, 0:chans].astype(f32)).astype(low).astype(f32)
        )
        return carry + jnp.sum(fg * prod[rows, :].astype(f32), axis=0, keepdims=True)

    small_out[...] = jnp.zeros(small_out.shape, f32)
    small_out[153:154, :] = lax.fori_loop(
        0, length // tile_rows, streams_back, jnp.zeros((1, chans), f32)
    )
    step = 128
    for slot in (2, 0, 1, None):
        target = me if slot is None else peers[slot]

        def short_back(i, carry):
            start = pl.multiple_of(target * count + i * step, step)
            for g in range(3):
                cols = slice(g * chans, (g + 1) * chans)
                tile = mixed[pl.ds(start, step + 8), cols]
                now = tile[:step]
                after = pltpu.roll(tile, step + 7, 0)[:step]
                later = pltpu.roll(tile, step + 6, 0)[:step]
                proj_grad[pl.ds(start, step), cols] = (
                    small[144 + 3 * g : 145 + 3 * g, :] * now
                    + small[145 + 3 * g : 146 + 3 * g, :] * after
                    + small[146 + 3 * g : 147 + 3 * g, :] * later
                ).astype(low)
            return carry

        lax.fori_loop(0, count // step, short_back, 0)
        rows = rows_of(target, count)

        def through(i, carry):
            cols = pl.ds(pl.multiple_of(i * depth, depth), depth)
            value = mm_t(proj_grad[rows, :half], win[0, i]) + mm_t(proj_grad[rows, half:], win[1, i])
            if slot is None:
                input_grad_out[:, cols] = value
            else:
                send[slot, :, cols] = value.astype(low)
            return carry

        lax.fori_loop(0, width // depth, through, 0)
        if slot is not None:
            sends += reduce_send(slot, send, recv, reduce_sems, peers)

    def weights(i, carry):
        cols = pl.ds(pl.multiple_of(i * depth, depth), depth)
        for h in range(2):
            wgrad_in[h, i] = t_mm(normed[:, cols], proj_grad[:, h * half : (h + 1) * half]).astype(
                low
            )
        return carry

    lax.fori_loop(0, width // depth, weights, 0)
    for h in range(2):
        value = t_mm(gated[...], gather[:, h * width // 2 : (h + 1) * width // 2]).astype(low)
        wgrad_out_part[h] = value.reshape(wgrad_out_part.shape[1:])
    swapped = [(wgrad_in, other_in), (wgrad_out_part, other_out)]
    swaps = swap_begin(swapped, core_sems)
    sends += swaps
    sends += reduce_pass(send, recv, reduce_sems, peers)
    taps_sum[...] = jnp.zeros(taps_sum.shape, f32)

    def tap_sums(i, carry):
        start = pl.multiple_of(i * step, step)
        for g in range(3):
            cols = slice(g * chans, (g + 1) * chans)
            tile = mixed[pl.ds(start, step + 8), cols]
            seen = proj[pl.ds(start, step), cols].astype(f32)
            for at in range(3):
                shift = pltpu.roll(tile, step + 8 - at, 0)[:step] if at else tile[:step]
                taps_sum[8 * at : 8 * at + 8, cols] += jnp.sum(
                    (seen * shift).reshape(step // 8, 8, chans), axis=0
                )
        return carry

    lax.fori_loop(0, length // step, tap_sums, 0)

    def filter_spectrum(i, carry):
        up = pl.ds(pl.multiple_of(i * tile_rows, tile_rows), tile_rows)
        down = pl.ds(pl.multiple_of(i * tile_rows + length, tile_rows), tile_rows)
        prod_cos, prod_sin = spec[up, :].astype(f32), spec[down, :].astype(f32)
        fg_cos, fg_sin = grad_spec[up, :].astype(f32), grad_spec[down, :].astype(f32)
        both[up, :] = (prod_cos * fg_cos + prod_sin * fg_sin).astype(low)
        both[down, :] = (prod_cos * fg_sin - prod_sin * fg_cos).astype(low)
        return carry

    lax.fori_loop(0, length // tile_rows, filter_spectrum, 0)

    def filter_back(i, carry):
        rows = pl.ds(pl.multiple_of(i * tile_rows, tile_rows), tile_rows)
        times = lax.broadcasted_iota(jnp.int32, (tile_rows, 1), 0) + i * tile_rows
        fade = jnp.exp(-times.astype(f32) * small[154:155, :])
        filter_grad[rows, :] = mm(back[rows, :], both[...]) * (1.0 / length) * fade
        return carry

    lax.fori_loop(0, length // tile_rows, filter_back, 0)
    small_out[0:64, :] = t_mm_exact(waves2[...], filter_grad[...])
    back2 = mm_t_exact(filter_grad[...], small[0:64, :]) * steep2[...]
    small_out[64:128, 0:64] = t_mm_exact(waves1[...], back2)
    back1 = mm_t_exact(back2, small[64:128, 0:64]) * steep1[...]
    small_out[64:128, 128:192] = t_mm_exact(embedding[:, 0:64], back1)
    for g in range(3):
        for at in range(3):
            small_out[144 + 3 * g + at : 145 + 3 * g + at, :] = jnp.sum(
                taps_sum[8 * at : 8 * at + 8, g * chans : (g + 1) * chans], axis=0, keepdims=True
            )
    swap_end(swaps, swapped)
    stores = fetch(half_pairs_mixer(half_out, wgrad_in, wgrad_out_part), store_sems)
    plane_sum.end(summed)
    sends += plane_sum.sends
    reduce_wait(send, recv, reduce_sems, peers)
    norm_back_parts(input_grad_out, recv, grad, x, par[0:1, :], sums)
    for q in range(width // chans):
        cols = slice(q * chans, (q + 1) * chans)
        small_out[128 + 2 * q : 130 + 2 * q, :] = sums[:, cols]
        small_out[136 + 2 * q : 138 + 2 * q, :] = late[:, cols]
    for copy in sends:
        copy.wait_send()
    for store in stores:
        store.wait()


def run_kernel(kernel, name, collective_id, operands, in_vmem, outs, out_vmem, scratch, flops):
    inside = pl.BlockSpec(memory_space=pltpu.VMEM)
    outside = pl.BlockSpec(memory_space=pl.ANY)
    scalars = pl.BlockSpec(memory_space=pltpu.SMEM)
    return pl.pallas_call(
        kernel,
        out_shape=[jax.ShapeDtypeStruct(shape, kind) for shape, kind in outs],
        in_specs=[
            scalars if item.dtype == jnp.int32 else inside if at in in_vmem else outside
            for at, item in enumerate(operands)
        ],
        out_specs=[inside if at in out_vmem else outside for at in range(len(outs))],
        scratch_shapes=scratch,
        compiler_params=pltpu.CompilerParams(
            collective_id=collective_id, has_side_effects=True, vmem_limit_bytes=60 * 2**20
        ),
        cost_estimate=pl.CostEstimate(flops=flops, bytes_accessed=2**25, transcendentals=0),
        name=name,
    )(*operands)


def exchange_scratch(count, width):
    return [pltpu.VMEM((3, count, width), low), pltpu.VMEM((3, count, width), low)]


def exchange_semaphores(count):
    return [pltpu.SemaphoreType.DMA((2, count)), pltpu.SemaphoreType.DMA((count,))]


def semaphores(loads, stores):
    return [
        pltpu.SemaphoreType.DMA((2, 6)),
        pltpu.SemaphoreType.DMA((2, 10)),
        pltpu.SemaphoreType.DMA((loads,)),
        pltpu.SemaphoreType.DMA((stores,)),
    ]


def mixer_weights_scratch(pack, width):
    _, dp_count, depth, cols = pack.shape
    return [
        pltpu.VMEM((2, dp_count, depth, 3 * cols // 4), low),
        pltpu.VMEM((2, dp_count, depth // 4, cols), low),
    ]


def mixer_forward(s, x, lengths, weights, waves, back, gathered):
    gathers = gathered is not None
    count, width = x.shape[-2:]
    length = waves.shape[1]
    chans, half = width // 4, width // 2
    knots, dp_count = chans // 4, lax.axis_size("dp")
    pack_shape = (2, dp_count, width // dp_count, half)
    pack = jax.ShapeDtypeStruct(pack_shape, low)
    vm, dma = pltpu.VMEM, pltpu.SemaphoreType.DMA
    outs = [
        ((length, width), low),
        ((length, 3 * chans), low),
        ((length, 3 * chans), low),
        ((length, chans), low),
        ((2 * length, chans), low),
        ((length, chans), f32),
        ((length, chans), low),
        ((count, width), f32),
    ]
    more = []
    if gathers:
        cotangent, embedding = gathered
        depth = weights[0].shape[0]
        units = 2 * half
        ff_shape = (2, dp_count, 2 * width // dp_count, half)
        half_in = 3 * chans // 2
        filters = [((2 * length, chans), f32), *[((length, knots), f32)] * 4]
        outs = [
            (pack_shape, low),
            (ff_shape, low),
            ((length, width), low),
            ((2, 8, width), f32),
            ((2, 160, chans), f32),
            (pack_shape, low),
            (ff_shape[2:], low),
            *filters,
            *filters,
            ((length, width), low),
            ((length, units), low),
            ((length, units), low),
            ((count, width), f32),
        ] + outs
        more = [
            *[vm((length, knots), f32)] * 4,
            vm((length, chans), low),
            vm((*pack_shape[:3], half // 4), low),
            vm(ff_shape, low),
            vm((length, width), low),
            vm(pack_shape, low),
            *[dma((2, 4)), dma((2, 3))] * 4,
            dma((2, 6)),
            dma((15,)),
            vm((2, *pack_shape[2:]), low),
            vm((2, *ff_shape[2:]), low),
            vm((2, 8, width), f32),
            vm((2, 160, chans), f32),
            vm((2, 4, depth, half_in), low),
            vm((2, 4 * depth, half_in // 3), low),
            vm((2, 4, depth, half), low),
            dma((2, 7)),
            dma((2, 1)),
            dma((2, 7)),
            dma((2, 1)),
            dma((2, 1)),
            dma((2, 1)),
            vm((length, width), low),
            *exchange_scratch(count, width),
            dma((2, 6)),
            dma((2, 10)),
            dma((5,)),
        ]
        operands = (cotangent, embedding, lengths, *weights, waves, back)
        inside = range(len(operands) - 1)
        out_inside = (len(outs) - 9, len(outs) - 1)
    else:
        par, small, weights, filt = weights
        operands = (par, small, lengths, weights, filt, waves, back)
        inside = range(3)
        out_inside = (len(outs) - 1,)
    return run_kernel(
        partial(mixer_forward_kernel, s, gathers),
        "opening" if gathers else "mixer_forward",
        1 + s,
        (x, *operands),
        inside,
        outs,
        out_inside,
        [vm((length, width), low)]
        + mixer_weights_scratch(pack, width)
        + [
            vm((2 * length, chans), f32),
            vm((2 * length, length), low),
            vm((length, 2 * length), low),
            vm((length + 8, 3 * chans), f32),
            vm((length, 3 * chans), low),
            vm((length, 3 * chans), low),
            vm((length, chans), low),
            vm((2 * length, chans), low),
            vm((2 * length, chans), low),
            vm((length, chans), f32),
            vm((length, chans), low),
        ]
        + exchange_scratch(count, width)
        + semaphores(8, 7)
        + more,
        10**10,
    )


def ff_turn(s, cotangent, x, par, lengths, pack, late):
    count, width = x.shape
    _, dp_count, rows, half = pack.shape
    length, units = 4 * count, 2 * half
    vm = pltpu.VMEM
    return run_kernel(
        partial(ff_turn_kernel, s),
        "ff_turn",
        4,
        (cotangent, x, par, lengths, pack, late),
        range(3),
        [
            (pack.shape[1:], low),
            ((length, units), low),
            ((count, width), f32),
            ((2, width), f32),
        ],
        (2, 3),
        [vm((length, width), low)] * 2
        + [vm((2, dp_count, rows // 2, half), low)] * 2
        + [vm((length, units), low)] * 2
        + [vm(pack.shape, low), vm(pack.shape[1:], low)]
        + exchange_scratch(count, width)
        + semaphores(3, 2)
        + [pltpu.SemaphoreType.DMA((2, 2, 1))],
        3 * 10**10,
    )


def ff_backward(s, grad, middle, par, lengths, pack, second, value, slope, earlier):
    count, width = grad.shape
    _, dp_count, rows, half = pack.shape
    length, units = value.shape
    vm = pltpu.VMEM
    weights = [vm((2, dp_count, rows // 2, half), low)] * 2
    return run_kernel(
        partial(ff_backward_kernel, s),
        "ff_backward",
        5,
        (grad, middle, par, lengths, pack, second, value, slope, earlier),
        range(3),
        [
            (pack.shape[1:], low),
            ((count, width), f32),
            ((2, width), f32),
            (earlier.shape[1:], low),
        ],
        (1, 2, 3),
        [vm((length, width), low)]
        + weights
        + [vm((length, width), low)]
        + [vm((length, units), low)] * 3
        + [vm(pack.shape, low), vm(pack.shape[1:], low)]
        + exchange_scratch(count, width)
        + semaphores(5, 1)
        + plane_sum_scratch(earlier)
        + [pltpu.SemaphoreType.DMA((2, 2, 1))],
        2 * 10**10,
    )


def mixer_backward(
    s, grad, x, par, small, embedding, late, lengths, pack, waves, back, kept, earlier
):
    normed, proj, streams, prod, spec, filtered, gated, filt, *network = kept
    count, width = grad.shape
    length, chans = prod.shape
    knots = network[0].shape[1]
    vm = pltpu.VMEM
    weights = mixer_weights_scratch(pack, width)
    return run_kernel(
        partial(mixer_backward_kernel, s),
        "mixer_backward",
        7 + s,
        (grad, x, par, small, embedding, late, lengths, pack, filt, waves, back, normed, proj,
         streams, prod, spec, filtered, gated, *network, earlier),
        range(6),
        [
            (pack.shape[1:], low),
            (small.shape[1:], f32),
            ((count, width), f32),
            (earlier.shape[1:], low),
        ],
        (1, 2, 3),
        [vm((length, width), low)]
        + weights
        + [
            vm((2 * length, chans), f32),
            vm((2 * length, length), low),
            vm((length, 2 * length), low),
            vm((length, width), low),
            vm((length, 3 * chans), low),
            vm((length, 3 * chans), low),
            vm((length, chans), low),
            vm((2 * length, chans), low),
            vm((length, chans), f32),
            vm((length, chans), low),
            vm((length, chans), low),
            vm((length, chans), low),
            vm((2 * length, chans), low),
            vm((2 * length, chans), low),
            vm((2 * length, chans), f32),
            vm((length, chans), f32),
            vm((length + 8, 3 * chans), f32),
            vm((length, 3 * chans), low),
        ]
        + weights
        + [vm(item.shape[1:], low) for item in weights]
        + [vm((length, knots), f32)] * 4
        + [vm((2, width), f32), vm((24, 3 * chans), f32)]
        + exchange_scratch(count, width)
        + semaphores(19, 5)
        + plane_sum_scratch(earlier)
        + [pltpu.SemaphoreType.DMA((2, 2))],
        2 * 10**10,
    )


def shuffle_stage(w_in, w_out, w_up, stage_in, stage_out, stage_up):
    depth, chans = w_in.shape[0], w_out.shape[1] // 4
    count = lax.axis_size("dp")
    half_in = stage_in.shape[3]
    piece = chans // count
    for h in range(2):
        for j in range(4):
            for c in range(0, half_in, 2 * piece):
                pair = []
                for col in (c, c + piece):
                    g, d = divmod((h * half_in + col) // piece, count)
                    at = ((g * count + d) * 4 + j) * piece
                    pair.append(w_in[:, at : at + piece].astype(f32))
                stage_in[h, j, :, c : c + 2 * piece] = jnp.concatenate(pair, 1).astype(low)
            for d in range(2):
                at = ((2 * h + d) * 4 + j) * chans
                stage_up[h, j, :, d * chans : (d + 1) * chans] = w_up[:, at : at + chans]
    part = half_in // 3
    for h in range(2):
        for q in range(4):
            at = (h * 4 + q) * part
            stage_out[h, q * depth : (q + 1) * depth, :] = w_out[:, at : at + part]


def parameters_stage(me, par, small, gain, shift, taps, first, second, last, direct, rates):
    chans = small.shape[1]
    count = lax.axis_size("dp")
    piece = chans // count
    width = last.shape[2]
    par[0:1, :] = gain[0, 0:1, :]
    par[1:2, :] = shift[0, 0:1, :]
    par[2:3, :] = gain[0, 1:2, :]
    par[3:4, :] = shift[0, 1:2, :]
    par[4:8, :] = jnp.zeros((4, width), f32)
    small[64:160, :] = jnp.zeros((96, chans), f32)
    small[64:128, 0:64] = second[0]
    for row in range(first.shape[0]):
        small[64 + row : 65 + row, 128:192] = first[row]
    for j in range(4):

        @pl.when(me == j)
        def _():
            for d in range(0, count, 2):
                cols = slice(d * piece, (d + 2) * piece)

                def picked(ref, rows, base=0):
                    at = [base + ((d + k) * 4 + j) * piece for k in range(2)]
                    return jnp.concatenate([ref[rows, a : a + piece] for a in at], 1)

                small[0:64, cols] = picked(last.at[0], slice(0, 64))
                for g in range(3):
                    for tap in range(3):
                        row = 144 + 3 * g + tap
                        small[row : row + 1, cols] = picked(
                            taps.at[tap], slice(0, 1), g * width
                        )
                small[153:154, cols] = picked(direct, slice(0, 1))
                small[154:155, cols] = picked(rates, slice(0, 1))


def shuffle_send(section, me, targets, sources, parts, parameters, sems):
    stage_in, stage_out, stage_up, w_down = sources
    mixer_parts, ff_parts = parts
    in_sems, out_sems, up_sems, down_sems, par_sems, small_sems = sems
    depth, half_in = stage_in.shape[2:]
    half = stage_up.shape[3]
    copies = [
        remote_to(item.at[section], item.at[section], at, 0, other_core())
        for item, at in zip(parameters, (par_sems, small_sems))
    ]
    for e, (t, seq, device) in enumerate(targets):
        target = mixer_parts.at[section, rows_of(me, depth), pl.ds(0, half_in)]
        copies.append(remote_to(stage_in.at[t, seq], target, in_sems, e, device))
    target = mixer_parts.at[section, :, pl.ds(half_in, half_in // 3)]
    copies.append(remote_to(stage_out.at[1 - section], target, out_sems, 0, other_core()))
    for e, (t, seq, device) in enumerate(targets):
        target = ff_parts.at[section, rows_of(me, depth), :]
        copies.append(remote_to(stage_up.at[t, seq], target, up_sems, e, device))
    cols = pl.ds(pl.multiple_of((1 - section) * half, half), half)
    target = ff_parts.at[section, pl.ds(4 * depth, 4 * depth), :]
    copies.append(remote_to(w_down.at[:, cols], target, down_sems, 0, other_core()))
    for copy in copies:
        copy.start()
    mixer_parts[section, rows_of(me, depth), 0:half_in] = stage_in[section, me]
    mixer_parts[section, :, half_in:] = stage_out[section]
    ff_parts[section, rows_of(me, depth), :] = stage_up[section, me]
    cols = pl.ds(pl.multiple_of(section * half, half), half)
    ff_parts[section, 4 * depth : 8 * depth, :] = w_down[:, cols]
    return copies


def shuffle_wait_mixer(section, me, targets, parts, stage_in, in_sems, out_sems):
    depth, half_in = stage_in.shape[2:]
    for e, (t, seq, device) in enumerate(targets):
        block = parts.at[t, rows_of(seq, depth), pl.ds(0, half_in)]
        remote_to(block, block, in_sems, e, device).wait_recv()
    block = parts.at[1 - section, :, pl.ds(half_in, half_in // 3)]
    remote_to(block, block, out_sems, 0, other_core()).wait_recv()


def shuffle_wait_ff(section, me, targets, parts, stage_up, up_sems, down_sems):
    depth = stage_up.shape[2]
    for e, (t, seq, device) in enumerate(targets):
        block = parts.at[t, rows_of(seq, depth), :]
        remote_to(block, block, up_sems, e, device).wait_recv()
    block = parts.at[1 - section, pl.ds(4 * depth, 4 * depth), :]
    remote_to(block, block, down_sems, 0, other_core()).wait_recv()


def shuffle_targets(section, me, peers):
    targets = [(section, peer, {"seq": peer}) for peer in peers]
    targets.append((1 - section, me, other_core()))
    targets += [(1 - section, peer, {**other_core(), "seq": peer}) for peer in peers]
    return targets


def finish_kernel(
    vec0, vec1, mixer0, mixer1, ff0, ff1, grad0, grad1, value_hbm, pack_hbm, x, out0, lengths,
    block_outputs, input_grads, got_in, got_out, got_up, got_down, vec_out,
    mine0, arrived0, plane_sems0, sum_sems0, mine1, arrived1, plane_sems1, sum_sems1,
    vec_other, vec_sum, vec_arrived, vec_all, stage_mixer, stage_ff, own_sems, load_sems,
    layer_sems, keep_sems, vec_core_sems, vec_sum_sems, vec_plane_sems, vec_seq_sems, in_sems, out_sems, up_sems, down_sems,
    send, recv, out1, reduce_sems, value, wdown, early_sems,
):
    section = lax.axis_index("section")
    me = lax.axis_index("seq")
    here, near, far = along_planes()
    planes = (near, far, (near + 2) % 4)
    peers = neighbours(me)
    depth, half_in = got_in.shape[2:]
    targets = shuffle_targets(section, me, peers)
    greeted = greet([device for _, _, device in targets] + [{"dp": plane} for plane in planes])
    inner = wdown.shape[2]
    early = fetch(
        [(value_hbm, value), (pack_hbm.at[:, :, pl.ds(inner, inner)], wdown)], early_sems
    )
    middle = mixer0.shape[2] // 2
    chunks = (pl.ds(0, middle), pl.ds(middle, middle))
    in_cols = (pl.ds(0, middle), pl.ds(middle, half_in - middle))

    def columns(e, at):
        t, seq, device = targets[e]
        return remote_to(
            stage_mixer.at[t, rows_of(seq, depth), in_cols[at]],
            got_in.at[section, me, :, in_cols[at]],
            in_sems,
            2 * e + at,
            device,
        )

    out_columns = remote_to(
        stage_mixer.at[1 - section, :, pl.ds(half_in, half_in // 3)], got_out.at[section], out_sems,
        0, other_core(),
    )

    def send_layer(s, at):
        for index in range(2):

            @pl.when(section == index)
            def _():
                for e in range(3) if index == s else range(3, 7):
                    columns(e, at).start()
                if at == 1 and index != s:
                    out_columns.start()

    all_here(greeted)
    for index, vec in enumerate((vec1, vec0)):

        @pl.when(section == index)
        def _():
            remote_to(vec, vec_other, vec_core_sems, 0, other_core()).start()

    sends = []
    count, width = x.shape

    def result_part(slot):
        rows = rows_of(me if slot is None else peers[slot], count)
        for h in range(2):
            cols = slice(h * width // 2, (h + 1) * width // 2)
            out = mm(value[rows, :], wdown[h].reshape(4 * inner, width // 2))
            if slot is None:
                out1[:, cols] = out
            else:
                send[slot, :, cols] = out.astype(low)
        return [] if slot is None else reduce_send(slot, send, recv, reduce_sems, peers)

    for load in early:
        load.wait()
    sends += result_part(2)
    vec_swap = remote_to(vec_other, vec_other, vec_core_sems, 0, other_core())
    vec_swap.wait_recv()
    sends.append(vec_swap)

    @pl.when(section == 0)
    def _():
        vec_sum[...] = vec0[...] + vec_other[...]

    @pl.when(section == 1)
    def _():
        vec_sum[...] = vec1[...] + vec_other[...]

    chunk = vec_sum.shape[0] // 4
    moves = [
        remote_to(
            vec_sum.at[rows_of(plane, chunk)], vec_arrived.at[slot], vec_sum_sems, slot,
            {"dp": plane},
        )
        for slot, plane in enumerate(planes)
    ]
    for copy in moves:
        copy.start()
    sends += moves
    plane_sums = [
        PlaneSum(mixer0.at[:, :, chunks[0]], mine0, arrived0, plane_sems0, sum_sems0),
        PlaneSum(mixer0.at[:, :, chunks[1]], mine1, arrived1, plane_sems1, sum_sems1),
    ]
    for plane_sum in plane_sums:
        plane_sum.begin()
    loads = fetch(
        [
            (ff0, stage_ff.at[0]),
            (ff1, stage_ff.at[1]),
            (mixer1, stage_mixer.at[1]),
        ],
        load_sems,
    )
    by_layer(True, ((grad0, grad1, input_grads),), layer_sems, keep_sems)
    sends += result_part(0)
    sends += result_part(1)
    for load in loads:
        load.wait()
    ups = []
    for e, (t, seq, device) in enumerate(targets):
        ups.append(
            remote_to(
                stage_ff.at[t, rows_of(seq, depth), :], got_up.at[section, me], up_sems, e, device
            )
        )
    downs = [
        remote_to(
            stage_ff.at[1 - section, pl.ds(4 * depth, 4 * depth), :], got_down.at[section],
            down_sems, 0, other_core(),
        )
    ]
    for copy in ups + downs:
        copy.start()
    sends += ups + downs
    send_layer(1, 0)
    send_layer(1, 1)
    keeps = fetch(
        [
            (stage_ff.at[section, rows_of(me, depth), :], got_up.at[section, me]),
            (stage_ff.at[section, pl.ds(4 * depth, 4 * depth), :], got_down.at[section]),
        ],
        own_sems,
    )

    result_part(None)
    for copy in moves:
        copy.wait_recv()
    own_chunk = rows_of(here, chunk)
    total = vec_sum[own_chunk, :]
    for slot in range(len(planes)):
        total = total + vec_arrived[slot]
    vec_all[me, own_chunk, :] = total
    moves = [
        remote_to(
            vec_all.at[me, own_chunk], vec_all.at[me, own_chunk], vec_plane_sems, slot,
            {"dp": plane},
        )
        for slot, plane in enumerate(planes)
    ]
    for copy in moves:
        copy.start()
    sends += moves
    for plane_sum in plane_sums:
        plane_sum.forward()
    sends += reduce_pass(send, recv, reduce_sems, peers)
    for slot, plane in enumerate(planes):
        block = vec_all.at[me, rows_of(plane, chunk)]
        remote_to(block, block, vec_plane_sems, slot, {"dp": plane}).wait_recv()
    moves = [
        remote(vec_all.at[me], vec_all.at[me], vec_seq_sems, slot, peer)
        for slot, peer in enumerate(peers)
    ]
    for copy in moves:
        copy.start()
    sends += moves

    for at, plane_sum in enumerate(plane_sums):
        plane_sum.end(stage_mixer.at[0, :, chunks[at]])
        sends += plane_sum.sends
        send_layer(0, at)
    sends += [columns(e, at) for e in range(7) for at in range(2)] + [out_columns]
    reduce_wait(send, recv, reduce_sems, peers)
    add_parts(out1, recv, x, me * count, lengths)
    by_layer(True, ((out0, out1, block_outputs),), layer_sems, keep_sems, 1)
    keeps += fetch(
        [
            (
                stage_mixer.at[section, rows_of(me, depth), pl.ds(0, half_in)],
                got_in.at[section, me],
            ),
            (stage_mixer.at[section, :, pl.ds(half_in, half_in // 3)], got_out.at[section]),
        ],
        own_sems,
        2,
    )
    for slot, peer in enumerate(peers):
        block = vec_all.at[peer]
        remote(block, block, vec_seq_sems, slot, peer).wait_recv()
    keeps += fetch([(vec_all, vec_out)], own_sems, 4)
    for e, (t, seq, device) in enumerate(targets):
        block = got_up.at[t, seq]
        remote_to(block, block, up_sems, e, device).wait_recv()
        for at in range(2):
            block = got_in.at[t, seq, :, in_cols[at]]
            remote_to(block, block, in_sems, 2 * e + at, device).wait_recv()
    downs[0].wait_recv()
    out_columns.wait_recv()
    by_layer(False, ((grad0, grad1, input_grads),), layer_sems, keep_sems)
    by_layer(False, ((out0, out1, block_outputs),), layer_sems, keep_sems, 1)
    for copy in sends:
        copy.wait_send()
    for keep in keeps:
        keep.wait()


def unpack_kernel(
    blocks, grads, got_in, got_out, got_up, got_down, vec_all,
    block_outputs, input_grads, g_in, g_out, g_up, g_down, g_gain, g_bias, g_taps, g_first,
    g_second, g_last, g_direct,
    stage_blocks, stage_grads, load_sems, copy_sems,
):
    loads = fetch([(blocks, stage_blocks), (grads, stage_grads)], load_sems)
    depth = g_in.shape[0]
    half_in, half_up = got_in.shape[3], got_up.shape[3]
    chans = vec_all.shape[2]
    count = 4
    piece = chans // count
    for j in range(4):
        for d in range(count):
            at = (d * 4 + j) * chans
            h, col = divmod(d * chans, half_up)
            g_up[:, at : at + chans] = got_up[h, j, :, col : col + chans].astype(f32)
    for h in range(2):
        g_down[:, h * half_up : (h + 1) * half_up] = got_down[h].astype(f32)
    for load in loads:
        load.wait()
    copies = fetch([(stage_blocks, block_outputs), (stage_grads, input_grads)], copy_sems)
    for g in range(3):
        for d in range(count):
            h, col = divmod(g * chans + d * piece, half_in)
            for j in range(0, 4, 2):
                at = ((g * count + d) * 4 + j) * piece
                g_in[:, at : at + 2 * piece] = jnp.concatenate(
                    [got_in[h, j + k, :, col : col + piece].astype(f32) for k in range(2)], 1
                )
    part = half_in // 3
    for h in range(2):
        for q in range(4):
            at = (h * 4 + q) * part
            g_out[:, at : at + part] = got_out[h, q * depth : (q + 1) * depth, :].astype(f32)
    first = sum_of(vec_all, slice(64, 64 + g_first.shape[0]), slice(128, 192))
    for row in range(g_first.shape[0]):
        g_first[row] = first[row : row + 1]
    g_second[...] = sum_of(vec_all, slice(64, 128), slice(0, 64))
    for q in range(4):
        cols = slice(q * chans, (q + 1) * chans)
        early = sum_of(vec_all, slice(128 + 2 * q, 130 + 2 * q), slice(None))
        late = sum_of(vec_all, slice(136 + 2 * q, 138 + 2 * q), slice(None))
        g_gain[0:1, cols] = early[0:1]
        g_gain[1:2, cols] = late[0:1]
        g_bias[0:1, cols] = early[1:2]
        g_bias[1:2, cols] = late[1:2]
    for d in range(count):
        cols = slice(d * piece, (d + 1) * piece)
        for j in range(0, 4, 2):
            at = (d * 4 + j) * piece
            pair = slice(at, at + 2 * piece)

            def joined(rows):
                return jnp.concatenate([vec_all[j, rows, cols], vec_all[j + 1, rows, cols]], 1)

            g_last[:, pair] = joined(slice(0, 64))
            for g in range(3):
                for tap in range(3):
                    row = 144 + 3 * g + tap
                    start = g * 4 * chans + at
                    g_taps[tap, :, start : start + 2 * piece] = joined(slice(row, row + 1))
            g_direct[:, pair] = joined(slice(153, 154))

    for copy in copies:
        copy.wait()


def sum_of(blocks, rows, cols):
    return (blocks[0, rows, cols] + blocks[1, rows, cols]) + (
        blocks[2, rows, cols] + blocks[3, rows, cols]
    )


def finish(
    vec0, vec1, mixer0, mixer1, ff0, ff1, grad0, grad1, value, pack, x, out0, lengths
):
    count, width = grad0.shape
    dp_count, rows, half = mixer0.shape
    depth = rows // 4
    chans = vec0.shape[1]
    half_in = 3 * chans // 2
    vm, dma = pltpu.VMEM, pltpu.SemaphoreType.DMA
    vec_rows = vec0.shape[0]
    chunk = jax.ShapeDtypeStruct((dp_count, rows, half // 2), low)
    return run_kernel(
        finish_kernel,
        "finish",
        10,
        (vec0, vec1, mixer0, mixer1, ff0, ff1, grad0, grad1, value, pack, x, out0, lengths),
        (0, 1, 6, 7, 10, 11),
        [
            ((2, count, width), f32),
            ((2, count, width), f32),
            ((2, 4, depth, half_in), low),
            ((2, rows, half_in // 3), low),
            ((2, 4, depth, half), low),
            ((2, rows, half), low),
            ((4, vec_rows, chans), f32),
        ],
        (),
        plane_sum_scratch(chunk)
        + plane_sum_scratch(chunk)
        + [
            vm((vec_rows, chans), f32),
            vm((vec_rows, chans), f32),
            vm((3, vec_rows // 4, chans), f32),
            vm((4, vec_rows, chans), f32),
            vm((2, *mixer1.shape), low),
            vm((2, *ff1.shape), low),
            dma((5,)),
            dma((3,)),
            *exchange_semaphores(2),
            dma((2, 1)),
            dma((2, 3)),
            dma((2, 3)),
            dma((2, 3)),
            dma((2, 14)),
            dma((2, 1)),
            dma((2, 7)),
            dma((2, 1)),
            *exchange_scratch(count, width),
            vm((count, width), f32),
            dma((2, 10)),
            vm(value.shape, low),
            vm((*pack.shape[:2], pack.shape[2] // 2, pack.shape[3]), low),
            dma((2,)),
        ],
        10**9,
    )


def unpack(blocks, grads, got, first_shape):
    width = blocks.shape[2]
    depth = got[0].shape[2]
    units = 4 * 2 * got[2].shape[3]
    knots = first_shape[1]
    inside = pl.BlockSpec(memory_space=pltpu.VMEM)
    outside = pl.BlockSpec(memory_space=pl.ANY)
    shapes = (
        blocks.shape, grads.shape, (depth, 3 * width), (depth, width), (depth, units),
        (4 * depth, width), (2, width), (2, width), (3, 1, 3 * width),
        (first_shape[0], 1, knots), (knots, knots),
        (knots, width), (1, width),
    )
    return pl.pallas_call(
        unpack_kernel,
        out_shape=[jax.ShapeDtypeStruct(shape, f32) for shape in shapes],
        in_specs=[outside] * 2 + [inside] * 5,
        out_specs=[outside] * 2 + [inside] * 11,
        scratch_shapes=[
            pltpu.VMEM(blocks.shape, f32),
            pltpu.VMEM(grads.shape, f32),
            pltpu.SemaphoreType.DMA((2,)),
            pltpu.SemaphoreType.DMA((2,)),
        ],
        compiler_params=pltpu.CompilerParams(vmem_limit_bytes=56 * 2**20),
        name="unpack",
    )(blocks, grads, *got)


def any_device(
    tokens,
    cotangent,
    lengths,
    norm_gain,
    norm_bias,
    mixer_in,
    short_kernel,
    filter_first,
    filter_second,
    filter_last,
    filter_bias,
    decay_rates,
    mixer_out,
    up_weight,
    down_weight,
):
    section = lax.axis_index("section")
    seq_index = lax.axis_index("seq")
    seq_count = lax.axis_size("seq")
    dp_count = lax.axis_size("dp")
    own_layer_first = section == 0
    local_len = tokens.shape[2]
    width = tokens.shape[3]
    hidden = up_weight.shape[2]
    row_len = local_len * seq_count
    chans = width // seq_count
    units = hidden // seq_count

    def share_columns(block, groups):
        rows = block.shape[0]
        inner = block.shape[1] // (groups * dp_count * seq_count)
        split = block.reshape(rows, groups, dp_count, seq_count, inner)
        split = jnp.transpose(split, (3, 0, 1, 2, 4))
        moved = lax.all_to_all(split, "seq", split_axis=0, concat_axis=0, tiled=True)
        return moved.reshape(seq_count * rows, groups * dp_count * inner)

    def unshare_columns(block, groups):
        rows = block.shape[0] // seq_count
        inner = block.shape[1] // (groups * dp_count)
        split = block.reshape(seq_count, rows, groups, dp_count, inner)
        moved = lax.all_to_all(split, "seq", split_axis=0, concat_axis=0, tiled=True)
        moved = jnp.transpose(moved, (1, 2, 3, 0, 4))
        return moved.reshape(rows, groups * dp_count * seq_count * inner)

    def gathered(block):
        whole = lax.all_gather(block, ("section", "dp"))
        return whole.reshape(2, dp_count * block.shape[0], block.shape[1])

    weights = (
        gathered(share_columns(mixer_in[0], 3)),
        gathered(mixer_out[0]),
        gathered(share_columns(up_weight[0], 1)),
        gathered(down_weight[0]),
    )

    def both(value):
        return lax.all_gather(value[0], "section")

    gains, shifts = both(norm_gain), both(norm_bias)
    taps, first_w, second_w = both(short_kernel), both(filter_first), both(filter_second)
    last_w, direct, rates = both(filter_last), both(filter_bias), both(decay_rates)

    def mine(value):
        lead = value.shape[:-1]
        split = value.reshape(*lead, dp_count, seq_count, -1)
        picked = lax.dynamic_index_in_dim(split, seq_index, len(lead) + 1, False)
        return picked.reshape(*lead, chans)

    def placed(value):
        lead = value.shape[:-1]
        split = value.reshape(*lead, dp_count, 1, -1)
        inner = split.shape[-1]
        empty = jnp.zeros((*lead, dp_count, seq_count, inner), value.dtype)
        at = [0] * len(lead) + [0, seq_index, 0]
        return lax.dynamic_update_slice(empty, split, at).reshape(*lead, width)

    waves = jnp.asarray(wave_tables(row_len))
    waves_back = waves

    def to_waves(x):
        both_parts = mm(waves, x)
        return both_parts[:row_len], both_parts[row_len:]

    def from_waves(cos_part, sin_part):
        joined = jnp.concatenate([cos_part, sin_part], 0).astype(low)
        return t_mm(waves_back, joined) * (1.0 / row_len)

    def ag(x):
        return lax.all_gather(x, "seq", axis=0, tiled=True)

    def rs(x):
        return lax.psum_scatter(x.astype(low), "seq", scatter_dimension=0, tiled=True).astype(f32)

    length_now = lax.dynamic_index_in_dim(lengths, section, 0, False)[0]
    positions = seq_index * local_len + jnp.arange(local_len)
    mask = (positions < length_now).astype(f32)[:, None]
    row_mask = (jnp.arange(row_len) < length_now).astype(f32)[:, None]
    own_tokens = lax.dynamic_index_in_dim(tokens, section, 0, False)[0].astype(f32)
    own_cotangent = lax.dynamic_index_in_dim(cotangent, section, 0, False)[0].astype(f32)

    def layer_forward(s, inputs):
        w_in, w_out, w_up, w_down = [w[s] for w in weights]
        kernel = mine(taps[s].reshape(3, 3, width))
        last_mine, direct_mine, rates_mine = mine(last_w[s]), mine(direct[s]), mine(rates[s])

        def own_filter(a, b, c):
            return filter_taps(a, b, c, rates_mine, row_len)

        filter_rows, filter_back = jax.vjp(own_filter, first_w[s], second_w[s], last_mine)
        filt_cos, filt_sin = to_waves(filter_rows.astype(low))
        normed = (norm_stats(inputs)[0] * gains[s, 0] + shifts[s, 0]).astype(low)
        normed = ag(normed)
        projected = [mm(normed, w_in[:, g * chans : (g + 1) * chans]) for g in range(3)]
        streams = [
            (
                kernel[0, g] * projected[g]
                + kernel[1, g] * shifted(projected[g], 1)
                + kernel[2, g] * shifted(projected[g], 2)
            ).astype(low)
            for g in range(3)
        ]
        wide = [x.astype(f32) for x in streams]
        product = (wide[0] * wide[2] * row_mask).astype(low)
        prod_cos, prod_sin = to_waves(product)
        filtered = from_waves(
            prod_cos * filt_cos - prod_sin * filt_sin, prod_cos * filt_sin + prod_sin * filt_cos
        ) + direct_mine * product.astype(f32)
        gated = (wide[1] * filtered).astype(low)
        middle = inputs + mask * rs(mm(gated, w_out))
        second = (norm_stats(middle)[0] * gains[s, 1] + shifts[s, 1]).astype(low)
        second = ag(second)
        value, slope = gelu_both(mm(second, w_up))
        value = value.astype(low)
        slope = slope.astype(low)
        result = middle + mask * rs(mm(value, w_down))
        saved = (
            inputs, normed, projected, wide, product, prod_cos, prod_sin, filt_cos, filt_sin,
            filtered, gated, middle, second, value, slope, kernel, direct_mine, filter_back,
        )
        return result, saved

    def layer_backward(s, grad, saved):
        w_in, w_out, w_up, w_down = [w[s] for w in weights]
        (
            inputs, normed, projected, wide, product, prod_cos, prod_sin, filt_cos, filt_sin,
            filtered, gated, middle, second, value, slope, kernel, direct_mine, filter_back,
        ) = saved
        out_low = ag((grad * mask).astype(low))
        pre = (mm_t(out_low, w_down) * slope.astype(f32)).astype(low)
        grad_down = t_mm(value, out_low)
        grad_up = t_mm(second, pre)
        mid_part, gain_late, bias_late = norm_back(rs(mm_t(pre, w_up)), middle, gains[s, 1])
        middle_grad = grad + mid_part
        branch = ag((middle_grad * mask).astype(low))
        gated_grad = mm_t(branch, w_out).astype(low)
        grad_out = t_mm(gated, branch)
        gated_grad = gated_grad.astype(f32)
        filtered_grad = (gated_grad * wide[1]).astype(low)
        fg_cos, fg_sin = to_waves(filtered_grad)
        fg_wide = filtered_grad.astype(f32)
        prod32 = product.astype(f32)
        product_grad = from_waves(
            filt_cos * fg_cos + filt_sin * fg_sin, filt_cos * fg_sin - filt_sin * fg_cos
        ) + direct_mine * fg_wide
        product_grad = product_grad.astype(low).astype(f32)
        filter_grad = from_waves(
            prod_cos * fg_cos + prod_sin * fg_sin, prod_cos * fg_sin - prod_sin * fg_cos
        )
        grad_first, grad_second, grad_last = filter_back(filter_grad)
        grad_direct = jnp.sum(fg_wide * prod32, 0)
        mixed = [
            (product_grad * wide[2]).astype(low).astype(f32),
            (gated_grad * filtered).astype(low).astype(f32),
            (product_grad * wide[0]).astype(low).astype(f32),
        ]
        proj = [
            (
                kernel[0, g] * mixed[g]
                + kernel[1, g] * shifted(mixed[g], -1)
                + kernel[2, g] * shifted(mixed[g], -2)
            ).astype(low)
            for g in range(3)
        ]
        grad_taps = jnp.stack(
            [
                jnp.stack(
                    [jnp.sum(mixed[g] * (shifted(projected[g], k) if k else projected[g]), 0) for g in range(3)]
                )
                for k in range(3)
            ]
        )
        proj = jnp.concatenate(proj, 1)
        grad_in = t_mm(normed, proj)
        in_part, gain_early, bias_early = norm_back(rs(mm_t(proj, w_in)), inputs, gains[s, 0])
        small = (
            jnp.stack([gain_early, gain_late]),
            jnp.stack([bias_early, bias_late]),
            placed(grad_taps).reshape(3, 3 * width),
            grad_first,
            grad_second,
            placed(grad_last),
            placed(grad_direct),
        )
        large = (grad_in, grad_out, grad_up, grad_down)
        return middle_grad + in_part, small, large

    first_out, first_saved = layer_forward(0, own_tokens)
    second_out, second_saved = layer_forward(1, first_out)
    second_grad, second_small, second_large = layer_backward(1, own_cotangent, second_saved)
    first_grad, first_small, first_large = layer_backward(0, second_grad, first_saved)

    swap = [(0, 1), (1, 0)]

    def by_layer(first, second):
        other = lax.ppermute(jnp.where(own_layer_first, second, first), "section", swap)
        return jnp.where(
            own_layer_first, jnp.stack([first, other]), jnp.stack([other, second])
        )[None, :, None]

    def summed(first, second):
        stacked = jnp.stack([first, second]).astype(low)
        rows = first.shape[0] // dp_count
        stacked = stacked.reshape(2 * dp_count, rows, first.shape[1])
        return lax.psum_scatter(stacked, ("section", "dp"), scatter_dimension=0, tiled=True)[0]

    sums = [summed(a, b) for a, b in zip(first_large, second_large)]
    sum_in = unshare_columns(sums[0], 3).astype(f32)
    sum_out = sums[1].astype(f32)
    sum_up = unshare_columns(sums[2], 1).astype(f32)
    sum_down = sums[3].astype(f32)
    stacked = jax.tree.map(lambda a, b: jnp.stack([a, b]), first_small, second_small)
    small = lax.psum(stacked, ("section", "dp", "seq"))
    small = [lax.dynamic_slice_in_dim(x, section, 1, 0) for x in small]
    sum_gain, sum_bias, sum_taps, sum_first, sum_second, sum_last, sum_direct = small
    return (
        by_layer(first_out, second_out),
        by_layer(first_grad, second_grad),
        sum_gain,
        sum_bias,
        sum_in[None],
        sum_taps,
        sum_first,
        sum_second,
        sum_last,
        sum_direct,
        sum_out[None],
        sum_up[None],
        sum_down[None],
    )


def plane_device(
    tokens,
    cotangent,
    lengths,
    norm_gain,
    norm_bias,
    mixer_in,
    short_kernel,
    filter_first,
    filter_second,
    filter_last,
    filter_bias,
    decay_rates,
    mixer_out,
    up_weight,
    down_weight,
):
    section = lax.axis_index("section")
    seq_count = lax.axis_size("seq")
    dp_count = lax.axis_size("dp")
    row_len = tokens.shape[2] * seq_count
    lengths = jnp.transpose(lengths)
    short_kernel = jnp.transpose(short_kernel, (1, 0, 2))
    filter_first = jnp.transpose(filter_first, (1, 0, 2))

    def gathered(part):
        whole = lax.all_gather(part, ("section", "dp"))
        return whole.reshape(2, dp_count, *part.shape)

    tables = wave_tables(row_len)
    waves = jnp.asarray(tables)
    waves_back = jnp.asarray(np.ascontiguousarray(tables.T))
    embedding = jnp.asarray(np.pad(position_rows(row_len), ((0, 0), (0, 95))))

    weights = (
        mixer_in[0], mixer_out[0], up_weight[0], down_weight[0], norm_gain, norm_bias, short_kernel,
        filter_first, filter_second, filter_last, filter_bias, decay_rates,
    )
    (
        first_mixer_pack, first_ff_pack, cotangent_low, par, small, second_mixer_pack, ff_part,
        *outs,
    ) = mixer_forward(
        0, tokens, lengths, weights, waves, waves_back, (cotangent, embedding)
    )
    first_filter, second_filter, first_saved, outs = outs[:5], outs[5:10], outs[10:13], outs[13:]
    first_out, *first_kept, first_middle = outs
    second_ff_pack = gathered(ff_part)
    *second_kept, second_middle = mixer_forward(
        1, first_out, lengths, (par, small, second_mixer_pack, second_filter[0]), waves, waves_back,
        None,
    )
    first_kept, second_kept = [*first_kept, *first_filter], [*second_kept, *second_filter]
    second_ff, second_value, middle_grad, late = ff_turn(
        1, cotangent, second_middle, par, lengths, second_ff_pack, cotangent_low
    )

    def mixer_back(s, grad, x, late, pack, kept, earlier):
        return mixer_backward(
            s, grad, x, par, small, embedding, late, lengths, pack, waves, waves_back, kept, earlier
        )

    second_mixer, second_vec, second_grad, second_ff = mixer_back(
        1, middle_grad, first_out, late, second_mixer_pack, second_kept, second_ff
    )
    first_ff, middle_grad, late, second_mixer = ff_backward(
        0, second_grad, first_middle, par, lengths, first_ff_pack, *first_saved, second_mixer
    )
    first_mixer, first_vec, first_grad, first_ff = mixer_back(
        0, middle_grad, tokens, late, first_mixer_pack, first_kept, first_ff
    )
    block_outputs, input_grads, *got = finish(
        first_vec, second_vec, first_mixer, second_mixer, first_ff, second_ff, first_grad,
        second_grad, second_value, second_ff_pack, second_middle, first_out, lengths,
    )
    (
        block_outputs, input_grads, sum_in, sum_out, sum_up, sum_down, sum_gain, sum_bias, sum_taps,
        sum_first, sum_second, sum_last, sum_direct,
    ) = unpack(block_outputs, input_grads, got, filter_first.shape[::2])
    return (
        block_outputs[None, :, None],
        input_grads[None, :, None],
        sum_gain[None],
        sum_bias[None],
        sum_in[None],
        jnp.transpose(sum_taps, (1, 0, 2)),
        jnp.transpose(sum_first, (1, 0, 2)),
        sum_second[None],
        sum_last[None],
        sum_direct,
        sum_out[None],
        sum_up[None],
        sum_down[None],
    )


def solution(mesh):
    in_specs = (
        P(None, "dp", "seq", None),
        P(None, "dp", "seq", None),
        P(None, "dp"),
        P("section", None, None),
        P("section", None, None),
        P("section", ("dp", "seq"), None),
        P("section", None, None),
        P("section", None, None),
        P("section", None, None),
        P("section", None, None),
        P("section", None),
        P("section", None),
        P("section", ("dp", "seq"), None),
        P("section", ("dp", "seq"), None),
        P("section", ("dp", "seq"), None),
    )
    out_specs = (
        P("section", None, "dp", "seq", None),
        P("section", None, "dp", "seq", None),
        P("section", None, None),
        P("section", None, None),
        P("section", ("dp", "seq"), None),
        P("section", None, None),
        P("section", None, None),
        P("section", None, None),
        P("section", None, None),
        P("section", None),
        P("section", ("dp", "seq"), None),
        P("section", ("dp", "seq"), None),
        P("section", ("dp", "seq"), None),
    )
    planes = mesh.shape["seq"] == 4 and mesh.shape["dp"] == 4
    per_device = plane_device if planes else any_device
    return jax.shard_map(
        per_device, mesh=mesh, in_specs=in_specs, out_specs=out_specs, check_vma=False
    )
```

```python
from functools import partial
import math

import jax
import jax.numpy as jnp
import numpy as np
from jax import lax
from jax.experimental import pallas as pl
from jax.experimental.pallas import tpu as pltpu
from jax.sharding import PartitionSpec as P

precise = lax.Precision.HIGHEST
low = jnp.bfloat16
f32 = jnp.float32
MESH = pl.DeviceIdType.MESH


def dot(a, b, dims):
    return lax.dot_general(a, b, (dims, ((), ())), preferred_element_type=f32)


def mm(a, b):
    return dot(a, b, ((1,), (0,)))


def mm_t(a, b):
    return dot(a, b, ((1,), (1,)))


def t_mm(a, b):
    return dot(a, b, ((0,), (0,)))


def norm_stats(x):
    mean = jnp.mean(x, axis=-1, keepdims=True)
    centred = x - mean
    inverse = lax.rsqrt(jnp.mean(centred * centred, axis=-1, keepdims=True) + 1e-05)
    return centred * inverse, inverse


def norm_back(grad, x, gain):
    hat, inverse = norm_stats(x)
    scaled = grad * gain
    back = inverse * (
        scaled
        - jnp.mean(scaled, axis=-1, keepdims=True)
        - hat * jnp.mean(scaled * hat, axis=-1, keepdims=True)
    )
    return back, jnp.sum(grad * hat, 0), jnp.sum(grad, 0)


def gelu_both(x):
    scale = math.sqrt(2.0 / math.pi)
    inner = scale * (x + 0.044715 * x * x * x)
    bend = jnp.tanh(inner)
    value = 0.5 * x * (1.0 + bend)
    slope = 0.5 * (1.0 + bend) + 0.5 * x * (1.0 - bend * bend) * scale * (
        1.0 + 3.0 * 0.044715 * x * x
    )
    return value, slope


def position_table(length):
    offsets = jnp.arange(length, dtype=jnp.float32)
    frequencies = jnp.linspace(0.0001, 15.0, 16, dtype=jnp.float32)
    angles = 2.0 * math.pi * offsets[:, None] * frequencies[None, :] / length
    return jnp.concatenate(
        [offsets[:, None] / (length - 1), jnp.cos(angles), -jnp.sin(angles)], axis=1
    )


def position_rows(length):
    offsets = np.arange(length, dtype=np.float32)
    frequencies = np.linspace(0.0001, 15.0, 16, dtype=np.float32)
    angles = np.float32(2.0 * math.pi) * offsets[:, None] * frequencies[None, :] / np.float32(length)
    return np.concatenate(
        [offsets[:, None] / np.float32(length - 1), np.cos(angles), -np.sin(angles)], axis=1
    )


def filter_taps(first_w, second_w, last_w, rates, length):
    embedding = position_table(length)
    hidden = jnp.sin(jnp.dot(embedding, first_w, precision=precise))
    hidden = jnp.sin(jnp.dot(hidden, second_w, precision=precise))
    offsets = jnp.arange(length, dtype=jnp.float32)
    return jnp.dot(hidden, last_w, precision=precise) * jnp.exp(-offsets[:, None] * rates[None, :])


def wave_tables(length):
    turns = (2 * np.arange(length)[:, None] + 1) * np.arange(length)[None, :] % (4 * length)
    angles = turns * (math.pi / (2 * length))
    both = np.concatenate([np.cos(angles), np.sin(angles)], 0)
    return both.astype(jnp.bfloat16)


def shifted(x, by):
    if by > 0:
        return jnp.pad(x[:-by], ((by, 0), (0, 0)))
    return jnp.pad(x[-by:], ((0, -by), (0, 0)))


def neighbours(me):
    return (me + 1 - 2 * (me % 2), (me + 2) % 4, 3 - me)


def greet(devices):
    barrier = pltpu.get_barrier_semaphore()
    for device in devices:
        pl.semaphore_signal(barrier, inc=1, device_id=device, device_id_type=MESH)
    return len(devices)


def all_here(greeted):
    pl.semaphore_wait(pltpu.get_barrier_semaphore(), greeted)


def in_plane(peers):
    return [{"seq": peer} for peer in peers]


def along_planes():
    here = lax.axis_index("dp")
    return here, here + 1 - 2 * (here % 2), (here + 2) % 4


def other_core():
    return {"section": 1 - lax.axis_index("section")}


def plane_devices():
    _, near, far = along_planes()
    return [{"dp": near}, {"dp": far}]


def add_low(target, source):
    def add(at):
        target[at, :] = (target[at, :].astype(f32) + source[at, :].astype(f32)).astype(low)

    by_rows(target.shape[0], 32, add)


def swap_begin(pairs, core_sems):
    section = lax.axis_index("section")
    copies = [
        remote_to(made.at[1 - section], other, core_sems, at, other_core())
        for at, (made, other) in enumerate(pairs)
    ]
    for copy in copies:
        copy.start()
    return copies


def swap_end(copies, pairs):
    section = lax.axis_index("section")
    for copy, (made, other) in zip(copies, pairs):
        copy.wait_recv()
        for block in range(other.shape[0]):
            add_low(made.at[section, block], other.at[block])


class PlaneSum:
    def __init__(self, pack, mine, arrived, sems, load_sems):
        self.here, self.near, self.far = along_planes()
        self.pack, self.mine, self.arrived = pack, mine, arrived
        self.sems, self.load_sems = sems, load_sems

    def begin(self):
        self.sends = [
            remote_to(self.pack.at[block], self.arrived.at[slot], self.sems, slot, {"dp": self.near})
            for slot, block in enumerate(((self.near + 2) % 4, self.near))
        ]
        for copy in self.sends:
            copy.start()
        self.loads = fetch(
            [(self.pack.at[self.far], self.mine.at[0]), (self.pack.at[self.here], self.mine.at[1])],
            self.load_sems,
        )

    def forward(self):
        self.loads[0].wait()
        self.sends[0].wait_recv()
        add_low(self.mine.at[0], self.arrived.at[0])
        copy = remote_to(self.mine.at[0], self.arrived.at[2], self.sems, 2, {"dp": self.far})
        copy.start()
        self.sends.append(copy)

    def end(self, result):
        self.loads[1].wait()
        self.sends[1].wait_recv()
        self.sends[2].wait_recv()

        def add(at):
            total = self.mine[1, at, :].astype(f32)
            for slot in (1, 2):
                total = total + self.arrived[slot, at, :].astype(f32)
            result[at, :] = total.astype(low)

        by_rows(result.shape[0], 32, add)


def plane_sum_scratch(half_pack):
    _, rows, cols = half_pack.shape
    return [
        pltpu.VMEM((2, rows, cols), low),
        pltpu.VMEM((3, rows, cols), low),
        pltpu.SemaphoreType.DMA((2, 3)),
        pltpu.SemaphoreType.DMA((2,)),
    ]


def remote_to(source, target, sems, slot, device):
    return pltpu.make_async_remote_copy(
        src_ref=source,
        dst_ref=target,
        send_sem=sems.at[0, slot],
        recv_sem=sems.at[1, slot],
        device_id=device,
        device_id_type=MESH,
    )


def remote(source, target, sems, slot, peer):
    return remote_to(source, target, sems, slot, {"seq": peer})


def rows_of(index, count):
    return pl.ds(pl.multiple_of(index * count, count), count)


def half_of(ref, index, part, count):
    half = count // 2
    return ref.at[pl.ds(pl.multiple_of(index * count + part * half, half), half)]


def gather_begin(gather, sems, me, peers, count):
    x, y, _ = peers
    first, second = half_of(gather, me, 0, count), half_of(gather, me, 1, count)
    copies = [
        remote(first, first, sems, 0, x),
        remote(second, second, sems, 2, y),
        remote(second, second, sems, 1, x),
        remote(first, first, sems, 3, y),
    ]
    for copy in copies:
        copy.start()
    return copies


def gather_forward(gather, sems, peers, count):
    x, y, _ = peers
    from_x, from_y = half_of(gather, x, 0, count), half_of(gather, y, 1, count)
    remote(from_x, from_x, sems, 0, x).wait_recv()
    onward = remote(from_x, from_x, sems, 4, y)
    onward.start()
    remote(from_y, from_y, sems, 2, y).wait_recv()
    across = remote(from_y, from_y, sems, 5, x)
    across.start()
    return [onward, across]


def gather_wait(gather, sems, slot, peers, count):
    for part, at in (((1, 1),), ((0, 3),), ((0, 4), (1, 5)))[slot]:
        block = half_of(gather, peers[slot], part, count)
        remote(block, block, sems, at, peers[slot]).wait_recv()


HALF_ORDER = ((0, 0), (1, 1), (0, 1), (1, 0), (2, 0), (2, 1))


def half_rows(index, part, count):
    half = count // 2
    return pl.ds(pl.multiple_of(index * count + part * half, half), half)


def gather_wait_half(gather, sems, slot, part, peers, count):
    at = {(0, 1): 1, (1, 0): 3, (2, 0): 4, (2, 1): 5}.get((slot, part))
    if at is not None:
        block = half_of(gather, peers[slot], part, count)
        remote(block, block, sems, at, peers[slot]).wait_recv()


def reduce_send_half(slot, part, send, recv, sems, peers):
    half = send.shape[1] // 2
    quarter = half // 2
    plan = {
        (0, 0): [(0, half, 0, 0)],
        (1, 1): [(half, half, 1, 1)],
        (2, 0): [(0, quarter, 2, 0), (quarter, quarter, 3, 0)],
        (2, 1): [(half, quarter, 4, 1), (half + quarter, quarter, 5, 1)],
    }.get((slot, part), [])
    copies = [
        remote(
            send.at[slot, pl.ds(start, size)], recv.at[slot, pl.ds(start, size)], sems, at,
            peers[to],
        )
        for start, size, at, to in plan
    ]
    for copy in copies:
        copy.start()
    return copies


def reduce_send(slot, send, recv, sems, peers):
    x, y, _ = peers
    half = send.shape[1] // 2
    quarter = half // 2
    if slot == 2:
        plan = [(0, quarter, 2, x), (half, quarter, 4, y), (quarter, quarter, 3, x)]
        plan.append((half + quarter, quarter, 5, y))
    else:
        plan = [(slot * half, half, slot, (x, y)[slot])]
    copies = [
        remote(
            send.at[slot, pl.ds(start, size)], recv.at[slot, pl.ds(start, size)], sems, at, peer
        )
        for start, size, at, peer in plan
    ]
    for copy in copies:
        copy.start()
    return copies


def reduce_pass(send, recv, sems, peers):
    x, y, _ = peers
    half = send.shape[1] // 2
    quarter = half // 2
    copies = []
    for start, at, source, slot, peer in (
        (half, 4, y, 0, x),
        (0, 2, x, 1, y),
        (half + quarter, 5, y, 0, x),
        (quarter, 3, x, 1, y),
    ):
        rows = pl.ds(start, quarter)
        remote(send.at[2, rows], recv.at[2, rows], sems, at, source).wait_recv()
        add_low(send.at[slot, rows], recv.at[2, rows])
        copy = remote(send.at[slot, rows], recv.at[slot, rows], sems, at + 4, peer)
        copy.start()
        copies.append(copy)
    return copies


def reduce_wait(send, recv, sems, peers):
    x, y, _ = peers
    half = send.shape[1] // 2
    quarter = half // 2
    for slot, start, size, at, peer in (
        (0, 0, half, 0, x),
        (1, half, half, 1, y),
        (0, half, quarter, 8, x),
        (1, 0, quarter, 6, y),
        (0, half + quarter, quarter, 9, x),
        (1, quarter, quarter, 7, y),
    ):
        rows = pl.ds(start, size)
        remote(send.at[slot, rows], recv.at[slot, rows], sems, at, peer).wait_recv()


def by_rows(total, step, body):
    def run(i, carry):
        body(pl.ds(pl.multiple_of(i * step, step), step))
        return carry

    lax.fori_loop(0, total // step, run, 0)


def valid_rows(lengths, start, count):
    at = lax.broadcasted_iota(jnp.int32, (count, 1), 0) + start
    return (at < lengths[0, lax.axis_index("section")]).astype(f32)


def normed_rows(x, gain, shift):
    mean = jnp.mean(x, axis=-1, keepdims=True)
    centred = x - mean
    inverse = lax.rsqrt(jnp.mean(centred * centred, axis=-1, keepdims=True) + 1e-05)
    return centred * inverse * gain + shift


def norm_back_rows(grad, x, gain):
    mean = jnp.mean(x, axis=-1, keepdims=True)
    centred = x - mean
    inverse = lax.rsqrt(jnp.mean(centred * centred, axis=-1, keepdims=True) + 1e-05)
    hat = centred * inverse
    scaled = grad * gain
    back = inverse * (
        scaled
        - jnp.mean(scaled, axis=-1, keepdims=True)
        - hat * jnp.mean(scaled * hat, axis=-1, keepdims=True)
    )
    return back, jnp.sum(grad * hat, axis=0, keepdims=True), jnp.sum(grad, axis=0, keepdims=True)


def norm_into(gather, start, x, gain, shift):
    step = 32

    def body(i, carry):
        rows = pl.ds(pl.multiple_of(i * step, step), step)
        at = pl.ds(pl.multiple_of(start + i * step, step), step)
        gather[at, :] = normed_rows(x[rows, :].astype(f32), gain, shift).astype(low)
        return carry

    lax.fori_loop(0, x.shape[0] // step, body, 0)


def masked_into(gather, start, grad, lengths):
    step = 32

    def body(i, carry):
        rows = pl.ds(pl.multiple_of(i * step, step), step)
        at = pl.ds(pl.multiple_of(start + i * step, step), step)
        value = grad[rows, :].astype(f32) * valid_rows(lengths, start + i * step, step)
        gather[at, :] = value.astype(low)
        return carry

    lax.fori_loop(0, grad.shape[0] // step, body, 0)


def add_parts(own, recv, x, start, lengths):
    def body(rows):
        total = own[rows, :] + recv[0, rows, :].astype(f32) + recv[1, rows, :].astype(f32)
        mask = valid_rows(lengths, start + rows.start, 32)
        own[rows, :] = x[rows, :].astype(f32) + mask * total

    by_rows(own.shape[0], 32, body)


def norm_back_parts(own, recv, grad, x, gain, sums):
    sums[...] = jnp.zeros(sums.shape, f32)

    def body(rows):
        total = own[rows, :] + recv[0, rows, :].astype(f32) + recv[1, rows, :].astype(f32)
        back, gain_sum, shift_sum = norm_back_rows(total, x[rows, :].astype(f32), gain)
        own[rows, :] = grad[rows, :].astype(f32) + back
        sums[0:1, :] += gain_sum
        sums[1:2, :] += shift_sum

    by_rows(own.shape[0], 32, body)


def fetch(pairs, sems, first=0):
    copies = [
        pltpu.make_async_copy(source, target, sems.at[first + at])
        for at, (source, target) in enumerate(pairs)
    ]
    for copy in copies:
        copy.start()
    return copies


def weight_pairs_mixer(pack, win, wout):
    rows, cols = wout.shape[2], wout.shape[3] // 4
    split = win.shape[3]
    pairs = [(pack.at[:, :, :, pl.ds(0, split)], win)]
    for q in range(4):
        pairs.append(
            (
                pack.at[:, :, pl.ds(q * rows, rows), pl.ds(split, cols)],
                wout.at[:, :, :, pl.ds(q * cols, cols)],
            )
        )
    return pairs


def half_pairs_mixer(half_pack, win, wout):
    rows, cols = wout.shape[2], wout.shape[3] // 4
    split = win.shape[3]
    section = lax.axis_index("section")
    pairs = [(win.at[section], half_pack.at[:, :, pl.ds(0, split)])]
    for q in range(4):
        pairs.append(
            (
                wout.at[section, :, :, pl.ds(q * cols, cols)],
                half_pack.at[:, pl.ds(q * rows, rows), pl.ds(split, cols)],
            )
        )
    return pairs


class ChipGather:
    def __init__(self, own, pack, plane_sems, core_sems):
        self.section = lax.axis_index("section")
        here, near, far = along_planes()
        self.pack, self.plane_sems, self.core_sems = pack, plane_sems, core_sems
        self.near, self.far = near, far
        self.order = (here, near, far, (near + 2) % 4)
        self.own = own
        self.sends = []

    def move(self, at, sems, slot, device):
        block = self.pack.at[self.section, self.order[at]]
        copy = remote_to(self.own if at == 0 else block, block, sems, slot, device)
        copy.start()
        self.sends.append(copy)

    def to_core(self, slot):
        self.move(slot, self.core_sems, slot, other_core())

    def begin(self, load_sem):
        self.move(0, self.plane_sems, 1, {"dp": self.far})
        self.move(0, self.plane_sems, 0, {"dp": self.near})
        self.to_core(0)
        self.keep = pltpu.make_async_copy(
            self.own, self.pack.at[self.section, self.order[0]], load_sem
        )
        self.keep.start()

    def arrived(self, slot):
        block = self.pack.at[self.section, self.order[slot + 1]]
        remote_to(block, block, self.plane_sems, slot, {"dp": self.near}).wait_recv()

    def forward(self):
        self.arrived(1)
        self.move(2, self.plane_sems, 2, {"dp": self.near})
        self.to_core(2)
        self.arrived(0)
        self.to_core(1)

    def end(self):
        self.arrived(2)
        self.to_core(3)
        self.keep.wait()
        for slot in range(4):
            block = self.pack.at[1 - self.section, self.order[slot]]
            remote_to(block, block, self.core_sems, slot, other_core()).wait_recv()


def sine_pair(x):
    turns = jnp.floor(x * (2.0 / math.pi) + 0.5)
    rest = x - turns * 1.5703125
    rest = rest - turns * 4.837512969970703125e-4
    rest = rest - turns * 7.54978995489188e-8
    square = rest * rest
    sine = -1.9515295891e-4 * square + 8.3321608736e-3
    sine = (sine * square - 1.6666654611e-1) * square * rest + rest
    cosine = 2.443315711809948e-5 * square - 1.388731625493765e-3
    cosine = (cosine * square + 4.166664568298827e-2) * square * square - 0.5 * square + 1.0
    halves = jnp.floor(turns * 0.5)
    odd = turns - 2.0 * halves
    back = halves - 2.0 * jnp.floor(halves * 0.5)
    swapped = odd > 0.5
    side = 1.0 - 2.0 * back
    wave = jnp.where(swapped, cosine, sine) * side
    slope = jnp.where(swapped, -sine, cosine) * side
    return wave, slope


def network_rows(small, embedding, network, taps_low, i):
    step = 256
    waves1, waves2, steep1, steep2 = network
    knots = waves1.shape[1]
    pair = (pl.ds(i * step, step), pl.ds(embedding.shape[0] // 2 + i * step, step))

    def layer(sources, weights, waves, steep):
        inner = jnp.concatenate([dot_exact(item, weights) for item in sources], 1)
        wave, slope = sine_pair(inner)
        for at, rows in enumerate(pair):
            cols = slice(at * knots, (at + 1) * knots)
            waves[rows, :] = wave[:, cols]
            steep[rows, :] = slope[:, cols]

    layer([embedding[rows, 0:64] for rows in pair], small[64:128, 128:192], waves1, steep1)
    layer([waves1[rows, :] for rows in pair], small[64:128, 0:64], waves2, steep2)
    for rows in pair:
        times = lax.broadcasted_iota(jnp.int32, (step, 1), 0) + rows.start
        fade = jnp.exp(-times.astype(f32) * small[154:155, :])
        taps_low[rows, :] = (dot_exact(waves2[rows, :], small[0:64, :]) * fade).astype(low)


def ff_blocks(
    gather, wup, wdown, value, slope, result_out, send, recv, gather_sems, reduce_sems, me, peers,
    pause,
):
    count, width = result_out.shape
    half = wup.shape[3]
    sends = []
    for slot, part in ((None, None), *HALF_ORDER):
        if slot is None:
            rows, sent = rows_of(me, count), None
        else:
            rows = half_rows(peers[slot], part, count)
            sent = slice(part * count // 2, (part + 1) * count // 2)
            gather_wait_half(gather, gather_sems, slot, part, peers, count)

        def hidden(i, carry):
            cols = pl.ds(pl.multiple_of(i * 256, 256), 256)
            for h in range(2):
                pre = mm(gather[rows, :], wup[h, :, :, cols].reshape(width, 256))
                after, steep = gelu_both(pre)
                at = pl.ds(pl.multiple_of(h * half + i * 256, 256), 256)
                value[rows, at] = after.astype(low)
                slope[rows, at] = steep.astype(low)
            return carry

        lax.fori_loop(0, half // 256, hidden, 0)
        for h in range(2):
            cols = slice(h * width // 2, (h + 1) * width // 2)
            out = mm(value[rows, :], wdown[h].reshape(2 * half, width // 2))
            if slot is None:
                result_out[:, cols] = out
            else:
                send[slot, sent, cols] = out.astype(low)
        if slot is not None:
            sends += reduce_send_half(slot, part, send, recv, reduce_sems, peers)
            pause(slot, part)
    return sends


def mixer_forward_kernel(
    s, gathers, x, *refs
):
    if gathers:
        (
            cotangent, embedding, lengths, w_in, w_out, w_up, w_down, gain, shift, tap_rows, first_w,
            second_w, last_w, direct, rates, waves_hbm, back_hbm,
            pack_out, ff_out, late_out, par_out, small_out, next_pack_out, ff_part_out,
            *refs,
        ) = refs
        network_outs, next_outs, refs = refs[:5], refs[5:10], refs[10:]
        second_out, value_out, slope_out, result_out, *refs = refs
        (
            *refs, waves1, waves2, steep1, steep2, taps_low, raw_out, ff_all, late, next_pack, core_sems,
            plane_sems, out_core_sems, out_plane_sems, ff_core_sems, ff_plane_sems, next_core_sems, next_plane_sems, late_sems,
            pack_sems, mixer_parts, ff_parts, par_all, small_all, stage_in, stage_out, stage_up,
            in_sems, out_sems, up_sems, down_sems, par_sems, small_sems,
            second, ff_send, ff_recv, second_sems, ff_sems, network_sems,
        ) = refs
        x = x.at[lax.axis_index("section"), 0]
        cotangent = cotangent.at[lax.axis_index("section"), 0]
        network = (waves1, waves2, steep1, steep2)
    else:
        par_all, small_all, lengths, weights_hbm, filt_hbm, waves_hbm, back_hbm, *refs = refs
    (
        normed_out, proj_out, stream_out, prod_out, spec_out, filtered_out, gated_out, middle_out,
        gather, win, wout, filt, waves, back, proj, proj_low, streams, prod, spec, mixed, filtered,
        gated, send, recv, gather_sems, reduce_sems, load_sems, store_sems,
    ) = refs
    par, small = par_all.at[s], small_all.at[s]
    me = lax.axis_index("seq")
    peers = neighbours(me)
    count, width = x.shape
    length = gather.shape[0]
    chans = prod.shape[1]
    half = win.shape[3]
    if gathers:
        section = lax.axis_index("section")
        targets = shuffle_targets(section, me, peers)
        greeted = greet([device for _, _, device in targets] + plane_devices())
    else:
        greeted = greet(in_plane(peers[:2]))
    tables = fetch([(waves_hbm, waves), (back_hbm, back)], load_sems)
    sends = []
    if gathers:
        shuffle_stage(w_in, w_out, w_up, stage_in, stage_out, stage_up)
        parameters_stage(
            me, par_all.at[section], small_all.at[section], gain, shift, tap_rows, first_w, second_w,
            last_w, direct, rates,
        )
        all_here(greeted)
        sends += shuffle_send(
            section, me, targets, (stage_in, stage_out, stage_up, w_down), (mixer_parts, ff_parts),
            (par_all, small_all), (in_sems, out_sems, up_sems, down_sems, par_sems, small_sems),
        )
        in_cols, out_cols = pl.ds(0, half), pl.ds(half, raw_out.shape[3])
        in_pack = ChipGather(mixer_parts.at[0, :, in_cols], win, plane_sems, core_sems)
        out_pack = ChipGather(mixer_parts.at[0, :, out_cols], raw_out, out_plane_sems, out_core_sems)
        ff_pack = ChipGather(ff_parts.at[0], ff_all, ff_plane_sems, ff_core_sems)
        for sems, item in ((par_sems, par_all), (small_sems, small_all)):
            block = item.at[1 - section]
            remote_to(block, block, sems, 0, other_core()).wait_recv()
        norm_into(gather, me * count, x, par[0:1, :], par[1:2, :])
        shuffle_wait_mixer(section, me, targets, mixer_parts, stage_in, in_sems, out_sems)
        in_pack.begin(pack_sems.at[0])
        sends += gather_begin(gather, gather_sems, me, peers, count)
        masked_into(late, me * count, cotangent, lengths)
    else:
        weights = fetch(weight_pairs_mixer(weights_hbm, win, wout), load_sems, 2)
        filt_load = fetch([(filt_hbm, filt)], load_sems, 7)
        norm_into(gather, me * count, x, par[0:1, :], par[1:2, :])
        all_here(greeted)
        sends += gather_begin(gather, gather_sems, me, peers, count)
    proj[0:8, :] = jnp.zeros((8, proj.shape[1]), f32)
    tile_rows = 256

    def filter_spectrum(i, carry):
        rows = pl.ds(pl.multiple_of(i * tile_rows, tile_rows), tile_rows)
        filt[rows, :] = mm(waves[rows, :], taps_low[...])
        return carry

    stores = []
    if gathers:
        network_rows(small, embedding, network, taps_low, 0)
    sends += gather_forward(gather, gather_sems, peers, count)
    if gathers:
        sends += gather_begin(late, late_sems, me, peers, count)
        in_pack.forward()
        out_pack.begin(pack_sems.at[13])
        network_rows(small, embedding, network, taps_low, 1)
        tables[0].wait()
        lax.fori_loop(0, 2 * length // tile_rows, filter_spectrum, 0)
        network_stores = fetch(list(zip((filt, *network), network_outs)), network_sems)
        out_pack.forward()
        shuffle_wait_ff(section, me, targets, ff_parts, stage_up, up_sems, down_sems)
        ff_pack.begin(pack_sems.at[1])
        in_pack.end()
        stores += fetch(
            [
                (win, pack_out.at[:, :, :, in_cols]),
                (par_all, par_out),
                (small_all, small_out),
                (ff_parts.at[1], ff_part_out),
            ],
            pack_sems,
            4,
        )
    else:
        tables[0].wait()
    if not gathers:
        weights[0].wait()
    step = 64
    steps = count // step

    def short_conv(start):
        for g in range(3):
            cols = slice(g * chans, (g + 1) * chans)
            tile = proj[pl.ds(start, step + 8), cols]
            proj_low[pl.ds(start, step), cols] = tile[8:].astype(low)
            value = (
                small[144 + 3 * g : 145 + 3 * g, :] * tile[8:]
                + small[145 + 3 * g : 146 + 3 * g, :] * pltpu.roll(tile, 1, 0)[8:]
                + small[146 + 3 * g : 147 + 3 * g, :] * pltpu.roll(tile, 2, 0)[8:]
            )
            streams[pl.ds(start, step), cols] = value.astype(low)
        first = streams[pl.ds(start, step), 0:chans].astype(f32)
        third = streams[pl.ds(start, step), 2 * chans : 3 * chans].astype(f32)
        prod[pl.ds(start, step), :] = (first * third * valid_rows(lengths, start, step)).astype(low)

    def within(source):
        def body(i, carry):
            short_conv(pl.multiple_of(source * count + i * step, step))
            return carry

        lax.fori_loop(1, steps, body, 0)

    for slot in (None, 0, 1, 2):
        source = me if slot is None else peers[slot]
        if slot is not None:
            gather_wait(gather, gather_sems, slot, peers, count)
        block = gather[rows_of(source, count), :]
        for h in range(2):
            proj[pl.ds(pl.multiple_of(source * count + 8, 8), count), h * half : (h + 1) * half] = mm(
                block, win[h].reshape(width, half)
            )
        within(source)
    if gathers:
        sends += gather_forward(late, late_sems, peers, count)

    def seams(i, carry):
        short_conv(pl.multiple_of(i * count, step))
        return carry

    lax.fori_loop(0, length // count, seams, 0)
    stores += fetch(
        [(gather, normed_out), (proj_low, proj_out), (streams, stream_out), (prod, prod_out)],
        store_sems,
    )
    if not gathers:
        filt_load[0].wait()

    def spectrum(i, carry):
        up = pl.ds(pl.multiple_of(i * tile_rows, tile_rows), tile_rows)
        down = pl.ds(pl.multiple_of(i * tile_rows + length, tile_rows), tile_rows)
        prod_cos = mm(waves[up, :], prod[...])
        prod_sin = mm(waves[down, :], prod[...])
        filt_cos, filt_sin = filt[up, :], filt[down, :]
        spec[up, :] = prod_cos.astype(low)
        spec[down, :] = prod_sin.astype(low)
        mixed[up, :] = (prod_cos * filt_cos - prod_sin * filt_sin).astype(low)
        mixed[down, :] = (prod_cos * filt_sin + prod_sin * filt_cos).astype(low)
        return carry

    lax.fori_loop(0, length // tile_rows, spectrum, 0)
    tables[1].wait()
    if gathers:
        out_pack.end()
        cols = raw_out.shape[3]
        weights = fetch(
            [
                (
                    raw_out.at[:, :, pl.ds(q * wout.shape[2], wout.shape[2]), :],
                    wout.at[:, :, :, pl.ds(q * cols, cols)],
                )
                for q in range(4)
            ],
            load_sems,
            3,
        )
        stores += fetch([(raw_out, pack_out.at[:, :, :, out_cols])], pack_sems, 14)
        for load in weights:
            load.wait()
    else:
        for load in weights[1:]:
            load.wait()
    for slot in (2, 0, 1, None):
        target = me if slot is None else peers[slot]
        rows = rows_of(target, count)
        value = mm(back[rows, :], mixed[...]) * (1.0 / length)
        value = value + small[153:154, :] * prod[rows, :].astype(f32)
        filtered[rows, :] = value
        gate = (streams[rows, chans : 2 * chans].astype(f32) * value).astype(low)
        gated[rows, :] = gate
        outs = [mm(gate, wout[h].reshape(chans, width // 2)) for h in range(2)]
        for h in range(2):
            cols = slice(h * width // 2, (h + 1) * width // 2)
            if slot is None:
                middle_out[:, cols] = outs[h]
            else:
                send[slot, :, cols] = outs[h].astype(low)
        if slot is not None:
            sends += reduce_send(slot, send, recv, reduce_sems, peers)
    if gathers:
        ff_pack.forward()
        for slot in range(3):
            gather_wait(late, late_sems, slot, peers, count)
        stores += fetch([(late, late_out)], pack_sems, 2)
    sends += reduce_pass(send, recv, reduce_sems, peers)
    stores += fetch(
        [(spec, spec_out), (filtered, filtered_out), (gated, gated_out)],
        store_sems,
        4,
    )
    if gathers:
        for store in network_stores:
            store.wait()
        for i in range(2):
            network_rows(small_all.at[1], embedding, network, taps_low, i)
        lax.fori_loop(0, 2 * length // tile_rows, filter_spectrum, 0)
        network_stores = fetch(list(zip((filt, *network), next_outs)), network_sems)
    reduce_wait(send, recv, reduce_sems, peers)
    add_parts(middle_out, recv, x, me * count, lengths)
    if gathers:
        next_mixer = ChipGather(mixer_parts.at[1], next_pack, next_plane_sems, next_core_sems)
        norm_into(second, me * count, middle_out, par[2:3, :], par[3:4, :])
        sends += gather_begin(second, second_sems, me, peers, count)
        sends += gather_forward(second, second_sems, peers, count)
        ff_pack.end()
        next_mixer.begin(pack_sems.at[8])
        stores += fetch([(ff_all, ff_out)], pack_sems, 3)
        rows_up = ff_all.shape[2] // 2
        value, slope = waves.at[pl.ds(0, length)], waves.at[pl.ds(length, length)]

        def pause(slot, part):
            if (slot, part) == (1, 1):
                next_mixer.forward()

        sends += ff_blocks(
            second, ff_all.at[:, :, pl.ds(0, rows_up)], ff_all.at[:, :, pl.ds(rows_up, rows_up)],
            value, slope, result_out, ff_send, ff_recv, second_sems, ff_sems, me, peers, pause,
        )
        sends += reduce_pass(ff_send, ff_recv, ff_sems, peers)
        stores += fetch([(second, second_out), (value, value_out), (slope, slope_out)], pack_sems, 9)
        next_mixer.end()
        stores += fetch([(next_pack, next_pack_out)], pack_sems, 12)
        reduce_wait(ff_send, ff_recv, ff_sems, peers)
        add_parts(result_out, ff_recv, middle_out, me * count, lengths)
        sends += in_pack.sends + out_pack.sends + ff_pack.sends + next_mixer.sends
        stores += network_stores
    for copy in sends:
        copy.wait_send()
    for store in stores:
        store.wait()


def ff_turn_kernel(
    s, cotangent, x, par_all, lengths, pack, late_hbm,
    half_out, value_out, middle_grad_out, sums_out,
    gather, late, wup, wdown, value, pre, wgrad, other, send_back, recv_back,
    gather_sems, back_sems, load_sems, store_sems, core_sems,
):
    par = par_all.at[s]
    grad = cotangent.at[lax.axis_index("section"), 0]
    me = lax.axis_index("seq")
    peers = neighbours(me)
    count, width = x.shape
    half = wup.shape[3]
    rows_up = wup.shape[2]
    greeted = greet(in_plane(peers[:2]) + [other_core()])
    loads = fetch(
        [
            (pack.at[:, :, pl.ds(0, rows_up), :], wup),
            (pack.at[:, :, pl.ds(rows_up, wdown.shape[2]), :], wdown),
            (late_hbm, late),
        ],
        load_sems,
    )
    norm_into(gather, me * count, x, par[2:3, :], par[3:4, :])
    all_here(greeted)
    sends = gather_begin(gather, gather_sems, me, peers, count)
    for load in loads:
        load.wait()
    for slot, part in ((None, None), *HALF_ORDER):
        if slot is None:
            rows, sent = rows_of(me, count), None
        else:
            rows = half_rows(peers[slot], part, count)
            sent = slice(part * count // 2, (part + 1) * count // 2)
            gather_wait_half(gather, gather_sems, slot, part, peers, count)

        def hidden(i, carry):
            cols = pl.ds(pl.multiple_of(i * rows_up, rows_up), rows_up)
            for h in range(2):
                block = h * (half // rows_up) + i
                at = pl.ds(pl.multiple_of(block * rows_up, rows_up), rows_up)
                after, steep = gelu_both(
                    mm(gather[rows, :], wup[h, :, :, cols].reshape(width, rows_up))
                )
                value[rows, at] = after.astype(low)
                back = mm_t(late[rows, : width // 2], wdown[0, block]) + mm_t(
                    late[rows, width // 2 :], wdown[1, block]
                )
                pre[rows, at] = (back * steep).astype(low)
            return carry

        lax.fori_loop(0, half // rows_up, hidden, 0)

        def through(i, carry):
            cols = pl.ds(pl.multiple_of(i * rows_up, rows_up), rows_up)
            back = mm_t(pre[rows, :half], wup[0, i]) + mm_t(pre[rows, half:], wup[1, i])
            if slot is None:
                middle_grad_out[:, cols] = back
            else:
                send_back[slot, sent, cols] = back.astype(low)
            return carry

        lax.fori_loop(0, width // rows_up, through, 0)
        if slot is None:
            sends += gather_forward(gather, gather_sems, peers, count)
        else:
            sends += reduce_send_half(slot, part, send_back, recv_back, back_sems, peers)
    stores = fetch([(value, value_out)], store_sems, 1)

    def weights(i, carry):
        cols = pl.ds(pl.multiple_of(i * rows_up, rows_up), rows_up)
        for h in range(2):
            wgrad[h, i, 0:rows_up, :] = t_mm(
                gather[:, cols], pre[:, h * half : (h + 1) * half]
            ).astype(low)
            wgrad[h, i, rows_up : 2 * rows_up, :] = t_mm(
                value[:, cols], late[:, h * width // 2 : (h + 1) * width // 2]
            ).astype(low)
        return carry

    middle = width // rows_up // 2
    early, late_part = pl.ds(0, middle), pl.ds(middle, middle)
    lax.fori_loop(0, middle, weights, 0)
    swapped = [(wgrad.at[:, early], other.at[early])]
    swaps = swap_begin(swapped, core_sems.at[0])
    sends += reduce_pass(send_back, recv_back, back_sems, peers)
    lax.fori_loop(middle, 2 * middle, weights, 0)
    swapped_late = [(wgrad.at[:, late_part], other.at[late_part])]
    swaps_late = swap_begin(swapped_late, core_sems.at[1])
    sends += swaps + swaps_late
    swap_end(swaps, swapped)
    reduce_wait(send_back, recv_back, back_sems, peers)
    norm_back_parts(middle_grad_out, recv_back, grad, x, par[2:3, :], sums_out)
    swap_end(swaps_late, swapped_late)
    stores += fetch([(wgrad.at[lax.axis_index("section")], half_out)], store_sems)
    for copy in sends:
        copy.wait_send()
    for store in stores:
        store.wait()


def ff_backward_kernel(
    s, grad, middle, par_all, lengths, pack, second_hbm, value_hbm, slope_hbm, earlier,
    half_out, middle_grad_out, sums_out, summed,
    gather, wup, wdown, second, value, slope, pre, wgrad, other, send, recv, gather_sems,
    reduce_sems, load_sems, store_sems, mine, arrived, plane_sems, sum_sems, core_sems,
):
    par = par_all.at[s]
    me = lax.axis_index("seq")
    peers = neighbours(me)
    count, width = grad.shape
    greeted = greet(in_plane(peers[:2]) + plane_devices() + [other_core()])
    half = wup.shape[3]
    units = 2 * half
    up_rows = wup.shape[2]
    loads = fetch(
        [
            (pack.at[:, :, pl.ds(0, up_rows), :], wup),
            (pack.at[:, :, pl.ds(up_rows, wdown.shape[2]), :], wdown),
            (slope_hbm, slope),
            (second_hbm, second),
            (value_hbm, value),
        ],
        load_sems,
    )
    masked_into(gather, me * count, grad, lengths)
    all_here(greeted)
    sends = gather_begin(gather, gather_sems, me, peers, count)
    plane_sum = PlaneSum(earlier, mine, arrived, plane_sems, sum_sems)
    plane_sum.begin()
    for load in loads[:3]:
        load.wait()
    for slot, part in ((None, None), *HALF_ORDER):
        if slot is None:
            rows, sent = rows_of(me, count), None
        else:
            rows = half_rows(peers[slot], part, count)
            sent = slice(part * count // 2, (part + 1) * count // 2)
            gather_wait_half(gather, gather_sems, slot, part, peers, count)

        def hidden(i, carry):
            cols = pl.ds(pl.multiple_of(i * up_rows, up_rows), up_rows)
            back = mm_t(gather[rows, : width // 2], wdown[0, i]) + mm_t(
                gather[rows, width // 2 :], wdown[1, i]
            )
            pre[rows, cols] = (back * slope[rows, cols].astype(f32)).astype(low)
            return carry

        lax.fori_loop(0, units // up_rows, hidden, 0)

        def through(i, carry):
            cols = pl.ds(pl.multiple_of(i * up_rows, up_rows), up_rows)
            back = mm_t(pre[rows, :half], wup[0, i]) + mm_t(pre[rows, half:], wup[1, i])
            if slot is None:
                middle_grad_out[:, cols] = back
            else:
                send[slot, sent, cols] = back.astype(low)
            return carry

        lax.fori_loop(0, width // up_rows, through, 0)
        if slot is None:
            sends += gather_forward(gather, gather_sems, peers, count)
        else:
            sends += reduce_send_half(slot, part, send, recv, reduce_sems, peers)
    plane_sum.forward()
    for load in loads[3:]:
        load.wait()

    def weights(i, carry):
        cols = pl.ds(pl.multiple_of(i * up_rows, up_rows), up_rows)
        for h in range(2):
            wgrad[h, i, 0:up_rows, :] = t_mm(
                second[:, cols], pre[:, h * half : (h + 1) * half]
            ).astype(low)
            wgrad[h, i, up_rows : 2 * up_rows, :] = t_mm(
                value[:, cols], gather[:, h * width // 2 : (h + 1) * width // 2]
            ).astype(low)
        return carry

    half_blocks = width // up_rows // 2
    early, late_part = pl.ds(0, half_blocks), pl.ds(half_blocks, half_blocks)
    lax.fori_loop(0, half_blocks, weights, 0)
    swapped = [(wgrad.at[:, early], other.at[early])]
    swaps = swap_begin(swapped, core_sems.at[0])
    sends += reduce_pass(send, recv, reduce_sems, peers)
    lax.fori_loop(half_blocks, 2 * half_blocks, weights, 0)
    swapped_late = [(wgrad.at[:, late_part], other.at[late_part])]
    swaps_late = swap_begin(swapped_late, core_sems.at[1])
    sends += swaps + swaps_late
    plane_sum.end(summed)
    sends += plane_sum.sends
    swap_end(swaps, swapped)
    swap_end(swaps_late, swapped_late)
    stores = fetch([(wgrad.at[lax.axis_index("section")], half_out)], store_sems)
    reduce_wait(send, recv, reduce_sems, peers)
    norm_back_parts(middle_grad_out, recv, grad, middle, par[2:3, :], sums_out)
    for copy in sends:
        copy.wait_send()
    for store in stores:
        store.wait()


def t_mm_exact(a, b):
    return lax.dot_general(
        a, b, (((0,), (0,)), ((), ())), preferred_element_type=f32, precision=precise
    )


def mm_t_exact(a, b):
    return lax.dot_general(
        a, b, (((1,), (1,)), ((), ())), preferred_element_type=f32, precision=precise
    )


def dot_exact(a, b):
    return jnp.dot(a, b, preferred_element_type=f32, precision=precise)


def by_layer(begin, triples, layer_sems, keep_sems, base=0):
    section = lax.axis_index("section")
    for index in range(2):

        @pl.when(section == index)
        def _():
            for at, (first, second, target) in enumerate(triples, base):
                kept, sent = (first, second) if index == 0 else (second, first)
                slot = target.at[index]
                copies = (
                    pltpu.make_async_copy(kept, slot, keep_sems.at[at]),
                    remote_to(sent, slot, layer_sems, at, other_core()),
                )
                for copy in copies:
                    if begin:
                        copy.start()
                    else:
                        copy.wait()


def mixer_backward_kernel(
    s, grad, x, par_all, small_all, embedding, late, lengths, pack, filt_hbm, waves_hbm, back_hbm, normed_hbm, proj_hbm,
    stream_hbm, prod_hbm, spec_hbm, filtered_hbm, gated_hbm, waves1_hbm, waves2_hbm, steep1_hbm,
    steep2_hbm, earlier,
    half_out, small_out, input_grad_out, summed,
    gather, win, wout, filt, waves, back, normed, proj, streams, prod, spec, filtered, gated,
    gated_grad, filtered_grad, both, grad_spec, grad_sum, filter_grad, mixed, proj_grad, wgrad_in, wgrad_out_part,
    other_in, other_out, waves1, waves2, steep1, steep2, sums, taps_sum, send, recv, gather_sems, reduce_sems, load_sems, store_sems,
    mine, arrived, plane_sems, sum_sems, core_sems,
):
    par, small = par_all.at[s], small_all.at[s]
    me = lax.axis_index("seq")
    peers = neighbours(me)
    if s == 0:
        x = x.at[lax.axis_index("section"), 0]
    count, width = grad.shape
    greeted = greet(in_plane(peers[:2]) + plane_devices() + [other_core()])
    length = gather.shape[0]
    chans = prod.shape[1]
    half = win.shape[3]
    depth = win.shape[2]
    loads = fetch(
        weight_pairs_mixer(pack, win, wout)
        + [
            (stream_hbm, streams),
            (waves_hbm, waves),
            (filt_hbm, filt),
            (spec_hbm, spec),
            (back_hbm, back),
            (prod_hbm, prod),
            (filtered_hbm, filtered),
            (proj_hbm, proj),
            (normed_hbm, normed),
            (gated_hbm, gated),
            (waves1_hbm, waves1),
            (waves2_hbm, waves2),
            (steep1_hbm, steep1),
            (steep2_hbm, steep2),
        ],
        load_sems,
    )
    masked_into(gather, me * count, grad, lengths)
    all_here(greeted)
    sends = gather_begin(gather, gather_sems, me, peers, count)
    plane_sum = PlaneSum(earlier, mine, arrived, plane_sems, sum_sems)
    plane_sum.begin()
    for load in loads[1:6]:
        load.wait()
    tile_rows = 256
    for slot in (None, 0, 1, 2):
        source = me if slot is None else peers[slot]
        rows = rows_of(source, count)
        if slot is not None:
            gather_wait(gather, gather_sems, slot, peers, count)
        value = (
            mm_t(gather[rows, : width // 2], wout[0].reshape(chans, width // 2))
            + mm_t(gather[rows, width // 2 :], wout[1].reshape(chans, width // 2))
        ).astype(low)
        gated_grad[rows, :] = value
        filtered_grad[rows, :] = (
            value.astype(f32) * streams[rows, chans : 2 * chans].astype(f32)
        ).astype(low)
        if slot is None:
            sends += gather_forward(gather, gather_sems, peers, count)
            for load in loads[6:]:
                load.wait()
            loads[0].wait()
        if slot == 2:
            plane_sum.forward()

        def spectrum(i, carry):
            up = pl.ds(pl.multiple_of(i * tile_rows, tile_rows), tile_rows)
            down = pl.ds(pl.multiple_of(i * tile_rows + length, tile_rows), tile_rows)
            fg_cos = mm(waves[up, rows], filtered_grad[rows, :])
            fg_sin = mm(waves[down, rows], filtered_grad[rows, :])
            if slot is not None:
                fg_cos = fg_cos + grad_sum[up, :]
                fg_sin = fg_sin + grad_sum[down, :]
            if slot != 2:
                grad_sum[up, :] = fg_cos
                grad_sum[down, :] = fg_sin
            else:
                filt_cos, filt_sin = filt[up, :], filt[down, :]
                grad_spec[up, :] = fg_cos.astype(low)
                grad_spec[down, :] = fg_sin.astype(low)
                both[up, :] = (filt_cos * fg_cos + filt_sin * fg_sin).astype(low)
                both[down, :] = (filt_cos * fg_sin - filt_sin * fg_cos).astype(low)
            return carry

        lax.fori_loop(0, length // tile_rows, spectrum, 0)
    mixed[pl.ds(length, 8), :] = jnp.zeros((8, mixed.shape[1]), f32)

    def streams_back(i, carry):
        rows = pl.ds(pl.multiple_of(i * tile_rows, tile_rows), tile_rows)
        value = mm(back[rows, :], both[...]) * (1.0 / length)
        fg = filtered_grad[rows, :].astype(f32)
        prod_grad = (value + small[153:154, :] * fg).astype(low).astype(f32)
        mixed[rows, 0:chans] = (
            (prod_grad * streams[rows, 2 * chans : 3 * chans].astype(f32)).astype(low).astype(f32)
        )
        mixed[rows, chans : 2 * chans] = (
            (gated_grad[rows, :].astype(f32) * filtered[rows, :]).astype(low).astype(f32)
        )
        mixed[rows, 2 * chans : 3 * chans] = (
            (prod_grad * streams[rows, 0:chans].astype(f32)).astype(low).astype(f32)
        )
        return carry + jnp.sum(fg * prod[rows, :].astype(f32), axis=0, keepdims=True)

    small_out[...] = jnp.zeros(small_out.shape, f32)
    small_out[153:154, :] = lax.fori_loop(
        0, length // tile_rows, streams_back, jnp.zeros((1, chans), f32)
    )
    step = 128
    for slot in (2, 0, 1, None):
        target = me if slot is None else peers[slot]

        def short_back(i, carry):
            start = pl.multiple_of(target * count + i * step, step)
            for g in range(3):
                cols = slice(g * chans, (g + 1) * chans)
                tile = mixed[pl.ds(start, step + 8), cols]
                now = tile[:step]
                after = pltpu.roll(tile, step + 7, 0)[:step]
                later = pltpu.roll(tile, step + 6, 0)[:step]
                proj_grad[pl.ds(start, step), cols] = (
                    small[144 + 3 * g : 145 + 3 * g, :] * now
                    + small[145 + 3 * g : 146 + 3 * g, :] * after
                    + small[146 + 3 * g : 147 + 3 * g, :] * later
                ).astype(low)
            return carry

        lax.fori_loop(0, count // step, short_back, 0)
        rows = rows_of(target, count)

        def through(i, carry):
            cols = pl.ds(pl.multiple_of(i * depth, depth), depth)
            value = mm_t(proj_grad[rows, :half], win[0, i]) + mm_t(proj_grad[rows, half:], win[1, i])
            if slot is None:
                input_grad_out[:, cols] = value
            else:
                send[slot, :, cols] = value.astype(low)
            return carry

        lax.fori_loop(0, width // depth, through, 0)
        if slot is not None:
            sends += reduce_send(slot, send, recv, reduce_sems, peers)

    def weights(i, carry):
        cols = pl.ds(pl.multiple_of(i * depth, depth), depth)
        for h in range(2):
            wgrad_in[h, i] = t_mm(normed[:, cols], proj_grad[:, h * half : (h + 1) * half]).astype(
                low
            )
        return carry

    sends += reduce_pass(send, recv, reduce_sems, peers)
    lax.fori_loop(0, width // depth, weights, 0)
    for h in range(2):
        value = t_mm(gated[...], gather[:, h * width // 2 : (h + 1) * width // 2]).astype(low)
        wgrad_out_part[h] = value.reshape(wgrad_out_part.shape[1:])
    swapped = [(wgrad_in, other_in), (wgrad_out_part, other_out)]
    swaps = swap_begin(swapped, core_sems)
    sends += swaps
    taps_sum[...] = jnp.zeros(taps_sum.shape, f32)

    def tap_sums(i, carry):
        start = pl.multiple_of(i * step, step)
        for g in range(3):
            cols = slice(g * chans, (g + 1) * chans)
            tile = mixed[pl.ds(start, step + 8), cols]
            seen = proj[pl.ds(start, step), cols].astype(f32)
            for at in range(3):
                shift = pltpu.roll(tile, step + 8 - at, 0)[:step] if at else tile[:step]
                taps_sum[8 * at : 8 * at + 8, cols] += jnp.sum(
                    (seen * shift).reshape(step // 8, 8, chans), axis=0
                )
        return carry

    lax.fori_loop(0, length // step, tap_sums, 0)

    def filter_spectrum(i, carry):
        up = pl.ds(pl.multiple_of(i * tile_rows, tile_rows), tile_rows)
        down = pl.ds(pl.multiple_of(i * tile_rows + length, tile_rows), tile_rows)
        prod_cos, prod_sin = spec[up, :].astype(f32), spec[down, :].astype(f32)
        fg_cos, fg_sin = grad_spec[up, :].astype(f32), grad_spec[down, :].astype(f32)
        both[up, :] = (prod_cos * fg_cos + prod_sin * fg_sin).astype(low)
        both[down, :] = (prod_cos * fg_sin - prod_sin * fg_cos).astype(low)
        return carry

    lax.fori_loop(0, length // tile_rows, filter_spectrum, 0)

    def filter_back(i, carry):
        rows = pl.ds(pl.multiple_of(i * tile_rows, tile_rows), tile_rows)
        times = lax.broadcasted_iota(jnp.int32, (tile_rows, 1), 0) + i * tile_rows
        fade = jnp.exp(-times.astype(f32) * small[154:155, :])
        filter_grad[rows, :] = mm(back[rows, :], both[...]) * (1.0 / length) * fade
        return carry

    lax.fori_loop(0, length // tile_rows, filter_back, 0)
    small_out[0:64, :] = t_mm_exact(waves2[...], filter_grad[...])
    back2 = mm_t_exact(filter_grad[...], small[0:64, :]) * steep2[...]
    small_out[64:128, 0:64] = t_mm_exact(waves1[...], back2)
    back1 = mm_t_exact(back2, small[64:128, 0:64]) * steep1[...]
    small_out[64:128, 128:192] = t_mm_exact(embedding[:, 0:64], back1)
    for g in range(3):
        for at in range(3):
            small_out[144 + 3 * g + at : 145 + 3 * g + at, :] = jnp.sum(
                taps_sum[8 * at : 8 * at + 8, g * chans : (g + 1) * chans], axis=0, keepdims=True
            )
    swap_end(swaps, swapped)
    stores = fetch(half_pairs_mixer(half_out, wgrad_in, wgrad_out_part), store_sems)
    plane_sum.end(summed)
    sends += plane_sum.sends
    reduce_wait(send, recv, reduce_sems, peers)
    norm_back_parts(input_grad_out, recv, grad, x, par[0:1, :], sums)
    for q in range(width // chans):
        cols = slice(q * chans, (q + 1) * chans)
        small_out[128 + 2 * q : 130 + 2 * q, :] = sums[:, cols]
        small_out[136 + 2 * q : 138 + 2 * q, :] = late[:, cols]
    for copy in sends:
        copy.wait_send()
    for store in stores:
        store.wait()


def run_kernel(kernel, name, collective_id, operands, in_vmem, outs, out_vmem, scratch, flops):
    inside = pl.BlockSpec(memory_space=pltpu.VMEM)
    outside = pl.BlockSpec(memory_space=pl.ANY)
    scalars = pl.BlockSpec(memory_space=pltpu.SMEM)
    return pl.pallas_call(
        kernel,
        out_shape=[jax.ShapeDtypeStruct(shape, kind) for shape, kind in outs],
        in_specs=[
            scalars if item.dtype == jnp.int32 else inside if at in in_vmem else outside
            for at, item in enumerate(operands)
        ],
        out_specs=[inside if at in out_vmem else outside for at in range(len(outs))],
        scratch_shapes=scratch,
        compiler_params=pltpu.CompilerParams(
            collective_id=collective_id, has_side_effects=True, vmem_limit_bytes=60 * 2**20
        ),
        cost_estimate=pl.CostEstimate(flops=flops, bytes_accessed=2**25, transcendentals=0),
        name=name,
    )(*operands)


def exchange_scratch(count, width):
    return [pltpu.VMEM((3, count, width), low), pltpu.VMEM((3, count, width), low)]


def exchange_semaphores(count):
    return [pltpu.SemaphoreType.DMA((2, count)), pltpu.SemaphoreType.DMA((count,))]


def semaphores(loads, stores):
    return [
        pltpu.SemaphoreType.DMA((2, 6)),
        pltpu.SemaphoreType.DMA((2, 10)),
        pltpu.SemaphoreType.DMA((loads,)),
        pltpu.SemaphoreType.DMA((stores,)),
    ]


def mixer_weights_scratch(pack, width):
    _, dp_count, depth, cols = pack.shape
    return [
        pltpu.VMEM((2, dp_count, depth, 3 * cols // 4), low),
        pltpu.VMEM((2, dp_count, depth // 4, cols), low),
    ]


def mixer_forward(s, x, lengths, weights, waves, back, gathered):
    gathers = gathered is not None
    count, width = x.shape[-2:]
    length = waves.shape[1]
    chans, half = width // 4, width // 2
    knots, dp_count = chans // 4, lax.axis_size("dp")
    pack_shape = (2, dp_count, width // dp_count, half)
    pack = jax.ShapeDtypeStruct(pack_shape, low)
    vm, dma = pltpu.VMEM, pltpu.SemaphoreType.DMA
    outs = [
        ((length, width), low),
        ((length, 3 * chans), low),
        ((length, 3 * chans), low),
        ((length, chans), low),
        ((2 * length, chans), low),
        ((length, chans), f32),
        ((length, chans), low),
        ((count, width), f32),
    ]
    more = []
    if gathers:
        cotangent, embedding = gathered
        depth = weights[0].shape[0]
        units = 2 * half
        ff_shape = (2, dp_count, 2 * width // dp_count, half)
        half_in = 3 * chans // 2
        filters = [((2 * length, chans), f32), *[((length, knots), f32)] * 4]
        outs = [
            (pack_shape, low),
            (ff_shape, low),
            ((length, width), low),
            ((2, 8, width), f32),
            ((2, 160, chans), f32),
            (pack_shape, low),
            (ff_shape[2:], low),
            *filters,
            *filters,
            ((length, width), low),
            ((length, units), low),
            ((length, units), low),
            ((count, width), f32),
        ] + outs
        more = [
            *[vm((length, knots), f32)] * 4,
            vm((length, chans), low),
            vm((*pack_shape[:3], half // 4), low),
            vm(ff_shape, low),
            vm((length, width), low),
            vm(pack_shape, low),
            *[dma((2, 4)), dma((2, 3))] * 4,
            dma((2, 6)),
            dma((15,)),
            vm((2, *pack_shape[2:]), low),
            vm((2, *ff_shape[2:]), low),
            vm((2, 8, width), f32),
            vm((2, 160, chans), f32),
            vm((2, 4, depth, half_in), low),
            vm((2, 4 * depth, half_in // 3), low),
            vm((2, 4, depth, half), low),
            dma((2, 7)),
            dma((2, 1)),
            dma((2, 7)),
            dma((2, 1)),
            dma((2, 1)),
            dma((2, 1)),
            vm((length, width), low),
            *exchange_scratch(count, width),
            dma((2, 6)),
            dma((2, 10)),
            dma((5,)),
        ]
        operands = (cotangent, embedding, lengths, *weights, waves, back)
        inside = range(len(operands) - 1)
        out_inside = (len(outs) - 9, len(outs) - 1)
    else:
        par, small, weights, filt = weights
        operands = (par, small, lengths, weights, filt, waves, back)
        inside = range(3)
        out_inside = (len(outs) - 1,)
    return run_kernel(
        partial(mixer_forward_kernel, s, gathers),
        "opening" if gathers else "mixer_forward",
        1 + s,
        (x, *operands),
        inside,
        outs,
        out_inside,
        [vm((length, width), low)]
        + mixer_weights_scratch(pack, width)
        + [
            vm((2 * length, chans), f32),
            vm((2 * length, length), low),
            vm((length, 2 * length), low),
            vm((length + 8, 3 * chans), f32),
            vm((length, 3 * chans), low),
            vm((length, 3 * chans), low),
            vm((length, chans), low),
            vm((2 * length, chans), low),
            vm((2 * length, chans), low),
            vm((length, chans), f32),
            vm((length, chans), low),
        ]
        + exchange_scratch(count, width)
        + semaphores(8, 7)
        + more,
        10**10,
    )


def ff_turn(s, cotangent, x, par, lengths, pack, late):
    count, width = x.shape
    _, dp_count, rows, half = pack.shape
    length, units = 4 * count, 2 * half
    vm = pltpu.VMEM
    return run_kernel(
        partial(ff_turn_kernel, s),
        "ff_turn",
        4,
        (cotangent, x, par, lengths, pack, late),
        range(3),
        [
            (pack.shape[1:], low),
            ((length, units), low),
            ((count, width), f32),
            ((2, width), f32),
        ],
        (2, 3),
        [vm((length, width), low)] * 2
        + [vm((2, dp_count, rows // 2, half), low)] * 2
        + [vm((length, units), low)] * 2
        + [vm(pack.shape, low), vm(pack.shape[1:], low)]
        + exchange_scratch(count, width)
        + semaphores(3, 2)
        + [pltpu.SemaphoreType.DMA((2, 2, 1))],
        3 * 10**10,
    )


def ff_backward(s, grad, middle, par, lengths, pack, second, value, slope, earlier):
    count, width = grad.shape
    _, dp_count, rows, half = pack.shape
    length, units = value.shape
    vm = pltpu.VMEM
    weights = [vm((2, dp_count, rows // 2, half), low)] * 2
    return run_kernel(
        partial(ff_backward_kernel, s),
        "ff_backward",
        5,
        (grad, middle, par, lengths, pack, second, value, slope, earlier),
        range(3),
        [
            (pack.shape[1:], low),
            ((count, width), f32),
            ((2, width), f32),
            (earlier.shape[1:], low),
        ],
        (1, 2, 3),
        [vm((length, width), low)]
        + weights
        + [vm((length, width), low)]
        + [vm((length, units), low)] * 3
        + [vm(pack.shape, low), vm(pack.shape[1:], low)]
        + exchange_scratch(count, width)
        + semaphores(5, 1)
        + plane_sum_scratch(earlier)
        + [pltpu.SemaphoreType.DMA((2, 2, 1))],
        2 * 10**10,
    )


def mixer_backward(
    s, grad, x, par, small, embedding, late, lengths, pack, waves, back, kept, earlier
):
    normed, proj, streams, prod, spec, filtered, gated, filt, *network = kept
    count, width = grad.shape
    length, chans = prod.shape
    knots = network[0].shape[1]
    vm = pltpu.VMEM
    weights = mixer_weights_scratch(pack, width)
    return run_kernel(
        partial(mixer_backward_kernel, s),
        "mixer_backward",
        7 + s,
        (grad, x, par, small, embedding, late, lengths, pack, filt, waves, back, normed, proj,
         streams, prod, spec, filtered, gated, *network, earlier),
        range(6),
        [
            (pack.shape[1:], low),
            (small.shape[1:], f32),
            ((count, width), f32),
            (earlier.shape[1:], low),
        ],
        (1, 2, 3),
        [vm((length, width), low)]
        + weights
        + [
            vm((2 * length, chans), f32),
            vm((2 * length, length), low),
            vm((length, 2 * length), low),
            vm((length, width), low),
            vm((length, 3 * chans), low),
            vm((length, 3 * chans), low),
            vm((length, chans), low),
            vm((2 * length, chans), low),
            vm((length, chans), f32),
            vm((length, chans), low),
            vm((length, chans), low),
            vm((length, chans), low),
            vm((2 * length, chans), low),
            vm((2 * length, chans), low),
            vm((2 * length, chans), f32),
            vm((length, chans), f32),
            vm((length + 8, 3 * chans), f32),
            vm((length, 3 * chans), low),
        ]
        + weights
        + [vm(item.shape[1:], low) for item in weights]
        + [vm((length, knots), f32)] * 4
        + [vm((2, width), f32), vm((24, 3 * chans), f32)]
        + exchange_scratch(count, width)
        + semaphores(19, 5)
        + plane_sum_scratch(earlier)
        + [pltpu.SemaphoreType.DMA((2, 2))],
        2 * 10**10,
    )


def shuffle_stage(w_in, w_out, w_up, stage_in, stage_out, stage_up):
    depth, chans = w_in.shape[0], w_out.shape[1] // 4
    count = lax.axis_size("dp")
    half_in = stage_in.shape[3]
    piece = chans // count
    for h in range(2):
        for j in range(4):
            for c in range(0, half_in, 2 * piece):
                pair = []
                for col in (c, c + piece):
                    g, d = divmod((h * half_in + col) // piece, count)
                    at = ((g * count + d) * 4 + j) * piece
                    pair.append(w_in[:, at : at + piece].astype(f32))
                stage_in[h, j, :, c : c + 2 * piece] = jnp.concatenate(pair, 1).astype(low)
            for d in range(2):
                at = ((2 * h + d) * 4 + j) * chans
                stage_up[h, j, :, d * chans : (d + 1) * chans] = w_up[:, at : at + chans]
    part = half_in // 3
    for h in range(2):
        for q in range(4):
            at = (h * 4 + q) * part
            stage_out[h, q * depth : (q + 1) * depth, :] = w_out[:, at : at + part]


def parameters_stage(me, par, small, gain, shift, taps, first, second, last, direct, rates):
    chans = small.shape[1]
    count = lax.axis_size("dp")
    piece = chans // count
    width = last.shape[2]
    par[0:1, :] = gain[0, 0:1, :]
    par[1:2, :] = shift[0, 0:1, :]
    par[2:3, :] = gain[0, 1:2, :]
    par[3:4, :] = shift[0, 1:2, :]
    par[4:8, :] = jnp.zeros((4, width), f32)
    small[64:160, :] = jnp.zeros((96, chans), f32)
    small[64:128, 0:64] = second[0]
    for row in range(first.shape[0]):
        small[64 + row : 65 + row, 128:192] = first[row]
    for j in range(4):

        @pl.when(me == j)
        def _():
            for d in range(0, count, 2):
                cols = slice(d * piece, (d + 2) * piece)

                def picked(ref, rows, base=0):
                    at = [base + ((d + k) * 4 + j) * piece for k in range(2)]
                    return jnp.concatenate([ref[rows, a : a + piece] for a in at], 1)

                small[0:64, cols] = picked(last.at[0], slice(0, 64))
                for g in range(3):
                    for tap in range(3):
                        row = 144 + 3 * g + tap
                        small[row : row + 1, cols] = picked(
                            taps.at[tap], slice(0, 1), g * width
                        )
                small[153:154, cols] = picked(direct, slice(0, 1))
                small[154:155, cols] = picked(rates, slice(0, 1))


def shuffle_send(section, me, targets, sources, parts, parameters, sems):
    stage_in, stage_out, stage_up, w_down = sources
    mixer_parts, ff_parts = parts
    in_sems, out_sems, up_sems, down_sems, par_sems, small_sems = sems
    depth, half_in = stage_in.shape[2:]
    half = stage_up.shape[3]
    copies = [
        remote_to(item.at[section], item.at[section], at, 0, other_core())
        for item, at in zip(parameters, (par_sems, small_sems))
    ]
    for e, (t, seq, device) in enumerate(targets):
        target = mixer_parts.at[section, rows_of(me, depth), pl.ds(0, half_in)]
        copies.append(remote_to(stage_in.at[t, seq], target, in_sems, e, device))
    target = mixer_parts.at[section, :, pl.ds(half_in, half_in // 3)]
    copies.append(remote_to(stage_out.at[1 - section], target, out_sems, 0, other_core()))
    for e, (t, seq, device) in enumerate(targets):
        target = ff_parts.at[section, rows_of(me, depth), :]
        copies.append(remote_to(stage_up.at[t, seq], target, up_sems, e, device))
    cols = pl.ds(pl.multiple_of((1 - section) * half, half), half)
    target = ff_parts.at[section, pl.ds(4 * depth, 4 * depth), :]
    copies.append(remote_to(w_down.at[:, cols], target, down_sems, 0, other_core()))
    for copy in copies:
        copy.start()
    mixer_parts[section, rows_of(me, depth), 0:half_in] = stage_in[section, me]
    mixer_parts[section, :, half_in:] = stage_out[section]
    ff_parts[section, rows_of(me, depth), :] = stage_up[section, me]
    cols = pl.ds(pl.multiple_of(section * half, half), half)
    ff_parts[section, 4 * depth : 8 * depth, :] = w_down[:, cols]
    return copies


def shuffle_wait_mixer(section, me, targets, parts, stage_in, in_sems, out_sems):
    depth, half_in = stage_in.shape[2:]
    for e, (t, seq, device) in enumerate(targets):
        block = parts.at[t, rows_of(seq, depth), pl.ds(0, half_in)]
        remote_to(block, block, in_sems, e, device).wait_recv()
    block = parts.at[1 - section, :, pl.ds(half_in, half_in // 3)]
    remote_to(block, block, out_sems, 0, other_core()).wait_recv()


def shuffle_wait_ff(section, me, targets, parts, stage_up, up_sems, down_sems):
    depth = stage_up.shape[2]
    for e, (t, seq, device) in enumerate(targets):
        block = parts.at[t, rows_of(seq, depth), :]
        remote_to(block, block, up_sems, e, device).wait_recv()
    block = parts.at[1 - section, pl.ds(4 * depth, 4 * depth), :]
    remote_to(block, block, down_sems, 0, other_core()).wait_recv()


def shuffle_targets(section, me, peers):
    targets = [(section, peer, {"seq": peer}) for peer in peers]
    targets.append((1 - section, me, other_core()))
    targets += [(1 - section, peer, {**other_core(), "seq": peer}) for peer in peers]
    return targets


def finish_kernel(
    vec0, vec1, mixer0, mixer1, ff0, ff1, grad0, grad1, value_hbm, pack_hbm, x, out0, lengths,
    block_outputs, input_grads, got_in, got_out, got_up, got_down, vec_out,
    mine0, arrived0, plane_sems0, sum_sems0, mine1, arrived1, plane_sems1, sum_sems1,
    vec_other, vec_sum, vec_arrived, vec_all, stage_mixer, stage_ff, own_sems, load_sems,
    layer_sems, keep_sems, vec_core_sems, vec_sum_sems, vec_plane_sems, vec_seq_sems, in_sems, out_sems, up_sems, down_sems,
    send, recv, out1, reduce_sems, value, wdown, early_sems,
):
    section = lax.axis_index("section")
    me = lax.axis_index("seq")
    here, near, far = along_planes()
    planes = (near, far, (near + 2) % 4)
    peers = neighbours(me)
    depth, half_in = got_in.shape[2:]
    targets = shuffle_targets(section, me, peers)
    greeted = greet([device for _, _, device in targets] + [{"dp": plane} for plane in planes])
    inner = wdown.shape[2]
    early = fetch(
        [(value_hbm, value), (pack_hbm.at[:, :, pl.ds(inner, inner)], wdown)], early_sems
    )
    middle = mixer0.shape[2] // 2
    chunks = (pl.ds(0, middle), pl.ds(middle, middle))
    in_cols = (pl.ds(0, middle), pl.ds(middle, half_in - middle))

    def columns(e, at):
        t, seq, device = targets[e]
        return remote_to(
            stage_mixer.at[t, rows_of(seq, depth), in_cols[at]],
            got_in.at[section, me, :, in_cols[at]],
            in_sems,
            2 * e + at,
            device,
        )

    out_columns = remote_to(
        stage_mixer.at[1 - section, :, pl.ds(half_in, half_in // 3)], got_out.at[section], out_sems,
        0, other_core(),
    )

    def send_layer(s, at):
        for index in range(2):

            @pl.when(section == index)
            def _():
                for e in range(3) if index == s else range(3, 7):
                    columns(e, at).start()
                if at == 1 and index != s:
                    out_columns.start()

    all_here(greeted)
    for index, vec in enumerate((vec1, vec0)):

        @pl.when(section == index)
        def _():
            remote_to(vec, vec_other, vec_core_sems, 0, other_core()).start()

    sends = []
    count, width = x.shape

    def result_part(slot):
        rows = rows_of(me if slot is None else peers[slot], count)
        for h in range(2):
            cols = slice(h * width // 2, (h + 1) * width // 2)
            out = mm(value[rows, :], wdown[h].reshape(4 * inner, width // 2))
            if slot is None:
                out1[:, cols] = out
            else:
                send[slot, :, cols] = out.astype(low)
        return [] if slot is None else reduce_send(slot, send, recv, reduce_sems, peers)

    for load in early:
        load.wait()
    sends += result_part(2)
    vec_swap = remote_to(vec_other, vec_other, vec_core_sems, 0, other_core())
    vec_swap.wait_recv()
    sends.append(vec_swap)

    @pl.when(section == 0)
    def _():
        vec_sum[...] = vec0[...] + vec_other[...]

    @pl.when(section == 1)
    def _():
        vec_sum[...] = vec1[...] + vec_other[...]

    chunk = vec_sum.shape[0] // 4
    moves = [
        remote_to(
            vec_sum.at[rows_of(plane, chunk)], vec_arrived.at[slot], vec_sum_sems, slot,
            {"dp": plane},
        )
        for slot, plane in enumerate(planes)
    ]
    for copy in moves:
        copy.start()
    sends += moves
    plane_sums = [
        PlaneSum(mixer0.at[:, :, chunks[0]], mine0, arrived0, plane_sems0, sum_sems0),
        PlaneSum(mixer0.at[:, :, chunks[1]], mine1, arrived1, plane_sems1, sum_sems1),
    ]
    for plane_sum in plane_sums:
        plane_sum.begin()
    loads = fetch(
        [
            (ff0, stage_ff.at[0]),
            (ff1, stage_ff.at[1]),
            (mixer1, stage_mixer.at[1]),
        ],
        load_sems,
    )
    by_layer(True, ((grad0, grad1, input_grads),), layer_sems, keep_sems)
    sends += result_part(0)
    sends += result_part(1)
    for load in loads:
        load.wait()
    ups = []
    for e, (t, seq, device) in enumerate(targets):
        ups.append(
            remote_to(
                stage_ff.at[t, rows_of(seq, depth), :], got_up.at[section, me], up_sems, e, device
            )
        )
    downs = [
        remote_to(
            stage_ff.at[1 - section, pl.ds(4 * depth, 4 * depth), :], got_down.at[section],
            down_sems, 0, other_core(),
        )
    ]
    for copy in ups + downs:
        copy.start()
    sends += ups + downs
    send_layer(1, 0)
    send_layer(1, 1)
    keeps = fetch(
        [
            (stage_ff.at[section, rows_of(me, depth), :], got_up.at[section, me]),
            (stage_ff.at[section, pl.ds(4 * depth, 4 * depth), :], got_down.at[section]),
        ],
        own_sems,
    )

    result_part(None)
    for copy in moves:
        copy.wait_recv()
    own_chunk = rows_of(here, chunk)
    total = vec_sum[own_chunk, :]
    for slot in range(len(planes)):
        total = total + vec_arrived[slot]
    vec_all[me, own_chunk, :] = total
    moves = [
        remote_to(
            vec_all.at[me, own_chunk], vec_all.at[me, own_chunk], vec_plane_sems, slot,
            {"dp": plane},
        )
        for slot, plane in enumerate(planes)
    ]
    for copy in moves:
        copy.start()
    sends += moves
    for plane_sum in plane_sums:
        plane_sum.forward()
    sends += reduce_pass(send, recv, reduce_sems, peers)
    for slot, plane in enumerate(planes):
        block = vec_all.at[me, rows_of(plane, chunk)]
        remote_to(block, block, vec_plane_sems, slot, {"dp": plane}).wait_recv()
    moves = [
        remote(vec_all.at[me], vec_all.at[me], vec_seq_sems, slot, peer)
        for slot, peer in enumerate(peers)
    ]
    for copy in moves:
        copy.start()
    sends += moves

    for at, plane_sum in enumerate(plane_sums):
        plane_sum.end(stage_mixer.at[0, :, chunks[at]])
        sends += plane_sum.sends
        send_layer(0, at)
    sends += [columns(e, at) for e in range(7) for at in range(2)] + [out_columns]
    reduce_wait(send, recv, reduce_sems, peers)
    add_parts(out1, recv, x, me * count, lengths)
    by_layer(True, ((out0, out1, block_outputs),), layer_sems, keep_sems, 1)
    keeps += fetch(
        [
            (
                stage_mixer.at[section, rows_of(me, depth), pl.ds(0, half_in)],
                got_in.at[section, me],
            ),
            (stage_mixer.at[section, :, pl.ds(half_in, half_in // 3)], got_out.at[section]),
        ],
        own_sems,
        2,
    )
    for slot, peer in enumerate(peers):
        block = vec_all.at[peer]
        remote(block, block, vec_seq_sems, slot, peer).wait_recv()
    keeps += fetch([(vec_all, vec_out)], own_sems, 4)
    for e, (t, seq, device) in enumerate(targets):
        block = got_up.at[t, seq]
        remote_to(block, block, up_sems, e, device).wait_recv()
        for at in range(2):
            block = got_in.at[t, seq, :, in_cols[at]]
            remote_to(block, block, in_sems, 2 * e + at, device).wait_recv()
    downs[0].wait_recv()
    out_columns.wait_recv()
    by_layer(False, ((grad0, grad1, input_grads),), layer_sems, keep_sems)
    by_layer(False, ((out0, out1, block_outputs),), layer_sems, keep_sems, 1)
    for copy in sends:
        copy.wait_send()
    for keep in keeps:
        keep.wait()


def unpack_kernel(
    blocks, grads, got_in, got_out, got_up, got_down, vec_all,
    block_outputs, input_grads, g_in, g_out, g_up, g_down, g_gain, g_bias, g_taps, g_first,
    g_second, g_last, g_direct,
    stage_blocks, stage_grads, load_sems, copy_sems,
):
    loads = fetch([(blocks, stage_blocks), (grads, stage_grads)], load_sems)
    depth = g_in.shape[0]
    half_in, half_up = got_in.shape[3], got_up.shape[3]
    chans = vec_all.shape[2]
    count = 4
    piece = chans // count
    for j in range(4):
        for d in range(count):
            at = (d * 4 + j) * chans
            h, col = divmod(d * chans, half_up)
            g_up[:, at : at + chans] = got_up[h, j, :, col : col + chans].astype(f32)
    for h in range(2):
        g_down[:, h * half_up : (h + 1) * half_up] = got_down[h].astype(f32)
    for load in loads:
        load.wait()
    copies = fetch([(stage_blocks, block_outputs), (stage_grads, input_grads)], copy_sems)
    for g in range(3):
        for d in range(count):
            h, col = divmod(g * chans + d * piece, half_in)
            for j in range(0, 4, 2):
                at = ((g * count + d) * 4 + j) * piece
                g_in[:, at : at + 2 * piece] = jnp.concatenate(
                    [got_in[h, j + k, :, col : col + piece].astype(f32) for k in range(2)], 1
                )
    part = half_in // 3
    for h in range(2):
        for q in range(4):
            at = (h * 4 + q) * part
            g_out[:, at : at + part] = got_out[h, q * depth : (q + 1) * depth, :].astype(f32)
    first = sum_of(vec_all, slice(64, 64 + g_first.shape[0]), slice(128, 192))
    for row in range(g_first.shape[0]):
        g_first[row] = first[row : row + 1]
    g_second[...] = sum_of(vec_all, slice(64, 128), slice(0, 64))
    for q in range(4):
        cols = slice(q * chans, (q + 1) * chans)
        early = sum_of(vec_all, slice(128 + 2 * q, 130 + 2 * q), slice(None))
        late = sum_of(vec_all, slice(136 + 2 * q, 138 + 2 * q), slice(None))
        g_gain[0:1, cols] = early[0:1]
        g_gain[1:2, cols] = late[0:1]
        g_bias[0:1, cols] = early[1:2]
        g_bias[1:2, cols] = late[1:2]
    for d in range(count):
        cols = slice(d * piece, (d + 1) * piece)
        for j in range(0, 4, 2):
            at = (d * 4 + j) * piece
            pair = slice(at, at + 2 * piece)

            def joined(rows):
                return jnp.concatenate([vec_all[j, rows, cols], vec_all[j + 1, rows, cols]], 1)

            g_last[:, pair] = joined(slice(0, 64))
            for g in range(3):
                for tap in range(3):
                    row = 144 + 3 * g + tap
                    start = g * 4 * chans + at
                    g_taps[tap, :, start : start + 2 * piece] = joined(slice(row, row + 1))
            g_direct[:, pair] = joined(slice(153, 154))

    for copy in copies:
        copy.wait()


def sum_of(blocks, rows, cols):
    return (blocks[0, rows, cols] + blocks[1, rows, cols]) + (
        blocks[2, rows, cols] + blocks[3, rows, cols]
    )


def finish(
    vec0, vec1, mixer0, mixer1, ff0, ff1, grad0, grad1, value, pack, x, out0, lengths
):
    count, width = grad0.shape
    dp_count, rows, half = mixer0.shape
    depth = rows // 4
    chans = vec0.shape[1]
    half_in = 3 * chans // 2
    vm, dma = pltpu.VMEM, pltpu.SemaphoreType.DMA
    vec_rows = vec0.shape[0]
    chunk = jax.ShapeDtypeStruct((dp_count, rows, half // 2), low)
    return run_kernel(
        finish_kernel,
        "finish",
        10,
        (vec0, vec1, mixer0, mixer1, ff0, ff1, grad0, grad1, value, pack, x, out0, lengths),
        (0, 1, 6, 7, 10, 11),
        [
            ((2, count, width), f32),
            ((2, count, width), f32),
            ((2, 4, depth, half_in), low),
            ((2, rows, half_in // 3), low),
            ((2, 4, depth, half), low),
            ((2, rows, half), low),
            ((4, vec_rows, chans), f32),
        ],
        (),
        plane_sum_scratch(chunk)
        + plane_sum_scratch(chunk)
        + [
            vm((vec_rows, chans), f32),
            vm((vec_rows, chans), f32),
            vm((3, vec_rows // 4, chans), f32),
            vm((4, vec_rows, chans), f32),
            vm((2, *mixer1.shape), low),
            vm((2, *ff1.shape), low),
            dma((5,)),
            dma((3,)),
            *exchange_semaphores(2),
            dma((2, 1)),
            dma((2, 3)),
            dma((2, 3)),
            dma((2, 3)),
            dma((2, 14)),
            dma((2, 1)),
            dma((2, 7)),
            dma((2, 1)),
            *exchange_scratch(count, width),
            vm((count, width), f32),
            dma((2, 10)),
            vm(value.shape, low),
            vm((*pack.shape[:2], pack.shape[2] // 2, pack.shape[3]), low),
            dma((2,)),
        ],
        10**9,
    )


def unpack(blocks, grads, got, first_shape):
    width = blocks.shape[2]
    depth = got[0].shape[2]
    units = 4 * 2 * got[2].shape[3]
    knots = first_shape[1]
    inside = pl.BlockSpec(memory_space=pltpu.VMEM)
    outside = pl.BlockSpec(memory_space=pl.ANY)
    shapes = (
        blocks.shape, grads.shape, (depth, 3 * width), (depth, width), (depth, units),
        (4 * depth, width), (2, width), (2, width), (3, 1, 3 * width),
        (first_shape[0], 1, knots), (knots, knots),
        (knots, width), (1, width),
    )
    return pl.pallas_call(
        unpack_kernel,
        out_shape=[jax.ShapeDtypeStruct(shape, f32) for shape in shapes],
        in_specs=[outside] * 2 + [inside] * 5,
        out_specs=[outside] * 2 + [inside] * 11,
        scratch_shapes=[
            pltpu.VMEM(blocks.shape, f32),
            pltpu.VMEM(grads.shape, f32),
            pltpu.SemaphoreType.DMA((2,)),
            pltpu.SemaphoreType.DMA((2,)),
        ],
        compiler_params=pltpu.CompilerParams(vmem_limit_bytes=56 * 2**20),
        name="unpack",
    )(blocks, grads, *got)


def any_device(
    tokens,
    cotangent,
    lengths,
    norm_gain,
    norm_bias,
    mixer_in,
    short_kernel,
    filter_first,
    filter_second,
    filter_last,
    filter_bias,
    decay_rates,
    mixer_out,
    up_weight,
    down_weight,
):
    section = lax.axis_index("section")
    seq_index = lax.axis_index("seq")
    seq_count = lax.axis_size("seq")
    dp_count = lax.axis_size("dp")
    own_layer_first = section == 0
    local_len = tokens.shape[2]
    width = tokens.shape[3]
    hidden = up_weight.shape[2]
    row_len = local_len * seq_count
    chans = width // seq_count
    units = hidden // seq_count

    def share_columns(block, groups):
        rows = block.shape[0]
        inner = block.shape[1] // (groups * dp_count * seq_count)
        split = block.reshape(rows, groups, dp_count, seq_count, inner)
        split = jnp.transpose(split, (3, 0, 1, 2, 4))
        moved = lax.all_to_all(split, "seq", split_axis=0, concat_axis=0, tiled=True)
        return moved.reshape(seq_count * rows, groups * dp_count * inner)

    def unshare_columns(block, groups):
        rows = block.shape[0] // seq_count
        inner = block.shape[1] // (groups * dp_count)
        split = block.reshape(seq_count, rows, groups, dp_count, inner)
        moved = lax.all_to_all(split, "seq", split_axis=0, concat_axis=0, tiled=True)
        moved = jnp.transpose(moved, (1, 2, 3, 0, 4))
        return moved.reshape(rows, groups * dp_count * seq_count * inner)

    def gathered(block):
        whole = lax.all_gather(block, ("section", "dp"))
        return whole.reshape(2, dp_count * block.shape[0], block.shape[1])

    weights = (
        gathered(share_columns(mixer_in[0], 3)),
        gathered(mixer_out[0]),
        gathered(share_columns(up_weight[0], 1)),
        gathered(down_weight[0]),
    )

    def both(value):
        return lax.all_gather(value[0], "section")

    gains, shifts = both(norm_gain), both(norm_bias)
    taps, first_w, second_w = both(short_kernel), both(filter_first), both(filter_second)
    last_w, direct, rates = both(filter_last), both(filter_bias), both(decay_rates)

    def mine(value):
        lead = value.shape[:-1]
        split = value.reshape(*lead, dp_count, seq_count, -1)
        picked = lax.dynamic_index_in_dim(split, seq_index, len(lead) + 1, False)
        return picked.reshape(*lead, chans)

    def placed(value):
        lead = value.shape[:-1]
        split = value.reshape(*lead, dp_count, 1, -1)
        inner = split.shape[-1]
        empty = jnp.zeros((*lead, dp_count, seq_count, inner), value.dtype)
        at = [0] * len(lead) + [0, seq_index, 0]
        return lax.dynamic_update_slice(empty, split, at).reshape(*lead, width)

    waves = jnp.asarray(wave_tables(row_len))
    waves_back = waves

    def to_waves(x):
        both_parts = mm(waves, x)
        return both_parts[:row_len], both_parts[row_len:]

    def from_waves(cos_part, sin_part):
        joined = jnp.concatenate([cos_part, sin_part], 0).astype(low)
        return t_mm(waves_back, joined) * (1.0 / row_len)

    def ag(x):
        return lax.all_gather(x, "seq", axis=0, tiled=True)

    def rs(x):
        return lax.psum_scatter(x.astype(low), "seq", scatter_dimension=0, tiled=True).astype(f32)

    length_now = lax.dynamic_index_in_dim(lengths, section, 0, False)[0]
    positions = seq_index * local_len + jnp.arange(local_len)
    mask = (positions < length_now).astype(f32)[:, None]
    row_mask = (jnp.arange(row_len) < length_now).astype(f32)[:, None]
    own_tokens = lax.dynamic_index_in_dim(tokens, section, 0, False)[0].astype(f32)
    own_cotangent = lax.dynamic_index_in_dim(cotangent, section, 0, False)[0].astype(f32)

    def layer_forward(s, inputs):
        w_in, w_out, w_up, w_down = [w[s] for w in weights]
        kernel = mine(taps[s].reshape(3, 3, width))
        last_mine, direct_mine, rates_mine = mine(last_w[s]), mine(direct[s]), mine(rates[s])

        def own_filter(a, b, c):
            return filter_taps(a, b, c, rates_mine, row_len)

        filter_rows, filter_back = jax.vjp(own_filter, first_w[s], second_w[s], last_mine)
        filt_cos, filt_sin = to_waves(filter_rows.astype(low))
        normed = (norm_stats(inputs)[0] * gains[s, 0] + shifts[s, 0]).astype(low)
        normed = ag(normed)
        projected = [mm(normed, w_in[:, g * chans : (g + 1) * chans]) for g in range(3)]
        streams = [
            (
                kernel[0, g] * projected[g]
                + kernel[1, g] * shifted(projected[g], 1)
                + kernel[2, g] * shifted(projected[g], 2)
            ).astype(low)
            for g in range(3)
        ]
        wide = [x.astype(f32) for x in streams]
        product = (wide[0] * wide[2] * row_mask).astype(low)
        prod_cos, prod_sin = to_waves(product)
        filtered = from_waves(
            prod_cos * filt_cos - prod_sin * filt_sin, prod_cos * filt_sin + prod_sin * filt_cos
        ) + direct_mine * product.astype(f32)
        gated = (wide[1] * filtered).astype(low)
        middle = inputs + mask * rs(mm(gated, w_out))
        second = (norm_stats(middle)[0] * gains[s, 1] + shifts[s, 1]).astype(low)
        second = ag(second)
        value, slope = gelu_both(mm(second, w_up))
        value = value.astype(low)
        slope = slope.astype(low)
        result = middle + mask * rs(mm(value, w_down))
        saved = (
            inputs, normed, projected, wide, product, prod_cos, prod_sin, filt_cos, filt_sin,
            filtered, gated, middle, second, value, slope, kernel, direct_mine, filter_back,
        )
        return result, saved

    def layer_backward(s, grad, saved):
        w_in, w_out, w_up, w_down = [w[s] for w in weights]
        (
            inputs, normed, projected, wide, product, prod_cos, prod_sin, filt_cos, filt_sin,
            filtered, gated, middle, second, value, slope, kernel, direct_mine, filter_back,
        ) = saved
        out_low = ag((grad * mask).astype(low))
        pre = (mm_t(out_low, w_down) * slope.astype(f32)).astype(low)
        grad_down = t_mm(value, out_low)
        grad_up = t_mm(second, pre)
        mid_part, gain_late, bias_late = norm_back(rs(mm_t(pre, w_up)), middle, gains[s, 1])
        middle_grad = grad + mid_part
        branch = ag((middle_grad * mask).astype(low))
        gated_grad = mm_t(branch, w_out).astype(low)
        grad_out = t_mm(gated, branch)
        gated_grad = gated_grad.astype(f32)
        filtered_grad = (gated_grad * wide[1]).astype(low)
        fg_cos, fg_sin = to_waves(filtered_grad)
        fg_wide = filtered_grad.astype(f32)
        prod32 = product.astype(f32)
        product_grad = from_waves(
            filt_cos * fg_cos + filt_sin * fg_sin, filt_cos * fg_sin - filt_sin * fg_cos
        ) + direct_mine * fg_wide
        product_grad = product_grad.astype(low).astype(f32)
        filter_grad = from_waves(
            prod_cos * fg_cos + prod_sin * fg_sin, prod_cos * fg_sin - prod_sin * fg_cos
        )
        grad_first, grad_second, grad_last = filter_back(filter_grad)
        grad_direct = jnp.sum(fg_wide * prod32, 0)
        mixed = [
            (product_grad * wide[2]).astype(low).astype(f32),
            (gated_grad * filtered).astype(low).astype(f32),
            (product_grad * wide[0]).astype(low).astype(f32),
        ]
        proj = [
            (
                kernel[0, g] * mixed[g]
                + kernel[1, g] * shifted(mixed[g], -1)
                + kernel[2, g] * shifted(mixed[g], -2)
            ).astype(low)
            for g in range(3)
        ]
        grad_taps = jnp.stack(
            [
                jnp.stack(
                    [jnp.sum(mixed[g] * (shifted(projected[g], k) if k else projected[g]), 0) for g in range(3)]
                )
                for k in range(3)
            ]
        )
        proj = jnp.concatenate(proj, 1)
        grad_in = t_mm(normed, proj)
        in_part, gain_early, bias_early = norm_back(rs(mm_t(proj, w_in)), inputs, gains[s, 0])
        small = (
            jnp.stack([gain_early, gain_late]),
            jnp.stack([bias_early, bias_late]),
            placed(grad_taps).reshape(3, 3 * width),
            grad_first,
            grad_second,
            placed(grad_last),
            placed(grad_direct),
        )
        large = (grad_in, grad_out, grad_up, grad_down)
        return middle_grad + in_part, small, large

    first_out, first_saved = layer_forward(0, own_tokens)
    second_out, second_saved = layer_forward(1, first_out)
    second_grad, second_small, second_large = layer_backward(1, own_cotangent, second_saved)
    first_grad, first_small, first_large = layer_backward(0, second_grad, first_saved)

    swap = [(0, 1), (1, 0)]

    def by_layer(first, second):
        other = lax.ppermute(jnp.where(own_layer_first, second, first), "section", swap)
        return jnp.where(
            own_layer_first, jnp.stack([first, other]), jnp.stack([other, second])
        )[None, :, None]

    def summed(first, second):
        stacked = jnp.stack([first, second]).astype(low)
        rows = first.shape[0] // dp_count
        stacked = stacked.reshape(2 * dp_count, rows, first.shape[1])
        return lax.psum_scatter(stacked, ("section", "dp"), scatter_dimension=0, tiled=True)[0]

    sums = [summed(a, b) for a, b in zip(first_large, second_large)]
    sum_in = unshare_columns(sums[0], 3).astype(f32)
    sum_out = sums[1].astype(f32)
    sum_up = unshare_columns(sums[2], 1).astype(f32)
    sum_down = sums[3].astype(f32)
    stacked = jax.tree.map(lambda a, b: jnp.stack([a, b]), first_small, second_small)
    small = lax.psum(stacked, ("section", "dp", "seq"))
    small = [lax.dynamic_slice_in_dim(x, section, 1, 0) for x in small]
    sum_gain, sum_bias, sum_taps, sum_first, sum_second, sum_last, sum_direct = small
    return (
        by_layer(first_out, second_out),
        by_layer(first_grad, second_grad),
        sum_gain,
        sum_bias,
        sum_in[None],
        sum_taps,
        sum_first,
        sum_second,
        sum_last,
        sum_direct,
        sum_out[None],
        sum_up[None],
        sum_down[None],
    )


def plane_device(
    tokens,
    cotangent,
    lengths,
    norm_gain,
    norm_bias,
    mixer_in,
    short_kernel,
    filter_first,
    filter_second,
    filter_last,
    filter_bias,
    decay_rates,
    mixer_out,
    up_weight,
    down_weight,
):
    section = lax.axis_index("section")
    seq_count = lax.axis_size("seq")
    dp_count = lax.axis_size("dp")
    row_len = tokens.shape[2] * seq_count
    lengths = jnp.transpose(lengths)
    short_kernel = jnp.transpose(short_kernel, (1, 0, 2))
    filter_first = jnp.transpose(filter_first, (1, 0, 2))

    def gathered(part):
        whole = lax.all_gather(part, ("section", "dp"))
        return whole.reshape(2, dp_count, *part.shape)

    tables = wave_tables(row_len)
    waves = jnp.asarray(tables)
    waves_back = jnp.asarray(np.ascontiguousarray(tables.T))
    embedding = jnp.asarray(np.pad(position_rows(row_len), ((0, 0), (0, 95))))

    weights = (
        mixer_in[0], mixer_out[0], up_weight[0], down_weight[0], norm_gain, norm_bias, short_kernel,
        filter_first, filter_second, filter_last, filter_bias, decay_rates,
    )
    (
        first_mixer_pack, first_ff_pack, cotangent_low, par, small, second_mixer_pack, ff_part,
        *outs,
    ) = mixer_forward(
        0, tokens, lengths, weights, waves, waves_back, (cotangent, embedding)
    )
    first_filter, second_filter, first_saved, outs = outs[:5], outs[5:10], outs[10:13], outs[13:]
    first_out, *first_kept, first_middle = outs
    second_ff_pack = gathered(ff_part)
    *second_kept, second_middle = mixer_forward(
        1, first_out, lengths, (par, small, second_mixer_pack, second_filter[0]), waves, waves_back,
        None,
    )
    first_kept, second_kept = [*first_kept, *first_filter], [*second_kept, *second_filter]
    second_ff, second_value, middle_grad, late = ff_turn(
        1, cotangent, second_middle, par, lengths, second_ff_pack, cotangent_low
    )

    def mixer_back(s, grad, x, late, pack, kept, earlier):
        return mixer_backward(
            s, grad, x, par, small, embedding, late, lengths, pack, waves, waves_back, kept, earlier
        )

    second_mixer, second_vec, second_grad, second_ff = mixer_back(
        1, middle_grad, first_out, late, second_mixer_pack, second_kept, second_ff
    )
    first_ff, middle_grad, late, second_mixer = ff_backward(
        0, second_grad, first_middle, par, lengths, first_ff_pack, *first_saved, second_mixer
    )
    first_mixer, first_vec, first_grad, first_ff = mixer_back(
        0, middle_grad, tokens, late, first_mixer_pack, first_kept, first_ff
    )
    block_outputs, input_grads, *got = finish(
        first_vec, second_vec, first_mixer, second_mixer, first_ff, second_ff, first_grad,
        second_grad, second_value, second_ff_pack, second_middle, first_out, lengths,
    )
    (
        block_outputs, input_grads, sum_in, sum_out, sum_up, sum_down, sum_gain, sum_bias, sum_taps,
        sum_first, sum_second, sum_last, sum_direct,
    ) = unpack(block_outputs, input_grads, got, filter_first.shape[::2])
    return (
        block_outputs[None, :, None],
        input_grads[None, :, None],
        sum_gain[None],
        sum_bias[None],
        sum_in[None],
        jnp.transpose(sum_taps, (1, 0, 2)),
        jnp.transpose(sum_first, (1, 0, 2)),
        sum_second[None],
        sum_last[None],
        sum_direct,
        sum_out[None],
        sum_up[None],
        sum_down[None],
    )


def solution(mesh):
    in_specs = (
        P(None, "dp", "seq", None),
        P(None, "dp", "seq", None),
        P(None, "dp"),
        P("section", None, None),
        P("section", None, None),
        P("section", ("dp", "seq"), None),
        P("section", None, None),
        P("section", None, None),
        P("section", None, None),
        P("section", None, None),
        P("section", None),
        P("section", None),
        P("section", ("dp", "seq"), None),
        P("section", ("dp", "seq"), None),
        P("section", ("dp", "seq"), None),
    )
    out_specs = (
        P("section", None, "dp", "seq", None),
        P("section", None, "dp", "seq", None),
        P("section", None, None),
        P("section", None, None),
        P("section", ("dp", "seq"), None),
        P("section", None, None),
        P("section", None, None),
        P("section", None, None),
        P("section", None, None),
        P("section", None),
        P("section", ("dp", "seq"), None),
        P("section", ("dp", "seq"), None),
        P("section", ("dp", "seq"), None),
    )
    planes = mesh.shape["seq"] == 4 and mesh.shape["dp"] == 4
    per_device = plane_device if planes else any_device
    return jax.shard_map(
        per_device, mesh=mesh, in_specs=in_specs, out_specs=out_specs, check_vma=False
    )
```
